32 devices in a mesh: dp: 8 (over z, y), mp: 4 (over x, core).
Axes of the slice: x: 2, y: 2, z: 4, core: 2. Of those that a mesh axis runs over, the one named last changes fastest.
Arguments:
- block_input: bfloat16 [8, 1024, 1024], P('dp')
- segment_ids: int32 [8, 1024], P('dp'), may hold values from 0 to 7, never falling along the last dimension, each value on 1 to 512 neighbouring positions
- live_length: int32 [8], P('dp'), may hold values from 256 to 1024, as said below
- output_grad: bfloat16 [8, 1024, 1024], P('dp'), may hold values from -6 to 6
- mixer_weight: float32 [5, 1024, 1024], P(None, 'dp'), may hold values from -0.1875 to 0.1875
- mixer_momentum: float32 [5, 1024, 1024], P(None, 'dp'), may hold values from -0.00390625 to 0.00390625
- mixer_shadow: float32 [5, 1024, 1024], P(None, 'dp'), may hold values from -0.1875 to 0.1875
- expand_weight: float32 [2, 1024, 2816], P(None, 'dp', 'mp'), may hold values from -0.1875 to 0.1875
- expand_momentum: float32 [2, 1024, 2816], P(None, 'dp', 'mp'), may hold values from -0.00390625 to 0.00390625
- expand_shadow: float32 [2, 1024, 2816], P(None, 'dp', 'mp'), may hold values from -0.1875 to 0.1875
- shrink_weight: float32 [2816, 1024], P('mp', 'dp')
- shrink_momentum: float32 [2816, 1024], P('mp', 'dp'), may hold values from -0.00390625 to 0.00390625
- shrink_shadow: float32 [2816, 1024], P('mp', 'dp'), may hold values from -0.109375 to 0.109375
Outputs:
- block_output: bfloat16 [8, 1024, 1024], P('dp')
- input_grad: bfloat16 [8, 1024, 1024], P('dp')
- global_norm: float32 [], replicated
- mixer_velocity: float32 [5, 1024, 1024], P(None, 'dp')
- mixer_average: float32 [5, 1024, 1024], P(None, 'dp')
- mixer_updated: float32 [5, 1024, 1024], P(None, 'dp')
- expand_velocity: float32 [2, 1024, 2816], P(None, 'dp', 'mp')
- expand_average: float32 [2, 1024, 2816], P(None, 'dp', 'mp')
- expand_updated: float32 [2, 1024, 2816], P(None, 'dp', 'mp')
- shrink_velocity: float32 [2816, 1024], P('mp', 'dp')
- shrink_average: float32 [2816, 1024], P('mp', 'dp')
- shrink_updated: float32 [2816, 1024], P('mp', 'dp')
The draws below stay inside these ranges and needn't reach their ends.
Inputs may be any that keep to these rules, and one draw needn't show every extreme that they name: `segment_ids`: within a row, document numbers never fall; a document covers 1 to 512 positions. `live_length`: row 0 holds no padding.
All inputs are finite; a program needn't handle non-finite values.
Results may differ from the reference program's by a relative error of at most 0.015.
Values may be sent and summed in bfloat16 or wider, within the bound.
A program may use at most 256 MiB of HBM per device.

```python
import math
from functools import partial
import jax
import jax.numpy as jnp
import numpy as np
from jax import lax

D = 1024
HEAD = 128
FF = 2816
SEQ = 1024
SEGMENTS = 8
ROWS = 8


def draw_block_input(key, part):
    key = jax.random.fold_in(key, 11)
    column = jnp.arange(D, dtype=jnp.float32) / D
    scale = 1.0 + 2.0 * column
    values = jax.random.normal(key, (ROWS, SEQ, D), jnp.float32)
    return (values * scale[None, None, :]).astype(jnp.bfloat16)


def draw_live_length(key, part):
    key = jax.random.fold_in(key, 23)
    lengths = jax.random.randint(key, (ROWS,), SEQ // 4, SEQ + 1)
    return jnp.where(jnp.arange(ROWS) == 0, SEQ, lengths).astype(jnp.int32)


def draw_shrink_weight(key, part):
    key = jax.random.fold_in(key, 37)
    row_place = jnp.arange(FF, dtype=jnp.float32) / FF
    scale = 1.0 + 2.0 * row_place
    values = jax.random.normal(key, (FF, D), jnp.float32)
    return (values * scale[:, None] * FF ** (-0.5)).astype(jnp.float32)


def steps_of(rng, extent, cuts, low, largest):
    loudness, own = 1.0, jax.random.fold_in(rng, 6)
    for position, blocks in cuts:
        steps = jnp.exp(jax.random.uniform(jax.random.fold_in(own, position), (blocks,), jnp.float32, low / len(cuts), largest / len(cuts)))
        loudness = loudness * jnp.repeat(steps, extent[position] // blocks).reshape([-1 if axis == position else 1 for axis in range(len(extent))])
    return loudness


def length_profile(count, total, reach, slope):
    portions = [(1 << 20) // math.isqrt(grade ** slope) + 1 for grade in range(2, count + 1)]
    spare, counts = total - reach - (count - 1), [1] * (count - 1)
    while spare > 0:
        candidates = [i for i in range(count - 1) if counts[i] < reach]
        mass, budget = sum([portions[i] for i in candidates]), spare
        for i in candidates:
            more = min(reach - counts[i], max(1, budget * portions[i] // mass), spare)
            counts[i] = counts[i] + more
            spare = spare - more
    return np.array([reach] + counts)


def ragged(key, number_of, total, limit, lean):
    if number_of == 2:
        one = jax.random.randint(key, (), max(1, total - limit), min(limit, total - 1) + 1)
        return jnp.stack([one, total - one])
    tallies = jnp.asarray(length_profile(number_of, total, limit, lean), jnp.int32)
    pairs = (number_of - 1) // 2
    giver, receiver = tallies[1:1 + 2 * pairs:2], tallies[2:2 + 2 * pairs:2]
    slack = jnp.minimum(giver - 1, limit - receiver)
    passed = jax.random.randint(jax.random.fold_in(key, 1), (pairs,), 0, 1 << 20) % (slack + 1)
    tallies = tallies.at[1:1 + 2 * pairs:2].set(giver - passed).at[2:2 + 2 * pairs:2].set(receiver + passed)
    return tallies[jax.random.permutation(jax.random.fold_in(key, 2), number_of)]


def normal_values(key, dims, spread, reach, cuts=(), kind=jnp.bfloat16):
    gain = steps_of(key, dims, cuts, -0.22, 0.18) if cuts else 1.0
    values = jax.random.normal(key, dims, jnp.float32) * spread * gain
    return jnp.minimum(jnp.maximum(values, -reach), reach).astype(kind)


def setup_inputs(seed: int = 0) -> dict:
    key_list = jax.random.split(jax.random.key(seed), 14)
    block_input = draw_block_input(jax.random.fold_in(key_list[13], 71), 0)
    segment_ids = jax.vmap(lambda own: jnp.searchsorted(jnp.cumsum(ragged(own, SEGMENTS, SEQ, SEQ // 2, 0)), jnp.arange(SEQ), side="right"))(jax.random.split(key_list[1], ROWS)).reshape((ROWS, SEQ)).astype(jnp.int32)
    live_length = draw_live_length(jax.random.fold_in(key_list[13], 71), 0)
    output_grad = normal_values(key_list[3], (ROWS, SEQ, D), 1.0, 6.0, ((0, 8),))
    mixer_weight = normal_values(key_list[4], (5, D, D), D ** -0.5, 0.1875, ((1, 8),), jnp.float32)
    mixer_momentum = normal_values(key_list[5], (5, D, D), ((5 * D * D + 3 * D * FF) ** -0.5), 0.00390625, ((1, 8),), jnp.float32)
    mixer_shadow = normal_values(key_list[6], (5, D, D), D ** -0.5, 0.1875, ((1, 8),), jnp.float32)
    expand_weight = normal_values(key_list[7], (2, D, FF), D ** -0.5, 0.1875, ((1, 8), (2, 4)), jnp.float32)
    expand_momentum = normal_values(key_list[8], (2, D, FF), ((5 * D * D + 3 * D * FF) ** -0.5), 0.00390625, ((1, 8), (2, 4)), jnp.float32)
    expand_shadow = normal_values(key_list[9], (2, D, FF), D ** -0.5, 0.1875, ((1, 8), (2, 4)), jnp.float32)
    shrink_weight = draw_shrink_weight(jax.random.fold_in(key_list[13], 71), 0)
    shrink_momentum = normal_values(key_list[11], (FF, D), ((5 * D * D + 3 * D * FF) ** -0.5), 0.00390625, ((0, 4), (1, 8)), jnp.float32)
    shrink_shadow = normal_values(key_list[12], (FF, D), FF ** -0.5, 0.109375, ((0, 4), (1, 8)), jnp.float32)
    return {"block_input": block_input, "segment_ids": segment_ids, "live_length": live_length, "output_grad": output_grad, "mixer_weight": mixer_weight, "mixer_momentum": mixer_momentum, "mixer_shadow": mixer_shadow, "expand_weight": expand_weight, "expand_momentum": expand_momentum, "expand_shadow": expand_shadow, "shrink_weight": shrink_weight, "shrink_momentum": shrink_momentum, "shrink_shadow": shrink_shadow}


EPSILON = 1e-06
LEARN_RATE = 32.0
MOMENTUM = 0.5
SHADOW_DECAY = 0.5
LAYER_PLACE = 12.0 / 24.0
PRECISE = lax.Precision.HIGHEST

@jax.custom_vjp
def low(v):
    return lax.optimization_barrier(v.astype(jnp.bfloat16)).astype(jnp.float32)

@jax.custom_vjp
def low_back(v):
    return v

def low_keep(v):
    return (low(v), None)

def low_pass(kept, grad):
    return (grad,)

def back_keep(v):
    return (v, None)

def back_low(kept, grad):
    return (low(grad),)
low.defvjp(low_keep, low_pass)
low_back.defvjp(back_keep, back_low)

def norm_rows(values):
    return values * lax.rsqrt(lax.optimization_barrier(jnp.mean(values * values, axis=-1, keepdims=True)) + EPSILON)

def swish(values):
    return values * jax.nn.sigmoid(values)

def head_rates(heads):
    index = jnp.arange(heads, dtype=jnp.float32)
    return -(8.0 * index / heads) * (1.0 - LAYER_PLACE)

def relative_turn(values, positions, width):
    theta = 10000.0 ** (-jnp.arange(width, dtype=jnp.float32) / width)
    angle = positions.astype(jnp.float32)[:, None] * theta[None, :]
    return jnp.concatenate([values * jnp.cos(angle)[:, None, :], values * jnp.sin(angle)[:, None, :]], axis=-1)

def mixer_dense(segment, live, query_pre, key_pre, values):
    heads = D // HEAD
    rates = head_rates(heads)
    positions = jnp.arange(SEQ)
    query_rot = low(relative_turn(swish(query_pre).reshape(SEQ, heads, HEAD), positions, HEAD))
    key_rot = low(relative_turn(swish(key_pre).reshape(SEQ, heads, HEAD), positions, HEAD))
    value_heads = values.reshape(SEQ, heads, HEAD)
    offset = positions[:, None] - positions[None, :]
    allowed = (offset >= 0) & (segment[:, None] == segment[None, :])
    decay = jnp.exp(rates[:, None, None] * jnp.maximum(offset, 0).astype(jnp.float32)[None])
    decay = jnp.where(allowed[None], decay, 0.0) * live[None, :, None] * live[None, None, :]
    scores = jnp.einsum('the,she->hts', query_rot, key_rot, precision=PRECISE) * decay
    return jnp.einsum('hts,she->the', scores, value_heads, precision=PRECISE).reshape(SEQ, D)

def layer_row(segment, live, row_in, mixer_w, expand_w, shrink_w):
    mixer_low = low(mixer_w)
    expand_low = low(expand_w)
    shrink_low = low(shrink_w)
    normed_in = low(norm_rows(row_in))
    query_pre = low_back(jnp.dot(normed_in, mixer_low[0], precision=PRECISE))
    key_pre = low_back(jnp.dot(normed_in, mixer_low[1], precision=PRECISE))
    value_in = low(low_back(jnp.dot(normed_in, mixer_low[2], precision=PRECISE)))
    gate_pre = low_back(jnp.dot(normed_in, mixer_low[3], precision=PRECISE))
    mixed = jax.checkpoint(mixer_dense)(segment, live, query_pre, key_pre, value_in)
    gated = low(norm_rows(mixed) * gate_pre)
    mixer_out = low_back(jnp.dot(gated, mixer_low[4], precision=PRECISE))
    hidden = row_in + mixer_out
    normed_mid = low(norm_rows(hidden))
    gate_act = low_back(jnp.dot(normed_mid, expand_low[0], precision=PRECISE))
    up_act = low_back(jnp.dot(normed_mid, expand_low[1], precision=PRECISE))
    product = low(gate_act * up_act)
    expand_out = low_back(jnp.dot(product, shrink_low, precision=PRECISE))
    return hidden + expand_out

def renew(weight, momentum, shadow, grad, clip_factor):
    clipped = grad * clip_factor
    velocity = MOMENTUM * momentum + clipped
    updated = weight - LEARN_RATE * (clipped + MOMENTUM * velocity)
    average = SHADOW_DECAY * shadow + (1.0 - SHADOW_DECAY) * updated
    return (velocity, average, updated)

def reference(block_input, segment_ids, live_length, output_grad, mixer_weight, mixer_momentum, mixer_shadow, expand_weight, expand_momentum, expand_shadow, shrink_weight, shrink_momentum, shrink_shadow):
    positions = jnp.arange(SEQ)
    live = (positions[None, :] < live_length[:, None]).astype(jnp.float32)
    inputs = block_input.astype(jnp.float32)
    upstream = output_grad.astype(jnp.float32) * live[:, :, None]
    weights = (mixer_weight, expand_weight, shrink_weight)

    def per_row(carry, pieces):
        row_in, row_segment, row_live, row_upstream = pieces
        result, pull = jax.vjp(partial(layer_row, row_segment, row_live), row_in, *weights)
        grads = pull(row_upstream)
        return (jax.tree.map(jnp.add, carry, tuple(grads[1:])), (result, grads[0]))
    start = tuple((jnp.zeros_like(weight) for weight in weights))
    totals, (results, input_grads) = lax.scan(per_row, start, (inputs, segment_ids, live, upstream))
    grad_mixer, grad_expand, grad_shrink = totals
    squares = jnp.sum(grad_mixer * grad_mixer) + jnp.sum(grad_expand * grad_expand) + jnp.sum(grad_shrink * grad_shrink)
    global_norm = jnp.sqrt(squares)
    clip_factor = 1.0 / jnp.maximum(global_norm, 1.0)
    mixer_new = renew(mixer_weight, mixer_momentum, mixer_shadow, grad_mixer, clip_factor)
    expand_new = renew(expand_weight, expand_momentum, expand_shadow, grad_expand, clip_factor)
    shrink_new = renew(shrink_weight, shrink_momentum, shrink_shadow, grad_shrink, clip_factor)
    return (results.astype(jnp.bfloat16), input_grads.astype(jnp.bfloat16), global_norm, mixer_new[0], mixer_new[1], mixer_new[2], expand_new[0], expand_new[1], expand_new[2], shrink_new[0], shrink_new[1], shrink_new[2])
```

```python
from functools import partial
from types import SimpleNamespace

import jax
import jax.numpy as jnp
import numpy as np
from jax import lax
from jax.experimental import pallas as pl
from jax.experimental.pallas import tpu as pltpu
from jax.sharding import PartitionSpec as P

HEAD = 128
EPSILON = 1e-06
LEARN_RATE = 32.0
MOMENTUM = 0.5
SHADOW_DECAY = 0.5
LAYER_PLACE = 12.0 / 24.0
LONGEST = 512
MESH = pl.DeviceIdType.MESH
BF = jnp.bfloat16
F32 = jnp.float32


def dot_nn(a, b):
    return lax.dot_general(a, b, (((1,), (0,)), ((), ())), preferred_element_type=F32)


def dot_nt(a, b):
    return lax.dot_general(a, b, (((1,), (1,)), ((), ())), preferred_element_type=F32)


def dot_tn(a, b):
    return lax.dot_general(a, b, (((0,), (0,)), ((), ())), preferred_element_type=F32)


def rows_of(index, size):
    return pl.ds(pl.multiple_of(index * size, size), size)


def each(count, body):
    def step(t, carry):
        body(t)
        return carry

    lax.fori_loop(0, count, step, 0)


def widen(column, width):
    return jnp.concatenate([column] * (width // 128), axis=1)


def plan_of(mesh, tokens, width, inner):
    n, mp = mesh.shape["dp"], mesh.shape["mp"]
    lo, core = 2, 2
    return SimpleNamespace(
        n=n, mp=mp, LO=lo, HI=n // lo, X=mp // core, T=tokens, D=width, C=width // mp, F=inner,
        S=width // n, H=width // mp // HEAD, TB=tokens // mp, B=min(256, tokens),
    )


def scratch_of(p):
    T, D, C, F, S, HI, LO, X, TB, B = p.T, p.D, p.C, p.F, p.S, p.HI, p.LO, p.X, p.TB, p.B
    dma = pltpu.SemaphoreType.DMA
    v = pltpu.VMEM
    return dict(
        mixw=v((4, D, C), BF), wo=v((D, D), BF), ffw=v((3, D, F), BF),
        xown=v((TB, D), BF), nin=v((T, D), BF), up=v((T, D), BF),
        cosv=v((T, HEAD), F32), sinv=v((T, HEAD), F32),
        segq=v((T, 128), F32), segk=v((8, T), F32), dec=v((2, p.H, B, B), F32),
        qpre=v((T, C), F32), kpre=v((T, C), F32), gpre=v((T, C), F32), val=v((T, C), BF),
        qrot=v((T, 2 * C), BF), krot=v((T, 2 * C), BF), mixed=v((T, C), F32),
        ufull=v((T, D), BF), ss=v((p.mp, 8, T), F32), rcol=v((T, 128), F32), icol=v((T, 128), F32),
        inn=v((p.mp, 8, TB), F32), hown=v((TB, D), F32), nmid=v((T, D), BF),
        gprod=v((T, max(F, 3 * HEAD)), F32), prod=v((T, F), BF), ggate=v((T, F), BF), gup=v((T, F), BF),
        part=v((X, 2, TB, D), BF), recc=v((2, X, TB, D), BF), recx=v((2, X - 1, TB, D), BF),
        ghid=v((TB, D), F32), hlow=v((T, D), BF), otile=v((2, TB, D), BF),
        gm=v((5, HI, LO, S, C), BF), gf=v((3, HI, LO, S, F), BF),
        rym=v((5, HI, S, C), BF), ryf=v((3, HI, S, F), BF),
        rzm=v((5, HI - 1, S, C), BF), rzf=v((3, HI - 1, S, F), BF),
        gown=v((5, S, C), BF), s1=v((p.mp, 8, 128), F32), s2=v((p.n, 8, 128), F32),
        loc=dma((8,)),
        zs=dma((8, HI - 1)), zr=dma((8, HI - 1)), ys=dma((8, HI)), yr=dma((8, HI)),
        xs=dma((16, X - 1)), xr=dma((16, X - 1)), cs=dma((16, X)), cr=dma((16, X)),
        acs=dma((3,)), acr=dma((3,)), axs=dma((3, X - 1)), axr=dma((3, X - 1)),
        bys=dma((8,)), byr=dma((8,)), bzs=dma((8, HI - 1)), bzr=dma((8, HI - 1)),
        q1s=dma((p.mp,)), q1r=dma((p.mp,)), q2s=dma((p.n,)), q2r=dma((p.n,)),
    )


IN_NAMES = ("x", "og", "seg", "live", "cos", "sin", "mixsh", "ffsh")
OUT_NAMES = ("bo", "ig", "gmo", "gfo", "sqo")


def body(p, names, *refs):
    r = SimpleNamespace(**dict(zip(names, refs)))
    n, mp, LO, HI, X, T, D, C, F, S, H, TB, B = (
        p.n, p.mp, p.LO, p.HI, p.X, p.T, p.D, p.C, p.F, p.S, p.H, p.TB, p.B,
    )
    i, j = lax.axis_index("dp"), lax.axis_index("mp")
    zi, yi = i // LO, lax.rem(i, LO)
    xi, ci = j // 2, lax.rem(j, 2)
    jcols = pl.ds(pl.multiple_of(j * C, C), C)
    pending = []
    r.xv = r.hlow
    r.dk, r.dv = r.gprod.at[:, 0:2 * HEAD], r.gprod.at[:, 2 * HEAD:3 * HEAD]
    r.gproj = [r.ggate.at[:, 0:C], r.ggate.at[:, C:2 * C], r.gup.at[:, 0:C], r.gup.at[:, C:2 * C]]
    r.gmix, r.rh = r.prod.at[:, 0:C], r.prod.at[:, C:2 * C]

    def go(src, dst, ssem, rsem, **device):
        copy = pltpu.make_async_remote_copy(
            src_ref=src, dst_ref=dst, send_sem=ssem, recv_sem=rsem,
            device_id=device, device_id_type=MESH,
        )
        copy.start()
        pending.append(copy)
        return copy

    def arrived(dst, sem):
        pltpu.make_async_copy(dst, dst, sem).wait()

    def settle(copy):
        copy.wait_send()
        pending[:] = [other for other in pending if other is not copy]

    loads = [
        pltpu.make_async_copy(r.x, r.xv, r.loc.at[0]),
        pltpu.make_async_copy(r.og, r.up, r.loc.at[1]),
        pltpu.make_async_copy(r.cos, r.cosv, r.loc.at[2]),
        pltpu.make_async_copy(r.sin, r.sinv, r.loc.at[3]),
        pltpu.make_async_copy(r.mixsh.at[0:4], r.mixw.at[:, rows_of(i, S)], r.loc.at[4]),
        pltpu.make_async_copy(r.mixsh.at[4], r.wo.at[rows_of(i, S), jcols], r.loc.at[6]),
        pltpu.make_async_copy(r.x.at[rows_of(j, TB)], r.xown, r.loc.at[7]),
        pltpu.make_async_copy(r.ffsh, r.ffw.at[:, rows_of(i, S)], r.loc.at[5]),
    ]
    for copy in loads:
        copy.start()

    barrier = pltpu.get_barrier_semaphore()
    for d in range(1, n):
        pl.semaphore_signal(barrier, inc=1, device_id={"dp": lax.rem(i + d, n)}, device_id_type=MESH)
    for d in range(1, mp):
        pl.semaphore_signal(barrier, inc=1, device_id={"mp": lax.rem(j + d, mp)}, device_id_type=MESH)
    pl.semaphore_wait(barrier, n - 1 + mp - 1)

    def slot(k, device):
        if k == 4:
            return r.wo.at[rows_of(device, S), jcols]
        return (r.mixw.at[k] if k < 4 else r.ffw.at[k - 5]).at[rows_of(device, S)]

    def gather_send(k):
        src, dst = (r.mixsh.at[k] if k < 5 else r.ffsh.at[k - 5]), slot(k, i)
        for d in range(1, HI):
            go(src, dst, r.zs.at[k, d - 1], r.zr.at[k, d - 1], dp=lax.rem(zi + d, HI) * LO + yi)
        go(src, dst, r.ys.at[k, 0], r.yr.at[k, 0], dp=zi * LO + 1 - yi)

    def gather_forward(k):
        for d in range(1, HI):
            block = slot(k, lax.rem(zi - d + HI, HI) * LO + yi)
            arrived(block, r.zr.at[k, d - 1])
            go(block, block, r.ys.at[k, d], r.yr.at[k, d], dp=zi * LO + 1 - yi)

    def gather_wait(k):
        for d in range(HI):
            arrived(slot(k, lax.rem(zi - d + HI, HI) * LO + 1 - yi), r.yr.at[k, d])

    def share_send(s, block, src=None):
        own = block(j)
        src = own if src is None else src
        for d in range(1, X):
            go(src, own, r.xs.at[s, d - 1], r.xr.at[s, d - 1], mp=lax.rem(xi + d, X) * 2 + ci)
        go(src, own, r.cs.at[s, 0], r.cr.at[s, 0], mp=xi * 2 + 1 - ci)

    def share_forward(s, block):
        for d in range(1, X):
            part = block(lax.rem(xi - d + X, X) * 2 + ci)
            arrived(part, r.xr.at[s, d - 1])
            go(part, part, r.cs.at[s, d], r.cr.at[s, d], mp=xi * 2 + 1 - ci)

    def share_wait(s, block):
        for d in range(X):
            arrived(block(lax.rem(xi - d + X, X) * 2 + 1 - ci), r.cr.at[s, d])

    def sum_first(s, b):
        return go(r.part.at[:, 1 - ci], r.recc.at[b], r.acs.at[s], r.acr.at[s], mp=xi * 2 + 1 - ci)

    def sum_second(s, b):
        arrived(r.recc.at[b], r.acr.at[s])
        sent = []
        for d in range(1, X):
            to = lax.rem(xi + d, X)

            def add(t, to=to):
                q = rows_of(t, 128)
                r.part[to, ci, q] = (
                    r.part[to, ci, q].astype(F32) + r.recc[b, to, q].astype(F32)
                ).astype(BF)

            each(TB // 128, add)
            sent.append(go(
                r.part.at[to, ci], r.recx.at[b, d - 1], r.axs.at[s, d - 1], r.axr.at[s, d - 1],
                mp=to * 2 + ci,
            ))
        return sent

    def sum_arrived(s, b):
        for d in range(1, X):
            arrived(r.recx.at[b, d - 1], r.axr.at[s, d - 1])

    def sum_tile(b, q):
        total = r.part[xi, ci, q].astype(F32) + r.recc[b, xi, q].astype(F32)
        for d in range(1, X):
            total = total + r.recx[b, d - 1, q].astype(F32)
        return total

    def grad_ref(k):
        return r.gm.at[k] if k < 5 else r.gf.at[k - 5]

    def rec_y(k):
        return r.rym.at[k] if k < 5 else r.ryf.at[k - 5]

    def rec_z(k):
        return r.rzm.at[k] if k < 5 else r.rzf.at[k - 5]

    def scatter_first(k):
        go(grad_ref(k).at[:, 1 - yi], rec_y(k), r.bys.at[k], r.byr.at[k], dp=zi * LO + 1 - yi)

    def scatter_second(k):
        arrived(rec_y(k), r.byr.at[k])
        g, ry = grad_ref(k), rec_y(k)
        for d in range(1, HI):
            to = lax.rem(zi + d, HI)
            g[to, yi] = (g[to, yi].astype(F32) + ry[to].astype(F32)).astype(BF)
            go(g.at[to, yi], rec_z(k).at[d - 1], r.bzs.at[k, d - 1], r.bzr.at[k, d - 1], dp=to * LO + yi)

    def scatter_total(k):
        g, ry, rz = grad_ref(k), rec_y(k), rec_z(k)
        for d in range(1, HI):
            arrived(rz.at[d - 1], r.bzr.at[k, d - 1])
        total = g[zi, yi].astype(F32) + ry[zi].astype(F32)
        for d in range(1, HI):
            total = total + rz[d - 1].astype(F32)
        return total

    def put_grad(k, lhs, rhs):
        g = grad_ref(k)
        per = 256 // (LO * S)

        def tile(t):
            cols = pl.ds(pl.multiple_of(t * 256, 256), 256)
            out = dot_tn(lhs[:, cols], rhs[...])
            g[pl.ds(t * per, per)] = out.astype(BF).reshape(per, LO, S, out.shape[-1])

        each(D // 256, tile)

    for k in range(3):
        gather_send(k)

    length = r.live[0]
    loads[0].wait()

    def norm_tile(t):
        q = rows_of(t, 128)
        v = r.xv[q, :].astype(F32)
        r.nin[q, :] = (v * lax.rsqrt(jnp.mean(v * v, axis=-1, keepdims=True) + EPSILON)).astype(BF)

    each(T // 128, norm_tile)
    loads[1].wait()

    def live_tile(t):
        q = rows_of(t, 128)
        place = lax.broadcasted_iota(jnp.int32, (128, D), 0) + t * 128
        r.up[q, :] = jnp.where(place < length, r.up[q, :].astype(F32), 0.0).astype(BF)

    each(T // 128, live_tile)

    place = lax.broadcasted_iota(jnp.int32, (1, T), 1)
    segment = r.seg[...].astype(F32)
    r.segk[...] = jnp.broadcast_to(jnp.where(place < length, segment, -2.0), (8, T))
    seg_q = jnp.where(place < length, segment, -1.0)
    for t in range(T // 128):
        q = slice(t * 128, t * 128 + 128)
        r.segq[q, :] = jnp.transpose(jnp.broadcast_to(seg_q[:, q], (128, 128)))

    down = lax.broadcasted_iota(jnp.int32, (B, B), 0)
    over = lax.broadcasted_iota(jnp.int32, (B, B), 1)
    heads = D // HEAD

    def rate_of(h):
        return -(8.0 * (j * H + h).astype(F32) / heads) * (1.0 - LAYER_PLACE)

    for h in range(H):
        rate = rate_of(h)
        for o in range(2):
            distance = down - over + o * B
            fade = jnp.exp(rate * jnp.maximum(distance, 0).astype(F32))
            r.dec[o, h] = jnp.where(distance >= 0, fade, 0.0)

    loads[2].wait()
    loads[3].wait()
    for copy in loads[4:]:
        copy.wait()

    def turn_into(pre_ref, rot_ref, k):
        def tile(t):
            q = rows_of(t, 256)
            pre = dot_nn(r.nin[q, :], r.mixw[k])
            pre_ref[q, :] = pre
            act = pre * jax.nn.sigmoid(pre)
            c, s = r.cosv[q, :], r.sinv[q, :]
            for h in range(H):
                a = act[:, h * HEAD:(h + 1) * HEAD]
                rot_ref[q, 2 * h * HEAD:(2 * h + 1) * HEAD] = (a * c).astype(BF)
                rot_ref[q, (2 * h + 1) * HEAD:(2 * h + 2) * HEAD] = (a * s).astype(BF)

        each(T // 256, tile)

    def project_into(ref, k):
        def tile(t):
            q = rows_of(t, 256)
            ref[q, :] = dot_nn(r.nin[q, :], r.mixw[k]).astype(ref.dtype)

        each(T // 256, tile)

    gather_forward(0)
    gather_send(3)
    gather_forward(1)
    gather_send(4)
    gather_wait(0)
    turn_into(r.qpre, r.qrot, 0)
    gather_forward(2)
    gather_send(5)
    gather_wait(1)
    turn_into(r.kpre, r.krot, 1)
    gather_forward(3)
    gather_send(6)
    gather_wait(2)
    project_into(r.val, 2)
    gather_forward(4)
    gather_send(7)
    gather_wait(3)
    project_into(r.gpre, 3)

    def wo_block(owner):
        return r.wo.at[:, pl.ds(pl.multiple_of(owner * C, C), C)]

    gather_wait(4)
    share_send(0, wo_block)

    NB = T // B
    REACH = LONGEST // B

    def weights_of(qb, kb, h):
        seen = jnp.broadcast_to(r.segk[0:1, kb * B:(kb + 1) * B], (B, B))
        same = widen(r.segq[qb * B:(qb + 1) * B, :], B) == seen
        if qb - kb < 2:
            return jnp.where(same, r.dec[qb - kb, h], 0.0)
        return jnp.where(same, r.dec[1, h] * jnp.exp(rate_of(h) * ((qb - kb - 1) * B)), 0.0)

    def u_block(qb):
        return lambda owner: r.ufull.at[qb * B:(qb + 1) * B, pl.ds(pl.multiple_of(owner * C, C), C)]

    def attend(qb):
        q = slice(qb * B, (qb + 1) * B)
        squares = jnp.zeros((B, 1), F32)
        for h in range(H):
            rot = slice(2 * h * HEAD, 2 * (h + 1) * HEAD)
            chan = slice(h * HEAD, (h + 1) * HEAD)
            total = jnp.zeros((B, HEAD), F32)
            for kb in range(max(0, qb - REACH), qb + 1):
                key = slice(kb * B, (kb + 1) * B)
                scores = dot_nt(r.qrot[q, rot], r.krot[key, rot]) * weights_of(qb, kb, h)
                total = total + dot_nn(scores.astype(BF), r.val[key, chan])
            r.mixed[q, chan] = total
            squares = squares + jnp.sum(total * total, axis=-1, keepdims=True)
            r.ufull[q, pl.ds(pl.multiple_of(j * C + h * HEAD, HEAD), HEAD)] = (
                total * r.gpre[q, chan]
            ).astype(BF)
        r.ss[j, :, q] = jnp.transpose(jnp.broadcast_to(squares, (B, 128)))[0:8, :]

    def ss_block(owner):
        return r.ss.at[owner]

    for qb in range(NB):
        attend(qb)
        share_send(1 + qb, u_block(qb))
        if qb == 0:
            gather_forward(5)
        if qb == NB - 1:
            share_send(1 + NB, ss_block)
        if qb == 1:
            share_forward(0, wo_block)
        if qb == 2:
            gather_forward(6)
        if qb > 0:
            share_forward(qb, u_block(qb - 1))
    share_forward(NB, u_block(NB - 1))
    share_forward(1 + NB, ss_block)
    gather_wait(5)

    def gprod_tile(t):
        q = rows_of(t, 256)
        r.gprod[q, 0:F] = dot_nn(r.up[q, :], r.ffw[0])

    each(T // 256, gprod_tile)
    gather_forward(7)
    share_wait(0, wo_block)
    for qb in range(NB):
        share_wait(1 + qb, u_block(qb))
    share_wait(1 + NB, ss_block)

    total_ss = r.ss[0]
    for owner in range(1, mp):
        total_ss = total_ss + r.ss[owner]
    inverse = lax.rsqrt(total_ss * (1.0 / D) + EPSILON)
    for t in range(T // 128):
        q = slice(t * 128, t * 128 + 128)
        r.rcol[q, :] = jnp.transpose(jnp.broadcast_to(inverse[0:1, q], (128, 128)))

    def hidden_tile(t):
        q = rows_of(t, TB)
        out = widen(r.rcol[q, :], D) * dot_nn(r.ufull[q, :], r.wo[...])
        hidden = r.xv[q, :].astype(F32) + out
        scale = lax.rsqrt(jnp.mean(hidden * hidden, axis=-1, keepdims=True) + EPSILON)
        r.nmid[q, :] = (hidden * scale).astype(BF)

        @pl.when(t == j)
        def _():
            r.hown[...] = hidden

    each(T // TB, hidden_tile)
    gather_wait(6)
    gather_wait(7)

    def ff_tile(t):
        q = rows_of(t, 256)
        gate = dot_nn(r.nmid[q, :], r.ffw[1])
        upper = dot_nn(r.nmid[q, :], r.ffw[2])
        r.prod[q, :] = (gate * upper).astype(BF)
        g = r.gprod[q, 0:F]
        r.ggate[q, :] = (g * upper).astype(BF)
        r.gup[q, :] = (g * gate).astype(BF)

    each(T // 256, ff_tile)

    def mid_tile(t):
        q = rows_of(t, TB)
        out = dot_nt(r.ggate[q, :], r.ffw[1]) + dot_nt(r.gup[q, :], r.ffw[2])
        r.part[t // 2, lax.rem(t, 2)] = out.astype(BF)

    each(mp, mid_tile)
    used = [sum_first(0, 0)]
    put_grad(5, r.up, r.prod)
    scatter_first(5)
    used += sum_second(0, 0)
    put_grad(6, r.nmid, r.ggate)
    scatter_first(6)
    sum_arrived(0, 0)

    def back_tile(t):
        q = rows_of(t, 128)
        here = rows_of(j * (TB // 128) + t, 128)
        grad = sum_tile(0, q)
        hidden = r.hown[q, :]
        scale = lax.rsqrt(jnp.mean(hidden * hidden, axis=-1, keepdims=True) + EPSILON)
        normed = hidden * scale
        inner = jnp.mean(grad * normed, axis=-1, keepdims=True)
        out = r.up[here, :].astype(F32) + scale * (grad - normed * inner)
        r.ghid[q, :] = out
        low = out.astype(BF)
        r.hlow[here, :] = low
        mixer_out = hidden - r.xown[q, :].astype(F32)
        product = jnp.sum(low.astype(F32) * mixer_out, axis=-1, keepdims=True) * (1.0 / D)
        r.inn[j, :, q] = jnp.transpose(jnp.broadcast_to(product, (128, 128)))[0:8, :]

    each(TB // 128, back_tile)

    def token_block(ref):
        return lambda owner: ref.at[rows_of(owner, TB)]

    HL, BO, IG, IN = 2 + NB, 3 + NB, 4 + NB, 10 + NB

    def inn_block(owner):
        return r.inn.at[owner]

    share_send(IN, inn_block)
    share_send(HL, token_block(r.hlow))
    put_grad(7, r.nmid, r.gup)
    scatter_first(7)
    scatter_second(5)
    share_forward(IN, inn_block)
    share_forward(HL, token_block(r.hlow))
    for copy in used:
        settle(copy)

    def expand_tile(t):
        q = rows_of(t, TB)
        r.part[t // 2, lax.rem(t, 2)] = dot_nt(r.prod[q, :], r.ffw[0]).astype(BF)

    each(mp, expand_tile)
    used = [sum_first(1, 1)]
    share_wait(HL, token_block(r.hlow))
    share_wait(IN, inn_block)
    for owner in range(mp):
        for t in range(TB // 128):
            row = r.inn[owner, 0:1, t * 128:(t + 1) * 128]
            q = slice(owner * TB + t * 128, owner * TB + (t + 1) * 128)
            r.icol[q, :] = jnp.transpose(jnp.broadcast_to(row, (128, 128)))

    wo_rows = rows_of(j, C)

    def gated_tile(t):
        q = rows_of(t, 256)
        low = r.hlow[q, :]
        grad = dot_nt(low, r.wo[wo_rows, :])
        inner = widen(r.icol[q, :], C)
        inverse = widen(r.rcol[q, :], C)
        normed = r.mixed[q, :] * inverse
        r.gproj[3][q, :] = (grad * normed).astype(BF)
        r.gmix[q, :] = (inverse * (grad * r.gpre[q, :] - normed * inner)).astype(BF)
        r.rh[q, :] = (inverse * r.hlow[q, jcols].astype(F32)).astype(BF)

    each(T // 256, gated_tile)
    put_grad(4, r.ufull, r.rh)
    scatter_first(4)
    scatter_second(6)
    used += sum_second(1, 1)

    def swish_back(pre, grad):
        gate = jax.nn.sigmoid(pre)
        return grad * (gate * (1.0 + pre * (1.0 - gate)))

    def attend_back(h):
        rot = slice(2 * h * HEAD, 2 * (h + 1) * HEAD)
        chan = slice(h * HEAD, (h + 1) * HEAD)
        r.dk[...] = jnp.zeros_like(r.dk)
        r.dv[...] = jnp.zeros_like(r.dv)
        for qb in range(NB):
            q = slice(qb * B, (qb + 1) * B)
            total = jnp.zeros((B, 2 * HEAD), F32)
            for kb in range(max(0, qb - REACH), qb + 1):
                key = slice(kb * B, (kb + 1) * B)
                weights = weights_of(qb, kb, h)
                scores = (dot_nt(r.qrot[q, rot], r.krot[key, rot]) * weights).astype(BF)
                back = (dot_nt(r.gmix[q, chan], r.val[key, chan]) * weights).astype(BF)
                r.dv[key, :] += dot_tn(scores, r.gmix[q, chan])
                r.dk[key, :] += dot_tn(back, r.qrot[q, rot])
                total = total + dot_nn(back, r.krot[key, rot])
            turned = total[:, :HEAD] * r.cosv[q, :] + total[:, HEAD:] * r.sinv[q, :]
            r.gproj[0][q, chan] = swish_back(r.qpre[q, chan], turned).astype(BF)

        def tile(t):
            q = rows_of(t, 256)
            turned = r.dk[q, :HEAD] * r.cosv[q, :] + r.dk[q, HEAD:] * r.sinv[q, :]
            r.gproj[1][q, chan] = swish_back(r.kpre[q, chan], turned).astype(BF)
            r.gproj[2][q, chan] = r.dv[q, :].astype(BF)

        each(T // 256, tile)

    put_grad(3, r.nin, r.gproj[3])
    scatter_first(3)
    attend_back(0)
    scatter_second(7)
    sum_arrived(1, 1)

    def output_tile(t):
        q = rows_of(t, 128)
        r.otile[0, q, :] = (r.hown[q, :] + sum_tile(1, q)).astype(BF)

    each(TB // 128, output_tile)
    share_send(BO, token_block(r.bo), src=r.otile.at[0])
    own_bo = pltpu.make_async_copy(r.otile.at[0], token_block(r.bo)(j), r.loc.at[7])
    own_bo.start()
    for h in range(1, H):
        attend_back(h)
    scatter_second(4)
    scatter_second(3)
    share_forward(BO, token_block(r.bo))
    for k in range(3):
        put_grad(k, r.nin, r.gproj[k])
        scatter_first(k)
    for copy in used:
        settle(copy)

    def normed_tile(t):
        q = rows_of(t, TB)
        out = dot_nt(r.gproj[0][q, :], r.mixw[0])
        for k in range(1, 4):
            out = out + dot_nt(r.gproj[k][q, :], r.mixw[k])
        r.part[t // 2, lax.rem(t, 2)] = out.astype(BF)

    each(mp, normed_tile)
    used = [sum_first(2, 0)]
    for k in range(3):
        scatter_second(k)
    used += sum_second(2, 0)
    squares = jnp.zeros((), F32)
    for k in range(5, 8):
        total = scatter_total(k)
        r.gfo[k - 5] = total
        squares = squares + jnp.sum(total * total)
    sum_arrived(2, 0)

    def input_tile(t):
        q = rows_of(t, 128)
        grad = sum_tile(0, q)
        v = r.xown[q, :].astype(F32)
        scale = lax.rsqrt(jnp.mean(v * v, axis=-1, keepdims=True) + EPSILON)
        normed = v * scale
        inner = jnp.mean(grad * normed, axis=-1, keepdims=True)
        r.otile[1, q, :] = (r.ghid[q, :] + scale * (grad - normed * inner)).astype(BF)

    each(TB // 128, input_tile)
    share_send(IG, token_block(r.ig), src=r.otile.at[1])
    own_ig = pltpu.make_async_copy(r.otile.at[1], token_block(r.ig)(j), r.loc.at[6])
    own_ig.start()

    def grad_block(k):
        return lambda owner: r.gmo.at[k, :, pl.ds(pl.multiple_of(owner * C, C), C)]

    own_gm = []
    for k in (4, 3, 0, 1, 2):
        total = scatter_total(k).astype(BF)
        r.gown[k] = total
        squares = squares + jnp.sum(total.astype(F32) * total.astype(F32))
        share_send(IG + 1 + k, grad_block(k), src=r.gown.at[k])
        copy = pltpu.make_async_copy(r.gown.at[k], grad_block(k)(j), r.loc.at[k])
        copy.start()
        own_gm.append(copy)

    r.s1[j] = jnp.full((8, 128), squares, F32)
    for d in range(1, mp):
        go(r.s1.at[j], r.s1.at[j], r.q1s.at[d], r.q1r.at[d], mp=lax.rem(j + d, mp))
    share_forward(IG, token_block(r.ig))
    for d in range(1, mp):
        arrived(r.s1.at[lax.rem(j - d + mp, mp)], r.q1r.at[d])
    total = r.s1[0]
    for owner in range(1, mp):
        total = total + r.s1[owner]
    r.s2[i] = total
    for d in range(1, n):
        go(r.s2.at[i], r.s2.at[i], r.q2s.at[d], r.q2r.at[d], dp=lax.rem(i + d, n))
    for k in (4, 3, 0, 1, 2):
        share_forward(IG + 1 + k, grad_block(k))
    for d in range(1, n):
        arrived(r.s2.at[lax.rem(i - d + n, n)], r.q2r.at[d])
    total = r.s2[0]
    for owner in range(1, n):
        total = total + r.s2[owner]
    r.sqo[...] = total

    share_wait(BO, token_block(r.bo))
    share_wait(IG, token_block(r.ig))
    for k in (4, 3, 0, 1, 2):
        share_wait(IG + 1 + k, grad_block(k))
    for copy in [own_bo, own_ig] + own_gm:
        copy.wait()
    for copy in pending:
        copy.wait_send()


def fused(p, x, og, seg, live, cos, sin, mixsh, ffsh):
    scratch = scratch_of(p)
    names = IN_NAMES + OUT_NAMES + tuple(scratch)
    anywhere = pl.BlockSpec(memory_space=pl.ANY)
    vmem = pl.BlockSpec(memory_space=pltpu.VMEM)
    smem = pl.BlockSpec(memory_space=pltpu.SMEM)
    return pl.pallas_call(
        partial(body, p, names),
        out_shape=(
            jax.ShapeDtypeStruct((p.T, p.D), BF),
            jax.ShapeDtypeStruct((p.T, p.D), BF),
            jax.ShapeDtypeStruct((5, p.S, p.D), BF),
            jax.ShapeDtypeStruct((3, p.S, p.F), F32),
            jax.ShapeDtypeStruct((8, 128), F32),
        ),
        in_specs=[anywhere, anywhere, vmem, smem, anywhere, anywhere, anywhere, anywhere],
        out_specs=(anywhere, anywhere, anywhere, vmem, vmem),
        scratch_shapes=list(scratch.values()),
        compiler_params=pltpu.CompilerParams(
            collective_id=0, has_side_effects=True, vmem_limit_bytes=VMEM_LIMIT
        ),
    )(x, og, seg, live, cos, sin, mixsh, ffsh)


VMEM_LIMIT = 64 * 2**20 - 2**18


def renew(weight, momentum, shadow, grad, clip_factor):
    clipped = grad * clip_factor
    velocity = MOMENTUM * momentum + clipped
    updated = weight - LEARN_RATE * (clipped + MOMENTUM * velocity)
    average = SHADOW_DECAY * shadow + (1.0 - SHADOW_DECAY) * updated
    return (velocity, average, updated)


def turn_tables(tokens):
    theta = np.float32(10000.0) ** (-np.arange(HEAD, dtype=np.float32) / np.float32(HEAD))
    angle = np.arange(tokens, dtype=np.float32)[:, None] * theta.astype(np.float32)[None, :]
    angle = angle.astype(np.float64)
    return np.cos(angle).astype(np.float32), np.sin(angle).astype(np.float32)


def per_device(mesh, block_input, segment_ids, live_length, output_grad, mixer_weight, mixer_momentum, mixer_shadow,
               expand_weight, expand_momentum, expand_shadow, shrink_weight, shrink_momentum, shrink_shadow):
    rows, length, width = block_input.shape
    p = plan_of(mesh, length, width, shrink_weight.shape[0])
    j = lax.axis_index("mp")
    mixsh = lax.dynamic_slice_in_dim(mixer_weight, j * p.C, p.C, axis=2).astype(BF)
    ffsh = jnp.concatenate([shrink_weight.T[None], expand_weight], axis=0).astype(BF)
    cos, sin = turn_tables(length)
    out, grad_in, gm, gf, sq = fused(
        p, block_input[0], output_grad[0], segment_ids, live_length, jnp.asarray(cos), jnp.asarray(sin), mixsh, ffsh
    )
    global_norm = jnp.sqrt(sq[0, 0])
    clip_factor = 1.0 / jnp.maximum(global_norm, 1.0)
    mixer_new = renew(mixer_weight, mixer_momentum, mixer_shadow, gm.astype(F32), clip_factor)
    expand_new = renew(expand_weight, expand_momentum, expand_shadow, gf[1:], clip_factor)
    shrink_new = renew(shrink_weight, shrink_momentum, shrink_shadow, gf[0].T, clip_factor)
    return (out[None], grad_in[None], global_norm) + mixer_new + expand_new + shrink_new


def solution(mesh):
    row, mixer, expand, shrink = P("dp", None, None), P(None, "dp", None), P(None, "dp", "mp"), P("mp", "dp")
    return jax.shard_map(
        partial(per_device, mesh),
        mesh=mesh,
        in_specs=(row, P("dp", None), P("dp"), row) + (mixer,) * 3 + (expand,) * 3 + (shrink,) * 3,
        out_specs=(row, row, P()) + (mixer,) * 3 + (expand,) * 3 + (shrink,) * 3,
        check_vma=False,
    )
```

```python
from functools import partial
from types import SimpleNamespace

import jax
import jax.numpy as jnp
import numpy as np
from jax import lax
from jax.experimental import pallas as pl
from jax.experimental.pallas import tpu as pltpu
from jax.sharding import PartitionSpec as P

HEAD = 128
EPSILON = 1e-06
LEARN_RATE = 32.0
MOMENTUM = 0.5
SHADOW_DECAY = 0.5
LAYER_PLACE = 12.0 / 24.0
LONGEST = 512
MESH = pl.DeviceIdType.MESH
BF = jnp.bfloat16
F32 = jnp.float32


def dot_nn(a, b):
    return lax.dot_general(a, b, (((1,), (0,)), ((), ())), preferred_element_type=F32)


def dot_nt(a, b):
    return lax.dot_general(a, b, (((1,), (1,)), ((), ())), preferred_element_type=F32)


def dot_tn(a, b):
    return lax.dot_general(a, b, (((0,), (0,)), ((), ())), preferred_element_type=F32)


def rows_of(index, size):
    return pl.ds(pl.multiple_of(index * size, size), size)


def each(count, body):
    def step(t, carry):
        body(t)
        return carry

    lax.fori_loop(0, count, step, 0)


def widen(column, width):
    return jnp.concatenate([column] * (width // 128), axis=1)


def plan_of(mesh, tokens, width, inner):
    n, mp = mesh.shape["dp"], mesh.shape["mp"]
    lo, core = 2, 2
    return SimpleNamespace(
        n=n, mp=mp, LO=lo, HI=n // lo, X=mp // core, T=tokens, D=width, C=width // mp, F=inner,
        S=width // n, H=width // mp // HEAD, TB=tokens // mp, B=min(256, tokens),
        FD=(width // n) % 128 == 0,
    )


def scratch_of(p):
    T, D, C, F, S, HI, LO, X, TB, B = p.T, p.D, p.C, p.F, p.S, p.HI, p.LO, p.X, p.TB, p.B
    dma = pltpu.SemaphoreType.DMA
    v = pltpu.VMEM
    return dict(
        mixw=v((4, D, C), BF), wo=v((D, D), BF), ffw=v((3, F, D) if p.FD else (3, D, F), BF),
        xown=v((TB, D), BF), nin=v((T, D), BF), nint=v((D, T), BF), up=v((T, D), BF),
        cosv=v((T, HEAD), F32), sinv=v((T, HEAD), F32),
        segq=v((T, 128), F32), segk=v((8, T), F32), dec=v((2, p.H, B, B), F32),
        qpre=v((T, C), F32), kpre=v((T, C), F32), gpre=v((T, C), F32), val=v((T, C), BF),
        qrot=v((T, 2 * C), BF), krot=v((T, 2 * C), BF), mixed=v((T, C), F32),
        ufull=v((T, D), BF), ss=v((p.mp, 8, T), F32), rcol=v((T, 128), F32), icol=v((T, 128), F32),
        inn=v((p.mp, 8, TB), F32), hown=v((TB, D), F32),
        gprod=v((T, max(F, 3 * HEAD)), F32), prod=v((T, F), BF), ggate=v((T, F), BF), gup=v((T, F), BF),
        part=v((X, 2, TB, D), BF), recc=v((2, X, TB, D), BF), recx=v((2, X - 1, TB, D), BF),
        ghid=v((TB, D), F32), hlow=v((T, D), BF), otile=v((2, TB, D), BF),
        gm=v((5, HI, LO, S, C), BF), rym=v((5, HI, S, C), BF), rzm=v((5, HI - 1, S, C), BF),
        gf=v((3, LO, F, HI * S) if p.FD else (3, HI, LO, S, F), BF),
        ryf=v((3, F, HI * S) if p.FD else (3, HI, S, F), BF),
        rzf=v((3, HI - 1, F, S) if p.FD else (3, HI - 1, S, F), BF),
        gown=v((5, S, C), BF), s1=v((p.mp, 8, 128), F32), s2=v((p.n, 8, 128), F32),
        loc=dma((10,)),
        zs=dma((11, HI - 1)), zr=dma((11, HI - 1)), ys=dma((11, HI)), yr=dma((11, HI)),
        xs=dma((20, X - 1)), xr=dma((20, X - 1)), cs=dma((20, X)), cr=dma((20, X)),
        acs=dma((3, X)), acr=dma((3, X)), axs=dma((3, X - 1)), axr=dma((3, X - 1)),
        bys=dma((8,)), byr=dma((8,)), bzs=dma((8, HI - 1)), bzr=dma((8, HI - 1)),
        q1s=dma((p.mp,)), q1r=dma((p.mp,)), q2s=dma((p.n,)), q2r=dma((p.n,)),
    )


IN_NAMES = ("x", "og", "seg", "live", "cos", "sin", "mixsh", "exsh", "shsh")
OUT_NAMES = ("bo", "ig", "gmo", "gfo", "sqo")


def body(p, names, *refs):
    r = SimpleNamespace(**dict(zip(names, refs)))
    n, mp, LO, HI, X, T, D, C, F, S, H, TB, B = (
        p.n, p.mp, p.LO, p.HI, p.X, p.T, p.D, p.C, p.F, p.S, p.H, p.TB, p.B,
    )
    i, j = lax.axis_index("dp"), lax.axis_index("mp")
    zi, yi = i // LO, lax.rem(i, LO)
    xi, ci = j // 2, lax.rem(j, 2)
    jcols = pl.ds(pl.multiple_of(j * C, C), C)
    pending = []
    r.xv, r.nmid = r.hlow, r.nin
    r.dk, r.dv = r.gprod.at[:, 0:2 * HEAD], r.gprod.at[:, 2 * HEAD:3 * HEAD]
    r.gproj = [r.ggate.at[:, 0:C], r.ggate.at[:, C:2 * C], r.gup.at[:, 0:C], r.gup.at[:, C:2 * C]]
    r.gmix, r.rh = r.prod.at[:, 0:C], r.prod.at[:, C:2 * C]

    def go(src, dst, ssem, rsem, **device):
        copy = pltpu.make_async_remote_copy(
            src_ref=src, dst_ref=dst, send_sem=ssem, recv_sem=rsem,
            device_id=device, device_id_type=MESH,
        )
        copy.start()
        pending.append(copy)
        return copy

    def arrived(dst, sem):
        pltpu.make_async_copy(dst, dst, sem).wait()

    def settle(copy):
        copy.wait_send()
        pending[:] = [other for other in pending if other is not copy]

    def load(src, dst, sem):
        copy = pltpu.make_async_copy(src, dst, r.loc.at[sem])
        copy.start()
        return copy

    own_mix = [load(r.mixsh.at[k, :, jcols], r.qpre.at[k * S:(k + 1) * S], k) for k in range(5)]
    if p.FD:
        stage = [r.gprod.at[0:F, m * S:(m + 1) * S] for m in range(3)]
        own_ff = [load(r.shsh if m == 0 else r.exsh.at[m - 1], stage[m], 5 + m) for m in range(3)]
    else:
        own_ff = [load(r.exsh.at[m], r.ffw.at[m, rows_of(i, S)], 5 + m) for m in range(3)]
    load_x = load(r.x, r.xv, 8)
    load_og = load(r.og, r.up, 9)

    def enter():
        barrier = pltpu.get_barrier_semaphore()
        for d in range(1, n):
            pl.semaphore_signal(barrier, inc=1, device_id={"dp": lax.rem(i + d, n)}, device_id_type=MESH)
        for d in range(1, mp):
            pl.semaphore_signal(barrier, inc=1, device_id={"mp": lax.rem(j + d, mp)}, device_id_type=MESH)
        pl.semaphore_wait(barrier, n - 1 + mp - 1)

    def slot(k, device):
        rows = rows_of(device, S)
        if k == 4:
            return r.wo.at[rows, jcols]
        if k < 4:
            return r.mixw.at[k, rows]
        m, half = (k - 5) // 2, (k - 5) % 2
        if p.FD:
            return r.ffw.at[m, half * F // 2:(half + 1) * F // 2, rows]
        return r.ffw.at[m, pl.ds(pl.multiple_of(device * S + half * S // 2, S // 2), S // 2)]

    def gather_ready(k):
        if k < 5:
            own_mix[k].wait()
            slot(k, i)[...] = r.qpre[k * S:(k + 1) * S, :].astype(BF)
        else:
            m, half = (k - 5) // 2, (k - 5) % 2
            if half == 0:
                own_ff[m].wait()
            if p.FD:
                slot(k, i)[...] = stage[m][half * F // 2:(half + 1) * F // 2, :].astype(BF)

    def gather_send(k):
        src = slot(k, i)
        for d in range(1, HI):
            go(src, src, r.zs.at[k, d - 1], r.zr.at[k, d - 1], dp=lax.rem(zi + d, HI) * LO + yi)
        go(src, src, r.ys.at[k, 0], r.yr.at[k, 0], dp=zi * LO + 1 - yi)

    def gather_forward(k):
        for d in range(1, HI):
            block = slot(k, lax.rem(zi - d + HI, HI) * LO + yi)
            arrived(block, r.zr.at[k, d - 1])
            go(block, block, r.ys.at[k, d], r.yr.at[k, d], dp=zi * LO + 1 - yi)

    def gather_wait(k):
        for d in range(HI):
            arrived(slot(k, lax.rem(zi - d + HI, HI) * LO + 1 - yi), r.yr.at[k, d])

    def share_send(s, block, src=None):
        own = block(j)
        src = own if src is None else src
        for d in range(1, X):
            go(src, own, r.xs.at[s, d - 1], r.xr.at[s, d - 1], mp=lax.rem(xi + d, X) * 2 + ci)
        go(src, own, r.cs.at[s, 0], r.cr.at[s, 0], mp=xi * 2 + 1 - ci)

    def share_forward(s, block):
        for d in range(1, X):
            part = block(lax.rem(xi - d + X, X) * 2 + ci)
            arrived(part, r.xr.at[s, d - 1])
            go(part, part, r.cs.at[s, d], r.cr.at[s, d], mp=xi * 2 + 1 - ci)

    def share_wait(s, block):
        for d in range(X):
            arrived(block(lax.rem(xi - d + X, X) * 2 + 1 - ci), r.cr.at[s, d])

    def sum_begin(s, b, compute):
        sent = []
        for d in [*range(1, X), 0]:
            to = lax.rem(xi + d, X)
            compute(to, 1 - ci)
            sent.append(go(
                r.part.at[to, 1 - ci], r.recc.at[b, to], r.acs.at[s, d], r.acr.at[s, d], mp=xi * 2 + 1 - ci
            ))
        for d in range(1, X):
            to = lax.rem(xi + d, X)
            compute(to, ci)
            arrived(r.recc.at[b, to], r.acr.at[s, d])

            def add(t, to=to):
                q = rows_of(t, 128)
                r.part[to, ci, q] = (
                    r.part[to, ci, q].astype(F32) + r.recc[b, to, q].astype(F32)
                ).astype(BF)

            each(TB // 128, add)
            sent.append(go(
                r.part.at[to, ci], r.recx.at[b, d - 1], r.axs.at[s, d - 1], r.axr.at[s, d - 1],
                mp=to * 2 + ci,
            ))
        compute(xi, ci)
        return sent

    def sum_arrived(s, b):
        arrived(r.recc.at[b, xi], r.acr.at[s, 0])
        for d in range(1, X):
            arrived(r.recx.at[b, d - 1], r.axr.at[s, d - 1])

    def sum_tile(b, q):
        total = r.part[xi, ci, q].astype(F32) + r.recc[b, xi, q].astype(F32)
        for d in range(1, X):
            total = total + r.recx[b, d - 1, q].astype(F32)
        return total

    def grad_ref(k):
        return r.gm.at[k] if k < 5 else r.gf.at[k - 5]

    def rec_y(k):
        return r.rym.at[k] if k < 5 else r.ryf.at[k - 5]

    def rec_z(k):
        return r.rzm.at[k] if k < 5 else r.rzf.at[k - 5]

    flat = p.FD

    def lanes(k):
        return flat and k >= 5

    def part_of(ref, k, z):
        return ref.at[:, rows_of(z, S)] if lanes(k) else ref.at[z]

    def mine(k, z):
        return r.gf.at[k - 5, yi, :, rows_of(z, S)] if lanes(k) else grad_ref(k).at[z, yi]

    def scatter_first(k):
        src = r.gf.at[k - 5, 1 - yi] if lanes(k) else grad_ref(k).at[:, 1 - yi]
        go(src, rec_y(k), r.bys.at[k], r.byr.at[k], dp=zi * LO + 1 - yi)

    def scatter_second(k):
        arrived(rec_y(k), r.byr.at[k])
        for d in range(1, HI):
            to = lax.rem(zi + d, HI)
            block = mine(k, to)
            block[...] = (block[...].astype(F32) + part_of(rec_y(k), k, to)[...].astype(F32)).astype(BF)
            go(block, rec_z(k).at[d - 1], r.bzs.at[k, d - 1], r.bzr.at[k, d - 1], dp=to * LO + yi)

    def scatter_total(k):
        rz = rec_z(k)
        for d in range(1, HI):
            arrived(rz.at[d - 1], r.bzr.at[k, d - 1])
        total = mine(k, zi)[...].astype(F32) + part_of(rec_y(k), k, zi)[...].astype(F32)
        for d in range(1, HI):
            total = total + rz[d - 1].astype(F32)
        return total

    def put_grad(k, lhs, rhs, turned=False):
        g = grad_ref(k)
        per = 256 // (LO * S)

        def tile(t):
            if turned:
                out = dot_nn(lhs[rows_of(t, 256), :], rhs[...])
            else:
                out = dot_tn(lhs[:, rows_of(t, 256)], rhs[...])
            g[pl.ds(t * per, per)] = out.astype(BF).reshape(per, LO, S, out.shape[-1])

        each(D // 256, tile)

    def put_ff_grad(m, units, model):
        if not flat:
            return put_grad(5 + m, model, units)
        for f in range(0, F, 256):
            q = slice(f, min(f + 256, F))
            out = dot_tn(units[:, q], model[...]).astype(BF)
            for y in range(LO):
                for z in range(HI):
                    r.gf[m, y, q, z * S:(z + 1) * S] = out[:, (z * LO + y) * S:(z * LO + y + 1) * S]

    def to_units(a, m):
        return dot_nt(a, r.ffw[m]) if flat else dot_nn(a, r.ffw[m])

    def to_model(a, m):
        return dot_nn(a, r.ffw[m]) if flat else dot_nt(a, r.ffw[m])

    gather_ready(0)
    gather_ready(1)
    enter()
    gather_send(0)
    gather_send(1)

    length = r.live[0]
    load_x.wait()

    def norm_tile(t):
        q = rows_of(t, 128)
        v = r.xv[q, :].astype(F32)
        r.nin[q, :] = (v * lax.rsqrt(jnp.mean(v * v, axis=-1, keepdims=True) + EPSILON)).astype(BF)

    each(T // 128, norm_tile)
    for k in range(2, 11):
        gather_ready(k)
    load_x_own = load(r.x.at[rows_of(j, TB)], r.xown, 8)
    load_og.wait()
    load_cos = load(r.cos, r.cosv, 0)
    load_sin = load(r.sin, r.sinv, 1)

    def live_tile(t):
        q = rows_of(t, 128)
        place = lax.broadcasted_iota(jnp.int32, (128, D), 0) + t * 128
        r.up[q, :] = jnp.where(place < length, r.up[q, :].astype(F32), 0.0).astype(BF)

    each(T // 128, live_tile)

    place = lax.broadcasted_iota(jnp.int32, (1, T), 1)
    segment = r.seg[...].astype(F32)
    r.segk[...] = jnp.broadcast_to(jnp.where(place < length, segment, -2.0), (8, T))
    seg_q = jnp.where(place < length, segment, -1.0)
    for t in range(T // 128):
        q = slice(t * 128, t * 128 + 128)
        r.segq[q, :] = jnp.transpose(jnp.broadcast_to(seg_q[:, q], (128, 128)))

    down = lax.broadcasted_iota(jnp.int32, (B, B), 0)
    over = lax.broadcasted_iota(jnp.int32, (B, B), 1)
    heads = D // HEAD

    def rate_of(h):
        return -(8.0 * (j * H + h).astype(F32) / heads) * (1.0 - LAYER_PLACE)

    for h in range(H):
        rate = rate_of(h)
        for o in range(2):
            distance = down - over + o * B
            fade = jnp.exp(rate * jnp.maximum(distance, 0).astype(F32))
            r.dec[o, h] = jnp.where(distance >= 0, fade, 0.0)

    for t in range(D // 128):
        q = slice(t * 128, t * 128 + 128)
        r.nint[q, :] = jnp.transpose(r.nin[:, q])
    load_cos.wait()
    load_sin.wait()
    load_x_own.wait()

    def turn_into(pre_ref, rot_ref, k):
        def tile(t):
            q = rows_of(t, 256)
            pre = dot_nn(r.nin[q, :], r.mixw[k])
            pre_ref[q, :] = pre
            act = pre * jax.nn.sigmoid(pre)
            c, s = r.cosv[q, :], r.sinv[q, :]
            for h in range(H):
                a = act[:, h * HEAD:(h + 1) * HEAD]
                rot_ref[q, 2 * h * HEAD:(2 * h + 1) * HEAD] = (a * c).astype(BF)
                rot_ref[q, (2 * h + 1) * HEAD:(2 * h + 2) * HEAD] = (a * s).astype(BF)

        each(T // 256, tile)

    def project_into(ref, k):
        def tile(t):
            q = rows_of(t, 256)
            ref[q, :] = dot_nn(r.nin[q, :], r.mixw[k]).astype(ref.dtype)

        each(T // 256, tile)

    gather_forward(0)
    gather_send(2)
    gather_forward(1)
    gather_send(3)
    gather_wait(0)
    turn_into(r.qpre, r.qrot, 0)
    gather_forward(2)
    gather_send(4)
    gather_wait(1)
    turn_into(r.kpre, r.krot, 1)
    gather_forward(3)
    gather_send(5)
    gather_wait(2)
    project_into(r.val, 2)
    gather_forward(4)
    gather_send(6)
    gather_wait(3)
    project_into(r.gpre, 3)

    def wo_block(owner):
        return r.wo.at[:, pl.ds(pl.multiple_of(owner * C, C), C)]

    gather_wait(4)
    share_send(0, wo_block)

    NB = T // B
    REACH = LONGEST // B

    def weights_of(qb, kb, h):
        seen = jnp.broadcast_to(r.segk[0:1, kb * B:(kb + 1) * B], (B, B))
        same = widen(r.segq[qb * B:(qb + 1) * B, :], B) == seen
        if qb - kb < 2:
            return jnp.where(same, r.dec[qb - kb, h], 0.0)
        return jnp.where(same, r.dec[1, h] * jnp.exp(rate_of(h) * ((qb - kb - 1) * B)), 0.0)

    def u_block(qb):
        return lambda owner: r.ufull.at[qb * B:(qb + 1) * B, pl.ds(pl.multiple_of(owner * C, C), C)]

    def attend(qb):
        q = slice(qb * B, (qb + 1) * B)
        squares = jnp.zeros((B, 1), F32)
        for h in range(H):
            rot = slice(2 * h * HEAD, 2 * (h + 1) * HEAD)
            chan = slice(h * HEAD, (h + 1) * HEAD)
            total = jnp.zeros((B, HEAD), F32)
            for kb in range(max(0, qb - REACH), qb + 1):
                key = slice(kb * B, (kb + 1) * B)
                scores = dot_nt(r.qrot[q, rot], r.krot[key, rot]) * weights_of(qb, kb, h)
                total = total + dot_nn(scores.astype(BF), r.val[key, chan])
            r.mixed[q, chan] = total
            squares = squares + jnp.sum(total * total, axis=-1, keepdims=True)
            r.ufull[q, pl.ds(pl.multiple_of(j * C + h * HEAD, HEAD), HEAD)] = (
                total * r.gpre[q, chan]
            ).astype(BF)
        r.ss[j, :, q] = jnp.transpose(jnp.broadcast_to(squares, (B, 128)))[0:8, :]

    def ss_block(owner):
        return r.ss.at[owner]

    for qb in range(NB):
        attend(qb)
        share_send(1 + qb, u_block(qb))
        if qb == NB - 1:
            share_send(1 + NB, ss_block)
        if qb == 0:
            gather_forward(5)
            gather_send(7)
        if qb == 1:
            share_forward(0, wo_block)
        if qb == 2:
            gather_forward(6)
            gather_send(8)
        if qb > 0:
            share_forward(qb, u_block(qb - 1))
    share_forward(NB, u_block(NB - 1))
    share_forward(1 + NB, ss_block)
    gather_forward(7)
    gather_send(9)
    gather_wait(5)
    gather_wait(6)

    def gprod_tile(t):
        q = rows_of(t, 256)
        r.gprod[q, 0:F] = to_units(r.up[q, :], 0)

    each(T // 256, gprod_tile)
    gather_forward(8)
    gather_send(10)
    share_wait(0, wo_block)
    for qb in range(NB):
        share_wait(1 + qb, u_block(qb))
    share_wait(1 + NB, ss_block)

    total_ss = r.ss[0]
    for owner in range(1, mp):
        total_ss = total_ss + r.ss[owner]
    inverse = lax.rsqrt(total_ss * (1.0 / D) + EPSILON)
    for t in range(T // 128):
        q = slice(t * 128, t * 128 + 128)
        r.rcol[q, :] = jnp.transpose(jnp.broadcast_to(inverse[0:1, q], (128, 128)))

    def hidden_tile(t):
        q = rows_of(t, TB)
        out = widen(r.rcol[q, :], D) * dot_nn(r.ufull[q, :], r.wo[...])
        hidden = r.xv[q, :].astype(F32) + out
        scale = lax.rsqrt(jnp.mean(hidden * hidden, axis=-1, keepdims=True) + EPSILON)
        r.nmid[q, :] = (hidden * scale).astype(BF)

        @pl.when(t == j)
        def _():
            r.hown[...] = hidden

    each(T // TB, hidden_tile)
    gather_forward(9)
    gather_forward(10)
    for k in range(7, 11):
        gather_wait(k)

    def ff_block(x, c):
        q = rows_of(x * 2 + c, TB)
        gate = to_units(r.nmid[q, :], 1)
        upper = to_units(r.nmid[q, :], 2)
        r.prod[q, :] = (gate * upper).astype(BF)
        g = r.gprod[q, 0:F]
        grad_gate, grad_up = (g * upper).astype(BF), (g * gate).astype(BF)
        r.ggate[q, :] = grad_gate
        r.gup[q, :] = grad_up
        r.part[x, c] = (to_model(grad_gate, 1) + to_model(grad_up, 2)).astype(BF)

    used = sum_begin(0, 0, ff_block)
    put_ff_grad(0, r.prod, r.up)
    scatter_first(5)
    put_ff_grad(1, r.ggate, r.nmid)
    scatter_first(6)
    sum_arrived(0, 0)

    def back_tile(t):
        q = rows_of(t, 128)
        here = rows_of(j * (TB // 128) + t, 128)
        grad = sum_tile(0, q)
        hidden = r.hown[q, :]
        scale = lax.rsqrt(jnp.mean(hidden * hidden, axis=-1, keepdims=True) + EPSILON)
        normed = hidden * scale
        inner = jnp.mean(grad * normed, axis=-1, keepdims=True)
        out = r.up[here, :].astype(F32) + scale * (grad - normed * inner)
        r.ghid[q, :] = out
        low = out.astype(BF)
        r.hlow[here, :] = low
        mixer_out = hidden - r.xown[q, :].astype(F32)
        product = jnp.sum(low.astype(F32) * mixer_out, axis=-1, keepdims=True) * (1.0 / D)
        r.inn[j, :, q] = jnp.transpose(jnp.broadcast_to(product, (128, 128)))[0:8, :]

    def token_block(ref):
        return lambda owner: ref.at[rows_of(owner, TB)]

    NT = TB // 128
    BO, IN, GM, HL, IG = 2 + NB, 3 + NB, 4 + NB, 9 + NB, 9 + NB + NT

    def inn_block(owner):
        return r.inn.at[owner]

    def half_block(ref, t):
        return lambda owner: ref.at[rows_of(owner * NT + t, 128)]

    for t in range(NT):
        back_tile(t)
        share_send(HL + t, half_block(r.hlow, t))
    share_send(IN, inn_block)
    put_ff_grad(2, r.gup, r.nmid)
    scatter_first(7)
    scatter_second(5)
    for t in range(NT):
        share_forward(HL + t, half_block(r.hlow, t))
    share_forward(IN, inn_block)
    for copy in used:
        settle(copy)

    def expand_block(x, c):
        q = rows_of(x * 2 + c, TB)
        r.part[x, c] = to_model(r.prod[q, :], 0).astype(BF)

    used = sum_begin(1, 1, expand_block)
    for t in range(NT):
        share_wait(HL + t, half_block(r.hlow, t))
    share_wait(IN, inn_block)
    for owner in range(mp):
        for t in range(TB // 128):
            row = r.inn[owner, 0:1, t * 128:(t + 1) * 128]
            q = slice(owner * TB + t * 128, owner * TB + (t + 1) * 128)
            r.icol[q, :] = jnp.transpose(jnp.broadcast_to(row, (128, 128)))

    wo_rows = rows_of(j, C)

    def gated_tile(t):
        q = rows_of(t, 256)
        low = r.hlow[q, :]
        grad = dot_nt(low, r.wo[wo_rows, :])
        inner = widen(r.icol[q, :], C)
        inverse = widen(r.rcol[q, :], C)
        normed = r.mixed[q, :] * inverse
        r.gproj[3][q, :] = (grad * normed).astype(BF)
        r.gmix[q, :] = (inverse * (grad * r.gpre[q, :] - normed * inner)).astype(BF)
        r.rh[q, :] = (inverse * r.hlow[q, jcols].astype(F32)).astype(BF)

    each(T // 256, gated_tile)
    put_grad(4, r.ufull, r.rh)
    scatter_first(4)
    scatter_second(6)

    def swish_back(pre, grad):
        gate = jax.nn.sigmoid(pre)
        return grad * (gate * (1.0 + pre * (1.0 - gate)))

    def attend_back(h):
        rot = slice(2 * h * HEAD, 2 * (h + 1) * HEAD)
        chan = slice(h * HEAD, (h + 1) * HEAD)
        r.dk[...] = jnp.zeros_like(r.dk)
        r.dv[...] = jnp.zeros_like(r.dv)
        for qb in range(NB):
            q = slice(qb * B, (qb + 1) * B)
            total = jnp.zeros((B, 2 * HEAD), F32)
            for kb in range(max(0, qb - REACH), qb + 1):
                key = slice(kb * B, (kb + 1) * B)
                weights = weights_of(qb, kb, h)
                scores = (dot_nt(r.qrot[q, rot], r.krot[key, rot]) * weights).astype(BF)
                back = (dot_nt(r.gmix[q, chan], r.val[key, chan]) * weights).astype(BF)
                r.dv[key, :] += dot_tn(scores, r.gmix[q, chan])
                r.dk[key, :] += dot_tn(back, r.qrot[q, rot])
                total = total + dot_nn(back, r.krot[key, rot])
            turned = total[:, :HEAD] * r.cosv[q, :] + total[:, HEAD:] * r.sinv[q, :]
            r.gproj[0][q, chan] = swish_back(r.qpre[q, chan], turned).astype(BF)

        def tile(t):
            q = rows_of(t, 256)
            turned = r.dk[q, :HEAD] * r.cosv[q, :] + r.dk[q, HEAD:] * r.sinv[q, :]
            r.gproj[1][q, chan] = swish_back(r.kpre[q, chan], turned).astype(BF)
            r.gproj[2][q, chan] = r.dv[q, :].astype(BF)

        each(T // 256, tile)

    put_grad(3, r.nint, r.gproj[3], turned=True)
    scatter_first(3)
    attend_back(0)
    scatter_second(7)
    sum_arrived(1, 1)

    def output_tile(t):
        q = rows_of(t, 128)
        r.otile[0, q, :] = (r.hown[q, :] + sum_tile(1, q)).astype(BF)

    each(TB // 128, output_tile)
    share_send(BO, token_block(r.bo), src=r.otile.at[0])
    own_bo = pltpu.make_async_copy(r.otile.at[0], token_block(r.bo)(j), r.loc.at[7])
    own_bo.start()
    for h in range(1, H):
        attend_back(h)
    scatter_second(4)
    scatter_second(3)
    share_forward(BO, token_block(r.bo))
    for k in range(3):
        put_grad(k, r.nint, r.gproj[k], turned=True)
        scatter_first(k)
    for copy in used:
        settle(copy)

    def normed_block(x, c):
        q = rows_of(x * 2 + c, TB)
        out = dot_nt(r.gproj[0][q, :], r.mixw[0])
        for k in range(1, 4):
            out = out + dot_nt(r.gproj[k][q, :], r.mixw[k])
        r.part[x, c] = out.astype(BF)

    used = sum_begin(2, 0, normed_block)
    for k in range(3):
        scatter_second(k)
    squares = jnp.zeros((), F32)
    for k in range(5, 8):
        total = scatter_total(k)
        r.gfo[k - 5] = total
        squares = squares + jnp.sum(total * total)
    sum_arrived(2, 0)

    def input_tile(t):
        q = rows_of(t, 128)
        grad = sum_tile(0, q)
        v = r.xown[q, :].astype(F32)
        scale = lax.rsqrt(jnp.mean(v * v, axis=-1, keepdims=True) + EPSILON)
        normed = v * scale
        inner = jnp.mean(grad * normed, axis=-1, keepdims=True)
        r.otile[1, q, :] = (r.ghid[q, :] + scale * (grad - normed * inner)).astype(BF)

    for t in range(NT):
        input_tile(t)
        share_send(IG + t, half_block(r.ig, t), src=r.otile.at[1, t * 128:(t + 1) * 128])
    own_ig = pltpu.make_async_copy(r.otile.at[1], token_block(r.ig)(j), r.loc.at[6])
    own_ig.start()

    def grad_block(k):
        return lambda owner: r.gmo.at[k, :, pl.ds(pl.multiple_of(owner * C, C), C)]

    own_gm = []
    for k in (4, 3, 0, 1, 2):
        total = scatter_total(k).astype(BF)
        r.gown[k] = total
        squares = squares + jnp.sum(total.astype(F32) * total.astype(F32))
        share_send(GM + k, grad_block(k), src=r.gown.at[k])
        copy = pltpu.make_async_copy(r.gown.at[k], grad_block(k)(j), r.loc.at[k])
        copy.start()
        own_gm.append(copy)

    r.s1[j] = jnp.full((8, 128), squares, F32)
    for d in range(1, mp):
        go(r.s1.at[j], r.s1.at[j], r.q1s.at[d], r.q1r.at[d], mp=lax.rem(j + d, mp))
    for t in range(NT):
        share_forward(IG + t, half_block(r.ig, t))
    for d in range(1, mp):
        arrived(r.s1.at[lax.rem(j - d + mp, mp)], r.q1r.at[d])
    total = r.s1[0]
    for owner in range(1, mp):
        total = total + r.s1[owner]
    r.s2[i] = total
    for d in range(1, n):
        go(r.s2.at[i], r.s2.at[i], r.q2s.at[d], r.q2r.at[d], dp=lax.rem(i + d, n))
    for k in (4, 3, 0, 1, 2):
        share_forward(GM + k, grad_block(k))
    for d in range(1, n):
        arrived(r.s2.at[lax.rem(i - d + n, n)], r.q2r.at[d])
    total = r.s2[0]
    for owner in range(1, n):
        total = total + r.s2[owner]
    r.sqo[...] = total

    share_wait(BO, token_block(r.bo))
    for t in range(NT):
        share_wait(IG + t, half_block(r.ig, t))
    for k in (4, 3, 0, 1, 2):
        share_wait(GM + k, grad_block(k))
    for copy in [own_bo, own_ig] + own_gm:
        copy.wait()
    for copy in pending:
        copy.wait_send()


def fused(p, *operands):
    scratch = scratch_of(p)
    names = IN_NAMES + OUT_NAMES + tuple(scratch)
    anywhere = pl.BlockSpec(memory_space=pl.ANY)
    vmem = pl.BlockSpec(memory_space=pltpu.VMEM)
    smem = pl.BlockSpec(memory_space=pltpu.SMEM)
    return pl.pallas_call(
        partial(body, p, names),
        out_shape=(
            jax.ShapeDtypeStruct((p.T, p.D), BF),
            jax.ShapeDtypeStruct((p.T, p.D), BF),
            jax.ShapeDtypeStruct((5, p.S, p.D), BF),
            jax.ShapeDtypeStruct((3, p.F, p.S) if p.FD else (3, p.S, p.F), F32),
            jax.ShapeDtypeStruct((8, 128), F32),
        ),
        in_specs=[anywhere, anywhere, vmem, smem] + [anywhere] * 5,
        out_specs=(anywhere, anywhere, anywhere, vmem, vmem),
        scratch_shapes=list(scratch.values()),
        compiler_params=pltpu.CompilerParams(
            collective_id=0, has_side_effects=True, vmem_limit_bytes=VMEM_LIMIT
        ),
    )(*operands)


VMEM_LIMIT = 64 * 2**20 - 2**18


def renew(weight, momentum, shadow, grad, clip_factor):
    clipped = grad * clip_factor
    velocity = MOMENTUM * momentum + clipped
    updated = weight - LEARN_RATE * (clipped + MOMENTUM * velocity)
    average = SHADOW_DECAY * shadow + (1.0 - SHADOW_DECAY) * updated
    return (velocity, average, updated)


def turn_tables(tokens):
    theta = np.float32(10000.0) ** (-np.arange(HEAD, dtype=np.float32) / np.float32(HEAD))
    angle = np.arange(tokens, dtype=np.float32)[:, None] * theta.astype(np.float32)[None, :]
    angle = angle.astype(np.float64)
    return np.cos(angle).astype(np.float32), np.sin(angle).astype(np.float32)


def per_device(mesh, block_input, segment_ids, live_length, output_grad, mixer_weight, mixer_momentum, mixer_shadow,
               expand_weight, expand_momentum, expand_shadow, shrink_weight, shrink_momentum, shrink_shadow):
    rows, length, width = block_input.shape
    p = plan_of(mesh, length, width, shrink_weight.shape[0])
    turn = (lambda v: jnp.swapaxes(v, -1, -2)) if p.FD else (lambda v: v)
    if p.FD:
        shards = (turn(expand_weight), shrink_weight)
    else:
        shards = (jnp.concatenate([shrink_weight.T[None], expand_weight], axis=0).astype(BF), shrink_weight)
    cos, sin = turn_tables(length)
    out, grad_in, gm, gf, sq = fused(
        p, block_input[0], output_grad[0], segment_ids, live_length, jnp.asarray(cos), jnp.asarray(sin), mixer_weight, *shards
    )
    global_norm = jnp.sqrt(sq[0, 0])
    clip_factor = 1.0 / jnp.maximum(global_norm, 1.0)
    mixer_new = renew(mixer_weight, mixer_momentum, mixer_shadow, gm.astype(F32), clip_factor)
    expand_new = renew(turn(expand_weight), turn(expand_momentum), turn(expand_shadow), gf[1:], clip_factor)
    expand_new = tuple(turn(v) for v in expand_new)
    shrink_new = renew(shrink_weight, shrink_momentum, shrink_shadow, gf[0] if p.FD else gf[0].T, clip_factor)
    return (out[None], grad_in[None], global_norm) + mixer_new + expand_new + shrink_new


def solution(mesh):
    row, mixer, expand, shrink = P("dp", None, None), P(None, "dp", None), P(None, "dp", "mp"), P("mp", "dp")
    return jax.shard_map(
        partial(per_device, mesh),
        mesh=mesh,
        in_specs=(row, P("dp", None), P("dp"), row) + (mixer,) * 3 + (expand,) * 3 + (shrink,) * 3,
        out_specs=(row, row, P()) + (mixer,) * 3 + (expand,) * 3 + (shrink,) * 3,
        check_vma=False,
    )
```

```python
from functools import partial
from types import SimpleNamespace

import jax
import jax.numpy as jnp
import numpy as np
from jax import lax
from jax.experimental import pallas as pl
from jax.experimental.pallas import tpu as pltpu
from jax.sharding import PartitionSpec as P

HEAD = 128
EPSILON = 1e-06
LEARN_RATE = 32.0
MOMENTUM = 0.5
SHADOW_DECAY = 0.5
LAYER_PLACE = 12.0 / 24.0
LONGEST = 512
FF_ORDER = (1, 2, 0)
MESH = pl.DeviceIdType.MESH
BF = jnp.bfloat16
F32 = jnp.float32


def dot_nn(a, b):
    return lax.dot_general(a, b, (((1,), (0,)), ((), ())), preferred_element_type=F32)


def dot_nt(a, b):
    return lax.dot_general(a, b, (((1,), (1,)), ((), ())), preferred_element_type=F32)


def dot_tn(a, b):
    return lax.dot_general(a, b, (((0,), (0,)), ((), ())), preferred_element_type=F32)


def rows_of(index, size):
    return pl.ds(pl.multiple_of(index * size, size), size)


def each(count, body):
    def step(t, carry):
        body(t)
        return carry

    lax.fori_loop(0, count, step, 0)


def widen(column, width):
    return jnp.concatenate([column] * (width // 128), axis=1)


def plan_of(mesh, tokens, width, inner):
    n, mp = mesh.shape["dp"], mesh.shape["mp"]
    lo, core = 2, 2
    return SimpleNamespace(
        n=n, mp=mp, LO=lo, HI=n // lo, X=mp // core, T=tokens, D=width, C=width // mp, F=inner,
        S=width // n, H=width // mp // HEAD, TB=tokens // mp, B=min(256, tokens),
        NT=tokens // mp // 128, FD=(width // n) % 128 == 0,
    )


def scratch_of(p):
    T, D, C, F, S, HI, LO, X, TB, B = p.T, p.D, p.C, p.F, p.S, p.HI, p.LO, p.X, p.TB, p.B
    dma = pltpu.SemaphoreType.DMA
    v = pltpu.VMEM
    return dict(
        mixw=v((4, D, C), BF), wo=v((D, D), BF), ffw=v((3, F, D) if p.FD else (3, D, F), BF),
        xown=v((TB, D), BF), nin=v((T, D), BF), nint=v((D, T), BF), up=v((T, D), BF),
        cosv=v((T, HEAD), F32), sinv=v((T, HEAD), F32),
        segq=v((T, 128), F32), segk=v((8, T), F32), dec=v((2, p.H, B, B), F32),
        qpre=v((T, C), F32), kpre=v((T, C), F32), gpre=v((T, C), F32), val=v((T, C), BF),
        qrot=v((T, 2 * C), BF), krot=v((T, 2 * C), BF), mixed=v((T, C), F32),
        ufull=v((T, D), BF), ss=v((p.mp, 8, T), F32), rcol=v((T, 128), F32),
        inn=v((p.mp, 8, TB), F32), hown=v((TB, D), F32),
        gact=v((T, max(F, 4 * HEAD)), F32), uact=v((T, F), BF), prod=v((T, F), BF), ggate=v((T, F), BF), gup=v((T, F), BF),
        part=v((X, 2, TB, D), BF), recc=v((2, X, TB, D), BF), recx=v((2, X - 1, TB, D), BF),
        ghid=v((TB, D), F32), hlow=v((T, D), BF),
        gm=v((5, HI, LO, S, C), BF), rym=v((5, HI, S, C), BF), rzm=v((5, HI - 1, S, C), BF),
        gf=v((3, LO, F, HI * S) if p.FD else (3, HI, LO, S, F), BF),
        ryf=v((3, F, HI * S) if p.FD else (3, HI, S, F), BF),
        rzf=v((3, HI - 1, F, S) if p.FD else (3, HI - 1, S, F), BF),
        gown=v((5, S, C), BF), s1=v((p.mp, 8, 128), F32), s2=v((p.n, 8, 128), F32),
        loc=dma((10,)),
        zs=dma((11, HI - 1)), zr=dma((11, HI - 1)), ys=dma((11, HI)), yr=dma((11, HI)),
        xs=dma((20, X - 1)), xr=dma((20, X - 1)), cs=dma((20, X)), cr=dma((20, X)),
        acs=dma((3, X)), acr=dma((3, X)), axs=dma((3, X - 1, p.NT)), axr=dma((3, X - 1, p.NT)),
        bys=dma((8,)), byr=dma((8,)), bzs=dma((8, HI - 1)), bzr=dma((8, HI - 1)),
        q1s=dma((p.mp,)), q1r=dma((p.mp,)), q2s=dma((p.n,)), q2r=dma((p.n,)),
    )


IN_NAMES = ("x", "og", "seg", "live", "cos", "sin", "mixsh", "exsh", "shsh")
OUT_NAMES = ("bo", "ig", "gmo", "geo", "gso", "sqo")


def body(p, names, *refs):
    r = SimpleNamespace(**dict(zip(names, refs)))
    n, mp, LO, HI, X, T, D, C, F, S, H, TB, B = (
        p.n, p.mp, p.LO, p.HI, p.X, p.T, p.D, p.C, p.F, p.S, p.H, p.TB, p.B,
    )
    NT = p.NT
    i, j = lax.axis_index("dp"), lax.axis_index("mp")
    zi, yi = i // LO, lax.rem(i, LO)
    xi, ci = j // 2, lax.rem(j, 2)
    jcols = pl.ds(pl.multiple_of(j * C, C), C)
    pending = []
    r.xv, r.nmid = r.hlow, r.nin
    r.icol = r.gact.at[:, 3 * HEAD:4 * HEAD]
    r.dk, r.dv = r.gact.at[:, 0:2 * HEAD], r.gact.at[:, 2 * HEAD:3 * HEAD]
    r.gproj = [r.ggate.at[:, 0:C], r.ggate.at[:, C:2 * C], r.gup.at[:, 0:C], r.gup.at[:, C:2 * C]]
    r.gmix, r.rh = r.prod.at[:, 0:C], r.prod.at[:, C:2 * C]

    def go(src, dst, ssem, rsem, **device):
        copy = pltpu.make_async_remote_copy(
            src_ref=src, dst_ref=dst, send_sem=ssem, recv_sem=rsem,
            device_id=device, device_id_type=MESH,
        )
        copy.start()
        pending.append(copy)
        return copy

    def arrived(dst, sem):
        pltpu.make_async_copy(dst, dst, sem).wait()

    def settle(copy):
        copy.wait_send()
        pending[:] = [other for other in pending if other is not copy]

    def load(src, dst, sem):
        copy = pltpu.make_async_copy(src, dst, r.loc.at[sem])
        copy.start()
        return copy

    own_mix = [load(r.mixsh.at[k, :, jcols], r.qpre.at[k * S:(k + 1) * S], k) for k in range(5)]
    if p.FD:
        stage = [r.gact.at[0:F, m * S:(m + 1) * S] for m in range(3)]
        own_ff = [load(r.shsh if m == 0 else r.exsh.at[m - 1], stage[m], 5 + m) for m in range(3)]
    else:
        own_ff = [load(r.exsh.at[m], r.ffw.at[m, rows_of(i, S)], 5 + m) for m in range(3)]
    load_x = load(r.x, r.xv, 8)
    load_og = load(r.og, r.up, 9)

    def enter():
        barrier = pltpu.get_barrier_semaphore()
        for d in range(1, n):
            pl.semaphore_signal(barrier, inc=1, device_id={"dp": lax.rem(i + d, n)}, device_id_type=MESH)
        for d in range(1, mp):
            pl.semaphore_signal(barrier, inc=1, device_id={"mp": lax.rem(j + d, mp)}, device_id_type=MESH)
        pl.semaphore_wait(barrier, n - 1 + mp - 1)

    def slot(k, device):
        rows = rows_of(device, S)
        if k == 4:
            return r.wo.at[rows, jcols]
        if k < 4:
            return r.mixw.at[k, rows]
        m, half = FF_ORDER[(k - 5) // 2], (k - 5) % 2
        if p.FD:
            return r.ffw.at[m, half * F // 2:(half + 1) * F // 2, rows]
        return r.ffw.at[m, pl.ds(pl.multiple_of(device * S + half * S // 2, S // 2), S // 2)]

    def gather_ready(k):
        if k < 5:
            own_mix[k].wait()
            slot(k, i)[...] = r.qpre[k * S:(k + 1) * S, :].astype(BF)
        else:
            m, half = FF_ORDER[(k - 5) // 2], (k - 5) % 2
            if half == 0:
                own_ff[m].wait()
            if p.FD:
                slot(k, i)[...] = stage[m][half * F // 2:(half + 1) * F // 2, :].astype(BF)

    def gather_send(k):
        src = slot(k, i)
        for d in range(1, HI):
            go(src, src, r.zs.at[k, d - 1], r.zr.at[k, d - 1], dp=lax.rem(zi + d, HI) * LO + yi)
        go(src, src, r.ys.at[k, 0], r.yr.at[k, 0], dp=zi * LO + 1 - yi)

    def gather_forward(k):
        for d in range(1, HI):
            block = slot(k, lax.rem(zi - d + HI, HI) * LO + yi)
            arrived(block, r.zr.at[k, d - 1])
            go(block, block, r.ys.at[k, d], r.yr.at[k, d], dp=zi * LO + 1 - yi)

    def gather_wait(k):
        for d in range(HI):
            arrived(slot(k, lax.rem(zi - d + HI, HI) * LO + 1 - yi), r.yr.at[k, d])

    def share_send(s, block, src=None):
        own = block(j)
        src = own if src is None else src
        for d in range(1, X):
            go(src, own, r.xs.at[s, d - 1], r.xr.at[s, d - 1], mp=lax.rem(xi + d, X) * 2 + ci)
        go(src, own, r.cs.at[s, 0], r.cr.at[s, 0], mp=xi * 2 + 1 - ci)

    def share_forward(s, block):
        for d in range(1, X):
            part = block(lax.rem(xi - d + X, X) * 2 + ci)
            arrived(part, r.xr.at[s, d - 1])
            go(part, part, r.cs.at[s, d], r.cr.at[s, d], mp=xi * 2 + 1 - ci)

    def share_wait(s, block):
        for d in range(X):
            arrived(block(lax.rem(xi - d + X, X) * 2 + 1 - ci), r.cr.at[s, d])

    def sum_begin(s, b, compute):
        sent = []
        for d in [*range(1, X), 0]:
            to = lax.rem(xi + d, X)
            compute(to, 1 - ci)
            sent.append(go(
                r.part.at[to, 1 - ci], r.recc.at[b, to], r.acs.at[s, d], r.acr.at[s, d], mp=xi * 2 + 1 - ci
            ))
        for d in range(1, X):
            to = lax.rem(xi + d, X)
            compute(to, ci)
            arrived(r.recc.at[b, to], r.acr.at[s, d])
            for t in range(NT):
                q = slice(t * 128, (t + 1) * 128)
                r.part[to, ci, q] = (
                    r.part[to, ci, q].astype(F32) + r.recc[b, to, q].astype(F32)
                ).astype(BF)
                sent.append(go(
                    r.part.at[to, ci, q], r.recx.at[b, d - 1, q], r.axs.at[s, d - 1, t], r.axr.at[s, d - 1, t],
                    mp=to * 2 + ci,
                ))
        compute(xi, ci)
        return sent

    def sum_arrived(s, b, t):
        if t == 0:
            arrived(r.recc.at[b, xi], r.acr.at[s, 0])
        for d in range(1, X):
            arrived(r.recx.at[b, d - 1, t * 128:(t + 1) * 128], r.axr.at[s, d - 1, t])

    def sum_tile(b, q):
        total = r.part[xi, ci, q].astype(F32) + r.recc[b, xi, q].astype(F32)
        for d in range(1, X):
            total = total + r.recx[b, d - 1, q].astype(F32)
        return total

    def grad_ref(k):
        return r.gm.at[k] if k < 5 else r.gf.at[k - 5]

    def rec_y(k):
        return r.rym.at[k] if k < 5 else r.ryf.at[k - 5]

    def rec_z(k):
        return r.rzm.at[k] if k < 5 else r.rzf.at[k - 5]

    flat = p.FD

    def lanes(k):
        return flat and k >= 5

    def part_of(ref, k, z):
        return ref.at[:, rows_of(z, S)] if lanes(k) else ref.at[z]

    def mine(k, z):
        return r.gf.at[k - 5, yi, :, rows_of(z, S)] if lanes(k) else grad_ref(k).at[z, yi]

    def scatter_first(k):
        src = r.gf.at[k - 5, 1 - yi] if lanes(k) else grad_ref(k).at[:, 1 - yi]
        go(src, rec_y(k), r.bys.at[k], r.byr.at[k], dp=zi * LO + 1 - yi)

    def scatter_second(k):
        arrived(rec_y(k), r.byr.at[k])
        for d in range(1, HI):
            to = lax.rem(zi + d, HI)
            block = mine(k, to)
            block[...] = (block[...].astype(F32) + part_of(rec_y(k), k, to)[...].astype(F32)).astype(BF)
            go(block, rec_z(k).at[d - 1], r.bzs.at[k, d - 1], r.bzr.at[k, d - 1], dp=to * LO + yi)

    def scatter_total(k):
        rz = rec_z(k)
        for d in range(1, HI):
            arrived(rz.at[d - 1], r.bzr.at[k, d - 1])
        total = mine(k, zi)[...].astype(F32) + part_of(rec_y(k), k, zi)[...].astype(F32)
        for d in range(1, HI):
            total = total + rz[d - 1].astype(F32)
        return total

    def put_grad(k, lhs, rhs, turned=False):
        g = grad_ref(k)
        per = 256 // (LO * S)

        def tile(t):
            if turned:
                out = dot_nn(lhs[rows_of(t, 256), :], rhs[...])
            else:
                out = dot_tn(lhs[:, rows_of(t, 256)], rhs[...])
            g[pl.ds(t * per, per)] = out.astype(BF).reshape(per, LO, S, out.shape[-1])

        each(D // 256, tile)

    def put_ff_grad(m, units, model):
        if not flat:
            return put_grad(5 + m, model, units)
        for f in range(0, F, 256):
            q = slice(f, min(f + 256, F))
            out = dot_tn(units[:, q], model[...]).astype(BF)
            for y in range(LO):
                for z in range(HI):
                    r.gf[m, y, q, z * S:(z + 1) * S] = out[:, (z * LO + y) * S:(z * LO + y + 1) * S]

    def to_units(a, m):
        return dot_nt(a, r.ffw[m]) if flat else dot_nn(a, r.ffw[m])

    def to_model(a, m):
        return dot_nn(a, r.ffw[m]) if flat else dot_nt(a, r.ffw[m])

    gather_ready(0)
    gather_ready(1)
    enter()
    gather_send(0)
    gather_send(1)

    length = r.live[0]
    load_x.wait()

    def norm_tile(t):
        q = rows_of(t, 128)
        v = r.xv[q, :].astype(F32)
        r.nin[q, :] = (v * lax.rsqrt(jnp.mean(v * v, axis=-1, keepdims=True) + EPSILON)).astype(BF)

    each(T // 128, norm_tile)
    for k in range(2, 11):
        gather_ready(k)
    load_x_own = load(r.x.at[rows_of(j, TB)], r.xown, 8)
    load_og.wait()
    load_cos = load(r.cos, r.cosv, 0)
    load_sin = load(r.sin, r.sinv, 1)

    def live_tile(t):
        q = rows_of(t, 128)
        place = lax.broadcasted_iota(jnp.int32, (128, D), 0) + t * 128
        r.up[q, :] = jnp.where(place < length, r.up[q, :].astype(F32), 0.0).astype(BF)

    each(T // 128, live_tile)

    place = lax.broadcasted_iota(jnp.int32, (1, T), 1)
    segment = r.seg[...].astype(F32)
    r.segk[...] = jnp.broadcast_to(jnp.where(place < length, segment, -2.0), (8, T))
    seg_q = jnp.where(place < length, segment, -1.0)
    for t in range(T // 128):
        q = slice(t * 128, t * 128 + 128)
        r.segq[q, :] = jnp.transpose(jnp.broadcast_to(seg_q[:, q], (128, 128)))

    down = lax.broadcasted_iota(jnp.int32, (B, B), 0)
    over = lax.broadcasted_iota(jnp.int32, (B, B), 1)
    heads = D // HEAD

    def rate_of(h):
        return -(8.0 * (j * H + h).astype(F32) / heads) * (1.0 - LAYER_PLACE)

    for h in range(H):
        rate = rate_of(h)
        for o in range(2):
            distance = down - over + o * B
            fade = jnp.exp(rate * jnp.maximum(distance, 0).astype(F32))
            r.dec[o, h] = jnp.where(distance >= 0, fade, 0.0)

    for t in range(D // 128):
        q = slice(t * 128, t * 128 + 128)
        r.nint[q, :] = jnp.transpose(r.nin[:, q])
    load_cos.wait()
    load_sin.wait()
    load_x_own.wait()

    def turn_into(pre_ref, rot_ref, k):
        def tile(t):
            q = rows_of(t, 256)
            pre = dot_nn(r.nin[q, :], r.mixw[k])
            pre_ref[q, :] = pre
            act = pre * jax.nn.sigmoid(pre)
            c, s = r.cosv[q, :], r.sinv[q, :]
            for h in range(H):
                a = act[:, h * HEAD:(h + 1) * HEAD]
                rot_ref[q, 2 * h * HEAD:(2 * h + 1) * HEAD] = (a * c).astype(BF)
                rot_ref[q, (2 * h + 1) * HEAD:(2 * h + 2) * HEAD] = (a * s).astype(BF)

        each(T // 256, tile)

    def project_into(ref, k):
        def tile(t):
            q = rows_of(t, 256)
            ref[q, :] = dot_nn(r.nin[q, :], r.mixw[k]).astype(ref.dtype)

        each(T // 256, tile)

    gather_forward(0)
    gather_send(2)
    gather_forward(1)
    gather_send(3)
    gather_wait(0)
    turn_into(r.qpre, r.qrot, 0)
    gather_forward(2)
    gather_send(4)
    gather_wait(1)
    turn_into(r.kpre, r.krot, 1)
    gather_forward(3)
    gather_send(5)
    gather_wait(2)
    project_into(r.val, 2)
    gather_forward(4)
    gather_send(6)
    gather_wait(3)
    project_into(r.gpre, 3)

    def wo_block(owner):
        return r.wo.at[:, pl.ds(pl.multiple_of(owner * C, C), C)]

    gather_wait(4)
    share_send(0, wo_block)

    NB = T // B
    REACH = LONGEST // B

    def weights_of(qb, kb, h):
        seen = jnp.broadcast_to(r.segk[0:1, kb * B:(kb + 1) * B], (B, B))
        same = widen(r.segq[qb * B:(qb + 1) * B, :], B) == seen
        if qb - kb < 2:
            return jnp.where(same, r.dec[qb - kb, h], 0.0)
        return jnp.where(same, r.dec[1, h] * jnp.exp(rate_of(h) * ((qb - kb - 1) * B)), 0.0)

    def u_block(qb):
        return lambda owner: r.ufull.at[qb * B:(qb + 1) * B, pl.ds(pl.multiple_of(owner * C, C), C)]

    def attend(qb):
        q = slice(qb * B, (qb + 1) * B)
        squares = jnp.zeros((B, 1), F32)
        for h in range(H):
            rot = slice(2 * h * HEAD, 2 * (h + 1) * HEAD)
            chan = slice(h * HEAD, (h + 1) * HEAD)
            total = jnp.zeros((B, HEAD), F32)
            for kb in range(max(0, qb - REACH), qb + 1):
                key = slice(kb * B, (kb + 1) * B)
                scores = dot_nt(r.qrot[q, rot], r.krot[key, rot]) * weights_of(qb, kb, h)
                total = total + dot_nn(scores.astype(BF), r.val[key, chan])
            r.mixed[q, chan] = total
            squares = squares + jnp.sum(total * total, axis=-1, keepdims=True)
            r.ufull[q, pl.ds(pl.multiple_of(j * C + h * HEAD, HEAD), HEAD)] = (
                total * r.gpre[q, chan]
            ).astype(BF)
        r.ss[j, :, q] = jnp.transpose(jnp.broadcast_to(squares, (B, 128)))[0:8, :]

    def ss_block(owner):
        return r.ss.at[owner]

    for qb in range(NB):
        attend(qb)
        share_send(1 + qb, u_block(qb))
        if qb == NB - 1:
            share_send(1 + NB, ss_block)
        if qb == 0:
            gather_forward(5)
            gather_send(7)
        if qb == 1:
            share_forward(0, wo_block)
        if qb == 2:
            gather_forward(6)
            gather_send(8)
        if qb > 0:
            share_forward(qb, u_block(qb - 1))
    share_forward(NB, u_block(NB - 1))
    share_forward(1 + NB, ss_block)
    gather_forward(7)
    gather_send(9)
    gather_forward(8)
    gather_send(10)
    share_wait(0, wo_block)
    for qb in range(NB):
        share_wait(1 + qb, u_block(qb))
    share_wait(1 + NB, ss_block)

    total_ss = r.ss[0]
    for owner in range(1, mp):
        total_ss = total_ss + r.ss[owner]
    inverse = lax.rsqrt(total_ss * (1.0 / D) + EPSILON)
    for t in range(T // 128):
        q = slice(t * 128, t * 128 + 128)
        r.rcol[q, :] = jnp.transpose(jnp.broadcast_to(inverse[0:1, q], (128, 128)))

    def hidden_tile(t):
        q = rows_of(t, TB)
        out = widen(r.rcol[q, :], D) * dot_nn(r.ufull[q, :], r.wo[...])
        hidden = r.xv[q, :].astype(F32) + out
        scale = lax.rsqrt(jnp.mean(hidden * hidden, axis=-1, keepdims=True) + EPSILON)
        r.nmid[q, :] = (hidden * scale).astype(BF)

        @pl.when(t == j)
        def _():
            r.hown[...] = hidden

    each(T // TB, hidden_tile)
    gather_wait(5)
    gather_wait(6)

    def gate_tile(t):
        q = rows_of(t, 256)
        r.gact[q, 0:F] = to_units(r.nmid[q, :], 1)

    each(T // 256, gate_tile)
    gather_forward(9)
    gather_wait(7)
    gather_wait(8)

    def up_tile(t):
        q = rows_of(t, 256)
        upper = to_units(r.nmid[q, :], 2)
        r.uact[q, :] = upper.astype(BF)
        r.prod[q, :] = (r.gact[q, 0:F] * upper).astype(BF)

    each(T // 256, up_tile)
    put_ff_grad(0, r.prod, r.up)
    scatter_first(5)
    gather_forward(10)
    gather_wait(9)
    gather_wait(10)

    def mid_block(x, c):
        q = rows_of(x * 2 + c, TB)
        g = to_units(r.up[q, :], 0)
        grad_gate, grad_up = (g * r.uact[q, :].astype(F32)).astype(BF), (g * r.gact[q, 0:F]).astype(BF)
        r.ggate[q, :] = grad_gate
        r.gup[q, :] = grad_up
        r.part[x, c] = (to_model(grad_gate, 1) + to_model(grad_up, 2)).astype(BF)

    used = sum_begin(0, 0, mid_block)
    put_ff_grad(1, r.ggate, r.nmid)
    scatter_first(6)

    def back_tile(t):
        q = rows_of(t, 128)
        here = rows_of(j * (TB // 128) + t, 128)
        grad = sum_tile(0, q)
        hidden = r.hown[q, :]
        scale = lax.rsqrt(jnp.mean(hidden * hidden, axis=-1, keepdims=True) + EPSILON)
        normed = hidden * scale
        inner = jnp.mean(grad * normed, axis=-1, keepdims=True)
        out = r.up[here, :].astype(F32) + scale * (grad - normed * inner)
        r.ghid[q, :] = out
        low = out.astype(BF)
        r.hlow[here, :] = low
        mixer_out = hidden - r.xown[q, :].astype(F32)
        product = jnp.sum(low.astype(F32) * mixer_out, axis=-1, keepdims=True) * (1.0 / D)
        r.inn[j, :, q] = jnp.transpose(jnp.broadcast_to(product, (128, 128)))[0:8, :]

    def token_block(ref):
        return lambda owner: ref.at[rows_of(owner, TB)]

    BO, IN, GM, HL, IG = 2 + NB, 3 + NB, 4 + NB, 9 + NB, 9 + NB + NT

    def inn_block(owner):
        return r.inn.at[owner]

    def half_block(ref, t):
        return lambda owner: ref.at[rows_of(owner * NT + t, 128)]

    for t in range(NT):
        sum_arrived(0, 0, t)
        back_tile(t)
        share_send(HL + t, half_block(r.hlow, t))
    share_send(IN, inn_block)
    put_ff_grad(2, r.gup, r.nmid)
    scatter_first(7)
    scatter_second(5)
    for t in range(NT):
        share_forward(HL + t, half_block(r.hlow, t))
    share_forward(IN, inn_block)
    for copy in used:
        settle(copy)

    def expand_block(x, c):
        q = rows_of(x * 2 + c, TB)
        r.part[x, c] = to_model(r.prod[q, :], 0).astype(BF)

    used = sum_begin(1, 1, expand_block)
    for t in range(NT):
        share_wait(HL + t, half_block(r.hlow, t))
    share_wait(IN, inn_block)
    for owner in range(mp):
        for t in range(TB // 128):
            row = r.inn[owner, 0:1, t * 128:(t + 1) * 128]
            q = slice(owner * TB + t * 128, owner * TB + (t + 1) * 128)
            r.icol[q, :] = jnp.transpose(jnp.broadcast_to(row, (128, 128)))

    wo_rows = rows_of(j, C)

    def gated_tile(t):
        q = rows_of(t, 256)
        low = r.hlow[q, :]
        grad = dot_nt(low, r.wo[wo_rows, :])
        inner = widen(r.icol[q, :], C)
        inverse = widen(r.rcol[q, :], C)
        normed = r.mixed[q, :] * inverse
        r.gproj[3][q, :] = (grad * normed).astype(BF)
        r.gmix[q, :] = (inverse * (grad * r.gpre[q, :] - normed * inner)).astype(BF)
        r.rh[q, :] = (inverse * r.hlow[q, jcols].astype(F32)).astype(BF)

    each(T // 256, gated_tile)
    put_grad(4, r.ufull, r.rh)
    scatter_first(4)
    scatter_second(6)

    def swish_back(pre, grad):
        gate = jax.nn.sigmoid(pre)
        return grad * (gate * (1.0 + pre * (1.0 - gate)))

    def attend_back(h):
        rot = slice(2 * h * HEAD, 2 * (h + 1) * HEAD)
        chan = slice(h * HEAD, (h + 1) * HEAD)
        r.dk[...] = jnp.zeros_like(r.dk)
        r.dv[...] = jnp.zeros_like(r.dv)
        for qb in range(NB):
            q = slice(qb * B, (qb + 1) * B)
            total = jnp.zeros((B, 2 * HEAD), F32)
            for kb in range(max(0, qb - REACH), qb + 1):
                key = slice(kb * B, (kb + 1) * B)
                weights = weights_of(qb, kb, h)
                scores = (dot_nt(r.qrot[q, rot], r.krot[key, rot]) * weights).astype(BF)
                back = (dot_nt(r.gmix[q, chan], r.val[key, chan]) * weights).astype(BF)
                r.dv[key, :] += dot_tn(scores, r.gmix[q, chan])
                r.dk[key, :] += dot_tn(back, r.qrot[q, rot])
                total = total + dot_nn(back, r.krot[key, rot])
            turned = total[:, :HEAD] * r.cosv[q, :] + total[:, HEAD:] * r.sinv[q, :]
            r.gproj[0][q, chan] = swish_back(r.qpre[q, chan], turned).astype(BF)

        def tile(t):
            q = rows_of(t, 256)
            turned = r.dk[q, :HEAD] * r.cosv[q, :] + r.dk[q, HEAD:] * r.sinv[q, :]
            r.gproj[1][q, chan] = swish_back(r.kpre[q, chan], turned).astype(BF)
            r.gproj[2][q, chan] = r.dv[q, :].astype(BF)

        each(T // 256, tile)

    put_grad(3, r.nint, r.gproj[3], turned=True)
    scatter_first(3)
    attend_back(0)
    for t in range(NT):
        sum_arrived(1, 1, t)

    def output_tile(t):
        q = rows_of(t, 128)
        r.recx[1, 0, q] = (r.hown[q, :] + sum_tile(1, q)).astype(BF)

    each(TB // 128, output_tile)
    share_send(BO, token_block(r.bo), src=r.recx.at[1, 0])
    own_bo = pltpu.make_async_copy(r.recx.at[1, 0], token_block(r.bo)(j), r.loc.at[7])
    own_bo.start()
    for h in range(1, H):
        attend_back(h)
    scatter_second(7)
    scatter_second(4)
    scatter_second(3)
    share_forward(BO, token_block(r.bo))
    for k in range(3):
        put_grad(k, r.nint, r.gproj[k], turned=True)
        scatter_first(k)
    for copy in used:
        settle(copy)

    def normed_block(x, c):
        q = rows_of(x * 2 + c, TB)
        out = dot_nt(r.gproj[0][q, :], r.mixw[0])
        for k in range(1, 4):
            out = out + dot_nt(r.gproj[k][q, :], r.mixw[k])
        r.part[x, c] = out.astype(BF)

    used = sum_begin(2, 0, normed_block)
    for k in range(3):
        scatter_second(k)

    def input_tile(t):
        q = rows_of(t, 128)
        grad = sum_tile(0, q)
        v = r.xown[q, :].astype(F32)
        scale = lax.rsqrt(jnp.mean(v * v, axis=-1, keepdims=True) + EPSILON)
        normed = v * scale
        inner = jnp.mean(grad * normed, axis=-1, keepdims=True)
        r.recx[0, 0, q] = (r.ghid[q, :] + scale * (grad - normed * inner)).astype(BF)

    for t in range(NT):
        sum_arrived(2, 0, t)
        input_tile(t)
        share_send(IG + t, half_block(r.ig, t), src=r.recx.at[0, 0, t * 128:(t + 1) * 128])
    own_ig = pltpu.make_async_copy(r.recx.at[0, 0], token_block(r.ig)(j), r.loc.at[6])
    own_ig.start()

    def grad_block(k):
        return lambda owner: r.gmo.at[k, :, pl.ds(pl.multiple_of(owner * C, C), C)]

    squares = jnp.zeros((), F32)
    for k in range(5, 8):
        total = scatter_total(k)
        if k == 5:
            r.gso[...] = total
        else:
            r.geo[k - 6] = total
        squares = squares + jnp.sum(total * total)
    own_gm = []
    for k in (4, 3, 0, 1, 2):
        total = scatter_total(k).astype(BF)
        r.gown[k] = total
        squares = squares + jnp.sum(total.astype(F32) * total.astype(F32))
        share_send(GM + k, grad_block(k), src=r.gown.at[k])
        copy = pltpu.make_async_copy(r.gown.at[k], grad_block(k)(j), r.loc.at[k])
        copy.start()
        own_gm.append(copy)

    r.s1[j] = jnp.full((8, 128), squares, F32)
    for d in range(1, mp):
        go(r.s1.at[j], r.s1.at[j], r.q1s.at[d], r.q1r.at[d], mp=lax.rem(j + d, mp))
    for t in range(NT):
        share_forward(IG + t, half_block(r.ig, t))
    for d in range(1, mp):
        arrived(r.s1.at[lax.rem(j - d + mp, mp)], r.q1r.at[d])
    total = r.s1[0]
    for owner in range(1, mp):
        total = total + r.s1[owner]
    r.s2[i] = total
    for d in range(1, n):
        go(r.s2.at[i], r.s2.at[i], r.q2s.at[d], r.q2r.at[d], dp=lax.rem(i + d, n))
    for k in (4, 3, 0, 1, 2):
        share_forward(GM + k, grad_block(k))
    for d in range(1, n):
        arrived(r.s2.at[lax.rem(i - d + n, n)], r.q2r.at[d])
    total = r.s2[0]
    for owner in range(1, n):
        total = total + r.s2[owner]
    r.sqo[...] = total

    share_wait(BO, token_block(r.bo))
    for t in range(NT):
        share_wait(IG + t, half_block(r.ig, t))
    for k in (4, 3, 0, 1, 2):
        share_wait(GM + k, grad_block(k))
    for copy in [own_bo, own_ig] + own_gm:
        copy.wait()
    for copy in pending:
        copy.wait_send()


def fused(p, *operands):
    scratch = scratch_of(p)
    names = IN_NAMES + OUT_NAMES + tuple(scratch)
    anywhere = pl.BlockSpec(memory_space=pl.ANY)
    vmem = pl.BlockSpec(memory_space=pltpu.VMEM)
    smem = pl.BlockSpec(memory_space=pltpu.SMEM)
    return pl.pallas_call(
        partial(body, p, names),
        out_shape=(
            jax.ShapeDtypeStruct((p.T, p.D), BF),
            jax.ShapeDtypeStruct((p.T, p.D), BF),
            jax.ShapeDtypeStruct((5, p.S, p.D), BF),
            jax.ShapeDtypeStruct((2, p.F, p.S) if p.FD else (2, p.S, p.F), F32),
            jax.ShapeDtypeStruct((p.F, p.S) if p.FD else (p.S, p.F), F32),
            jax.ShapeDtypeStruct((8, 128), F32),
        ),
        in_specs=[anywhere, anywhere, vmem, smem] + [anywhere] * 5,
        out_specs=(anywhere, anywhere, anywhere, vmem, vmem, vmem),
        scratch_shapes=list(scratch.values()),
        compiler_params=pltpu.CompilerParams(
            collective_id=0, has_side_effects=True, vmem_limit_bytes=VMEM_LIMIT
        ),
    )(*operands)


VMEM_LIMIT = 64 * 2**20 - 2**18


def renew(weight, momentum, shadow, grad, clip_factor):
    clipped = grad * clip_factor
    velocity = MOMENTUM * momentum + clipped
    updated = weight - LEARN_RATE * (clipped + MOMENTUM * velocity)
    average = SHADOW_DECAY * shadow + (1.0 - SHADOW_DECAY) * updated
    return (velocity, average, updated)


def update_body(cuts, *refs):
    kinds, pieces = len(cuts), sum(len(c) for c in cuts)
    sq, carried = refs[0], refs[1:3]
    ins = [refs[3 + 4 * w:7 + 4 * w] for w in range(kinds)]
    refs = refs[3 + 4 * kinds:]
    norm_out, carried_out = refs[0], refs[1:3]
    outs = [refs[3 + 3 * w:6 + 3 * w] for w in range(kinds)]
    refs = refs[3 + 3 * kinds:]
    held = [refs[4 * w:4 * w + 4] for w in range(kinds)]
    made = [refs[4 * kinds + 3 * w:4 * kinds + 3 * w + 3] for w in range(kinds)]
    in_sem, out_sem, carry_sem = refs[7 * kinds:]
    loads, order = {}, [(w, c) for w in range(kinds) for c in range(len(cuts[w]))]
    for at, (w, c) in enumerate(order):
        for a in range(4):
            cut = cuts[w][c]
            loads[at, a] = pltpu.make_async_copy(ins[w][a].at[cut], held[w][a].at[cut], in_sem.at[at, a])
            loads[at, a].start()
    copies = [pltpu.make_async_copy(carried[a], carried_out[a], carry_sem.at[a]) for a in range(2)]
    for copy in copies:
        copy.start()
    norm = jnp.sqrt(sq[...])
    norm_out[...] = norm
    clip_factor = 1.0 / jnp.maximum(jnp.max(norm), 1.0)
    for at, (w, c) in enumerate(order):
        cut = cuts[w][c]
        for a in range(4):
            loads[at, a].wait()
        new = renew(*[held[w][a][cut] for a in range(3)], held[w][3][cut].astype(F32), clip_factor)
        for a in range(3):
            made[w][a][cut] = new[a]
            copy = pltpu.make_async_copy(made[w][a].at[cut], outs[w][a].at[cut], out_sem.at[at, a])
            copy.start()
            copies.append(copy)
    for copy in copies:
        copy.wait()


def update(sq, carried, weights):
    cuts = [[c for c in range(g[0].shape[0])] if g[0].ndim == 3 else [slice(None)] for g in weights]
    pieces = sum(len(c) for c in cuts)
    anywhere = pl.BlockSpec(memory_space=pl.ANY)
    vmem = pl.BlockSpec(memory_space=pltpu.VMEM)
    flat_in = [a for group in weights for a in group]
    flat_out = [a for group in weights for a in group[:3]]
    dma = pltpu.SemaphoreType.DMA
    size = sum(a.size * a.dtype.itemsize for a in flat_in + flat_out + 2 * list(carried))
    return pl.pallas_call(
        partial(update_body, cuts),
        out_shape=[jax.ShapeDtypeStruct(a.shape, a.dtype) for a in [sq, *carried, *flat_out]],
        in_specs=[vmem] + [anywhere] * (2 + len(flat_in)),
        out_specs=[vmem] + [anywhere] * (2 + len(flat_out)),
        scratch_shapes=[pltpu.VMEM(a.shape, a.dtype) for a in flat_in + flat_out]
        + [dma((pieces, 4)), dma((pieces, 3)), dma((2,))],
        cost_estimate=pl.CostEstimate(flops=size, bytes_accessed=size, transcendentals=0),
        compiler_params=pltpu.CompilerParams(vmem_limit_bytes=VMEM_LIMIT),
    )(sq, *carried, *flat_in)


def turn_tables(tokens):
    theta = np.float32(10000.0) ** (-np.arange(HEAD, dtype=np.float32) / np.float32(HEAD))
    angle = np.arange(tokens, dtype=np.float32)[:, None] * theta.astype(np.float32)[None, :]
    angle = angle.astype(np.float64)
    return np.cos(angle).astype(np.float32), np.sin(angle).astype(np.float32)


def per_device(mesh, block_input, segment_ids, live_length, output_grad, mixer_weight, mixer_momentum, mixer_shadow,
               expand_weight, expand_momentum, expand_shadow, shrink_weight, shrink_momentum, shrink_shadow):
    rows, length, width = block_input.shape
    p = plan_of(mesh, length, width, shrink_weight.shape[0])
    turn = (lambda v: jnp.swapaxes(v, -1, -2)) if p.FD else (lambda v: v)
    if p.FD:
        shards = (turn(expand_weight), shrink_weight)
    else:
        shards = (jnp.concatenate([shrink_weight.T[None], expand_weight], axis=0).astype(BF), shrink_weight)
    cos, sin = turn_tables(length)
    out, grad_in, gm, ge, gs, sq = fused(
        p, block_input[0], output_grad[0], segment_ids, live_length, jnp.asarray(cos), jnp.asarray(sin), mixer_weight, *shards
    )
    new = update(sq, (out, grad_in), (
        (mixer_weight, mixer_momentum, mixer_shadow, gm),
        (turn(expand_weight), turn(expand_momentum), turn(expand_shadow), ge),
        (shrink_weight, shrink_momentum, shrink_shadow, gs if p.FD else gs.T),
    ))
    norm, out, grad_in = new[:3]
    return (out[None], grad_in[None], norm[0, 0], *new[3:6], *(turn(v) for v in new[6:9]), *new[9:12])


def solution(mesh):
    row, mixer, expand, shrink = P("dp", None, None), P(None, "dp", None), P(None, "dp", "mp"), P("mp", "dp")
    return jax.shard_map(
        partial(per_device, mesh),
        mesh=mesh,
        in_specs=(row, P("dp", None), P("dp"), row) + (mixer,) * 3 + (expand,) * 3 + (shrink,) * 3,
        out_specs=(row, row, P()) + (mixer,) * 3 + (expand,) * 3 + (shrink,) * 3,
        check_vma=False,
    )
```

```python
from functools import partial
from types import SimpleNamespace

import jax
import jax.numpy as jnp
import numpy as np
from jax import lax
from jax.experimental import pallas as pl
from jax.experimental.pallas import tpu as pltpu
from jax.sharding import PartitionSpec as P

HEAD = 128
EPSILON = 1e-06
LEARN_RATE = 32.0
MOMENTUM = 0.5
SHADOW_DECAY = 0.5
LAYER_PLACE = 12.0 / 24.0
LONGEST = 512
FF_ORDER = (1, 2, 0)
MESH = pl.DeviceIdType.MESH
BF = jnp.bfloat16
F32 = jnp.float32


def dot_nn(a, b):
    return lax.dot_general(a, b, (((1,), (0,)), ((), ())), preferred_element_type=F32)


def dot_nt(a, b):
    return lax.dot_general(a, b, (((1,), (1,)), ((), ())), preferred_element_type=F32)


def dot_tn(a, b):
    return lax.dot_general(a, b, (((0,), (0,)), ((), ())), preferred_element_type=F32)


def rows_of(index, size):
    return pl.ds(pl.multiple_of(index * size, size), size)


def each(count, body):
    def step(t, carry):
        body(t)
        return carry

    lax.fori_loop(0, count, step, 0)


def widen(column, width):
    return jnp.concatenate([column] * (width // 128), axis=1)


def plan_of(mesh, tokens, width, inner):
    n, mp = mesh.shape["dp"], mesh.shape["mp"]
    lo, core = 2, 2
    return SimpleNamespace(
        n=n, mp=mp, LO=lo, HI=n // lo, X=mp // core, T=tokens, D=width, C=width // mp, F=inner,
        S=width // n, H=width // mp // HEAD, TB=tokens // mp, B=min(256, tokens),
        NT=tokens // mp // 128, FD=(width // n) % 128 == 0,
    )


def scratch_of(p):
    T, D, C, F, S, HI, LO, X, TB, B = p.T, p.D, p.C, p.F, p.S, p.HI, p.LO, p.X, p.TB, p.B
    dma = pltpu.SemaphoreType.DMA
    v = pltpu.VMEM
    return dict(
        mixw=v((4, D, C), BF), wo=v((D, D), BF), ffw=v((3, F, D) if p.FD else (3, D, F), BF),
        xown=v((TB, D), BF), nin=v((T, D), BF), nint=v((D, T), BF), up=v((T, D), BF),
        cosv=v((T, HEAD), F32), sinv=v((T, HEAD), F32),
        segq=v((T, 128), F32), segk=v((8, T), F32), dec=v((2, p.H, B, B), F32),
        qpre=v((T, C), F32), kpre=v((T, C), F32), gpre=v((T, C), F32), val=v((T, C), BF),
        qrot=v((T, 2 * C), BF), krot=v((T, 2 * C), BF), mixed=v((T, C), F32),
        ufull=v((T, D), BF), ss=v((p.mp, 8, T), F32), rcol=v((T, 128), F32),
        inn=v((p.mp, 8, TB), F32), hown=v((TB, D), F32),
        gact=v((T, max(F, 4 * HEAD)), F32), uact=v((T, F), BF), prod=v((T, F), BF), ggate=v((T, F), BF), gup=v((T, F), BF),
        part=v((X, 2, TB, D), BF), recc=v((2, X, TB, D), BF), recx=v((2, X - 1, TB, D), BF),
        ghid=v((TB, D), F32), hlow=v((T, D), BF),
        gm=v((5, HI, LO, S, C), BF), rym=v((5, HI, S, C), BF), rzm=v((5, HI - 1, S, C), BF),
        gf=v((3, LO, F, HI * S) if p.FD else (3, HI, LO, S, F), BF),
        ryf=v((3, F, HI * S) if p.FD else (3, HI, S, F), BF),
        rzf=v((3, HI - 1, F, S) if p.FD else (3, HI - 1, S, F), BF),
        s1=v((p.mp, 8, 128), F32), s2=v((p.n, 8, 128), F32),
        loc=dma((10,)),
        zs=dma((11, HI - 1)), zr=dma((11, HI - 1)), ys=dma((11, HI)), yr=dma((11, HI)),
        xs=dma((20, X - 1)), xr=dma((20, X - 1)), cs=dma((20, X)), cr=dma((20, X)),
        acs=dma((3, X)), acr=dma((3, X)), axs=dma((3, X - 1, p.NT)), axr=dma((3, X - 1, p.NT)),
        bys=dma((8,)), byr=dma((8,)), bzs=dma((8, HI - 1)), bzr=dma((8, HI - 1)),
        q1s=dma((p.mp,)), q1r=dma((p.mp,)), q2s=dma((p.n,)), q2r=dma((p.n,)),
    )


IN_NAMES = ("x", "og", "seg", "live", "cos", "sin", "mixsh", "exsh", "shsh")
OUT_NAMES = ("bo", "ig", "gmo", "geo", "gso", "sqo")


def body(p, names, *refs):
    r = SimpleNamespace(**dict(zip(names, refs)))
    n, mp, LO, HI, X, T, D, C, F, S, H, TB, B = (
        p.n, p.mp, p.LO, p.HI, p.X, p.T, p.D, p.C, p.F, p.S, p.H, p.TB, p.B,
    )
    NT = p.NT
    i, j = lax.axis_index("dp"), lax.axis_index("mp")
    zi, yi = i // LO, lax.rem(i, LO)
    xi, ci = j // 2, lax.rem(j, 2)
    jcols = pl.ds(pl.multiple_of(j * C, C), C)
    pending = []
    r.xv, r.nmid = r.hlow, r.nin
    r.bov, r.igv, r.gmv = r.up, r.ufull, r.wo
    r.icol = r.gact.at[:, 3 * HEAD:4 * HEAD]
    r.dk, r.dv = r.gact.at[:, 0:2 * HEAD], r.gact.at[:, 2 * HEAD:3 * HEAD]
    r.gproj = [r.ggate.at[:, 0:C], r.ggate.at[:, C:2 * C], r.gup.at[:, 0:C], r.gup.at[:, C:2 * C]]
    r.gmix, r.rh = r.prod.at[:, 0:C], r.prod.at[:, C:2 * C]

    def go(src, dst, ssem, rsem, **device):
        copy = pltpu.make_async_remote_copy(
            src_ref=src, dst_ref=dst, send_sem=ssem, recv_sem=rsem,
            device_id=device, device_id_type=MESH,
        )
        copy.start()
        pending.append(copy)
        return copy

    def arrived(dst, sem):
        pltpu.make_async_copy(dst, dst, sem).wait()

    def settle(copy):
        copy.wait_send()
        pending[:] = [other for other in pending if other is not copy]

    def load(src, dst, sem):
        copy = pltpu.make_async_copy(src, dst, r.loc.at[sem])
        copy.start()
        return copy

    own_mix = [load(r.mixsh.at[k, :, jcols], r.qpre.at[k * S:(k + 1) * S], k) for k in range(5)]
    if p.FD:
        stage = [r.gact.at[0:F, m * S:(m + 1) * S] for m in range(3)]
        own_ff = [load(r.shsh if m == 0 else r.exsh.at[m - 1], stage[m], 5 + m) for m in range(3)]
    else:
        own_ff = [load(r.exsh.at[m], r.ffw.at[m, rows_of(i, S)], 5 + m) for m in range(3)]
    load_x = load(r.x, r.xv, 8)
    load_og = load(r.og, r.up, 9)

    def enter():
        barrier = pltpu.get_barrier_semaphore()
        for d in range(1, n):
            pl.semaphore_signal(barrier, inc=1, device_id={"dp": lax.rem(i + d, n)}, device_id_type=MESH)
        for d in range(1, mp):
            pl.semaphore_signal(barrier, inc=1, device_id={"mp": lax.rem(j + d, mp)}, device_id_type=MESH)
        pl.semaphore_wait(barrier, n - 1 + mp - 1)

    def slot(k, device):
        rows = rows_of(device, S)
        if k == 4:
            return r.wo.at[rows, jcols]
        if k < 4:
            return r.mixw.at[k, rows]
        m, half = FF_ORDER[(k - 5) // 2], (k - 5) % 2
        if p.FD:
            return r.ffw.at[m, half * F // 2:(half + 1) * F // 2, rows]
        return r.ffw.at[m, pl.ds(pl.multiple_of(device * S + half * S // 2, S // 2), S // 2)]

    def gather_ready(k):
        if k < 5:
            own_mix[k].wait()
            slot(k, i)[...] = r.qpre[k * S:(k + 1) * S, :].astype(BF)
        else:
            m, half = FF_ORDER[(k - 5) // 2], (k - 5) % 2
            if half == 0:
                own_ff[m].wait()
            if p.FD:
                slot(k, i)[...] = stage[m][half * F // 2:(half + 1) * F // 2, :].astype(BF)

    def gather_send(k):
        src = slot(k, i)
        for d in range(1, HI):
            go(src, src, r.zs.at[k, d - 1], r.zr.at[k, d - 1], dp=lax.rem(zi + d, HI) * LO + yi)
        go(src, src, r.ys.at[k, 0], r.yr.at[k, 0], dp=zi * LO + 1 - yi)

    def gather_forward(k):
        for d in range(1, HI):
            block = slot(k, lax.rem(zi - d + HI, HI) * LO + yi)
            arrived(block, r.zr.at[k, d - 1])
            go(block, block, r.ys.at[k, d], r.yr.at[k, d], dp=zi * LO + 1 - yi)

    def gather_wait(k):
        for d in range(HI):
            arrived(slot(k, lax.rem(zi - d + HI, HI) * LO + 1 - yi), r.yr.at[k, d])

    def share_send(s, block, src=None):
        own = block(j)
        src = own if src is None else src
        for d in range(1, X):
            go(src, own, r.xs.at[s, d - 1], r.xr.at[s, d - 1], mp=lax.rem(xi + d, X) * 2 + ci)
        go(src, own, r.cs.at[s, 0], r.cr.at[s, 0], mp=xi * 2 + 1 - ci)

    def share_forward(s, block):
        for d in range(1, X):
            part = block(lax.rem(xi - d + X, X) * 2 + ci)
            arrived(part, r.xr.at[s, d - 1])
            go(part, part, r.cs.at[s, d], r.cr.at[s, d], mp=xi * 2 + 1 - ci)

    def share_wait(s, block):
        for d in range(X):
            arrived(block(lax.rem(xi - d + X, X) * 2 + 1 - ci), r.cr.at[s, d])

    def sum_begin(s, b, compute):
        sent = []
        for d in [*range(1, X), 0]:
            to = lax.rem(xi + d, X)
            compute(to, 1 - ci)
            sent.append(go(
                r.part.at[to, 1 - ci], r.recc.at[b, to], r.acs.at[s, d], r.acr.at[s, d], mp=xi * 2 + 1 - ci
            ))
        for d in range(1, X):
            to = lax.rem(xi + d, X)
            compute(to, ci)
            arrived(r.recc.at[b, to], r.acr.at[s, d])
            for t in range(NT):
                q = slice(t * 128, (t + 1) * 128)
                r.part[to, ci, q] = (
                    r.part[to, ci, q].astype(F32) + r.recc[b, to, q].astype(F32)
                ).astype(BF)
                sent.append(go(
                    r.part.at[to, ci, q], r.recx.at[b, d - 1, q], r.axs.at[s, d - 1, t], r.axr.at[s, d - 1, t],
                    mp=to * 2 + ci,
                ))
        compute(xi, ci)
        return sent

    def sum_arrived(s, b, t):
        if t == 0:
            arrived(r.recc.at[b, xi], r.acr.at[s, 0])
        for d in range(1, X):
            arrived(r.recx.at[b, d - 1, t * 128:(t + 1) * 128], r.axr.at[s, d - 1, t])

    def sum_tile(b, q):
        total = r.part[xi, ci, q].astype(F32) + r.recc[b, xi, q].astype(F32)
        for d in range(1, X):
            total = total + r.recx[b, d - 1, q].astype(F32)
        return total

    def grad_ref(k):
        return r.gm.at[k] if k < 5 else r.gf.at[k - 5]

    def rec_y(k):
        return r.rym.at[k] if k < 5 else r.ryf.at[k - 5]

    def rec_z(k):
        return r.rzm.at[k] if k < 5 else r.rzf.at[k - 5]

    flat = p.FD

    def lanes(k):
        return flat and k >= 5

    def part_of(ref, k, z):
        return ref.at[:, rows_of(z, S)] if lanes(k) else ref.at[z]

    def mine(k, z):
        return r.gf.at[k - 5, yi, :, rows_of(z, S)] if lanes(k) else grad_ref(k).at[z, yi]

    def scatter_first(k):
        src = r.gf.at[k - 5, 1 - yi] if lanes(k) else grad_ref(k).at[:, 1 - yi]
        go(src, rec_y(k), r.bys.at[k], r.byr.at[k], dp=zi * LO + 1 - yi)

    def scatter_second(k):
        arrived(rec_y(k), r.byr.at[k])
        for d in range(1, HI):
            to = lax.rem(zi + d, HI)
            block = mine(k, to)
            block[...] = (block[...].astype(F32) + part_of(rec_y(k), k, to)[...].astype(F32)).astype(BF)
            go(block, rec_z(k).at[d - 1], r.bzs.at[k, d - 1], r.bzr.at[k, d - 1], dp=to * LO + yi)

    def scatter_total(k):
        rz = rec_z(k)
        for d in range(1, HI):
            arrived(rz.at[d - 1], r.bzr.at[k, d - 1])
        total = mine(k, zi)[...].astype(F32) + part_of(rec_y(k), k, zi)[...].astype(F32)
        for d in range(1, HI):
            total = total + rz[d - 1].astype(F32)
        return total

    def put_grad(k, lhs, rhs, turned=False):
        g = grad_ref(k)
        per = 256 // (LO * S)

        def tile(t):
            if turned:
                out = dot_nn(lhs[rows_of(t, 256), :], rhs[...])
            else:
                out = dot_tn(lhs[:, rows_of(t, 256)], rhs[...])
            g[pl.ds(t * per, per)] = out.astype(BF).reshape(per, LO, S, out.shape[-1])

        each(D // 256, tile)

    def put_ff_grad(m, units, model):
        if not flat:
            return put_grad(5 + m, model, units)
        for f in range(0, F, 256):
            q = slice(f, min(f + 256, F))
            out = dot_tn(units[:, q], model[...]).astype(BF)
            for y in range(LO):
                for z in range(HI):
                    r.gf[m, y, q, z * S:(z + 1) * S] = out[:, (z * LO + y) * S:(z * LO + y + 1) * S]

    def to_units(a, m):
        return dot_nt(a, r.ffw[m]) if flat else dot_nn(a, r.ffw[m])

    def to_model(a, m):
        return dot_nn(a, r.ffw[m]) if flat else dot_nt(a, r.ffw[m])

    gather_ready(0)
    gather_ready(1)
    enter()
    gather_send(0)
    gather_send(1)

    length = r.live[0]
    load_x.wait()

    def norm_tile(t):
        q = rows_of(t, 128)
        v = r.xv[q, :].astype(F32)
        r.nin[q, :] = (v * lax.rsqrt(jnp.mean(v * v, axis=-1, keepdims=True) + EPSILON)).astype(BF)

    each(T // 128, norm_tile)
    for k in range(2, 11):
        gather_ready(k)
    load_x_own = load(r.x.at[rows_of(j, TB)], r.xown, 8)
    load_og.wait()
    load_cos = load(r.cos, r.cosv, 0)
    load_sin = load(r.sin, r.sinv, 1)

    def live_tile(t):
        q = rows_of(t, 128)
        place = lax.broadcasted_iota(jnp.int32, (128, D), 0) + t * 128
        r.up[q, :] = jnp.where(place < length, r.up[q, :].astype(F32), 0.0).astype(BF)

    each(T // 128, live_tile)

    place = lax.broadcasted_iota(jnp.int32, (1, T), 1)
    segment = r.seg[...].astype(F32)
    r.segk[...] = jnp.broadcast_to(jnp.where(place < length, segment, -2.0), (8, T))
    seg_q = jnp.where(place < length, segment, -1.0)
    for t in range(T // 128):
        q = slice(t * 128, t * 128 + 128)
        r.segq[q, :] = jnp.transpose(jnp.broadcast_to(seg_q[:, q], (128, 128)))

    down = lax.broadcasted_iota(jnp.int32, (B, B), 0)
    over = lax.broadcasted_iota(jnp.int32, (B, B), 1)
    heads = D // HEAD

    def rate_of(h):
        return -(8.0 * (j * H + h).astype(F32) / heads) * (1.0 - LAYER_PLACE)

    for h in range(H):
        rate = rate_of(h)
        for o in range(2):
            distance = down - over + o * B
            fade = jnp.exp(rate * jnp.maximum(distance, 0).astype(F32))
            r.dec[o, h] = jnp.where(distance >= 0, fade, 0.0)

    for t in range(D // 128):
        q = slice(t * 128, t * 128 + 128)
        r.nint[q, :] = jnp.transpose(r.nin[:, q])
    load_cos.wait()
    load_sin.wait()
    load_x_own.wait()

    def turn_into(pre_ref, rot_ref, k):
        def tile(t):
            q = rows_of(t, 256)
            pre = dot_nn(r.nin[q, :], r.mixw[k])
            pre_ref[q, :] = pre
            act = pre * jax.nn.sigmoid(pre)
            c, s = r.cosv[q, :], r.sinv[q, :]
            for h in range(H):
                a = act[:, h * HEAD:(h + 1) * HEAD]
                rot_ref[q, 2 * h * HEAD:(2 * h + 1) * HEAD] = (a * c).astype(BF)
                rot_ref[q, (2 * h + 1) * HEAD:(2 * h + 2) * HEAD] = (a * s).astype(BF)

        each(T // 256, tile)

    def project_into(ref, k):
        def tile(t):
            q = rows_of(t, 256)
            ref[q, :] = dot_nn(r.nin[q, :], r.mixw[k]).astype(ref.dtype)

        each(T // 256, tile)

    gather_forward(0)
    gather_send(2)
    gather_forward(1)
    gather_send(3)
    gather_wait(0)
    turn_into(r.qpre, r.qrot, 0)
    gather_forward(2)
    gather_send(4)
    gather_wait(1)
    turn_into(r.kpre, r.krot, 1)
    gather_forward(3)
    gather_send(5)
    gather_wait(2)
    project_into(r.val, 2)
    gather_forward(4)
    gather_send(6)
    gather_wait(3)
    project_into(r.gpre, 3)

    def wo_block(owner):
        return r.wo.at[:, pl.ds(pl.multiple_of(owner * C, C), C)]

    gather_wait(4)
    share_send(0, wo_block)

    NB = T // B
    REACH = LONGEST // B

    def weights_of(qb, kb, h):
        seen = jnp.broadcast_to(r.segk[0:1, kb * B:(kb + 1) * B], (B, B))
        same = widen(r.segq[qb * B:(qb + 1) * B, :], B) == seen
        if qb - kb < 2:
            return jnp.where(same, r.dec[qb - kb, h], 0.0)
        return jnp.where(same, r.dec[1, h] * jnp.exp(rate_of(h) * ((qb - kb - 1) * B)), 0.0)

    def u_block(qb):
        return lambda owner: r.ufull.at[qb * B:(qb + 1) * B, pl.ds(pl.multiple_of(owner * C, C), C)]

    def attend(qb):
        q = slice(qb * B, (qb + 1) * B)
        squares = jnp.zeros((B, 1), F32)
        for h in range(H):
            rot = slice(2 * h * HEAD, 2 * (h + 1) * HEAD)
            chan = slice(h * HEAD, (h + 1) * HEAD)
            total = jnp.zeros((B, HEAD), F32)
            for kb in range(max(0, qb - REACH), qb + 1):
                key = slice(kb * B, (kb + 1) * B)
                scores = dot_nt(r.qrot[q, rot], r.krot[key, rot]) * weights_of(qb, kb, h)
                total = total + dot_nn(scores.astype(BF), r.val[key, chan])
            r.mixed[q, chan] = total
            squares = squares + jnp.sum(total * total, axis=-1, keepdims=True)
            r.ufull[q, pl.ds(pl.multiple_of(j * C + h * HEAD, HEAD), HEAD)] = (
                total * r.gpre[q, chan]
            ).astype(BF)
        r.ss[j, :, q] = jnp.transpose(jnp.broadcast_to(squares, (B, 128)))[0:8, :]

    def ss_block(owner):
        return r.ss.at[owner]

    for qb in range(NB):
        attend(qb)
        share_send(1 + qb, u_block(qb))
        if qb == NB - 1:
            share_send(1 + NB, ss_block)
        if qb == 0:
            gather_forward(5)
            gather_send(7)
        if qb == 1:
            share_forward(0, wo_block)
        if qb == 2:
            gather_forward(6)
            gather_send(8)
        if qb > 0:
            share_forward(qb, u_block(qb - 1))
    share_forward(NB, u_block(NB - 1))
    share_forward(1 + NB, ss_block)
    gather_forward(7)
    gather_send(9)
    gather_forward(8)
    gather_send(10)
    share_wait(0, wo_block)
    for qb in range(NB):
        share_wait(1 + qb, u_block(qb))
    share_wait(1 + NB, ss_block)
    early = list(pending)

    total_ss = r.ss[0]
    for owner in range(1, mp):
        total_ss = total_ss + r.ss[owner]
    inverse = lax.rsqrt(total_ss * (1.0 / D) + EPSILON)
    for t in range(T // 128):
        q = slice(t * 128, t * 128 + 128)
        r.rcol[q, :] = jnp.transpose(jnp.broadcast_to(inverse[0:1, q], (128, 128)))

    def hidden_tile(t):
        q = rows_of(t, TB)
        out = widen(r.rcol[q, :], D) * dot_nn(r.ufull[q, :], r.wo[...])
        hidden = r.xv[q, :].astype(F32) + out
        scale = lax.rsqrt(jnp.mean(hidden * hidden, axis=-1, keepdims=True) + EPSILON)
        r.nmid[q, :] = (hidden * scale).astype(BF)

        @pl.when(t == j)
        def _():
            r.hown[...] = hidden

    each(T // TB, hidden_tile)
    gather_wait(5)
    gather_wait(6)

    def gate_tile(t):
        q = rows_of(t, 256)
        r.gact[q, 0:F] = to_units(r.nmid[q, :], 1)

    each(T // 256, gate_tile)
    gather_forward(9)
    gather_wait(7)
    gather_wait(8)

    def up_tile(t):
        q = rows_of(t, 256)
        upper = to_units(r.nmid[q, :], 2)
        r.uact[q, :] = upper.astype(BF)
        r.prod[q, :] = (r.gact[q, 0:F] * upper).astype(BF)

    each(T // 256, up_tile)
    put_ff_grad(0, r.prod, r.up)
    gather_forward(10)
    scatter_first(5)
    gather_wait(9)
    gather_wait(10)

    def mid_block(x, c):
        q = rows_of(x * 2 + c, TB)
        g = to_units(r.up[q, :], 0)
        grad_gate, grad_up = (g * r.uact[q, :].astype(F32)).astype(BF), (g * r.gact[q, 0:F]).astype(BF)
        r.ggate[q, :] = grad_gate
        r.gup[q, :] = grad_up
        r.part[x, c] = (to_model(grad_gate, 1) + to_model(grad_up, 2)).astype(BF)

    used = sum_begin(0, 0, mid_block)
    put_ff_grad(1, r.ggate, r.nmid)
    scatter_first(6)

    def back_tile(t):
        q = rows_of(t, 128)
        here = rows_of(j * (TB // 128) + t, 128)
        grad = sum_tile(0, q)
        hidden = r.hown[q, :]
        scale = lax.rsqrt(jnp.mean(hidden * hidden, axis=-1, keepdims=True) + EPSILON)
        normed = hidden * scale
        inner = jnp.mean(grad * normed, axis=-1, keepdims=True)
        out = r.up[here, :].astype(F32) + scale * (grad - normed * inner)
        r.ghid[q, :] = out
        low = out.astype(BF)
        r.hlow[here, :] = low
        mixer_out = hidden - r.xown[q, :].astype(F32)
        product = jnp.sum(low.astype(F32) * mixer_out, axis=-1, keepdims=True) * (1.0 / D)
        r.inn[j, :, q] = jnp.transpose(jnp.broadcast_to(product, (128, 128)))[0:8, :]

    def token_block(ref):
        return lambda owner: ref.at[rows_of(owner, TB)]

    BO, IN, GM, HL, IG = 2 + NB, 3 + NB, 4 + NB, 9 + NB, 9 + NB + NT

    def inn_block(owner):
        return r.inn.at[owner]

    def half_block(ref, t):
        return lambda owner: ref.at[rows_of(owner * NT + t, 128)]

    for t in range(NT):
        sum_arrived(0, 0, t)
        back_tile(t)
        share_send(HL + t, half_block(r.hlow, t))
    share_send(IN, inn_block)
    put_ff_grad(2, r.gup, r.nmid)
    scatter_first(7)
    scatter_second(5)
    for t in range(NT):
        share_forward(HL + t, half_block(r.hlow, t))
    share_forward(IN, inn_block)
    for copy in used:
        settle(copy)

    def expand_block(x, c):
        q = rows_of(x * 2 + c, TB)
        r.part[x, c] = to_model(r.prod[q, :], 0).astype(BF)

    used = sum_begin(1, 1, expand_block)
    for t in range(NT):
        share_wait(HL + t, half_block(r.hlow, t))
    share_wait(IN, inn_block)
    for owner in range(mp):
        for t in range(TB // 128):
            row = r.inn[owner, 0:1, t * 128:(t + 1) * 128]
            q = slice(owner * TB + t * 128, owner * TB + (t + 1) * 128)
            r.icol[q, :] = jnp.transpose(jnp.broadcast_to(row, (128, 128)))

    wo_rows = rows_of(j, C)

    def gated_tile(t):
        q = rows_of(t, 256)
        low = r.hlow[q, :]
        grad = dot_nt(low, r.wo[wo_rows, :])
        inner = widen(r.icol[q, :], C)
        inverse = widen(r.rcol[q, :], C)
        normed = r.mixed[q, :] * inverse
        r.gproj[3][q, :] = (grad * normed).astype(BF)
        r.gmix[q, :] = (inverse * (grad * r.gpre[q, :] - normed * inner)).astype(BF)
        r.rh[q, :] = (inverse * r.hlow[q, jcols].astype(F32)).astype(BF)

    each(T // 256, gated_tile)
    put_grad(4, r.ufull, r.rh)
    scatter_first(4)
    scatter_second(6)

    def swish_back(pre, grad):
        gate = jax.nn.sigmoid(pre)
        return grad * (gate * (1.0 + pre * (1.0 - gate)))

    def attend_back(h):
        rot = slice(2 * h * HEAD, 2 * (h + 1) * HEAD)
        chan = slice(h * HEAD, (h + 1) * HEAD)
        r.dk[...] = jnp.zeros_like(r.dk)
        r.dv[...] = jnp.zeros_like(r.dv)
        for qb in range(NB):
            q = slice(qb * B, (qb + 1) * B)
            total = jnp.zeros((B, 2 * HEAD), F32)
            for kb in range(max(0, qb - REACH), qb + 1):
                key = slice(kb * B, (kb + 1) * B)
                weights = weights_of(qb, kb, h)
                scores = (dot_nt(r.qrot[q, rot], r.krot[key, rot]) * weights).astype(BF)
                back = (dot_nt(r.gmix[q, chan], r.val[key, chan]) * weights).astype(BF)
                r.dv[key, :] += dot_tn(scores, r.gmix[q, chan])
                r.dk[key, :] += dot_tn(back, r.qrot[q, rot])
                total = total + dot_nn(back, r.krot[key, rot])
            turned = total[:, :HEAD] * r.cosv[q, :] + total[:, HEAD:] * r.sinv[q, :]
            r.gproj[0][q, chan] = swish_back(r.qpre[q, chan], turned).astype(BF)

        def tile(t):
            q = rows_of(t, 256)
            turned = r.dk[q, :HEAD] * r.cosv[q, :] + r.dk[q, HEAD:] * r.sinv[q, :]
            r.gproj[1][q, chan] = swish_back(r.kpre[q, chan], turned).astype(BF)
            r.gproj[2][q, chan] = r.dv[q, :].astype(BF)

        each(T // 256, tile)

    put_grad(3, r.nint, r.gproj[3], turned=True)
    scatter_first(3)
    attend_back(0)
    for t in range(NT):
        sum_arrived(1, 1, t)

    def output_tile(t):
        q = rows_of(t, 128)
        r.bov[rows_of(j * NT + t, 128), :] = (r.hown[q, :] + sum_tile(1, q)).astype(BF)

    each(TB // 128, output_tile)
    share_send(BO, token_block(r.bov))
    for h in range(1, H):
        attend_back(h)
    scatter_second(7)
    scatter_second(4)
    scatter_second(3)
    share_forward(BO, token_block(r.bov))
    for k in range(3):
        put_grad(k, r.nint, r.gproj[k], turned=True)
        scatter_first(k)
    for copy in used:
        settle(copy)

    def normed_block(x, c):
        q = rows_of(x * 2 + c, TB)
        out = dot_nt(r.gproj[0][q, :], r.mixw[0])
        for k in range(1, 4):
            out = out + dot_nt(r.gproj[k][q, :], r.mixw[k])
        r.part[x, c] = out.astype(BF)

    for copy in early:
        settle(copy)
    used = sum_begin(2, 0, normed_block)
    for k in range(3):
        scatter_second(k)

    def input_tile(t):
        q = rows_of(t, 128)
        grad = sum_tile(0, q)
        v = r.xown[q, :].astype(F32)
        scale = lax.rsqrt(jnp.mean(v * v, axis=-1, keepdims=True) + EPSILON)
        normed = v * scale
        inner = jnp.mean(grad * normed, axis=-1, keepdims=True)
        r.igv[rows_of(j * NT + t, 128), :] = (r.ghid[q, :] + scale * (grad - normed * inner)).astype(BF)

    for t in range(NT):
        sum_arrived(2, 0, t)
        input_tile(t)
        share_send(IG + t, half_block(r.igv, t))
    share_wait(BO, token_block(r.bov))
    stores = [load(r.bov, r.bo, 0)]

    def grad_block(k):
        return lambda owner: r.gmv.at[k * S:(k + 1) * S, pl.ds(pl.multiple_of(owner * C, C), C)]

    squares = jnp.zeros((), F32)
    for k in range(5, 8):
        total = scatter_total(k)
        if k == 5:
            r.gso[...] = total
        else:
            r.geo[k - 6] = total
        squares = squares + jnp.sum(total * total)
    for k in (4, 3, 0, 1, 2):
        total = scatter_total(k).astype(BF)
        r.gmv[k * S:(k + 1) * S, jcols] = total
        squares = squares + jnp.sum(total.astype(F32) * total.astype(F32))
        share_send(GM + k, grad_block(k))

    r.s1[j] = jnp.full((8, 128), squares, F32)
    for d in range(1, mp):
        go(r.s1.at[j], r.s1.at[j], r.q1s.at[d], r.q1r.at[d], mp=lax.rem(j + d, mp))
    for t in range(NT):
        share_forward(IG + t, half_block(r.igv, t))
    for d in range(1, mp):
        arrived(r.s1.at[lax.rem(j - d + mp, mp)], r.q1r.at[d])
    total = r.s1[0]
    for owner in range(1, mp):
        total = total + r.s1[owner]
    r.s2[i] = total
    for d in range(1, n):
        go(r.s2.at[i], r.s2.at[i], r.q2s.at[d], r.q2r.at[d], dp=lax.rem(i + d, n))
    for k in (4, 3, 0, 1, 2):
        share_forward(GM + k, grad_block(k))
    for d in range(1, n):
        arrived(r.s2.at[lax.rem(i - d + n, n)], r.q2r.at[d])
    total = r.s2[0]
    for owner in range(1, n):
        total = total + r.s2[owner]
    r.sqo[...] = total

    for t in range(NT):
        share_wait(IG + t, half_block(r.igv, t))
    stores.append(load(r.igv, r.ig, 1))
    for k in (4, 3, 0, 1, 2):
        share_wait(GM + k, grad_block(k))
        stores.append(load(r.gmv.at[k * S:(k + 1) * S], r.gmo.at[k], 2 + k))
    for copy in stores:
        copy.wait()
    for copy in pending:
        copy.wait_send()


def fused(p, *operands):
    scratch = scratch_of(p)
    names = IN_NAMES + OUT_NAMES + tuple(scratch)
    anywhere = pl.BlockSpec(memory_space=pl.ANY)
    vmem = pl.BlockSpec(memory_space=pltpu.VMEM)
    smem = pl.BlockSpec(memory_space=pltpu.SMEM)
    return pl.pallas_call(
        partial(body, p, names),
        out_shape=(
            jax.ShapeDtypeStruct((p.T, p.D), BF),
            jax.ShapeDtypeStruct((p.T, p.D), BF),
            jax.ShapeDtypeStruct((5, p.S, p.D), BF),
            jax.ShapeDtypeStruct((2, p.F, p.S) if p.FD else (2, p.S, p.F), F32),
            jax.ShapeDtypeStruct((p.F, p.S) if p.FD else (p.S, p.F), F32),
            jax.ShapeDtypeStruct((8, 128), F32),
        ),
        in_specs=[anywhere, anywhere, vmem, smem] + [anywhere] * 5,
        out_specs=(anywhere, anywhere, anywhere, vmem, vmem, vmem),
        scratch_shapes=list(scratch.values()),
        compiler_params=pltpu.CompilerParams(
            collective_id=0, has_side_effects=True, vmem_limit_bytes=VMEM_LIMIT
        ),
    )(*operands)


VMEM_LIMIT = 64 * 2**20 - 2**18


def renew(weight, momentum, shadow, grad, clip_factor):
    clipped = grad * clip_factor
    velocity = MOMENTUM * momentum + clipped
    updated = weight - LEARN_RATE * (clipped + MOMENTUM * velocity)
    average = SHADOW_DECAY * shadow + (1.0 - SHADOW_DECAY) * updated
    return (velocity, average, updated)


def update_body(cuts, *refs):
    kinds, pieces = len(cuts), sum(len(c) for c in cuts)
    sq, carried = refs[0], refs[1:3]
    ins = [refs[3 + 4 * w:7 + 4 * w] for w in range(kinds)]
    refs = refs[3 + 4 * kinds:]
    norm_out, carried_out = refs[0], refs[1:3]
    outs = [refs[3 + 3 * w:6 + 3 * w] for w in range(kinds)]
    refs = refs[3 + 3 * kinds:]
    held = [refs[4 * w:4 * w + 4] for w in range(kinds)]
    made = [refs[4 * kinds + 3 * w:4 * kinds + 3 * w + 3] for w in range(kinds)]
    bounce, (in_sem, out_sem, carry_sem) = refs[7 * kinds:7 * kinds + 2], refs[7 * kinds + 2:]
    loads, order = {}, [(w, c) for w in range(kinds) for c in range(len(cuts[w]))]
    for at, (w, c) in enumerate(order):
        for a in range(4):
            cut = cuts[w][c]
            loads[at, a] = pltpu.make_async_copy(ins[w][a].at[cut], held[w][a].at[cut], in_sem.at[at, a])
            loads[at, a].start()
    carry = [pltpu.make_async_copy(carried[a], bounce[a], carry_sem.at[a]) for a in range(2)]
    for copy in carry:
        copy.start()
    copies = []
    norm = jnp.sqrt(sq[...])
    norm_out[...] = norm
    clip_factor = 1.0 / jnp.maximum(jnp.max(norm), 1.0)
    for at, (w, c) in enumerate(order):
        cut = cuts[w][c]
        for a in range(4):
            loads[at, a].wait()
        new = renew(*[held[w][a][cut] for a in range(3)], held[w][3][cut].astype(F32), clip_factor)
        for a in range(3):
            made[w][a][cut] = new[a]
            copy = pltpu.make_async_copy(made[w][a].at[cut], outs[w][a].at[cut], out_sem.at[at, a])
            copy.start()
            copies.append(copy)
    for a in range(2):
        carry[a].wait()
        copy = pltpu.make_async_copy(bounce[a], carried_out[a], carry_sem.at[2 + a])
        copy.start()
        copies.append(copy)
    for copy in copies:
        copy.wait()


def update(sq, carried, weights):
    cuts = [[c for c in range(g[0].shape[0])] if g[0].ndim == 3 else [slice(None)] for g in weights]
    pieces = sum(len(c) for c in cuts)
    anywhere = pl.BlockSpec(memory_space=pl.ANY)
    vmem = pl.BlockSpec(memory_space=pltpu.VMEM)
    flat_in = [a for group in weights for a in group]
    flat_out = [a for group in weights for a in group[:3]]
    dma = pltpu.SemaphoreType.DMA
    size = sum(a.size * a.dtype.itemsize for a in flat_in + flat_out + 2 * list(carried))
    return pl.pallas_call(
        partial(update_body, cuts),
        out_shape=[jax.ShapeDtypeStruct(a.shape, a.dtype) for a in [sq, *carried, *flat_out]],
        in_specs=[vmem] + [anywhere] * (2 + len(flat_in)),
        out_specs=[vmem] + [anywhere] * (2 + len(flat_out)),
        scratch_shapes=[pltpu.VMEM(a.shape, a.dtype) for a in flat_in + flat_out + list(carried)]
        + [dma((pieces, 4)), dma((pieces, 3)), dma((4,))],
        cost_estimate=pl.CostEstimate(flops=size, bytes_accessed=size, transcendentals=0),
        compiler_params=pltpu.CompilerParams(vmem_limit_bytes=VMEM_LIMIT),
    )(sq, *carried, *flat_in)


def turn_tables(tokens):
    theta = np.float32(10000.0) ** (-np.arange(HEAD, dtype=np.float32) / np.float32(HEAD))
    angle = np.arange(tokens, dtype=np.float32)[:, None] * theta.astype(np.float32)[None, :]
    angle = angle.astype(np.float64)
    return np.cos(angle).astype(np.float32), np.sin(angle).astype(np.float32)


def per_device(mesh, block_input, segment_ids, live_length, output_grad, mixer_weight, mixer_momentum, mixer_shadow,
               expand_weight, expand_momentum, expand_shadow, shrink_weight, shrink_momentum, shrink_shadow):
    rows, length, width = block_input.shape
    p = plan_of(mesh, length, width, shrink_weight.shape[0])
    turn = (lambda v: jnp.swapaxes(v, -1, -2)) if p.FD else (lambda v: v)
    if p.FD:
        shards = (turn(expand_weight), shrink_weight)
    else:
        shards = (jnp.concatenate([shrink_weight.T[None], expand_weight], axis=0).astype(BF), shrink_weight)
    cos, sin = turn_tables(length)
    out, grad_in, gm, ge, gs, sq = fused(
        p, block_input[0], output_grad[0], segment_ids, live_length, jnp.asarray(cos), jnp.asarray(sin), mixer_weight, *shards
    )
    new = update(sq, (out, grad_in), (
        (mixer_weight, mixer_momentum, mixer_shadow, gm),
        (turn(expand_weight), turn(expand_momentum), turn(expand_shadow), ge),
        (shrink_weight, shrink_momentum, shrink_shadow, gs if p.FD else gs.T),
    ))
    norm, out, grad_in = new[:3]
    return (out[None], grad_in[None], norm[0, 0], *new[3:6], *(turn(v) for v in new[6:9]), *new[9:12])


def solution(mesh):
    row, mixer, expand, shrink = P("dp", None, None), P(None, "dp", None), P(None, "dp", "mp"), P("mp", "dp")
    return jax.shard_map(
        partial(per_device, mesh),
        mesh=mesh,
        in_specs=(row, P("dp", None), P("dp"), row) + (mixer,) * 3 + (expand,) * 3 + (shrink,) * 3,
        out_specs=(row, row, P()) + (mixer,) * 3 + (expand,) * 3 + (shrink,) * 3,
        check_vma=False,
    )
```

```python
from functools import partial
from types import SimpleNamespace

import jax
import jax.numpy as jnp
import numpy as np
from jax import lax
from jax.experimental import pallas as pl
from jax.experimental.pallas import tpu as pltpu
from jax.sharding import PartitionSpec as P

HEAD = 128
EPSILON = 1e-06
LEARN_RATE = 32.0
MOMENTUM = 0.5
SHADOW_DECAY = 0.5
LAYER_PLACE = 12.0 / 24.0
LONGEST = 512
FF_ORDER = (1, 2, 0)
MESH = pl.DeviceIdType.MESH
BF = jnp.bfloat16
F32 = jnp.float32


def dot_nn(a, b):
    return lax.dot_general(a, b, (((1,), (0,)), ((), ())), preferred_element_type=F32)


def dot_nt(a, b):
    return lax.dot_general(a, b, (((1,), (1,)), ((), ())), preferred_element_type=F32)


def dot_tn(a, b):
    return lax.dot_general(a, b, (((0,), (0,)), ((), ())), preferred_element_type=F32)


def rows_of(index, size):
    return pl.ds(pl.multiple_of(index * size, size), size)


def each(count, body):
    def step(t, carry):
        body(t)
        return carry

    lax.fori_loop(0, count, step, 0)


def widen(column, width):
    return jnp.concatenate([column] * (width // 128), axis=1)


def plan_of(mesh, tokens, width, inner):
    n, mp = mesh.shape["dp"], mesh.shape["mp"]
    lo, core = 2, 2
    return SimpleNamespace(
        n=n, mp=mp, LO=lo, HI=n // lo, X=mp // core, T=tokens, D=width, C=width // mp, F=inner,
        S=width // n, H=width // mp // HEAD, TB=tokens // mp, B=min(256, tokens),
        NT=tokens // mp // 128, FD=(width // n) % 128 == 0,
    )


def scratch_of(p):
    T, D, C, F, S, HI, LO, X, TB, B = p.T, p.D, p.C, p.F, p.S, p.HI, p.LO, p.X, p.TB, p.B
    dma = pltpu.SemaphoreType.DMA
    v = pltpu.VMEM
    return dict(
        mixw=v((4, D, C), BF), wo=v((D, D), BF), ffw=v((3, F, D) if p.FD else (3, D, F), BF),
        xown=v((TB, D), BF), nin=v((T, D), BF), nint=v((D, T), BF), up=v((T, D), BF),
        cosv=v((T, HEAD), F32), sinv=v((T, HEAD), F32),
        segq=v((T, 128), F32), segk=v((8, T), F32), dec=v((2, p.H, B, B), F32),
        qpre=v((T, C), F32), kpre=v((T, C), F32), gpre=v((T, C), F32), val=v((T, C), BF),
        qrot=v((T, 2 * C), BF), krot=v((T, 2 * C), BF), mixed=v((T, C), F32),
        ufull=v((T, D), BF), ss=v((p.mp, 8, T), F32), rcol=v((T, 128), F32),
        inn=v((p.mp, 8, TB), F32), hown=v((TB, D), F32),
        gact=v((T, max(F, 2 * C + HEAD)), F32), uact=v((T, F), BF), prod=v((T, F), BF), ggate=v((T, F), BF), gup=v((T, F), BF),
        part=v((X, 2, TB, D), BF), recc=v((2, X, TB, D), BF), recx=v((2, X - 1, TB, D), BF),
        ghid=v((TB, D), F32), hlow=v((T, D), BF),
        gm=v((5, HI, LO, S, C), BF), rym=v((5, HI, S, C), BF), rzm=v((5, HI - 1, S, C), BF),
        gf=v((3, LO, F, HI * S) if p.FD else (3, HI, LO, S, F), BF),
        ryf=v((3, F, HI * S) if p.FD else (3, HI, S, F), BF),
        rzf=v((3, HI - 1, F, S) if p.FD else (3, HI - 1, S, F), BF),
        s1=v((p.mp, 8, 128), F32), s2=v((p.n, 8, 128), F32),
        loc=dma((10,)),
        zs=dma((11, HI - 1)), zr=dma((11, HI - 1)), ys=dma((11, HI)), yr=dma((11, HI)),
        xs=dma((20, X - 1)), xr=dma((20, X - 1)), cs=dma((20, X)), cr=dma((20, X)),
        acs=dma((3, X)), acr=dma((3, X)), axs=dma((3, X - 1, p.NT)), axr=dma((3, X - 1, p.NT)),
        bys=dma((8,)), byr=dma((8,)), bzs=dma((8, HI - 1)), bzr=dma((8, HI - 1)),
        q1s=dma((p.mp,)), q1r=dma((p.mp,)), q2s=dma((p.n,)), q2r=dma((p.n,)),
    )


IN_NAMES = ("x", "og", "seg", "live", "cos", "sin", "mixsh", "exsh", "shsh")
OUT_NAMES = ("bo", "ig", "gmo", "geo", "gso", "sqo")


def body(p, names, *refs):
    r = SimpleNamespace(**dict(zip(names, refs)))
    n, mp, LO, HI, X, T, D, C, F, S, H, TB, B = (
        p.n, p.mp, p.LO, p.HI, p.X, p.T, p.D, p.C, p.F, p.S, p.H, p.TB, p.B,
    )
    NT, TT = p.NT, min(512, p.T)
    i, j = lax.axis_index("dp"), lax.axis_index("mp")
    zi, yi = i // LO, lax.rem(i, LO)
    xi, ci = j // 2, lax.rem(j, 2)
    jcols = pl.ds(pl.multiple_of(j * C, C), C)
    pending = []
    r.xv, r.nmid = r.hlow, r.nin
    r.bov, r.igv, r.gmv = r.up, r.ufull, r.wo
    r.dk, r.icol, r.dv = r.gact.at[:, 0:2 * C], r.gact.at[:, 2 * C:2 * C + HEAD], r.mixed
    r.gproj = [r.ggate.at[:, 0:C], r.ggate.at[:, C:2 * C], r.gup.at[:, 0:C], r.gup.at[:, C:2 * C]]
    r.gmix, r.rh = r.prod.at[:, 0:C], r.prod.at[:, C:2 * C]

    def go(src, dst, ssem, rsem, **device):
        copy = pltpu.make_async_remote_copy(
            src_ref=src, dst_ref=dst, send_sem=ssem, recv_sem=rsem,
            device_id=device, device_id_type=MESH,
        )
        copy.start()
        pending.append(copy)
        return copy

    def arrived(dst, sem):
        pltpu.make_async_copy(dst, dst, sem).wait()

    def settle(copy):
        copy.wait_send()
        pending[:] = [other for other in pending if other is not copy]

    def load(src, dst, sem):
        copy = pltpu.make_async_copy(src, dst, r.loc.at[sem])
        copy.start()
        return copy

    own_mix = [load(r.mixsh.at[k, :, jcols], r.qpre.at[k * S:(k + 1) * S], k) for k in range(5)]
    if p.FD:
        stage = [r.gact.at[0:F, m * S:(m + 1) * S] for m in range(3)]
        own_ff = [load(r.shsh if m == 0 else r.exsh.at[m - 1], stage[m], 5 + m) for m in range(3)]
    else:
        own_ff = [load(r.exsh.at[m], r.ffw.at[m, rows_of(i, S)], 5 + m) for m in range(3)]
    load_x = load(r.x, r.xv, 8)
    load_og = load(r.og, r.up, 9)

    def enter():
        barrier = pltpu.get_barrier_semaphore()
        for d in range(1, n):
            pl.semaphore_signal(barrier, inc=1, device_id={"dp": lax.rem(i + d, n)}, device_id_type=MESH)
        for d in range(1, mp):
            pl.semaphore_signal(barrier, inc=1, device_id={"mp": lax.rem(j + d, mp)}, device_id_type=MESH)
        pl.semaphore_wait(barrier, n - 1 + mp - 1)

    def slot(k, device):
        rows = rows_of(device, S)
        if k == 4:
            return r.wo.at[rows, jcols]
        if k < 4:
            return r.mixw.at[k, rows]
        m, half = FF_ORDER[(k - 5) // 2], (k - 5) % 2
        if p.FD:
            return r.ffw.at[m, half * F // 2:(half + 1) * F // 2, rows]
        return r.ffw.at[m, pl.ds(pl.multiple_of(device * S + half * S // 2, S // 2), S // 2)]

    def gather_ready(k):
        if k < 5:
            own_mix[k].wait()
            slot(k, i)[...] = r.qpre[k * S:(k + 1) * S, :].astype(BF)
        else:
            m, half = FF_ORDER[(k - 5) // 2], (k - 5) % 2
            if half == 0:
                own_ff[m].wait()
            if p.FD:
                slot(k, i)[...] = stage[m][half * F // 2:(half + 1) * F // 2, :].astype(BF)

    def gather_send(k):
        src = slot(k, i)
        for d in range(1, HI):
            go(src, src, r.zs.at[k, d - 1], r.zr.at[k, d - 1], dp=lax.rem(zi + d, HI) * LO + yi)
        go(src, src, r.ys.at[k, 0], r.yr.at[k, 0], dp=zi * LO + 1 - yi)

    def gather_forward(k):
        for d in range(1, HI):
            block = slot(k, lax.rem(zi - d + HI, HI) * LO + yi)
            arrived(block, r.zr.at[k, d - 1])
            go(block, block, r.ys.at[k, d], r.yr.at[k, d], dp=zi * LO + 1 - yi)

    def gather_wait(k):
        for d in range(HI):
            arrived(slot(k, lax.rem(zi - d + HI, HI) * LO + 1 - yi), r.yr.at[k, d])

    def share_send(s, block, src=None):
        own = block(j)
        src = own if src is None else src
        for d in range(1, X):
            go(src, own, r.xs.at[s, d - 1], r.xr.at[s, d - 1], mp=lax.rem(xi + d, X) * 2 + ci)
        go(src, own, r.cs.at[s, 0], r.cr.at[s, 0], mp=xi * 2 + 1 - ci)

    def share_forward(s, block):
        for d in range(1, X):
            part = block(lax.rem(xi - d + X, X) * 2 + ci)
            arrived(part, r.xr.at[s, d - 1])
            go(part, part, r.cs.at[s, d], r.cr.at[s, d], mp=xi * 2 + 1 - ci)

    def share_wait(s, block):
        for d in range(X):
            arrived(block(lax.rem(xi - d + X, X) * 2 + 1 - ci), r.cr.at[s, d])

    def sum_begin(s, b, compute):
        sent = []
        for d in [*range(1, X), 0]:
            to = lax.rem(xi + d, X)
            compute(to, 1 - ci)
            sent.append(go(
                r.part.at[to, 1 - ci], r.recc.at[b, to], r.acs.at[s, d], r.acr.at[s, d], mp=xi * 2 + 1 - ci
            ))
        for d in range(1, X):
            to = lax.rem(xi + d, X)
            compute(to, ci)
            arrived(r.recc.at[b, to], r.acr.at[s, d])
            for t in range(NT):
                q = slice(t * 128, (t + 1) * 128)
                r.part[to, ci, q] = (
                    r.part[to, ci, q].astype(F32) + r.recc[b, to, q].astype(F32)
                ).astype(BF)
                sent.append(go(
                    r.part.at[to, ci, q], r.recx.at[b, d - 1, q], r.axs.at[s, d - 1, t], r.axr.at[s, d - 1, t],
                    mp=to * 2 + ci,
                ))
        compute(xi, ci)
        return sent

    def sum_arrived(s, b, t):
        if t == 0:
            arrived(r.recc.at[b, xi], r.acr.at[s, 0])
        for d in range(1, X):
            arrived(r.recx.at[b, d - 1, t * 128:(t + 1) * 128], r.axr.at[s, d - 1, t])

    def sum_tile(b, q):
        total = r.part[xi, ci, q].astype(F32) + r.recc[b, xi, q].astype(F32)
        for d in range(1, X):
            total = total + r.recx[b, d - 1, q].astype(F32)
        return total

    def grad_ref(k):
        return r.gm.at[k] if k < 5 else r.gf.at[k - 5]

    def rec_y(k):
        return r.rym.at[k] if k < 5 else r.ryf.at[k - 5]

    def rec_z(k):
        return r.rzm.at[k] if k < 5 else r.rzf.at[k - 5]

    flat = p.FD

    def lanes(k):
        return flat and k >= 5

    def part_of(ref, k, z):
        return ref.at[:, rows_of(z, S)] if lanes(k) else ref.at[z]

    def mine(k, z):
        return r.gf.at[k - 5, yi, :, rows_of(z, S)] if lanes(k) else grad_ref(k).at[z, yi]

    def scatter_first(k):
        src = r.gf.at[k - 5, 1 - yi] if lanes(k) else grad_ref(k).at[:, 1 - yi]
        go(src, rec_y(k), r.bys.at[k], r.byr.at[k], dp=zi * LO + 1 - yi)

    def scatter_second(k):
        arrived(rec_y(k), r.byr.at[k])
        for d in range(1, HI):
            to = lax.rem(zi + d, HI)
            block = mine(k, to)
            block[...] = (block[...].astype(F32) + part_of(rec_y(k), k, to)[...].astype(F32)).astype(BF)
            go(block, rec_z(k).at[d - 1], r.bzs.at[k, d - 1], r.bzr.at[k, d - 1], dp=to * LO + yi)

    def scatter_total(k):
        rz = rec_z(k)
        for d in range(1, HI):
            arrived(rz.at[d - 1], r.bzr.at[k, d - 1])
        total = mine(k, zi)[...].astype(F32) + part_of(rec_y(k), k, zi)[...].astype(F32)
        for d in range(1, HI):
            total = total + rz[d - 1].astype(F32)
        return total

    def put_grad(k, lhs, rhs, turned=False):
        g = grad_ref(k)
        per = TT // (LO * S)

        def tile(t):
            if turned:
                out = dot_nn(lhs[rows_of(t, TT), :], rhs[...])
            else:
                out = dot_tn(lhs[:, rows_of(t, TT)], rhs[...])
            g[pl.ds(t * per, per)] = out.astype(BF).reshape(per, LO, S, out.shape[-1])

        each(D // TT, tile)

    def put_ff_grad(m, units, model):
        if not flat:
            return put_grad(5 + m, model, units)
        for f in range(0, F, 384):
            q = slice(f, min(f + 384, F))
            out = dot_tn(units[:, q], model[...]).astype(BF)
            for y in range(LO):
                for z in range(HI):
                    r.gf[m, y, q, z * S:(z + 1) * S] = out[:, (z * LO + y) * S:(z * LO + y + 1) * S]

    def to_units(a, m):
        return dot_nt(a, r.ffw[m]) if flat else dot_nn(a, r.ffw[m])

    def to_model(a, m):
        return dot_nn(a, r.ffw[m]) if flat else dot_nt(a, r.ffw[m])

    gather_ready(0)
    gather_ready(1)
    enter()
    gather_send(0)
    gather_send(1)

    length = r.live[0]
    load_x.wait()

    def norm_tile(t):
        q = rows_of(t, 128)
        v = r.xv[q, :].astype(F32)
        r.nin[q, :] = (v * lax.rsqrt(jnp.mean(v * v, axis=-1, keepdims=True) + EPSILON)).astype(BF)

    each(T // 128, norm_tile)
    for k in range(2, 11):
        gather_ready(k)
    load_x_own = load(r.x.at[rows_of(j, TB)], r.xown, 8)
    load_og.wait()
    load_cos = load(r.cos, r.cosv, 0)
    load_sin = load(r.sin, r.sinv, 1)

    def live_tile(t):
        q = rows_of(t, 128)
        place = lax.broadcasted_iota(jnp.int32, (128, D), 0) + t * 128
        r.up[q, :] = jnp.where(place < length, r.up[q, :].astype(F32), 0.0).astype(BF)

    each(T // 128, live_tile)

    place = lax.broadcasted_iota(jnp.int32, (1, T), 1)
    segment = r.seg[...].astype(F32)
    r.segk[...] = jnp.broadcast_to(jnp.where(place < length, segment, -2.0), (8, T))
    seg_q = jnp.where(place < length, segment, -1.0)
    for t in range(T // 128):
        q = slice(t * 128, t * 128 + 128)
        r.segq[q, :] = jnp.transpose(jnp.broadcast_to(seg_q[:, q], (128, 128)))

    down = lax.broadcasted_iota(jnp.int32, (B, B), 0)
    over = lax.broadcasted_iota(jnp.int32, (B, B), 1)
    heads = D // HEAD

    def rate_of(h):
        return -(8.0 * (j * H + h).astype(F32) / heads) * (1.0 - LAYER_PLACE)

    for h in range(H):
        rate = rate_of(h)
        for o in range(2):
            distance = down - over + o * B
            fade = jnp.exp(rate * jnp.maximum(distance, 0).astype(F32))
            r.dec[o, h] = jnp.where(distance >= 0, fade, 0.0)

    for t in range(D // 128):
        q = slice(t * 128, t * 128 + 128)
        r.nint[q, :] = jnp.transpose(r.nin[:, q])
    load_cos.wait()
    load_sin.wait()
    load_x_own.wait()

    def turn_into(pre_ref, rot_ref, k):
        def tile(t):
            q = rows_of(t, TT)
            pre = dot_nn(r.nin[q, :], r.mixw[k])
            pre_ref[q, :] = pre
            act = pre * jax.nn.sigmoid(pre)
            c, s = r.cosv[q, :], r.sinv[q, :]
            for h in range(H):
                a = act[:, h * HEAD:(h + 1) * HEAD]
                rot_ref[q, 2 * h * HEAD:(2 * h + 1) * HEAD] = (a * c).astype(BF)
                rot_ref[q, (2 * h + 1) * HEAD:(2 * h + 2) * HEAD] = (a * s).astype(BF)

        each(T // TT, tile)

    def project_into(ref, k):
        def tile(t):
            q = rows_of(t, TT)
            ref[q, :] = dot_nn(r.nin[q, :], r.mixw[k]).astype(ref.dtype)

        each(T // TT, tile)

    gather_forward(0)
    gather_send(2)
    gather_forward(1)
    gather_send(3)
    gather_wait(0)
    turn_into(r.qpre, r.qrot, 0)
    gather_forward(2)
    gather_send(4)
    gather_wait(1)
    turn_into(r.kpre, r.krot, 1)
    gather_forward(3)
    gather_send(5)
    gather_wait(2)
    project_into(r.val, 2)
    gather_forward(4)
    gather_send(6)
    gather_wait(3)
    project_into(r.gpre, 3)

    def wo_block(owner):
        return r.wo.at[:, pl.ds(pl.multiple_of(owner * C, C), C)]

    gather_wait(4)
    share_send(0, wo_block)

    NB = T // B
    REACH = LONGEST // B

    def keys_of(qb):
        return slice(max(0, qb - REACH) * B, (qb + 1) * B)

    def weights_of(qb, h):
        key = keys_of(qb)
        width = key.stop - key.start
        fades = [r.dec[min(o, 1), h] for o in range(width // B - 1, -1, -1)]
        for o in range(2, width // B):
            fades[width // B - 1 - o] *= jnp.exp(rate_of(h) * ((o - 1) * B))
        seen = jnp.broadcast_to(r.segk[0:1, key], (B, width))
        same = widen(r.segq[qb * B:(qb + 1) * B, :], width) == seen
        return jnp.where(same, jnp.concatenate(fades, axis=1), 0.0)

    def u_block(qb):
        return lambda owner: r.ufull.at[qb * B:(qb + 1) * B, pl.ds(pl.multiple_of(owner * C, C), C)]

    def attend(qb):
        q = slice(qb * B, (qb + 1) * B)
        squares = jnp.zeros((B, 1), F32)
        for h in range(H):
            rot = slice(2 * h * HEAD, 2 * (h + 1) * HEAD)
            chan = slice(h * HEAD, (h + 1) * HEAD)
            key = keys_of(qb)
            scores = dot_nt(r.qrot[q, rot], r.krot[key, rot]) * weights_of(qb, h)
            total = dot_nn(scores.astype(BF), r.val[key, chan])
            r.mixed[q, chan] = total
            squares = squares + jnp.sum(total * total, axis=-1, keepdims=True)
            r.ufull[q, pl.ds(pl.multiple_of(j * C + h * HEAD, HEAD), HEAD)] = (
                total * r.gpre[q, chan]
            ).astype(BF)
        r.ss[j, :, q] = jnp.transpose(jnp.broadcast_to(squares, (B, 128)))[0:8, :]

    def ss_block(owner):
        return r.ss.at[owner]

    for qb in range(NB):
        attend(qb)
        share_send(1 + qb, u_block(qb))
        if qb == NB - 1:
            share_send(1 + NB, ss_block)
        if qb == 0:
            gather_forward(5)
            gather_send(7)
        if qb == 1:
            share_forward(0, wo_block)
        if qb == 2:
            gather_forward(6)
            gather_send(8)
        if qb > 0:
            share_forward(qb, u_block(qb - 1))
    share_forward(NB, u_block(NB - 1))
    share_forward(1 + NB, ss_block)
    gather_forward(7)
    gather_send(9)
    gather_forward(8)
    gather_send(10)
    share_wait(0, wo_block)
    for qb in range(NB):
        share_wait(1 + qb, u_block(qb))
    share_wait(1 + NB, ss_block)
    early = list(pending)

    total_ss = r.ss[0]
    for owner in range(1, mp):
        total_ss = total_ss + r.ss[owner]
    inverse = lax.rsqrt(total_ss * (1.0 / D) + EPSILON)
    for t in range(T // 128):
        q = slice(t * 128, t * 128 + 128)
        r.rcol[q, :] = jnp.transpose(jnp.broadcast_to(inverse[0:1, q], (128, 128)))

    def hidden_tile(t):
        q = rows_of(t, TB)
        out = widen(r.rcol[q, :], D) * dot_nn(r.ufull[q, :], r.wo[...])
        hidden = r.xv[q, :].astype(F32) + out
        scale = lax.rsqrt(jnp.mean(hidden * hidden, axis=-1, keepdims=True) + EPSILON)
        r.nmid[q, :] = (hidden * scale).astype(BF)

        @pl.when(t == j)
        def _():
            r.hown[...] = hidden

    each(T // TB, hidden_tile)
    gather_wait(5)
    gather_wait(6)

    def gate_tile(t):
        q = rows_of(t, TT)
        r.gact[q, 0:F] = to_units(r.nmid[q, :], 1)

    each(T // TT, gate_tile)
    gather_forward(9)
    gather_wait(7)
    gather_wait(8)

    def up_tile(t):
        q = rows_of(t, TT)
        upper = to_units(r.nmid[q, :], 2)
        r.uact[q, :] = upper.astype(BF)
        r.prod[q, :] = (r.gact[q, 0:F] * upper).astype(BF)

    each(T // TT, up_tile)
    put_ff_grad(0, r.prod, r.up)
    gather_forward(10)
    scatter_first(5)
    gather_wait(9)
    gather_wait(10)

    def mid_block(x, c):
        q = rows_of(x * 2 + c, TB)
        g = to_units(r.up[q, :], 0)
        grad_gate, grad_up = (g * r.uact[q, :].astype(F32)).astype(BF), (g * r.gact[q, 0:F]).astype(BF)
        r.ggate[q, :] = grad_gate
        r.gup[q, :] = grad_up
        r.part[x, c] = (to_model(grad_gate, 1) + to_model(grad_up, 2)).astype(BF)

    used = sum_begin(0, 0, mid_block)
    put_ff_grad(1, r.ggate, r.nmid)
    scatter_first(6)

    def back_tile(t):
        q = rows_of(t, 128)
        here = rows_of(j * (TB // 128) + t, 128)
        grad = sum_tile(0, q)
        hidden = r.hown[q, :]
        scale = lax.rsqrt(jnp.mean(hidden * hidden, axis=-1, keepdims=True) + EPSILON)
        normed = hidden * scale
        inner = jnp.mean(grad * normed, axis=-1, keepdims=True)
        out = r.up[here, :].astype(F32) + scale * (grad - normed * inner)
        r.ghid[q, :] = out
        low = out.astype(BF)
        r.hlow[here, :] = low
        mixer_out = hidden - r.xown[q, :].astype(F32)
        product = jnp.sum(low.astype(F32) * mixer_out, axis=-1, keepdims=True) * (1.0 / D)
        r.inn[j, :, q] = jnp.transpose(jnp.broadcast_to(product, (128, 128)))[0:8, :]

    def token_block(ref):
        return lambda owner: ref.at[rows_of(owner, TB)]

    BO, IN, GM, HL, IG = 2 + NB, 3 + NB, 4 + NB, 9 + NB, 9 + NB + NT

    def inn_block(owner):
        return r.inn.at[owner]

    def half_block(ref, t):
        return lambda owner: ref.at[rows_of(owner * NT + t, 128)]

    for t in range(NT):
        sum_arrived(0, 0, t)
        back_tile(t)
        share_send(HL + t, half_block(r.hlow, t))
    share_send(IN, inn_block)
    put_ff_grad(2, r.gup, r.nmid)
    scatter_first(7)
    scatter_second(5)
    for t in range(NT):
        share_forward(HL + t, half_block(r.hlow, t))
    share_forward(IN, inn_block)
    for copy in used:
        settle(copy)

    def expand_block(x, c):
        q = rows_of(x * 2 + c, TB)
        r.part[x, c] = to_model(r.prod[q, :], 0).astype(BF)

    used = sum_begin(1, 1, expand_block)
    for t in range(NT):
        share_wait(HL + t, half_block(r.hlow, t))
    share_wait(IN, inn_block)
    for owner in range(mp):
        for t in range(TB // 128):
            row = r.inn[owner, 0:1, t * 128:(t + 1) * 128]
            q = slice(owner * TB + t * 128, owner * TB + (t + 1) * 128)
            r.icol[q, :] = jnp.transpose(jnp.broadcast_to(row, (128, 128)))

    wo_rows = rows_of(j, C)

    def gated_tile(t):
        q = rows_of(t, TT)
        low = r.hlow[q, :]
        grad = dot_nt(low, r.wo[wo_rows, :])
        inner = widen(r.icol[q, :], C)
        inverse = widen(r.rcol[q, :], C)
        normed = r.mixed[q, :] * inverse
        r.gproj[3][q, :] = (grad * normed).astype(BF)
        r.gmix[q, :] = (inverse * (grad * r.gpre[q, :] - normed * inner)).astype(BF)
        r.rh[q, :] = (inverse * r.hlow[q, jcols].astype(F32)).astype(BF)

    each(T // TT, gated_tile)
    put_grad(4, r.ufull, r.rh)
    scatter_first(4)
    scatter_second(6)

    def swish_back(pre, grad):
        gate = jax.nn.sigmoid(pre)
        return grad * (gate * (1.0 + pre * (1.0 - gate)))

    def attend_back(qb):
        q, key = slice(qb * B, (qb + 1) * B), keys_of(qb)
        for h in range(H):
            rot = slice(2 * h * HEAD, 2 * (h + 1) * HEAD)
            chan = slice(h * HEAD, (h + 1) * HEAD)
            weights = weights_of(qb, h)
            scores = (dot_nt(r.qrot[q, rot], r.krot[key, rot]) * weights).astype(BF)
            back = (dot_nt(r.gmix[q, chan], r.val[key, chan]) * weights).astype(BF)
            dq = dot_nn(back, r.krot[key, rot])
            turned = dq[:, :HEAD] * r.cosv[q, :] + dq[:, HEAD:] * r.sinv[q, :]
            r.gproj[0][q, chan] = swish_back(r.qpre[q, chan], turned).astype(BF)
            dk = dot_tn(back, r.qrot[q, rot])
            dv = dot_tn(scores, r.gmix[q, chan])
            for kb in range(key.start // B, qb + 1):
                at = slice(kb * B - key.start, (kb + 1) * B - key.start)
                rows = slice(kb * B, (kb + 1) * B)
                dkb, dvb = dk[at], dv[at]
                if qb < min(kb + REACH, NB - 1):
                    dkb, dvb = dkb + r.dk[rows, rot], dvb + r.dv[rows, chan]
                if kb < qb:
                    r.dk[rows, rot], r.dv[rows, chan] = dkb, dvb
                else:
                    turned = dkb[:, :HEAD] * r.cosv[q, :] + dkb[:, HEAD:] * r.sinv[q, :]
                    r.gproj[1][q, chan] = swish_back(r.kpre[q, chan], turned).astype(BF)
                    r.gproj[2][q, chan] = dvb.astype(BF)

    def output_tile(t):
        q = rows_of(t, 128)
        r.bov[rows_of(j * NT + t, 128), :] = (r.hown[q, :] + sum_tile(1, q)).astype(BF)

    def late_core(x):
        return pltpu.make_async_remote_copy(
            src_ref=r.part.at[x, 1 - ci], dst_ref=r.recc.at[0, x], send_sem=r.acs.at[2, x], recv_sem=r.acr.at[2, x],
            device_id={"mp": xi * 2 + 1 - ci}, device_id_type=MESH,
        )

    def late_chip(x, d, t):
        q = slice(t * 128, (t + 1) * 128)
        return pltpu.make_async_remote_copy(
            src_ref=r.part.at[x, ci, q], dst_ref=r.recx.at[0, d - 1, q], send_sem=r.axs.at[2, d - 1, t],
            recv_sem=r.axr.at[2, d - 1, t], device_id={"mp": x * 2 + ci}, device_id_type=MESH,
        )

    def blocks_in(qb):
        return [divmod(at, 2) for at in range(qb * B // TB, (qb + 1) * B // TB)]

    def late_begin(x, c):
        q = slice((x * 2 + c) * TB, (x * 2 + c + 1) * TB)
        out = dot_nt(r.gproj[0][q, :], r.mixw[0])
        for k in range(1, 4):
            out = out + dot_nt(r.gproj[k][q, :], r.mixw[k])
        r.part[x, c] = out.astype(BF)

        @pl.when(ci != c)
        def _():
            late_core(x).start()

    def late_pass(x, c):
        @pl.when(ci == c)
        def _():
            arrived(r.recc.at[0, x], r.acr.at[2, x])

        @pl.when((ci == c) & (xi != x))
        def _():
            for t in range(NT):
                q = slice(t * 128, (t + 1) * 128)
                r.part[x, c, q] = (r.part[x, c, q].astype(F32) + r.recc[0, x, q].astype(F32)).astype(BF)
                late_chip(x, lax.rem(x - xi + X, X), t).start()

    put_grad(3, r.nint, r.gproj[3], turned=True)
    scatter_first(3)
    for qb in range(NB - 1, -1, -1):
        attend_back(qb)
        if qb == NB - 1:
            for t in range(NT):
                sum_arrived(1, 1, t)
            each(TB // 128, output_tile)
            share_send(BO, token_block(r.bov))
            for copy in used + early:
                settle(copy)
        for x, c in blocks_in(qb):
            late_begin(x, c)
        if qb < NB - 1:
            for x, c in blocks_in(qb + 1):
                late_pass(x, c)
        if qb == max(NB - 2, 0):
            scatter_second(7)
            share_forward(BO, token_block(r.bov))
        if qb == max(NB - 3, 0):
            scatter_second(4)
    for x, c in blocks_in(0):
        late_pass(x, c)
    pending.extend(late_core(x) for x in range(X))
    pending.extend(late_chip(lax.rem(xi + d, X), d, t) for d in range(1, X) for t in range(NT))
    for k in (2, 0, 1):
        put_grad(k, r.nint, r.gproj[k], turned=True)
        scatter_first(k)
    scatter_second(3)

    def input_tile(t):
        q = rows_of(t, 128)
        grad = sum_tile(0, q)
        v = r.xown[q, :].astype(F32)
        scale = lax.rsqrt(jnp.mean(v * v, axis=-1, keepdims=True) + EPSILON)
        normed = v * scale
        inner = jnp.mean(grad * normed, axis=-1, keepdims=True)
        r.igv[rows_of(j * NT + t, 128), :] = (r.ghid[q, :] + scale * (grad - normed * inner)).astype(BF)

    for t in range(NT):
        for d in range(1, X):
            arrived(r.recx.at[0, d - 1, t * 128:(t + 1) * 128], r.axr.at[2, d - 1, t])
        input_tile(t)
        share_send(IG + t, half_block(r.igv, t))
    for k in (2, 0, 1):
        scatter_second(k)
    share_wait(BO, token_block(r.bov))
    stores = [load(r.bov, r.bo, 0)]

    def grad_block(k):
        return lambda owner: r.gmv.at[k * S:(k + 1) * S, pl.ds(pl.multiple_of(owner * C, C), C)]

    squares = jnp.zeros((), F32)
    for k in range(5, 8):
        total = scatter_total(k)
        if k == 5:
            r.gso[...] = total
        else:
            r.geo[k - 6] = total
        squares = squares + jnp.sum(total * total)
    for k in (4, 3, 2, 0, 1):
        total = scatter_total(k).astype(BF)
        r.gmv[k * S:(k + 1) * S, jcols] = total
        squares = squares + jnp.sum(total.astype(F32) * total.astype(F32))
        share_send(GM + k, grad_block(k))

    r.s1[j] = jnp.full((8, 128), squares, F32)
    for d in range(1, mp):
        go(r.s1.at[j], r.s1.at[j], r.q1s.at[d], r.q1r.at[d], mp=lax.rem(j + d, mp))
    for t in range(NT):
        share_forward(IG + t, half_block(r.igv, t))
    for d in range(1, mp):
        arrived(r.s1.at[lax.rem(j - d + mp, mp)], r.q1r.at[d])
    total = r.s1[0]
    for owner in range(1, mp):
        total = total + r.s1[owner]
    r.s2[i] = total
    for d in range(1, n):
        go(r.s2.at[i], r.s2.at[i], r.q2s.at[d], r.q2r.at[d], dp=lax.rem(i + d, n))
    for k in (4, 3, 2, 0, 1):
        share_forward(GM + k, grad_block(k))
    for d in range(1, n):
        arrived(r.s2.at[lax.rem(i - d + n, n)], r.q2r.at[d])
    total = r.s2[0]
    for owner in range(1, n):
        total = total + r.s2[owner]
    r.sqo[...] = total

    for t in range(NT):
        share_wait(IG + t, half_block(r.igv, t))
    stores.append(load(r.igv, r.ig, 1))
    for k in (4, 3, 2, 0, 1):
        share_wait(GM + k, grad_block(k))
        stores.append(load(r.gmv.at[k * S:(k + 1) * S], r.gmo.at[k], 2 + k))
    for copy in stores:
        copy.wait()
    for copy in pending:
        copy.wait_send()


def fused(p, *operands):
    scratch = scratch_of(p)
    names = IN_NAMES + OUT_NAMES + tuple(scratch)
    anywhere = pl.BlockSpec(memory_space=pl.ANY)
    vmem = pl.BlockSpec(memory_space=pltpu.VMEM)
    smem = pl.BlockSpec(memory_space=pltpu.SMEM)
    return pl.pallas_call(
        partial(body, p, names),
        out_shape=(
            jax.ShapeDtypeStruct((p.T, p.D), BF),
            jax.ShapeDtypeStruct((p.T, p.D), BF),
            jax.ShapeDtypeStruct((5, p.S, p.D), BF),
            jax.ShapeDtypeStruct((2, p.F, p.S) if p.FD else (2, p.S, p.F), F32),
            jax.ShapeDtypeStruct((p.F, p.S) if p.FD else (p.S, p.F), F32),
            jax.ShapeDtypeStruct((8, 128), F32),
        ),
        in_specs=[anywhere, anywhere, vmem, smem] + [anywhere] * 5,
        out_specs=(anywhere, anywhere, anywhere, vmem, vmem, vmem),
        scratch_shapes=list(scratch.values()),
        compiler_params=pltpu.CompilerParams(
            collective_id=0, has_side_effects=True, vmem_limit_bytes=VMEM_LIMIT
        ),
    )(*operands)


VMEM_LIMIT = 64 * 2**20 - 2**18


def renew(weight, momentum, shadow, grad, clip_factor):
    clipped = grad * clip_factor
    velocity = MOMENTUM * momentum + clipped
    updated = weight - LEARN_RATE * (clipped + MOMENTUM * velocity)
    average = SHADOW_DECAY * shadow + (1.0 - SHADOW_DECAY) * updated
    return (velocity, average, updated)


def update_body(cuts, *refs):
    kinds, pieces = len(cuts), sum(len(c) for c in cuts)
    sq, carried = refs[0], refs[1:3]
    ins = [refs[3 + 4 * w:7 + 4 * w] for w in range(kinds)]
    refs = refs[3 + 4 * kinds:]
    norm_out, carried_out = refs[0], refs[1:3]
    outs = [refs[3 + 3 * w:6 + 3 * w] for w in range(kinds)]
    refs = refs[3 + 3 * kinds:]
    held = [refs[4 * w:4 * w + 4] for w in range(kinds)]
    made = [refs[4 * kinds + 3 * w:4 * kinds + 3 * w + 3] for w in range(kinds)]
    bounce, (in_sem, out_sem, carry_sem) = refs[7 * kinds:7 * kinds + 2], refs[7 * kinds + 2:]
    loads, order = {}, [(w, c) for w in range(kinds) for c in range(len(cuts[w]))]
    for at, (w, c) in enumerate(order):
        for a in range(4):
            cut = cuts[w][c]
            loads[at, a] = pltpu.make_async_copy(ins[w][a].at[cut], held[w][a].at[cut], in_sem.at[at, a])
            loads[at, a].start()
    carry = [pltpu.make_async_copy(carried[a], bounce[a], carry_sem.at[a]) for a in range(2)]
    for copy in carry:
        copy.start()
    copies = []
    norm = jnp.sqrt(sq[...])
    norm_out[...] = norm
    clip_factor = 1.0 / jnp.maximum(jnp.max(norm), 1.0)
    for at, (w, c) in enumerate(order):
        cut = cuts[w][c]
        for a in range(4):
            loads[at, a].wait()
        new = renew(*[held[w][a][cut] for a in range(3)], held[w][3][cut].astype(F32), clip_factor)
        for a in range(3):
            made[w][a][cut] = new[a]
            copy = pltpu.make_async_copy(made[w][a].at[cut], outs[w][a].at[cut], out_sem.at[at, a])
            copy.start()
            copies.append(copy)
    for a in range(2):
        carry[a].wait()
        copy = pltpu.make_async_copy(bounce[a], carried_out[a], carry_sem.at[2 + a])
        copy.start()
        copies.append(copy)
    for copy in copies:
        copy.wait()


def update(sq, carried, weights):
    cuts = [[c for c in range(g[0].shape[0])] if g[0].ndim == 3 else [slice(None)] for g in weights]
    pieces = sum(len(c) for c in cuts)
    anywhere = pl.BlockSpec(memory_space=pl.ANY)
    vmem = pl.BlockSpec(memory_space=pltpu.VMEM)
    flat_in = [a for group in weights for a in group]
    flat_out = [a for group in weights for a in group[:3]]
    dma = pltpu.SemaphoreType.DMA
    size = sum(a.size * a.dtype.itemsize for a in flat_in + flat_out + 2 * list(carried))
    return pl.pallas_call(
        partial(update_body, cuts),
        out_shape=[jax.ShapeDtypeStruct(a.shape, a.dtype) for a in [sq, *carried, *flat_out]],
        in_specs=[vmem] + [anywhere] * (2 + len(flat_in)),
        out_specs=[vmem] + [anywhere] * (2 + len(flat_out)),
        scratch_shapes=[pltpu.VMEM(a.shape, a.dtype) for a in flat_in + flat_out + list(carried)]
        + [dma((pieces, 4)), dma((pieces, 3)), dma((4,))],
        cost_estimate=pl.CostEstimate(flops=size, bytes_accessed=size, transcendentals=0),
        compiler_params=pltpu.CompilerParams(vmem_limit_bytes=VMEM_LIMIT),
    )(sq, *carried, *flat_in)


def turn_tables(tokens):
    theta = np.float32(10000.0) ** (-np.arange(HEAD, dtype=np.float32) / np.float32(HEAD))
    angle = np.arange(tokens, dtype=np.float32)[:, None] * theta.astype(np.float32)[None, :]
    angle = angle.astype(np.float64)
    return np.cos(angle).astype(np.float32), np.sin(angle).astype(np.float32)


def per_device(mesh, block_input, segment_ids, live_length, output_grad, mixer_weight, mixer_momentum, mixer_shadow,
               expand_weight, expand_momentum, expand_shadow, shrink_weight, shrink_momentum, shrink_shadow):
    rows, length, width = block_input.shape
    p = plan_of(mesh, length, width, shrink_weight.shape[0])
    turn = (lambda v: jnp.swapaxes(v, -1, -2)) if p.FD else (lambda v: v)
    if p.FD:
        shards = (turn(expand_weight), shrink_weight)
    else:
        shards = (jnp.concatenate([shrink_weight.T[None], expand_weight], axis=0).astype(BF), shrink_weight)
    cos, sin = turn_tables(length)
    out, grad_in, gm, ge, gs, sq = fused(
        p, block_input[0], output_grad[0], segment_ids, live_length, jnp.asarray(cos), jnp.asarray(sin), mixer_weight, *shards
    )
    new = update(sq, (out, grad_in), (
        (mixer_weight, mixer_momentum, mixer_shadow, gm),
        (turn(expand_weight), turn(expand_momentum), turn(expand_shadow), ge),
        (shrink_weight, shrink_momentum, shrink_shadow, gs if p.FD else gs.T),
    ))
    norm, out, grad_in = new[:3]
    return (out[None], grad_in[None], norm[0, 0], *new[3:6], *(turn(v) for v in new[6:9]), *new[9:12])


def solution(mesh):
    row, mixer, expand, shrink = P("dp", None, None), P(None, "dp", None), P(None, "dp", "mp"), P("mp", "dp")
    return jax.shard_map(
        partial(per_device, mesh),
        mesh=mesh,
        in_specs=(row, P("dp", None), P("dp"), row) + (mixer,) * 3 + (expand,) * 3 + (shrink,) * 3,
        out_specs=(row, row, P()) + (mixer,) * 3 + (expand,) * 3 + (shrink,) * 3,
        check_vma=False,
    )
```

```python
from functools import partial
from types import SimpleNamespace

import jax
import jax.numpy as jnp
import numpy as np
from jax import lax
from jax.experimental import pallas as pl
from jax.experimental.pallas import tpu as pltpu
from jax.sharding import PartitionSpec as P

HEAD = 128
EPSILON = 1e-06
LEARN_RATE = 32.0
MOMENTUM = 0.5
SHADOW_DECAY = 0.5
LAYER_PLACE = 12.0 / 24.0
LONGEST = 512
FF_ORDER = (1, 2, 0)
MESH = pl.DeviceIdType.MESH
BF = jnp.bfloat16
F32 = jnp.float32


def dot_nn(a, b):
    return lax.dot_general(a, b, (((1,), (0,)), ((), ())), preferred_element_type=F32)


def dot_nt(a, b):
    return lax.dot_general(a, b, (((1,), (1,)), ((), ())), preferred_element_type=F32)


def dot_tn(a, b):
    return lax.dot_general(a, b, (((0,), (0,)), ((), ())), preferred_element_type=F32)


def rows_of(index, size):
    return pl.ds(pl.multiple_of(index * size, size), size)


def each(count, body):
    def step(t, carry):
        body(t)
        return carry

    lax.fori_loop(0, count, step, 0)


def widen(column, width):
    return jnp.concatenate([column] * (width // 128), axis=1)


def plan_of(mesh, tokens, width, inner):
    n, mp = mesh.shape["dp"], mesh.shape["mp"]
    lo, core = 2, 2
    return SimpleNamespace(
        n=n, mp=mp, LO=lo, HI=n // lo, X=mp // core, T=tokens, D=width, C=width // mp, F=inner,
        S=width // n, H=width // mp // HEAD, TB=tokens // mp, B=min(256, tokens),
        NT=tokens // mp // 128, FD=(width // n) % 128 == 0,
    )


def scratch_of(p):
    T, D, C, F, S, HI, LO, X, TB, B = p.T, p.D, p.C, p.F, p.S, p.HI, p.LO, p.X, p.TB, p.B
    dma = pltpu.SemaphoreType.DMA
    v = pltpu.VMEM
    return dict(
        mixw=v((4, D, C), BF), wo=v((D, D), BF), ffw=v((3, F, D) if p.FD else (3, D, F), BF),
        xown=v((TB, D), BF), nin=v((T, D), BF), nint=v((D, T), BF), up=v((T, D), BF),
        cosv=v((T, HEAD), F32), sinv=v((T, HEAD), F32),
        segq=v((T, 128), F32), segk=v((8, T), F32), dec=v((2, p.H, B, B), F32),
        qpre=v((T, C), F32), kpre=v((T, C), F32), gpre=v((T, C), F32), val=v((T, C), BF),
        qrot=v((T, 2 * C), BF), krot=v((T, 2 * C), BF), mixed=v((T, C), F32),
        ufull=v((T, D), BF), ss=v((p.mp, 8, T), F32), rcol=v((T, 128), F32),
        inn=v((p.mp, 8, TB), F32), hown=v((TB, D), F32),
        gact=v((T, max(F, 2 * C + HEAD)), F32), uact=v((T, F), BF), prod=v((T, F), BF), ggate=v((T, F), BF), gup=v((T, F), BF),
        part=v((X, 2, TB, D), BF), recc=v((2, X, TB, D), BF), recx=v((2, X - 1, TB, D), BF),
        ghid=v((TB, D), F32), hlow=v((T, D), BF),
        gm=v((5, HI, LO, S, C), BF), rym=v((5, HI, S, C), BF), rzm=v((5, HI - 1, S, C), BF),
        gf=v((3, LO, F, HI * S) if p.FD else (3, HI, LO, S, F), BF),
        ryf=v((3, F, HI * S) if p.FD else (3, HI, S, F), BF),
        rzf=v((3, HI - 1, F, S) if p.FD else (3, HI - 1, S, F), BF),
        sqs=v((8, 128), F32), s1=v((p.mp, 8, 128), F32), s2=v((p.n, 8, 128), F32),
        loc=dma((10,)),
        zs=dma((11, HI - 1)), zr=dma((11, HI - 1)), ys=dma((11, HI)), yr=dma((11, HI)),
        xs=dma((20, X - 1)), xr=dma((20, X - 1)), cs=dma((20, X)), cr=dma((20, X)),
        acs=dma((3, X)), acr=dma((3, X)), axs=dma((3, X - 1, p.NT)), axr=dma((3, X - 1, p.NT)),
        bys=dma((11,)), byr=dma((11,)), bzs=dma((11, HI - 1)), bzr=dma((11, HI - 1)),
        q1s=dma((p.mp,)), q1r=dma((p.mp,)), q2s=dma((p.n,)), q2r=dma((p.n,)),
    )


IN_NAMES = ("x", "og", "seg", "live", "cos", "sin", "mixsh", "exsh", "shsh")
OUT_NAMES = ("bo", "ig", "gmo", "geo", "gso", "sqo")


def body(p, names, *refs):
    r = SimpleNamespace(**dict(zip(names, refs)))
    n, mp, LO, HI, X, T, D, C, F, S, H, TB, B = (
        p.n, p.mp, p.LO, p.HI, p.X, p.T, p.D, p.C, p.F, p.S, p.H, p.TB, p.B,
    )
    NT, TT = p.NT, min(512, p.T)
    i, j = lax.axis_index("dp"), lax.axis_index("mp")
    zi, yi = i // LO, lax.rem(i, LO)
    xi, ci = j // 2, lax.rem(j, 2)
    jcols = pl.ds(pl.multiple_of(j * C, C), C)
    pending = []
    r.xv, r.nmid = r.hlow, r.nin
    r.bov, r.igv, r.gmv = r.up, r.ufull, r.wo
    r.dk, r.icol, r.dv = r.gact.at[:, 0:2 * C], r.gact.at[:, 2 * C:2 * C + HEAD], r.mixed
    r.gproj = [r.ggate.at[:, 0:C], r.ggate.at[:, C:2 * C], r.gup.at[:, 0:C], r.gup.at[:, C:2 * C]]
    r.gmix, r.rh = r.prod.at[:, 0:C], r.prod.at[:, C:2 * C]

    def go(src, dst, ssem, rsem, **device):
        copy = pltpu.make_async_remote_copy(
            src_ref=src, dst_ref=dst, send_sem=ssem, recv_sem=rsem,
            device_id=device, device_id_type=MESH,
        )
        copy.start()
        pending.append(copy)
        return copy

    def arrived(dst, sem):
        pltpu.make_async_copy(dst, dst, sem).wait()

    def settle(copy):
        copy.wait_send()
        pending[:] = [other for other in pending if other is not copy]

    def load(src, dst, sem):
        copy = pltpu.make_async_copy(src, dst, r.loc.at[sem])
        copy.start()
        return copy

    own_mix = [load(r.mixsh.at[k, :, jcols], r.qpre.at[k * S:(k + 1) * S], k) for k in range(5)]
    if p.FD:
        stage = [r.gact.at[0:F, m * S:(m + 1) * S] for m in range(3)]
        own_ff = [load(r.shsh if m == 0 else r.exsh.at[m - 1], stage[m], 5 + m) for m in range(3)]
    else:
        own_ff = [load(r.exsh.at[m], r.ffw.at[m, rows_of(i, S)], 5 + m) for m in range(3)]
    load_x = load(r.x, r.xv, 8)
    load_og = load(r.og, r.up, 9)

    def enter():
        barrier = pltpu.get_barrier_semaphore()
        for d in range(1, n):
            pl.semaphore_signal(barrier, inc=1, device_id={"dp": lax.rem(i + d, n)}, device_id_type=MESH)
        for d in range(1, mp):
            pl.semaphore_signal(barrier, inc=1, device_id={"mp": lax.rem(j + d, mp)}, device_id_type=MESH)
        pl.semaphore_wait(barrier, n - 1 + mp - 1)

    def slot(k, device):
        rows = rows_of(device, S)
        if k == 4:
            return r.wo.at[rows, jcols]
        if k < 4:
            return r.mixw.at[k, rows]
        m, half = FF_ORDER[(k - 5) // 2], (k - 5) % 2
        if p.FD:
            return r.ffw.at[m, half * F // 2:(half + 1) * F // 2, rows]
        return r.ffw.at[m, pl.ds(pl.multiple_of(device * S + half * S // 2, S // 2), S // 2)]

    def gather_ready(k):
        if k < 5:
            own_mix[k].wait()
            slot(k, i)[...] = r.qpre[k * S:(k + 1) * S, :].astype(BF)
        else:
            m, half = FF_ORDER[(k - 5) // 2], (k - 5) % 2
            if half == 0:
                own_ff[m].wait()
            if p.FD:
                slot(k, i)[...] = stage[m][half * F // 2:(half + 1) * F // 2, :].astype(BF)

    def gather_send(k):
        src = slot(k, i)
        for d in range(1, HI):
            go(src, src, r.zs.at[k, d - 1], r.zr.at[k, d - 1], dp=lax.rem(zi + d, HI) * LO + yi)
        go(src, src, r.ys.at[k, 0], r.yr.at[k, 0], dp=zi * LO + 1 - yi)

    def gather_forward(k):
        for d in range(1, HI):
            block = slot(k, lax.rem(zi - d + HI, HI) * LO + yi)
            arrived(block, r.zr.at[k, d - 1])
            go(block, block, r.ys.at[k, d], r.yr.at[k, d], dp=zi * LO + 1 - yi)

    def gather_wait(k):
        for d in range(HI):
            arrived(slot(k, lax.rem(zi - d + HI, HI) * LO + 1 - yi), r.yr.at[k, d])

    def share_send(s, block, src=None):
        own = block(j)
        src = own if src is None else src
        for d in range(1, X):
            go(src, own, r.xs.at[s, d - 1], r.xr.at[s, d - 1], mp=lax.rem(xi + d, X) * 2 + ci)
        go(src, own, r.cs.at[s, 0], r.cr.at[s, 0], mp=xi * 2 + 1 - ci)

    def share_forward(s, block):
        for d in range(1, X):
            part = block(lax.rem(xi - d + X, X) * 2 + ci)
            arrived(part, r.xr.at[s, d - 1])
            go(part, part, r.cs.at[s, d], r.cr.at[s, d], mp=xi * 2 + 1 - ci)

    def share_wait(s, block):
        for d in range(X):
            arrived(block(lax.rem(xi - d + X, X) * 2 + 1 - ci), r.cr.at[s, d])

    def sum_begin(s, b, compute):
        sent = []
        for d in [*range(1, X), 0]:
            to = lax.rem(xi + d, X)
            compute(to, 1 - ci)
            sent.append(go(
                r.part.at[to, 1 - ci], r.recc.at[b, to], r.acs.at[s, d], r.acr.at[s, d], mp=xi * 2 + 1 - ci
            ))
        for d in range(1, X):
            to = lax.rem(xi + d, X)
            compute(to, ci)
            arrived(r.recc.at[b, to], r.acr.at[s, d])
            for t in range(NT):
                q = slice(t * 128, (t + 1) * 128)
                r.part[to, ci, q] = (
                    r.part[to, ci, q].astype(F32) + r.recc[b, to, q].astype(F32)
                ).astype(BF)
                sent.append(go(
                    r.part.at[to, ci, q], r.recx.at[b, d - 1, q], r.axs.at[s, d - 1, t], r.axr.at[s, d - 1, t],
                    mp=to * 2 + ci,
                ))
        compute(xi, ci)
        return sent

    def sum_arrived(s, b, t):
        if t == 0:
            arrived(r.recc.at[b, xi], r.acr.at[s, 0])
        for d in range(1, X):
            arrived(r.recx.at[b, d - 1, t * 128:(t + 1) * 128], r.axr.at[s, d - 1, t])

    def sum_tile(b, q):
        total = r.part[xi, ci, q].astype(F32) + r.recc[b, xi, q].astype(F32)
        for d in range(1, X):
            total = total + r.recx[b, d - 1, q].astype(F32)
        return total

    flat = p.FD

    def half_of(k):
        size = (F if flat else S) // 2
        return (k - 5) // 2, slice((k - 5) % 2 * size, ((k - 5) % 2 + 1) * size)

    def from_y(k):
        if k < 5:
            return r.rym.at[k]
        m, rows = half_of(k)
        return r.ryf.at[m, rows] if flat else r.ryf.at[m, :, rows]

    def from_y_block(k, z):
        ref = from_y(k)
        return ref.at[:, rows_of(z, S)] if flat and k >= 5 else ref.at[z]

    def from_z(k, d):
        if k < 5:
            return r.rzm.at[k, d - 1]
        m, rows = half_of(k)
        return r.rzf.at[m, d - 1, rows]

    def to_y(k):
        if k < 5:
            return r.gm.at[k, :, 1 - yi]
        m, rows = half_of(k)
        return r.gf.at[m, 1 - yi, rows] if flat else r.gf.at[m, :, 1 - yi, rows]

    def mine(k, z):
        if k < 5:
            return r.gm.at[k, z, yi]
        m, rows = half_of(k)
        return r.gf.at[m, yi, rows, rows_of(z, S)] if flat else r.gf.at[m, z, yi, rows]

    def scatter_first(*pieces):
        for k in pieces:
            go(to_y(k), from_y(k), r.bys.at[k], r.byr.at[k], dp=zi * LO + 1 - yi)

    def scatter_second(*pieces):
        for k in pieces:
            arrived(from_y(k), r.byr.at[k])
            for d in range(1, HI):
                to = lax.rem(zi + d, HI)
                block = mine(k, to)
                block[...] = (block[...].astype(F32) + from_y_block(k, to)[...].astype(F32)).astype(BF)
                go(block, from_z(k, d), r.bzs.at[k, d - 1], r.bzr.at[k, d - 1], dp=to * LO + yi)

    def scatter_total(k):
        for d in range(1, HI):
            arrived(from_z(k, d), r.bzr.at[k, d - 1])
        total = mine(k, zi)[...].astype(F32) + from_y_block(k, zi)[...].astype(F32)
        for d in range(1, HI):
            total = total + from_z(k, d)[...].astype(F32)
        return total

    def squares_of(total):
        squared = total * total
        if squared.shape[-1] % 128:
            corner = (lax.broadcasted_iota(jnp.int32, (8, 128), 0) + lax.broadcasted_iota(jnp.int32, (8, 128), 1)) == 0
            return jnp.where(corner, jnp.sum(squared), 0.0)
        folded = jnp.sum(squared.reshape(-1, 8, squared.shape[-1]), axis=0)
        return sum(folded[:, c:c + 128] for c in range(0, folded.shape[-1], 128))

    def finish_ff(*pieces):
        for k in pieces:
            m, rows = half_of(k)
            total = scatter_total(k)
            if m == 0:
                r.gso[rows] = total
            else:
                r.geo[m - 1, rows] = total
            r.sqs[...] += squares_of(total)

    def put_grad(k, lhs, rhs, turned=False):
        g = r.gm.at[k] if k < 5 else r.gf.at[k - 5]
        per = TT // (LO * S)

        def tile(t):
            if turned:
                out = dot_nn(lhs[rows_of(t, TT), :], rhs[...])
            else:
                out = dot_tn(lhs[:, rows_of(t, TT)], rhs[...])
            g[pl.ds(t * per, per)] = out.astype(BF).reshape(per, LO, S, out.shape[-1])

        each(D // TT, tile)

    def put_ff_grad(m, units, model):
        if not flat:
            return put_grad(5 + m, model, units)
        for f in range(0, F, 384):
            q = slice(f, min(f + 384, F))
            out = dot_tn(units[:, q], model[...]).astype(BF)
            for y in range(LO):
                for z in range(HI):
                    r.gf[m, y, q, z * S:(z + 1) * S] = out[:, (z * LO + y) * S:(z * LO + y + 1) * S]

    def to_units(a, m):
        return dot_nt(a, r.ffw[m]) if flat else dot_nn(a, r.ffw[m])

    def to_model(a, m):
        return dot_nn(a, r.ffw[m]) if flat else dot_nt(a, r.ffw[m])

    gather_ready(0)
    gather_ready(1)
    enter()
    gather_send(0)
    gather_send(1)
    gather_ready(2)
    gather_send(2)
    gather_ready(3)
    gather_send(3)
    r.sqs[...] = jnp.zeros_like(r.sqs)

    length = r.live[0]
    load_x.wait()

    def norm_tile(t):
        q = rows_of(t, 128)
        v = r.xv[q, :].astype(F32)
        r.nin[q, :] = (v * lax.rsqrt(jnp.mean(v * v, axis=-1, keepdims=True) + EPSILON)).astype(BF)

    each(T // 128, norm_tile)
    for k in range(4, 11):
        gather_ready(k)
    load_x_own = load(r.x.at[rows_of(j, TB)], r.xown, 8)
    load_og.wait()
    load_cos = load(r.cos, r.cosv, 0)
    load_sin = load(r.sin, r.sinv, 1)

    def live_tile(t):
        q = rows_of(t, 128)
        place = lax.broadcasted_iota(jnp.int32, (128, D), 0) + t * 128
        r.up[q, :] = jnp.where(place < length, r.up[q, :].astype(F32), 0.0).astype(BF)

    each(T // 128, live_tile)

    place = lax.broadcasted_iota(jnp.int32, (1, T), 1)
    segment = r.seg[...].astype(F32)
    r.segk[...] = jnp.broadcast_to(jnp.where(place < length, segment, -2.0), (8, T))
    seg_q = jnp.where(place < length, segment, -1.0)
    for t in range(T // 128):
        q = slice(t * 128, t * 128 + 128)
        r.segq[q, :] = jnp.transpose(jnp.broadcast_to(seg_q[:, q], (128, 128)))

    down = lax.broadcasted_iota(jnp.int32, (B, B), 0)
    over = lax.broadcasted_iota(jnp.int32, (B, B), 1)
    heads = D // HEAD

    def rate_of(h):
        return -(8.0 * (j * H + h).astype(F32) / heads) * (1.0 - LAYER_PLACE)

    for h in range(H):
        rate = rate_of(h)
        for o in range(2):
            distance = down - over + o * B
            fade = jnp.exp(rate * jnp.maximum(distance, 0).astype(F32))
            r.dec[o, h] = jnp.where(distance >= 0, fade, 0.0)

    for t in range(D // 128):
        q = slice(t * 128, t * 128 + 128)
        r.nint[q, :] = jnp.transpose(r.nin[:, q])
    load_cos.wait()
    load_sin.wait()
    load_x_own.wait()

    def turn_into(pre_ref, rot_ref, k):
        def tile(t):
            q = rows_of(t, TT)
            pre = dot_nn(r.nin[q, :], r.mixw[k])
            pre_ref[q, :] = pre
            act = pre * jax.nn.sigmoid(pre)
            c, s = r.cosv[q, :], r.sinv[q, :]
            for h in range(H):
                a = act[:, h * HEAD:(h + 1) * HEAD]
                rot_ref[q, 2 * h * HEAD:(2 * h + 1) * HEAD] = (a * c).astype(BF)
                rot_ref[q, (2 * h + 1) * HEAD:(2 * h + 2) * HEAD] = (a * s).astype(BF)

        each(T // TT, tile)

    def project_into(ref, k):
        def tile(t):
            q = rows_of(t, TT)
            ref[q, :] = dot_nn(r.nin[q, :], r.mixw[k]).astype(ref.dtype)

        each(T // TT, tile)

    gather_forward(0)
    gather_send(4)
    gather_forward(1)
    gather_send(5)
    gather_wait(0)
    turn_into(r.qpre, r.qrot, 0)
    gather_forward(2)
    gather_send(6)
    gather_wait(1)
    turn_into(r.kpre, r.krot, 1)
    gather_forward(3)
    gather_send(7)
    gather_wait(2)
    project_into(r.val, 2)
    gather_forward(4)
    gather_send(8)
    gather_wait(3)
    project_into(r.gpre, 3)

    def wo_block(owner):
        return r.wo.at[:, pl.ds(pl.multiple_of(owner * C, C), C)]

    gather_wait(4)
    share_send(0, wo_block)

    NB = T // B
    REACH = LONGEST // B

    def keys_of(qb):
        return slice(max(0, qb - REACH) * B, (qb + 1) * B)

    def weights_of(qb, h):
        key = keys_of(qb)
        width = key.stop - key.start
        fades = [r.dec[min(o, 1), h] for o in range(width // B - 1, -1, -1)]
        for o in range(2, width // B):
            fades[width // B - 1 - o] *= jnp.exp(rate_of(h) * ((o - 1) * B))
        seen = jnp.broadcast_to(r.segk[0:1, key], (B, width))
        same = widen(r.segq[qb * B:(qb + 1) * B, :], width) == seen
        return jnp.where(same, jnp.concatenate(fades, axis=1), 0.0)

    def u_block(qb):
        return lambda owner: r.ufull.at[qb * B:(qb + 1) * B, pl.ds(pl.multiple_of(owner * C, C), C)]

    def attend(qb):
        q = slice(qb * B, (qb + 1) * B)
        squares = jnp.zeros((B, 1), F32)
        for h in range(H):
            rot = slice(2 * h * HEAD, 2 * (h + 1) * HEAD)
            chan = slice(h * HEAD, (h + 1) * HEAD)
            key = keys_of(qb)
            scores = dot_nt(r.qrot[q, rot], r.krot[key, rot]) * weights_of(qb, h)
            total = dot_nn(scores.astype(BF), r.val[key, chan])
            r.mixed[q, chan] = total
            squares = squares + jnp.sum(total * total, axis=-1, keepdims=True)
            r.ufull[q, pl.ds(pl.multiple_of(j * C + h * HEAD, HEAD), HEAD)] = (
                total * r.gpre[q, chan]
            ).astype(BF)
        r.ss[j, :, q] = jnp.transpose(jnp.broadcast_to(squares, (B, 128)))[0:8, :]

    def ss_block(owner):
        return r.ss.at[owner]

    for qb in range(NB):
        attend(qb)
        share_send(1 + qb, u_block(qb))
        if qb == NB - 1:
            share_send(1 + NB, ss_block)
        if qb == 0:
            gather_forward(5)
            gather_send(9)
        if qb == 1:
            share_forward(0, wo_block)
        if qb == 2:
            gather_forward(6)
            gather_send(10)
        if qb > 0:
            share_forward(qb, u_block(qb - 1))
    share_forward(NB, u_block(NB - 1))
    share_forward(1 + NB, ss_block)
    gather_forward(7)
    gather_forward(8)
    share_wait(0, wo_block)
    for qb in range(NB):
        share_wait(1 + qb, u_block(qb))
    share_wait(1 + NB, ss_block)
    early = list(pending)

    total_ss = r.ss[0]
    for owner in range(1, mp):
        total_ss = total_ss + r.ss[owner]
    inverse = lax.rsqrt(total_ss * (1.0 / D) + EPSILON)
    for t in range(T // 128):
        q = slice(t * 128, t * 128 + 128)
        r.rcol[q, :] = jnp.transpose(jnp.broadcast_to(inverse[0:1, q], (128, 128)))

    def hidden_tile(t):
        q = rows_of(t, TB)
        out = widen(r.rcol[q, :], D) * dot_nn(r.ufull[q, :], r.wo[...])
        hidden = r.xv[q, :].astype(F32) + out
        scale = lax.rsqrt(jnp.mean(hidden * hidden, axis=-1, keepdims=True) + EPSILON)
        r.nmid[q, :] = (hidden * scale).astype(BF)

        @pl.when(t == j)
        def _():
            r.hown[...] = hidden

    each(T // TB, hidden_tile)
    gather_wait(5)
    gather_wait(6)

    def gate_tile(t):
        q = rows_of(t, TT)
        r.gact[q, 0:F] = to_units(r.nmid[q, :], 1)

    each(T // TT, gate_tile)
    gather_forward(9)
    gather_wait(7)
    gather_wait(8)

    def up_tile(t):
        q = rows_of(t, TT)
        upper = to_units(r.nmid[q, :], 2)
        r.uact[q, :] = upper.astype(BF)
        r.prod[q, :] = (r.gact[q, 0:F] * upper).astype(BF)

    each(T // TT, up_tile)
    put_ff_grad(0, r.prod, r.up)
    gather_forward(10)
    scatter_first(5, 6)
    gather_wait(9)
    gather_wait(10)

    def mid_block(x, c):
        q = rows_of(x * 2 + c, TB)
        g = to_units(r.up[q, :], 0)
        grad_gate, grad_up = (g * r.uact[q, :].astype(F32)).astype(BF), (g * r.gact[q, 0:F]).astype(BF)
        r.ggate[q, :] = grad_gate
        r.gup[q, :] = grad_up
        r.part[x, c] = (to_model(grad_gate, 1) + to_model(grad_up, 2)).astype(BF)

    used = sum_begin(0, 0, mid_block)
    scatter_second(5)
    put_ff_grad(1, r.ggate, r.nmid)
    scatter_first(7, 8)
    scatter_second(6)

    def back_tile(t):
        q = rows_of(t, 128)
        here = rows_of(j * (TB // 128) + t, 128)
        grad = sum_tile(0, q)
        hidden = r.hown[q, :]
        scale = lax.rsqrt(jnp.mean(hidden * hidden, axis=-1, keepdims=True) + EPSILON)
        normed = hidden * scale
        inner = jnp.mean(grad * normed, axis=-1, keepdims=True)
        out = r.up[here, :].astype(F32) + scale * (grad - normed * inner)
        r.ghid[q, :] = out
        low = out.astype(BF)
        r.hlow[here, :] = low
        mixer_out = hidden - r.xown[q, :].astype(F32)
        product = jnp.sum(low.astype(F32) * mixer_out, axis=-1, keepdims=True) * (1.0 / D)
        r.inn[j, :, q] = jnp.transpose(jnp.broadcast_to(product, (128, 128)))[0:8, :]

    def token_block(ref):
        return lambda owner: ref.at[rows_of(owner, TB)]

    BO, IN, GM, HL, IG = 2 + NB, 3 + NB, 4 + NB, 9 + NB, 9 + NB + NT

    def inn_block(owner):
        return r.inn.at[owner]

    def half_block(ref, t):
        return lambda owner: ref.at[rows_of(owner * NT + t, 128)]

    for t in range(NT):
        sum_arrived(0, 0, t)
        back_tile(t)
        share_send(HL + t, half_block(r.hlow, t))
    share_send(IN, inn_block)
    put_ff_grad(2, r.gup, r.nmid)
    scatter_first(9, 10)
    scatter_second(7)
    for t in range(NT):
        share_forward(HL + t, half_block(r.hlow, t))
    share_forward(IN, inn_block)
    for copy in used:
        settle(copy)

    def expand_block(x, c):
        q = rows_of(x * 2 + c, TB)
        r.part[x, c] = to_model(r.prod[q, :], 0).astype(BF)

    scatter_second(8)
    used = sum_begin(1, 1, expand_block)
    for t in range(NT):
        share_wait(HL + t, half_block(r.hlow, t))
    share_wait(IN, inn_block)
    for owner in range(mp):
        for t in range(TB // 128):
            row = r.inn[owner, 0:1, t * 128:(t + 1) * 128]
            q = slice(owner * TB + t * 128, owner * TB + (t + 1) * 128)
            r.icol[q, :] = jnp.transpose(jnp.broadcast_to(row, (128, 128)))

    wo_rows = rows_of(j, C)

    def gated_tile(t):
        q = rows_of(t, TT)
        low = r.hlow[q, :]
        grad = dot_nt(low, r.wo[wo_rows, :])
        inner = widen(r.icol[q, :], C)
        inverse = widen(r.rcol[q, :], C)
        normed = r.mixed[q, :] * inverse
        r.gproj[3][q, :] = (grad * normed).astype(BF)
        r.gmix[q, :] = (inverse * (grad * r.gpre[q, :] - normed * inner)).astype(BF)
        r.rh[q, :] = (inverse * r.hlow[q, jcols].astype(F32)).astype(BF)

    each(T // TT, gated_tile)
    put_grad(4, r.ufull, r.rh)
    scatter_first(4)

    def swish_back(pre, grad):
        gate = jax.nn.sigmoid(pre)
        return grad * (gate * (1.0 + pre * (1.0 - gate)))

    def attend_back(qb):
        q, key = slice(qb * B, (qb + 1) * B), keys_of(qb)
        for h in range(H):
            rot = slice(2 * h * HEAD, 2 * (h + 1) * HEAD)
            chan = slice(h * HEAD, (h + 1) * HEAD)
            weights = weights_of(qb, h)
            scores = (dot_nt(r.qrot[q, rot], r.krot[key, rot]) * weights).astype(BF)
            back = (dot_nt(r.gmix[q, chan], r.val[key, chan]) * weights).astype(BF)
            dq = dot_nn(back, r.krot[key, rot])
            turned = dq[:, :HEAD] * r.cosv[q, :] + dq[:, HEAD:] * r.sinv[q, :]
            r.gproj[0][q, chan] = swish_back(r.qpre[q, chan], turned).astype(BF)
            dk = dot_tn(back, r.qrot[q, rot])
            dv = dot_tn(scores, r.gmix[q, chan])
            for kb in range(key.start // B, qb + 1):
                at = slice(kb * B - key.start, (kb + 1) * B - key.start)
                rows = slice(kb * B, (kb + 1) * B)
                dkb, dvb = dk[at], dv[at]
                if qb < min(kb + REACH, NB - 1):
                    dkb, dvb = dkb + r.dk[rows, rot], dvb + r.dv[rows, chan]
                if kb < qb:
                    r.dk[rows, rot], r.dv[rows, chan] = dkb, dvb
                else:
                    turned = dkb[:, :HEAD] * r.cosv[q, :] + dkb[:, HEAD:] * r.sinv[q, :]
                    r.gproj[1][q, chan] = swish_back(r.kpre[q, chan], turned).astype(BF)
                    r.gproj[2][q, chan] = dvb.astype(BF)

    def output_tile(t):
        q = rows_of(t, 128)
        r.bov[rows_of(j * NT + t, 128), :] = (r.hown[q, :] + sum_tile(1, q)).astype(BF)

    def late_core(x):
        return pltpu.make_async_remote_copy(
            src_ref=r.part.at[x, 1 - ci], dst_ref=r.recc.at[0, x], send_sem=r.acs.at[2, x], recv_sem=r.acr.at[2, x],
            device_id={"mp": xi * 2 + 1 - ci}, device_id_type=MESH,
        )

    def late_chip(x, d, t):
        q = slice(t * 128, (t + 1) * 128)
        return pltpu.make_async_remote_copy(
            src_ref=r.part.at[x, ci, q], dst_ref=r.recx.at[0, d - 1, q], send_sem=r.axs.at[2, d - 1, t],
            recv_sem=r.axr.at[2, d - 1, t], device_id={"mp": x * 2 + ci}, device_id_type=MESH,
        )

    def blocks_in(qb):
        return [divmod(at, 2) for at in range(qb * B // TB, (qb + 1) * B // TB)]

    def late_begin(x, c):
        q = slice((x * 2 + c) * TB, (x * 2 + c + 1) * TB)
        out = dot_nt(r.gproj[0][q, :], r.mixw[0])
        for k in range(1, 4):
            out = out + dot_nt(r.gproj[k][q, :], r.mixw[k])
        r.part[x, c] = out.astype(BF)

        @pl.when(ci != c)
        def _():
            late_core(x).start()

    def late_pass(x, c):
        @pl.when(ci == c)
        def _():
            arrived(r.recc.at[0, x], r.acr.at[2, x])

        @pl.when((ci == c) & (xi != x))
        def _():
            for t in range(NT):
                q = slice(t * 128, (t + 1) * 128)
                r.part[x, c, q] = (r.part[x, c, q].astype(F32) + r.recc[0, x, q].astype(F32)).astype(BF)
                late_chip(x, lax.rem(x - xi + X, X), t).start()

    put_grad(3, r.nint, r.gproj[3], turned=True)
    scatter_first(3)
    scatter_second(9)
    for qb in range(NB - 1, -1, -1):
        attend_back(qb)
        if qb == NB - 1:
            for t in range(NT):
                sum_arrived(1, 1, t)
            each(TB // 128, output_tile)
            share_send(BO, token_block(r.bov))
            for copy in used + early:
                settle(copy)
        for x, c in blocks_in(qb):
            late_begin(x, c)
        if qb < NB - 1:
            for x, c in blocks_in(qb + 1):
                late_pass(x, c)
        if qb == NB - 1:
            scatter_second(10)
            finish_ff(5, 6)
        if qb == max(NB - 2, 0):
            scatter_second(4)
            share_forward(BO, token_block(r.bov))
            finish_ff(7)
        if qb == max(NB - 3, 0):
            scatter_second(3)
            finish_ff(8)
    for x, c in blocks_in(0):
        late_pass(x, c)
    pending.extend(late_core(x) for x in range(X))
    pending.extend(late_chip(lax.rem(xi + d, X), d, t) for d in range(1, X) for t in range(NT))
    for k in (2, 0, 1):
        put_grad(k, r.nint, r.gproj[k], turned=True)
        scatter_first(k)
    finish_ff(9, 10)

    def input_tile(t):
        q = rows_of(t, 128)
        grad = sum_tile(0, q)
        v = r.xown[q, :].astype(F32)
        scale = lax.rsqrt(jnp.mean(v * v, axis=-1, keepdims=True) + EPSILON)
        normed = v * scale
        inner = jnp.mean(grad * normed, axis=-1, keepdims=True)
        r.igv[rows_of(j * NT + t, 128), :] = (r.ghid[q, :] + scale * (grad - normed * inner)).astype(BF)

    for t in range(NT):
        for d in range(1, X):
            arrived(r.recx.at[0, d - 1, t * 128:(t + 1) * 128], r.axr.at[2, d - 1, t])
        input_tile(t)
        share_send(IG + t, half_block(r.igv, t))
    for k in (2, 0, 1):
        scatter_second(k)
    share_wait(BO, token_block(r.bov))
    stores = [load(r.bov, r.bo, 0)]

    def grad_block(k):
        return lambda owner: r.gmv.at[k * S:(k + 1) * S, pl.ds(pl.multiple_of(owner * C, C), C)]

    for k in (4, 3, 2, 0, 1):
        total = scatter_total(k).astype(BF)
        r.gmv[k * S:(k + 1) * S, jcols] = total
        r.sqs[...] += squares_of(total.astype(F32))
        share_send(GM + k, grad_block(k))

    r.s1[j] = r.sqs[...]
    for d in range(1, mp):
        go(r.s1.at[j], r.s1.at[j], r.q1s.at[d], r.q1r.at[d], mp=lax.rem(j + d, mp))
    for t in range(NT):
        share_forward(IG + t, half_block(r.igv, t))
    for d in range(1, mp):
        arrived(r.s1.at[lax.rem(j - d + mp, mp)], r.q1r.at[d])
    total = r.s1[0]
    for owner in range(1, mp):
        total = total + r.s1[owner]
    r.s2[i] = total
    for d in range(1, n):
        go(r.s2.at[i], r.s2.at[i], r.q2s.at[d], r.q2r.at[d], dp=lax.rem(i + d, n))
    for k in (4, 3, 2, 0, 1):
        share_forward(GM + k, grad_block(k))
    for d in range(1, n):
        arrived(r.s2.at[lax.rem(i - d + n, n)], r.q2r.at[d])
    total = r.s2[0]
    for owner in range(1, n):
        total = total + r.s2[owner]
    r.sqo[...] = total

    for t in range(NT):
        share_wait(IG + t, half_block(r.igv, t))
    stores.append(load(r.igv, r.ig, 1))
    for k in (4, 3, 2, 0, 1):
        share_wait(GM + k, grad_block(k))
        stores.append(load(r.gmv.at[k * S:(k + 1) * S], r.gmo.at[k], 2 + k))
    for copy in stores:
        copy.wait()
    for copy in pending:
        copy.wait_send()


def fused(p, *operands):
    scratch = scratch_of(p)
    names = IN_NAMES + OUT_NAMES + tuple(scratch)
    anywhere = pl.BlockSpec(memory_space=pl.ANY)
    vmem = pl.BlockSpec(memory_space=pltpu.VMEM)
    smem = pl.BlockSpec(memory_space=pltpu.SMEM)
    return pl.pallas_call(
        partial(body, p, names),
        out_shape=(
            jax.ShapeDtypeStruct((p.T, p.D), BF),
            jax.ShapeDtypeStruct((p.T, p.D), BF),
            jax.ShapeDtypeStruct((5, p.S, p.D), BF),
            jax.ShapeDtypeStruct((2, p.F, p.S) if p.FD else (2, p.S, p.F), F32),
            jax.ShapeDtypeStruct((p.F, p.S) if p.FD else (p.S, p.F), F32),
            jax.ShapeDtypeStruct((8, 128), F32),
        ),
        in_specs=[anywhere, anywhere, vmem, smem] + [anywhere] * 5,
        out_specs=(anywhere, anywhere, anywhere, vmem, vmem, vmem),
        scratch_shapes=list(scratch.values()),
        compiler_params=pltpu.CompilerParams(
            collective_id=0, has_side_effects=True, vmem_limit_bytes=VMEM_LIMIT
        ),
    )(*operands)


VMEM_LIMIT = 64 * 2**20 - 2**18


def renew(weight, momentum, shadow, grad, clip_factor):
    clipped = grad * clip_factor
    velocity = MOMENTUM * momentum + clipped
    updated = weight - LEARN_RATE * (clipped + MOMENTUM * velocity)
    average = SHADOW_DECAY * shadow + (1.0 - SHADOW_DECAY) * updated
    return (velocity, average, updated)


def update_body(cuts, *refs):
    kinds, pieces = len(cuts), sum(len(c) for c in cuts)
    sq, carried = refs[0], refs[1:3]
    ins = [refs[3 + 4 * w:7 + 4 * w] for w in range(kinds)]
    refs = refs[3 + 4 * kinds:]
    norm_out, carried_out = refs[0], refs[1:3]
    outs = [refs[3 + 3 * w:6 + 3 * w] for w in range(kinds)]
    refs = refs[3 + 3 * kinds:]
    held = [refs[4 * w:4 * w + 4] for w in range(kinds)]
    made = [refs[4 * kinds + 3 * w:4 * kinds + 3 * w + 3] for w in range(kinds)]
    bounce, (in_sem, out_sem, carry_sem) = refs[7 * kinds:7 * kinds + 2], refs[7 * kinds + 2:]
    loads, order = {}, [(w, c) for w in range(kinds) for c in range(len(cuts[w]))]
    for at, (w, c) in enumerate(order):
        for a in range(4):
            cut = cuts[w][c]
            loads[at, a] = pltpu.make_async_copy(ins[w][a].at[cut], held[w][a].at[cut], in_sem.at[at, a])
            loads[at, a].start()
    carry = [pltpu.make_async_copy(carried[a], bounce[a], carry_sem.at[a]) for a in range(2)]
    for copy in carry:
        copy.start()
    copies = []
    norm = jnp.sqrt(jnp.broadcast_to(jnp.sum(sq[...]), (8, 128)))
    norm_out[...] = norm
    clip_factor = 1.0 / jnp.maximum(jnp.max(norm), 1.0)
    for at, (w, c) in enumerate(order):
        cut = cuts[w][c]
        for a in range(4):
            loads[at, a].wait()
        new = renew(*[held[w][a][cut] for a in range(3)], held[w][3][cut].astype(F32), clip_factor)
        for a in range(3):
            made[w][a][cut] = new[a]
            copy = pltpu.make_async_copy(made[w][a].at[cut], outs[w][a].at[cut], out_sem.at[at, a])
            copy.start()
            copies.append(copy)
    for a in range(2):
        carry[a].wait()
        copy = pltpu.make_async_copy(bounce[a], carried_out[a], carry_sem.at[2 + a])
        copy.start()
        copies.append(copy)
    for copy in copies:
        copy.wait()


def update(sq, carried, weights):
    cuts = [[c for c in range(g[0].shape[0])] if g[0].ndim == 3 else [slice(None)] for g in weights]
    pieces = sum(len(c) for c in cuts)
    anywhere = pl.BlockSpec(memory_space=pl.ANY)
    vmem = pl.BlockSpec(memory_space=pltpu.VMEM)
    flat_in = [a for group in weights for a in group]
    flat_out = [a for group in weights for a in group[:3]]
    dma = pltpu.SemaphoreType.DMA
    size = sum(a.size * a.dtype.itemsize for a in flat_in + flat_out + 2 * list(carried))
    return pl.pallas_call(
        partial(update_body, cuts),
        out_shape=[jax.ShapeDtypeStruct(a.shape, a.dtype) for a in [sq, *carried, *flat_out]],
        in_specs=[vmem] + [anywhere] * (2 + len(flat_in)),
        out_specs=[vmem] + [anywhere] * (2 + len(flat_out)),
        scratch_shapes=[pltpu.VMEM(a.shape, a.dtype) for a in flat_in + flat_out + list(carried)]
        + [dma((pieces, 4)), dma((pieces, 3)), dma((4,))],
        cost_estimate=pl.CostEstimate(flops=size, bytes_accessed=size, transcendentals=0),
        compiler_params=pltpu.CompilerParams(vmem_limit_bytes=VMEM_LIMIT),
    )(sq, *carried, *flat_in)


def turn_tables(tokens):
    theta = np.float32(10000.0) ** (-np.arange(HEAD, dtype=np.float32) / np.float32(HEAD))
    angle = np.arange(tokens, dtype=np.float32)[:, None] * theta.astype(np.float32)[None, :]
    angle = angle.astype(np.float64)
    return np.cos(angle).astype(np.float32), np.sin(angle).astype(np.float32)


def per_device(mesh, block_input, segment_ids, live_length, output_grad, mixer_weight, mixer_momentum, mixer_shadow,
               expand_weight, expand_momentum, expand_shadow, shrink_weight, shrink_momentum, shrink_shadow):
    rows, length, width = block_input.shape
    p = plan_of(mesh, length, width, shrink_weight.shape[0])
    turn = (lambda v: jnp.swapaxes(v, -1, -2)) if p.FD else (lambda v: v)
    if p.FD:
        shards = (turn(expand_weight), shrink_weight)
    else:
        shards = (jnp.concatenate([shrink_weight.T[None], expand_weight], axis=0).astype(BF), shrink_weight)
    cos, sin = turn_tables(length)
    out, grad_in, gm, ge, gs, sq = fused(
        p, block_input[0], output_grad[0], segment_ids, live_length, jnp.asarray(cos), jnp.asarray(sin), mixer_weight, *shards
    )
    new = update(sq, (out, grad_in), (
        (mixer_weight, mixer_momentum, mixer_shadow, gm),
        (turn(expand_weight), turn(expand_momentum), turn(expand_shadow), ge),
        (shrink_weight, shrink_momentum, shrink_shadow, gs if p.FD else gs.T),
    ))
    norm, out, grad_in = new[:3]
    return (out[None], grad_in[None], norm[0, 0], *new[3:6], *(turn(v) for v in new[6:9]), *new[9:12])


def solution(mesh):
    row, mixer, expand, shrink = P("dp", None, None), P(None, "dp", None), P(None, "dp", "mp"), P("mp", "dp")
    return jax.shard_map(
        partial(per_device, mesh),
        mesh=mesh,
        in_specs=(row, P("dp", None), P("dp"), row) + (mixer,) * 3 + (expand,) * 3 + (shrink,) * 3,
        out_specs=(row, row, P()) + (mixer,) * 3 + (expand,) * 3 + (shrink,) * 3,
        check_vma=False,
    )
```

```python
from functools import partial
from types import SimpleNamespace

import jax
import jax.numpy as jnp
import numpy as np
from jax import lax
from jax.experimental import pallas as pl
from jax.experimental.pallas import tpu as pltpu
from jax.sharding import PartitionSpec as P

HEAD = 128
EPSILON = 1e-06
LEARN_RATE = 32.0
MOMENTUM = 0.5
SHADOW_DECAY = 0.5
LAYER_PLACE = 12.0 / 24.0
LONGEST = 512
FF_ORDER = (1, 2, 0)
Y_FIRST = (4, 6)
MESH = pl.DeviceIdType.MESH
BF = jnp.bfloat16
F32 = jnp.float32


def dot_nn(a, b):
    return lax.dot_general(a, b, (((1,), (0,)), ((), ())), preferred_element_type=F32)


def dot_nt(a, b):
    return lax.dot_general(a, b, (((1,), (1,)), ((), ())), preferred_element_type=F32)


def dot_tn(a, b):
    return lax.dot_general(a, b, (((0,), (0,)), ((), ())), preferred_element_type=F32)


def rows_of(index, size):
    return pl.ds(pl.multiple_of(index * size, size), size)


def each(count, body):
    def step(t, carry):
        body(t)
        return carry

    lax.fori_loop(0, count, step, 0)


def widen(column, width):
    return jnp.concatenate([column] * (width // 128), axis=1)


def plan_of(mesh, tokens, width, inner):
    n, mp = mesh.shape["dp"], mesh.shape["mp"]
    lo, core = 2, 2
    return SimpleNamespace(
        n=n, mp=mp, LO=lo, HI=n // lo, X=mp // core, T=tokens, D=width, C=width // mp, F=inner,
        S=width // n, H=width // mp // HEAD, TB=tokens // mp, B=min(256, tokens),
        NT=tokens // mp // 128, FD=(width // n) % 128 == 0,
    )


def scratch_of(p):
    T, D, C, F, S, HI, LO, X, TB, B = p.T, p.D, p.C, p.F, p.S, p.HI, p.LO, p.X, p.TB, p.B
    dma = pltpu.SemaphoreType.DMA
    v = pltpu.VMEM
    return dict(
        mixw=v((4, D, C), BF), wo=v((D, D), BF), ffw=v((3, F, D) if p.FD else (3, D, F), BF),
        xown=v((TB, D), BF), nin=v((T, D), BF), nint=v((D, T), BF), up=v((T, D), BF),
        cosv=v((T, HEAD), F32), sinv=v((T, HEAD), F32),
        segq=v((T, 128), F32), segk=v((8, T), F32), dec=v((2, p.H, B, B), F32),
        qpre=v((T, C), F32), kpre=v((T, C), F32), gpre=v((T, C), F32), val=v((T, C), BF),
        qrot=v((T, 2 * C), BF), krot=v((T, 2 * C), BF), mixed=v((T, C), F32),
        ufull=v((T, D), BF), ss=v((p.mp, 8, T), F32), rcol=v((T, 128), F32),
        inn=v((p.mp, 8, TB), F32), hown=v((TB, D), F32),
        gact=v((T, max(F, 2 * C + HEAD)), F32), uact=v((T, F), BF), prod=v((T, F), BF), ggate=v((T, F), BF), gup=v((T, F), BF),
        part=v((X, 2, TB, D), BF), recc=v((2, X, TB, D), BF), recx=v((2, X - 1, TB, D), BF),
        ghid=v((TB, D), F32), hlow=v((T, D), BF),
        gm=v((5, HI, LO, S, C), BF), rym=v((5, HI, S, C), BF), rzm=v((5, HI - 1, S, C), BF),
        gf=v((3, LO, F, HI * S) if p.FD else (3, HI, LO, S, F), BF),
        ryf=v((3, F, HI * S) if p.FD else (3, HI, S, F), BF),
        rzf=v((3, HI - 1, F, S) if p.FD else (3, HI - 1, S, F), BF),
        sqs=v((8, 128), F32), s1=v((p.mp, 8, 128), F32), s2=v((p.n, 8, 128), F32),
        loc=dma((10,)),
        zs=dma((11, HI - 1)), zr=dma((11, HI - 1)), us=dma((len(Y_FIRST), HI - 1)), ur=dma((len(Y_FIRST), HI - 1)),
        zp=dma((11,)), yp=dma((len(Y_FIRST),)), ys=dma((11, HI)), yr=dma((11, HI)),
        xs=dma((20, X - 1)), xr=dma((20, X - 1)), cs=dma((20, X)), cr=dma((20, X)),
        acs=dma((3, X)), acr=dma((3, X)), axs=dma((3, X - 1, p.NT)), axr=dma((3, X - 1, p.NT)),
        bys=dma((11,)), byr=dma((11,)), bzs=dma((11, HI - 1)), bzr=dma((11, HI - 1)),
        q1s=dma((p.mp,)), q1r=dma((p.mp,)), q2s=dma((p.n,)), q2r=dma((p.n,)),
    )


IN_NAMES = ("x", "og", "seg", "live", "cos", "sin", "mixsh", "exsh", "shsh")
OUT_NAMES = ("bo", "ig", "gmo", "geo", "gso", "sqo")


def body(p, names, *refs):
    r = SimpleNamespace(**dict(zip(names, refs)))
    n, mp, LO, HI, X, T, D, C, F, S, H, TB, B = (
        p.n, p.mp, p.LO, p.HI, p.X, p.T, p.D, p.C, p.F, p.S, p.H, p.TB, p.B,
    )
    NT, TT = p.NT, min(512, p.T)
    i, j = lax.axis_index("dp"), lax.axis_index("mp")
    zi, yi = i // LO, lax.rem(i, LO)
    xi, ci = j // 2, lax.rem(j, 2)
    jcols = pl.ds(pl.multiple_of(j * C, C), C)
    pending = []
    r.xv, r.nmid = r.hlow, r.nin
    r.bov, r.igv, r.gmv = r.up, r.ufull, r.wo
    r.dk, r.icol, r.dv = r.gact.at[:, 0:2 * C], r.gact.at[:, 2 * C:2 * C + HEAD], r.mixed
    r.gproj = [r.ggate.at[:, 0:C], r.ggate.at[:, C:2 * C], r.gup.at[:, 0:C], r.gup.at[:, C:2 * C]]
    r.gmix, r.rh = r.prod.at[:, 0:C], r.prod.at[:, C:2 * C]

    def go(src, dst, ssem, rsem, when=None, **device):
        copy = pltpu.make_async_remote_copy(
            src_ref=src, dst_ref=dst, send_sem=ssem, recv_sem=rsem,
            device_id=device, device_id_type=MESH,
        )
        guarded(when, copy.start)
        pending.append((copy, when))
        return copy

    def guarded(when, act):
        if when is None:
            act()
        else:
            pl.when(when)(lambda: act())

    def arrived(dst, sem):
        pltpu.make_async_copy(dst, dst, sem).wait()

    def settle(copy):
        for other, when in pending:
            if other is copy:
                guarded(when, copy.wait_send)
        pending[:] = [entry for entry in pending if entry[0] is not copy]

    def load(src, dst, sem):
        copy = pltpu.make_async_copy(src, dst, r.loc.at[sem])
        copy.start()
        return copy

    own_mix = [load(r.mixsh.at[k, :, jcols], r.qpre.at[k * S:(k + 1) * S], k) for k in range(5)]
    if p.FD:
        stage = [r.gact.at[0:F, m * S:(m + 1) * S] for m in range(3)]
        own_ff = [load(r.shsh if m == 0 else r.exsh.at[m - 1], stage[m], 5 + m) for m in range(3)]
    else:
        own_ff = [load(r.exsh.at[m], r.ffw.at[m, rows_of(i, S)], 5 + m) for m in range(3)]
    load_x = load(r.x, r.xv, 8)
    load_og = load(r.og, r.up, 9)

    def enter():
        barrier = pltpu.get_barrier_semaphore()
        for d in range(1, n):
            pl.semaphore_signal(barrier, inc=1, device_id={"dp": lax.rem(i + d, n)}, device_id_type=MESH)
        for d in range(1, mp):
            pl.semaphore_signal(barrier, inc=1, device_id={"mp": lax.rem(j + d, mp)}, device_id_type=MESH)
        pl.semaphore_wait(barrier, n - 1 + mp - 1)

    def slot(k, device):
        rows = rows_of(device, S)
        if k == 4:
            return r.wo.at[rows, jcols]
        if k < 4:
            return r.mixw.at[k, rows]
        m, half = FF_ORDER[(k - 5) // 2], (k - 5) % 2
        if p.FD:
            return r.ffw.at[m, half * F // 2:(half + 1) * F // 2, rows]
        return r.ffw.at[m, pl.ds(pl.multiple_of(device * S + half * S // 2, S // 2), S // 2)]

    def gather_ready(k):
        if k < 5:
            own_mix[k].wait()
            slot(k, i)[...] = r.qpre[k * S:(k + 1) * S, :].astype(BF)
        else:
            m, half = FF_ORDER[(k - 5) // 2], (k - 5) % 2
            if half == 0:
                own_ff[m].wait()
            if p.FD:
                slot(k, i)[...] = stage[m][half * F // 2:(half + 1) * F // 2, :].astype(BF)

    relays = HI == 4
    next_to_end = (zi == 1) | (zi == 2)

    def along_z(block, ssem, rsem):
        for d in range(1, HI):
            to = lax.rem(zi + d, HI)
            near = (jnp.abs(to - zi) < 3) if relays else None
            go(block, block, ssem.at[d - 1], rsem.at[d - 1], when=near, dp=to * LO + yi)

    def hand_on(block, ssem, rsem):
        if relays:
            end = jnp.where(zi == 2, 3, 0)
            go(block, block, ssem, rsem.at[jnp.where(zi == 2, 2, 0)], when=next_to_end, dp=end * LO + yi)

    def from_z_source(k, d, y):
        return slot(k, lax.rem(zi - d + HI, HI) * LO + y)

    WAYS = [2, 1, *range(3, HI)]

    def gather_send(k):
        src = slot(k, i)
        along_z(src, r.zs.at[k], r.zr.at[k])
        go(src, src, r.ys.at[k, 0], r.yr.at[k, 0], dp=zi * LO + 1 - yi)

    def gather_forward(k):
        if k - 1 in Y_FIRST:
            b = Y_FIRST.index(k - 1)
            block = from_z_source(k - 1, 2, 1 - yi)
            arrived(block, r.ur.at[b, 1])
            hand_on(block, r.yp.at[b], r.ur.at[b])
        if k in Y_FIRST:
            b = Y_FIRST.index(k)
            peers = slot(k, zi * LO + 1 - yi)
            arrived(peers, r.yr.at[k, 0])
            along_z(peers, r.us.at[b], r.ur.at[b])
        for d in WAYS:
            block = from_z_source(k, d, yi)
            arrived(block, r.zr.at[k, d - 1])
            if d == 2:
                hand_on(block, r.zp.at[k], r.zr.at[k])
            if k not in Y_FIRST:
                go(block, block, r.ys.at[k, d], r.yr.at[k, d], dp=zi * LO + 1 - yi)

    def gather_wait(k):
        for d in range(HI):
            if k not in Y_FIRST:
                arrived(from_z_source(k, d, 1 - yi), r.yr.at[k, d])
            elif d in (1, 3) or d > 3:
                arrived(from_z_source(k, d, 1 - yi), r.ur.at[Y_FIRST.index(k), d - 1])

    def share_send(s, block, src=None):
        own = block(j)
        src = own if src is None else src
        for d in range(1, X):
            go(src, own, r.xs.at[s, d - 1], r.xr.at[s, d - 1], mp=lax.rem(xi + d, X) * 2 + ci)
        go(src, own, r.cs.at[s, 0], r.cr.at[s, 0], mp=xi * 2 + 1 - ci)

    def share_forward(s, block):
        for d in range(1, X):
            part = block(lax.rem(xi - d + X, X) * 2 + ci)
            arrived(part, r.xr.at[s, d - 1])
            go(part, part, r.cs.at[s, d], r.cr.at[s, d], mp=xi * 2 + 1 - ci)

    def share_wait(s, block):
        for d in range(X):
            arrived(block(lax.rem(xi - d + X, X) * 2 + 1 - ci), r.cr.at[s, d])

    def sum_begin(s, b, compute):
        sent = []
        for d in [*range(1, X), 0]:
            to = lax.rem(xi + d, X)
            compute(to, 1 - ci)
            sent.append(go(
                r.part.at[to, 1 - ci], r.recc.at[b, to], r.acs.at[s, d], r.acr.at[s, d], mp=xi * 2 + 1 - ci
            ))
        for d in range(1, X):
            to = lax.rem(xi + d, X)
            compute(to, ci)
            arrived(r.recc.at[b, to], r.acr.at[s, d])
            for t in range(NT):
                q = slice(t * 128, (t + 1) * 128)
                r.part[to, ci, q] = (
                    r.part[to, ci, q].astype(F32) + r.recc[b, to, q].astype(F32)
                ).astype(BF)
                sent.append(go(
                    r.part.at[to, ci, q], r.recx.at[b, d - 1, q], r.axs.at[s, d - 1, t], r.axr.at[s, d - 1, t],
                    mp=to * 2 + ci,
                ))
        compute(xi, ci)
        return sent

    def sum_arrived(s, b, t):
        if t == 0:
            arrived(r.recc.at[b, xi], r.acr.at[s, 0])
        for d in range(1, X):
            arrived(r.recx.at[b, d - 1, t * 128:(t + 1) * 128], r.axr.at[s, d - 1, t])

    def sum_tile(b, q):
        total = r.part[xi, ci, q].astype(F32) + r.recc[b, xi, q].astype(F32)
        for d in range(1, X):
            total = total + r.recx[b, d - 1, q].astype(F32)
        return total

    flat = p.FD

    def half_of(k):
        size = (F if flat else S) // 2
        return (k - 5) // 2, slice((k - 5) % 2 * size, ((k - 5) % 2 + 1) * size)

    def from_y(k):
        if k < 5:
            return r.rym.at[k]
        m, rows = half_of(k)
        return r.ryf.at[m, rows] if flat else r.ryf.at[m, :, rows]

    def from_y_block(k, z):
        ref = from_y(k)
        return ref.at[:, rows_of(z, S)] if flat and k >= 5 else ref.at[z]

    def from_z(k, d):
        if k < 5:
            return r.rzm.at[k, d - 1]
        m, rows = half_of(k)
        return r.rzf.at[m, d - 1, rows]

    def to_y(k):
        if k < 5:
            return r.gm.at[k, :, 1 - yi]
        m, rows = half_of(k)
        return r.gf.at[m, 1 - yi, rows] if flat else r.gf.at[m, :, 1 - yi, rows]

    def mine(k, z):
        if k < 5:
            return r.gm.at[k, z, yi]
        m, rows = half_of(k)
        return r.gf.at[m, yi, rows, rows_of(z, S)] if flat else r.gf.at[m, z, yi, rows]

    def scatter_first(*pieces):
        for k in pieces:
            go(to_y(k), from_y(k), r.bys.at[k], r.byr.at[k], dp=zi * LO + 1 - yi)

    def scatter_second(*pieces):
        for k in pieces:
            arrived(from_y(k), r.byr.at[k])
            for d in range(1, HI):
                to = lax.rem(zi + d, HI)
                block = mine(k, to)
                block[...] = (block[...].astype(F32) + from_y_block(k, to)[...].astype(F32)).astype(BF)
                go(block, from_z(k, d), r.bzs.at[k, d - 1], r.bzr.at[k, d - 1], dp=to * LO + yi)

    def scatter_total(k):
        for d in range(1, HI):
            arrived(from_z(k, d), r.bzr.at[k, d - 1])
        total = mine(k, zi)[...].astype(F32) + from_y_block(k, zi)[...].astype(F32)
        for d in range(1, HI):
            total = total + from_z(k, d)[...].astype(F32)
        return total

    def squares_of(total):
        squared = total * total
        if squared.shape[-1] % 128:
            corner = (lax.broadcasted_iota(jnp.int32, (8, 128), 0) + lax.broadcasted_iota(jnp.int32, (8, 128), 1)) == 0
            return jnp.where(corner, jnp.sum(squared), 0.0)
        folded = jnp.sum(squared.reshape(-1, 8, squared.shape[-1]), axis=0)
        return sum(folded[:, c:c + 128] for c in range(0, folded.shape[-1], 128))

    def finish_ff(*pieces):
        for k in pieces:
            m, rows = half_of(k)
            total = scatter_total(k)
            if m == 0:
                r.gso[rows] = total
            else:
                r.geo[m - 1, rows] = total
            r.sqs[...] += squares_of(total)

    def put_grad(k, lhs, rhs, turned=False):
        g = r.gm.at[k] if k < 5 else r.gf.at[k - 5]
        per = TT // (LO * S)

        def tile(t):
            if turned:
                out = dot_nn(lhs[rows_of(t, TT), :], rhs[...])
            else:
                out = dot_tn(lhs[:, rows_of(t, TT)], rhs[...])
            g[pl.ds(t * per, per)] = out.astype(BF).reshape(per, LO, S, out.shape[-1])

        each(D // TT, tile)

    def put_ff_grad(m, units, model):
        if not flat:
            return put_grad(5 + m, model, units)
        for f in range(0, F, 384):
            q = slice(f, min(f + 384, F))
            out = dot_tn(units[:, q], model[...]).astype(BF)
            for y in range(LO):
                for z in range(HI):
                    r.gf[m, y, q, z * S:(z + 1) * S] = out[:, (z * LO + y) * S:(z * LO + y + 1) * S]

    def to_units(a, m):
        return dot_nt(a, r.ffw[m]) if flat else dot_nn(a, r.ffw[m])

    def to_model(a, m):
        return dot_nn(a, r.ffw[m]) if flat else dot_nt(a, r.ffw[m])

    gather_ready(0)
    gather_ready(1)
    enter()
    gather_send(0)
    gather_send(1)
    gather_ready(2)
    gather_send(2)
    r.sqs[...] = jnp.zeros_like(r.sqs)

    length = r.live[0]
    load_x.wait()

    def norm_tile(t):
        q = rows_of(t, 128)
        v = r.xv[q, :].astype(F32)
        r.nin[q, :] = (v * lax.rsqrt(jnp.mean(v * v, axis=-1, keepdims=True) + EPSILON)).astype(BF)

    each(T // 128, norm_tile)
    for k in range(3, 11):
        gather_ready(k)
    load_x_own = load(r.x.at[rows_of(j, TB)], r.xown, 8)
    load_og.wait()
    load_cos = load(r.cos, r.cosv, 0)
    load_sin = load(r.sin, r.sinv, 1)

    def live_tile(t):
        q = rows_of(t, 128)
        place = lax.broadcasted_iota(jnp.int32, (128, D), 0) + t * 128
        r.up[q, :] = jnp.where(place < length, r.up[q, :].astype(F32), 0.0).astype(BF)

    each(T // 128, live_tile)

    place = lax.broadcasted_iota(jnp.int32, (1, T), 1)
    segment = r.seg[...].astype(F32)
    r.segk[...] = jnp.broadcast_to(jnp.where(place < length, segment, -2.0), (8, T))
    seg_q = jnp.where(place < length, segment, -1.0)
    for t in range(T // 128):
        q = slice(t * 128, t * 128 + 128)
        r.segq[q, :] = jnp.transpose(jnp.broadcast_to(seg_q[:, q], (128, 128)))

    down = lax.broadcasted_iota(jnp.int32, (B, B), 0)
    over = lax.broadcasted_iota(jnp.int32, (B, B), 1)
    heads = D // HEAD

    def rate_of(h):
        return -(8.0 * (j * H + h).astype(F32) / heads) * (1.0 - LAYER_PLACE)

    for h in range(H):
        rate = rate_of(h)
        for o in range(2):
            distance = down - over + o * B
            fade = jnp.exp(rate * jnp.maximum(distance, 0).astype(F32))
            r.dec[o, h] = jnp.where(distance >= 0, fade, 0.0)

    for t in range(D // 128):
        q = slice(t * 128, t * 128 + 128)
        r.nint[q, :] = jnp.transpose(r.nin[:, q])
    load_cos.wait()
    load_sin.wait()
    load_x_own.wait()

    def turn_into(pre_ref, rot_ref, k):
        def tile(t):
            q = rows_of(t, TT)
            pre = dot_nn(r.nin[q, :], r.mixw[k])
            pre_ref[q, :] = pre
            act = pre * jax.nn.sigmoid(pre)
            c, s = r.cosv[q, :], r.sinv[q, :]
            for h in range(H):
                a = act[:, h * HEAD:(h + 1) * HEAD]
                rot_ref[q, 2 * h * HEAD:(2 * h + 1) * HEAD] = (a * c).astype(BF)
                rot_ref[q, (2 * h + 1) * HEAD:(2 * h + 2) * HEAD] = (a * s).astype(BF)

        each(T // TT, tile)

    def project_into(ref, k):
        def tile(t):
            q = rows_of(t, TT)
            ref[q, :] = dot_nn(r.nin[q, :], r.mixw[k]).astype(ref.dtype)

        each(T // TT, tile)

    gather_forward(0)
    gather_send(3)
    gather_forward(1)
    gather_send(4)
    gather_wait(0)
    turn_into(r.qpre, r.qrot, 0)
    gather_forward(2)
    gather_send(5)
    gather_wait(1)
    turn_into(r.kpre, r.krot, 1)
    gather_forward(3)
    gather_send(6)
    gather_wait(2)
    project_into(r.val, 2)
    gather_forward(4)
    gather_send(7)
    gather_wait(3)
    project_into(r.gpre, 3)

    def wo_block(owner):
        return r.wo.at[:, pl.ds(pl.multiple_of(owner * C, C), C)]


    NB = T // B
    REACH = LONGEST // B

    def keys_of(qb):
        return slice(max(0, qb - REACH) * B, (qb + 1) * B)

    def weights_of(qb, h):
        key = keys_of(qb)
        width = key.stop - key.start
        fades = [r.dec[min(o, 1), h] for o in range(width // B - 1, -1, -1)]
        for o in range(2, width // B):
            fades[width // B - 1 - o] *= jnp.exp(rate_of(h) * ((o - 1) * B))
        seen = jnp.broadcast_to(r.segk[0:1, key], (B, width))
        same = widen(r.segq[qb * B:(qb + 1) * B, :], width) == seen
        return jnp.where(same, jnp.concatenate(fades, axis=1), 0.0)

    def u_block(qb):
        return lambda owner: r.ufull.at[qb * B:(qb + 1) * B, pl.ds(pl.multiple_of(owner * C, C), C)]

    def attend(qb):
        q = slice(qb * B, (qb + 1) * B)
        squares = jnp.zeros((B, 1), F32)
        for h in range(H):
            rot = slice(2 * h * HEAD, 2 * (h + 1) * HEAD)
            chan = slice(h * HEAD, (h + 1) * HEAD)
            key = keys_of(qb)
            scores = dot_nt(r.qrot[q, rot], r.krot[key, rot]) * weights_of(qb, h)
            total = dot_nn(scores.astype(BF), r.val[key, chan])
            r.mixed[q, chan] = total
            squares = squares + jnp.sum(total * total, axis=-1, keepdims=True)
            r.ufull[q, pl.ds(pl.multiple_of(j * C + h * HEAD, HEAD), HEAD)] = (
                total * r.gpre[q, chan]
            ).astype(BF)
        r.ss[j, :, q] = jnp.transpose(jnp.broadcast_to(squares, (B, 128)))[0:8, :]

    def ss_block(owner):
        return r.ss.at[owner]

    for qb in range(NB):
        attend(qb)
        share_send(1 + qb, u_block(qb))
        if qb == NB - 1:
            share_send(1 + NB, ss_block)
        if qb == 0:
            gather_forward(5)
            gather_send(8)
        if qb == 1:
            gather_wait(4)
            share_send(0, wo_block)
        if qb == 3:
            share_forward(0, wo_block)
        if qb == 2:
            gather_forward(6)
            gather_send(9)
        if qb > 0:
            share_forward(qb, u_block(qb - 1))
    share_forward(NB, u_block(NB - 1))
    share_forward(1 + NB, ss_block)
    gather_forward(7)
    gather_send(10)
    gather_forward(8)
    share_wait(0, wo_block)
    for qb in range(NB):
        share_wait(1 + qb, u_block(qb))
    share_wait(1 + NB, ss_block)
    early = [copy for copy, when in pending]

    total_ss = r.ss[0]
    for owner in range(1, mp):
        total_ss = total_ss + r.ss[owner]
    inverse = lax.rsqrt(total_ss * (1.0 / D) + EPSILON)
    for t in range(T // 128):
        q = slice(t * 128, t * 128 + 128)
        r.rcol[q, :] = jnp.transpose(jnp.broadcast_to(inverse[0:1, q], (128, 128)))

    def hidden_tile(t):
        q = rows_of(t, TB)
        out = widen(r.rcol[q, :], D) * dot_nn(r.ufull[q, :], r.wo[...])
        hidden = r.xv[q, :].astype(F32) + out
        scale = lax.rsqrt(jnp.mean(hidden * hidden, axis=-1, keepdims=True) + EPSILON)
        r.nmid[q, :] = (hidden * scale).astype(BF)

        @pl.when(t == j)
        def _():
            r.hown[...] = hidden

    each(T // TB, hidden_tile)
    gather_wait(5)
    gather_wait(6)

    def gate_tile(t):
        q = rows_of(t, TT)
        r.gact[q, 0:F] = to_units(r.nmid[q, :], 1)

    each(T // TT, gate_tile)
    gather_forward(9)
    gather_wait(7)
    gather_wait(8)

    def up_tile(t):
        q = rows_of(t, TT)
        upper = to_units(r.nmid[q, :], 2)
        r.uact[q, :] = upper.astype(BF)
        r.prod[q, :] = (r.gact[q, 0:F] * upper).astype(BF)

    each(T // TT, up_tile)
    put_ff_grad(0, r.prod, r.up)
    gather_forward(10)
    scatter_first(5, 6)
    gather_wait(9)
    gather_wait(10)

    def mid_block(x, c):
        q = rows_of(x * 2 + c, TB)
        g = to_units(r.up[q, :], 0)
        grad_gate, grad_up = (g * r.uact[q, :].astype(F32)).astype(BF), (g * r.gact[q, 0:F]).astype(BF)
        r.ggate[q, :] = grad_gate
        r.gup[q, :] = grad_up
        r.part[x, c] = (to_model(grad_gate, 1) + to_model(grad_up, 2)).astype(BF)

    used = sum_begin(0, 0, mid_block)
    scatter_second(5)
    put_ff_grad(1, r.ggate, r.nmid)
    scatter_first(7, 8)
    scatter_second(6)

    def back_tile(t):
        q = rows_of(t, 128)
        here = rows_of(j * (TB // 128) + t, 128)
        grad = sum_tile(0, q)
        hidden = r.hown[q, :]
        scale = lax.rsqrt(jnp.mean(hidden * hidden, axis=-1, keepdims=True) + EPSILON)
        normed = hidden * scale
        inner = jnp.mean(grad * normed, axis=-1, keepdims=True)
        out = r.up[here, :].astype(F32) + scale * (grad - normed * inner)
        r.ghid[q, :] = out
        low = out.astype(BF)
        r.hlow[here, :] = low
        mixer_out = hidden - r.xown[q, :].astype(F32)
        product = jnp.sum(low.astype(F32) * mixer_out, axis=-1, keepdims=True) * (1.0 / D)
        r.inn[j, :, q] = jnp.transpose(jnp.broadcast_to(product, (128, 128)))[0:8, :]

    def token_block(ref):
        return lambda owner: ref.at[rows_of(owner, TB)]

    BO, IN, GM, HL, IG = 2 + NB, 3 + NB, 4 + NB, 9 + NB, 9 + NB + NT

    def inn_block(owner):
        return r.inn.at[owner]

    def half_block(ref, t):
        return lambda owner: ref.at[rows_of(owner * NT + t, 128)]

    for t in range(NT):
        sum_arrived(0, 0, t)
        back_tile(t)
        share_send(HL + t, half_block(r.hlow, t))
    share_send(IN, inn_block)
    put_ff_grad(2, r.gup, r.nmid)
    scatter_first(9, 10)
    scatter_second(7)
    for t in range(NT):
        share_forward(HL + t, half_block(r.hlow, t))
    share_forward(IN, inn_block)
    for copy in used:
        settle(copy)

    def expand_block(x, c):
        q = rows_of(x * 2 + c, TB)
        r.part[x, c] = to_model(r.prod[q, :], 0).astype(BF)

    scatter_second(8)
    used = sum_begin(1, 1, expand_block)
    for t in range(NT):
        share_wait(HL + t, half_block(r.hlow, t))
    share_wait(IN, inn_block)
    for owner in range(mp):
        for t in range(TB // 128):
            row = r.inn[owner, 0:1, t * 128:(t + 1) * 128]
            q = slice(owner * TB + t * 128, owner * TB + (t + 1) * 128)
            r.icol[q, :] = jnp.transpose(jnp.broadcast_to(row, (128, 128)))

    wo_rows = rows_of(j, C)

    def gated_tile(t):
        q = rows_of(t, TT)
        low = r.hlow[q, :]
        grad = dot_nt(low, r.wo[wo_rows, :])
        inner = widen(r.icol[q, :], C)
        inverse = widen(r.rcol[q, :], C)
        normed = r.mixed[q, :] * inverse
        r.gproj[3][q, :] = (grad * normed).astype(BF)
        r.gmix[q, :] = (inverse * (grad * r.gpre[q, :] - normed * inner)).astype(BF)
        r.rh[q, :] = (inverse * r.hlow[q, jcols].astype(F32)).astype(BF)

    each(T // TT, gated_tile)
    put_grad(4, r.ufull, r.rh)
    scatter_first(4)

    def swish_back(pre, grad):
        gate = jax.nn.sigmoid(pre)
        return grad * (gate * (1.0 + pre * (1.0 - gate)))

    def attend_back(qb):
        q, key = slice(qb * B, (qb + 1) * B), keys_of(qb)
        for h in range(H):
            rot = slice(2 * h * HEAD, 2 * (h + 1) * HEAD)
            chan = slice(h * HEAD, (h + 1) * HEAD)
            weights = weights_of(qb, h)
            scores = (dot_nt(r.qrot[q, rot], r.krot[key, rot]) * weights).astype(BF)
            back = (dot_nt(r.gmix[q, chan], r.val[key, chan]) * weights).astype(BF)
            dq = dot_nn(back, r.krot[key, rot])
            turned = dq[:, :HEAD] * r.cosv[q, :] + dq[:, HEAD:] * r.sinv[q, :]
            r.gproj[0][q, chan] = swish_back(r.qpre[q, chan], turned).astype(BF)
            dk = dot_tn(back, r.qrot[q, rot])
            dv = dot_tn(scores, r.gmix[q, chan])
            for kb in range(key.start // B, qb + 1):
                at = slice(kb * B - key.start, (kb + 1) * B - key.start)
                rows = slice(kb * B, (kb + 1) * B)
                dkb, dvb = dk[at], dv[at]
                if qb < min(kb + REACH, NB - 1):
                    dkb, dvb = dkb + r.dk[rows, rot], dvb + r.dv[rows, chan]
                if kb < qb:
                    r.dk[rows, rot], r.dv[rows, chan] = dkb, dvb
                else:
                    turned = dkb[:, :HEAD] * r.cosv[q, :] + dkb[:, HEAD:] * r.sinv[q, :]
                    r.gproj[1][q, chan] = swish_back(r.kpre[q, chan], turned).astype(BF)
                    r.gproj[2][q, chan] = dvb.astype(BF)

    def output_tile(t):
        q = rows_of(t, 128)
        r.bov[rows_of(j * NT + t, 128), :] = (r.hown[q, :] + sum_tile(1, q)).astype(BF)

    def late_core(x):
        return pltpu.make_async_remote_copy(
            src_ref=r.part.at[x, 1 - ci], dst_ref=r.recc.at[0, x], send_sem=r.acs.at[2, x], recv_sem=r.acr.at[2, x],
            device_id={"mp": xi * 2 + 1 - ci}, device_id_type=MESH,
        )

    def late_chip(x, d, t):
        q = slice(t * 128, (t + 1) * 128)
        return pltpu.make_async_remote_copy(
            src_ref=r.part.at[x, ci, q], dst_ref=r.recx.at[0, d - 1, q], send_sem=r.axs.at[2, d - 1, t],
            recv_sem=r.axr.at[2, d - 1, t], device_id={"mp": x * 2 + ci}, device_id_type=MESH,
        )

    def blocks_in(qb):
        return [divmod(at, 2) for at in range(qb * B // TB, (qb + 1) * B // TB)]

    def late_begin(x, c):
        q = slice((x * 2 + c) * TB, (x * 2 + c + 1) * TB)
        out = dot_nt(r.gproj[0][q, :], r.mixw[0])
        for k in range(1, 4):
            out = out + dot_nt(r.gproj[k][q, :], r.mixw[k])
        r.part[x, c] = out.astype(BF)

        @pl.when(ci != c)
        def _():
            late_core(x).start()

    def late_pass(x, c):
        @pl.when(ci == c)
        def _():
            arrived(r.recc.at[0, x], r.acr.at[2, x])

        @pl.when((ci == c) & (xi != x))
        def _():
            for t in range(NT):
                q = slice(t * 128, (t + 1) * 128)
                r.part[x, c, q] = (r.part[x, c, q].astype(F32) + r.recc[0, x, q].astype(F32)).astype(BF)
                late_chip(x, lax.rem(x - xi + X, X), t).start()

    put_grad(3, r.nint, r.gproj[3], turned=True)
    scatter_first(3)
    scatter_second(9)
    for qb in range(NB - 1, -1, -1):
        attend_back(qb)
        if qb == NB - 1:
            for t in range(NT):
                sum_arrived(1, 1, t)
            each(TB // 128, output_tile)
            share_send(BO, token_block(r.bov))
            for copy in used + early:
                settle(copy)
        for x, c in blocks_in(qb):
            late_begin(x, c)
        if qb < NB - 1:
            for x, c in blocks_in(qb + 1):
                late_pass(x, c)
        if qb == NB - 1:
            scatter_second(10)
            finish_ff(5, 6)
        if qb == max(NB - 2, 0):
            scatter_second(4)
            share_forward(BO, token_block(r.bov))
            finish_ff(7)
        if qb == max(NB - 3, 0):
            scatter_second(3)
            finish_ff(8)
    for x, c in blocks_in(0):
        late_pass(x, c)
    pending.extend((late_core(x), None) for x in range(X))
    pending.extend((late_chip(lax.rem(xi + d, X), d, t), None) for d in range(1, X) for t in range(NT))
    for k in (2, 0, 1):
        put_grad(k, r.nint, r.gproj[k], turned=True)
        scatter_first(k)
    finish_ff(9, 10)

    def input_tile(t):
        q = rows_of(t, 128)
        grad = sum_tile(0, q)
        v = r.xown[q, :].astype(F32)
        scale = lax.rsqrt(jnp.mean(v * v, axis=-1, keepdims=True) + EPSILON)
        normed = v * scale
        inner = jnp.mean(grad * normed, axis=-1, keepdims=True)
        r.igv[rows_of(j * NT + t, 128), :] = (r.ghid[q, :] + scale * (grad - normed * inner)).astype(BF)

    for t in range(NT):
        for d in range(1, X):
            arrived(r.recx.at[0, d - 1, t * 128:(t + 1) * 128], r.axr.at[2, d - 1, t])
        input_tile(t)
        share_send(IG + t, half_block(r.igv, t))
    for k in (2, 0, 1):
        scatter_second(k)
    share_wait(BO, token_block(r.bov))
    stores = [load(r.bov, r.bo, 0)]

    def grad_block(k):
        return lambda owner: r.gmv.at[k * S:(k + 1) * S, pl.ds(pl.multiple_of(owner * C, C), C)]

    for k in (4, 3, 2, 0, 1):
        total = scatter_total(k).astype(BF)
        r.gmv[k * S:(k + 1) * S, jcols] = total
        r.sqs[...] += squares_of(total.astype(F32))
        share_send(GM + k, grad_block(k))

    r.s1[j] = r.sqs[...]
    for d in range(1, mp):
        go(r.s1.at[j], r.s1.at[j], r.q1s.at[d], r.q1r.at[d], mp=lax.rem(j + d, mp))
    for t in range(NT):
        share_forward(IG + t, half_block(r.igv, t))
    for d in range(1, mp):
        arrived(r.s1.at[lax.rem(j - d + mp, mp)], r.q1r.at[d])
    total = r.s1[0]
    for owner in range(1, mp):
        total = total + r.s1[owner]
    r.s2[i] = total
    for d in range(1, n):
        go(r.s2.at[i], r.s2.at[i], r.q2s.at[d], r.q2r.at[d], dp=lax.rem(i + d, n))
    for k in (4, 3, 2, 0, 1):
        share_forward(GM + k, grad_block(k))
    for d in range(1, n):
        arrived(r.s2.at[lax.rem(i - d + n, n)], r.q2r.at[d])
    total = r.s2[0]
    for owner in range(1, n):
        total = total + r.s2[owner]
    r.sqo[...] = total

    for t in range(NT):
        share_wait(IG + t, half_block(r.igv, t))
    stores.append(load(r.igv, r.ig, 1))
    for k in (4, 3, 2, 0, 1):
        share_wait(GM + k, grad_block(k))
        stores.append(load(r.gmv.at[k * S:(k + 1) * S], r.gmo.at[k], 2 + k))
    for copy in stores:
        copy.wait()
    for copy, when in pending:
        guarded(when, copy.wait_send)


def fused(p, *operands):
    scratch = scratch_of(p)
    names = IN_NAMES + OUT_NAMES + tuple(scratch)
    anywhere = pl.BlockSpec(memory_space=pl.ANY)
    vmem = pl.BlockSpec(memory_space=pltpu.VMEM)
    smem = pl.BlockSpec(memory_space=pltpu.SMEM)
    return pl.pallas_call(
        partial(body, p, names),
        out_shape=(
            jax.ShapeDtypeStruct((p.T, p.D), BF),
            jax.ShapeDtypeStruct((p.T, p.D), BF),
            jax.ShapeDtypeStruct((5, p.S, p.D), BF),
            jax.ShapeDtypeStruct((2, p.F, p.S) if p.FD else (2, p.S, p.F), F32),
            jax.ShapeDtypeStruct((p.F, p.S) if p.FD else (p.S, p.F), F32),
            jax.ShapeDtypeStruct((8, 128), F32),
        ),
        in_specs=[anywhere, anywhere, vmem, smem] + [anywhere] * 5,
        out_specs=(anywhere, anywhere, anywhere, vmem, vmem, vmem),
        scratch_shapes=list(scratch.values()),
        compiler_params=pltpu.CompilerParams(
            collective_id=0, has_side_effects=True, vmem_limit_bytes=VMEM_LIMIT
        ),
    )(*operands)


VMEM_LIMIT = 64 * 2**20 - 2**18


def renew(weight, momentum, shadow, grad, clip_factor):
    clipped = grad * clip_factor
    velocity = MOMENTUM * momentum + clipped
    updated = weight - LEARN_RATE * (clipped + MOMENTUM * velocity)
    average = SHADOW_DECAY * shadow + (1.0 - SHADOW_DECAY) * updated
    return (velocity, average, updated)


def update_body(cuts, *refs):
    kinds, pieces = len(cuts), sum(len(c) for c in cuts)
    sq, carried = refs[0], refs[1:3]
    ins = [refs[3 + 4 * w:7 + 4 * w] for w in range(kinds)]
    refs = refs[3 + 4 * kinds:]
    norm_out, carried_out = refs[0], refs[1:3]
    outs = [refs[3 + 3 * w:6 + 3 * w] for w in range(kinds)]
    refs = refs[3 + 3 * kinds:]
    held = [refs[4 * w:4 * w + 4] for w in range(kinds)]
    made = [refs[4 * kinds + 3 * w:4 * kinds + 3 * w + 3] for w in range(kinds)]
    bounce, (in_sem, out_sem, carry_sem) = refs[7 * kinds:7 * kinds + 2], refs[7 * kinds + 2:]
    loads, order = {}, [(w, c) for w in range(kinds) for c in range(len(cuts[w]))]
    for at, (w, c) in enumerate(order):
        for a in range(4):
            cut = cuts[w][c]
            loads[at, a] = pltpu.make_async_copy(ins[w][a].at[cut], held[w][a].at[cut], in_sem.at[at, a])
            loads[at, a].start()
    carry = [pltpu.make_async_copy(carried[a], bounce[a], carry_sem.at[a]) for a in range(2)]
    for copy in carry:
        copy.start()
    copies = []
    norm = jnp.sqrt(jnp.broadcast_to(jnp.sum(sq[...]), (8, 128)))
    norm_out[...] = norm
    clip_factor = 1.0 / jnp.maximum(jnp.max(norm), 1.0)
    for at, (w, c) in enumerate(order):
        cut = cuts[w][c]
        for a in range(4):
            loads[at, a].wait()
        new = renew(*[held[w][a][cut] for a in range(3)], held[w][3][cut].astype(F32), clip_factor)
        for a in range(3):
            made[w][a][cut] = new[a]
            copy = pltpu.make_async_copy(made[w][a].at[cut], outs[w][a].at[cut], out_sem.at[at, a])
            copy.start()
            copies.append(copy)
    for a in range(2):
        carry[a].wait()
        copy = pltpu.make_async_copy(bounce[a], carried_out[a], carry_sem.at[2 + a])
        copy.start()
        copies.append(copy)
    for copy in copies:
        copy.wait()


def update(sq, carried, weights):
    cuts = [[c for c in range(g[0].shape[0])] if g[0].ndim == 3 else [slice(None)] for g in weights]
    pieces = sum(len(c) for c in cuts)
    anywhere = pl.BlockSpec(memory_space=pl.ANY)
    vmem = pl.BlockSpec(memory_space=pltpu.VMEM)
    flat_in = [a for group in weights for a in group]
    flat_out = [a for group in weights for a in group[:3]]
    dma = pltpu.SemaphoreType.DMA
    size = sum(a.size * a.dtype.itemsize for a in flat_in + flat_out + 2 * list(carried))
    return pl.pallas_call(
        partial(update_body, cuts),
        out_shape=[jax.ShapeDtypeStruct(a.shape, a.dtype) for a in [sq, *carried, *flat_out]],
        in_specs=[vmem] + [anywhere] * (2 + len(flat_in)),
        out_specs=[vmem] + [anywhere] * (2 + len(flat_out)),
        scratch_shapes=[pltpu.VMEM(a.shape, a.dtype) for a in flat_in + flat_out + list(carried)]
        + [dma((pieces, 4)), dma((pieces, 3)), dma((4,))],
        cost_estimate=pl.CostEstimate(flops=size, bytes_accessed=size, transcendentals=0),
        compiler_params=pltpu.CompilerParams(vmem_limit_bytes=VMEM_LIMIT),
    )(sq, *carried, *flat_in)


def turn_tables(tokens):
    theta = np.float32(10000.0) ** (-np.arange(HEAD, dtype=np.float32) / np.float32(HEAD))
    angle = np.arange(tokens, dtype=np.float32)[:, None] * theta.astype(np.float32)[None, :]
    angle = angle.astype(np.float64)
    return np.cos(angle).astype(np.float32), np.sin(angle).astype(np.float32)


def per_device(mesh, block_input, segment_ids, live_length, output_grad, mixer_weight, mixer_momentum, mixer_shadow,
               expand_weight, expand_momentum, expand_shadow, shrink_weight, shrink_momentum, shrink_shadow):
    rows, length, width = block_input.shape
    p = plan_of(mesh, length, width, shrink_weight.shape[0])
    turn = (lambda v: jnp.swapaxes(v, -1, -2)) if p.FD else (lambda v: v)
    if p.FD:
        shards = (turn(expand_weight), shrink_weight)
    else:
        shards = (jnp.concatenate([shrink_weight.T[None], expand_weight], axis=0).astype(BF), shrink_weight)
    cos, sin = turn_tables(length)
    out, grad_in, gm, ge, gs, sq = fused(
        p, block_input[0], output_grad[0], segment_ids, live_length, jnp.asarray(cos), jnp.asarray(sin), mixer_weight, *shards
    )
    new = update(sq, (out, grad_in), (
        (mixer_weight, mixer_momentum, mixer_shadow, gm),
        (turn(expand_weight), turn(expand_momentum), turn(expand_shadow), ge),
        (shrink_weight, shrink_momentum, shrink_shadow, gs if p.FD else gs.T),
    ))
    norm, out, grad_in = new[:3]
    return (out[None], grad_in[None], norm[0, 0], *new[3:6], *(turn(v) for v in new[6:9]), *new[9:12])


def solution(mesh):
    row, mixer, expand, shrink = P("dp", None, None), P(None, "dp", None), P(None, "dp", "mp"), P("mp", "dp")
    return jax.shard_map(
        partial(per_device, mesh),
        mesh=mesh,
        in_specs=(row, P("dp", None), P("dp"), row) + (mixer,) * 3 + (expand,) * 3 + (shrink,) * 3,
        out_specs=(row, row, P()) + (mixer,) * 3 + (expand,) * 3 + (shrink,) * 3,
        check_vma=False,
    )
```

```python
from functools import partial
from types import SimpleNamespace

import jax
import jax.numpy as jnp
import numpy as np
from jax import lax
from jax.experimental import pallas as pl
from jax.experimental.pallas import tpu as pltpu
from jax.sharding import PartitionSpec as P

HEAD = 128
EPSILON = 1e-06
LEARN_RATE = 32.0
MOMENTUM = 0.5
SHADOW_DECAY = 0.5
LAYER_PLACE = 12.0 / 24.0
LONGEST = 512
FF_ORDER = (1, 2, 0)
Y_FIRST = (4, 6)
Z_FIRST = (5, 4)
STRAIGHT = (0, 1)
MESH = pl.DeviceIdType.MESH
BF = jnp.bfloat16
F32 = jnp.float32


def dot_nn(a, b):
    return lax.dot_general(a, b, (((1,), (0,)), ((), ())), preferred_element_type=F32)


def dot_nt(a, b):
    return lax.dot_general(a, b, (((1,), (1,)), ((), ())), preferred_element_type=F32)


def dot_tn(a, b):
    return lax.dot_general(a, b, (((0,), (0,)), ((), ())), preferred_element_type=F32)


def rows_of(index, size):
    return pl.ds(pl.multiple_of(index * size, size), size)


def each(count, body):
    def step(t, carry):
        body(t)
        return carry

    lax.fori_loop(0, count, step, 0)


def widen(column, width):
    return jnp.concatenate([column] * (width // 128), axis=1)


def plan_of(mesh, tokens, width, inner):
    n, mp = mesh.shape["dp"], mesh.shape["mp"]
    lo, core = 2, 2
    return SimpleNamespace(
        n=n, mp=mp, LO=lo, HI=n // lo, X=mp // core, T=tokens, D=width, C=width // mp, F=inner,
        S=width // n, H=width // mp // HEAD, TB=tokens // mp, B=min(256, tokens),
        NT=tokens // mp // 128, FD=(width // n) % 128 == 0,
    )


def scratch_of(p):
    T, D, C, F, S, HI, LO, X, TB, B = p.T, p.D, p.C, p.F, p.S, p.HI, p.LO, p.X, p.TB, p.B
    dma = pltpu.SemaphoreType.DMA
    v = pltpu.VMEM
    return dict(
        mixw=v((4, D, C), BF), wo=v((D, D), BF), ffw=v((3, F, D) if p.FD else (3, D, F), BF),
        xown=v((TB, D), BF), nin=v((T, D), BF), nint=v((D, T), BF), up=v((T, D), BF),
        cosv=v((T, HEAD), F32), sinv=v((T, HEAD), F32),
        segq=v((T, 128), F32), segk=v((8, T), F32), dec=v((2, p.H, B, B), F32),
        qpre=v((T, C), F32), kpre=v((T, C), F32), gpre=v((T, C), F32), val=v((T, C), BF),
        qrot=v((T, 2 * C), BF), krot=v((T, 2 * C), BF), mixed=v((T, C), F32),
        ufull=v((T, D), BF), ss=v((p.mp, 8, T), F32), rcol=v((T, 128), F32),
        inn=v((p.mp, 8, TB), F32), hown=v((TB, D), F32),
        gact=v((T, max(F, 2 * C + HEAD)), F32), uact=v((T, F), BF), prod=v((T, F), BF), ggate=v((T, F), BF), gup=v((T, F), BF),
        part=v((X, 2, TB, D), BF), recc=v((2, X, TB, D), BF), recx=v((2, X - 1, TB, D), BF),
        hlow=v((T, D), BF),
        gm=v((5, HI, LO, S, C), BF), rym=v((5, HI, S, C), BF), rzm=v((5, HI - 1, S, C), BF),
        gf=v((3, LO, F, HI * S) if p.FD else (3, HI, LO, S, F), BF),
        ryf=v((3, F, HI * S) if p.FD else (3, HI, S, F), BF),
        rzf=v((3, HI - 1, F, S) if p.FD else (3, HI - 1, S, F), BF),
        relm=v((3, S, C), BF), relf=v((3, F, S) if p.FD else (3, S, F), BF),
        othm=v((HI, S, C), BF), othf=v((HI, F // 2, S) if p.FD else (HI, S // 2, F), BF),
        sqs=v((8, 128), F32), s1=v((p.mp, 8, 128), F32), s2=v((p.n, 8, 128), F32),
        loc=dma((10,)),
        zs=dma((11, HI - 1)), zr=dma((11, HI - 1)), us=dma((len(Y_FIRST), HI - 1)), ur=dma((len(Y_FIRST), HI - 1)),
        zp=dma((11,)), yp=dma((len(Y_FIRST),)), ys=dma((11, HI)), yr=dma((11, HI)),
        xs=dma((20, X - 1)), xr=dma((20, X - 1)), cs=dma((20, X)), cr=dma((20, X)),
        acs=dma((3, X)), acr=dma((3, X)), axs=dma((3, X - 1, p.NT)), axr=dma((3, X - 1, p.NT)),
        bys=dma((11,)), byr=dma((11,)), bzs=dma((11, HI - 1)), bzr=dma((11, HI - 1)),
        bts=dma((11,)), btr=dma((11,)), ozs=dma((2, HI - 1)), ozr=dma((2, HI - 1)), ots=dma((2,)), otr=dma((2,)),
        q1s=dma((p.mp,)), q1r=dma((p.mp,)), q2s=dma((p.n,)), q2r=dma((p.n,)),
    )


IN_NAMES = ("x", "og", "seg", "live", "cos", "sin", "mixsh", "exsh", "shsh")
OUT_NAMES = ("bo", "ig", "gmo", "geo", "gso", "sqo")


def body(p, names, *refs):
    r = SimpleNamespace(**dict(zip(names, refs)))
    n, mp, LO, HI, X, T, D, C, F, S, H, TB, B = (
        p.n, p.mp, p.LO, p.HI, p.X, p.T, p.D, p.C, p.F, p.S, p.H, p.TB, p.B,
    )
    NT, TT = p.NT, min(512, p.T)
    i, j = lax.axis_index("dp"), lax.axis_index("mp")
    zi, yi = i // LO, lax.rem(i, LO)
    xi, ci = j // 2, lax.rem(j, 2)
    jcols = pl.ds(pl.multiple_of(j * C, C), C)
    pending = []
    r.xv, r.nmid = r.hlow, r.nin
    r.bov, r.igv, r.gmv = r.up, r.ufull, r.wo
    r.dk, r.icol, r.dv = r.gact.at[:, 0:2 * C], r.gact.at[:, 2 * C:2 * C + HEAD], r.mixed
    r.gproj = [r.ggate.at[:, 0:C], r.ggate.at[:, C:2 * C], r.gup.at[:, 0:C], r.gup.at[:, C:2 * C]]
    r.gmix, r.rh = r.prod.at[:, 0:C], r.prod.at[:, C:2 * C]

    def go(src, dst, ssem, rsem, when=None, **device):
        copy = pltpu.make_async_remote_copy(
            src_ref=src, dst_ref=dst, send_sem=ssem, recv_sem=rsem,
            device_id=device, device_id_type=MESH,
        )
        guarded(when, copy.start)
        pending.append((copy, when))
        return copy

    def guarded(when, act):
        if when is None:
            act()
        else:
            pl.when(when)(lambda: act())

    def arrived(dst, sem):
        pltpu.make_async_copy(dst, dst, sem).wait()

    def settle(copy):
        for other, when in pending:
            if other is copy:
                guarded(when, copy.wait_send)
        pending[:] = [entry for entry in pending if entry[0] is not copy]

    def load(src, dst, sem):
        copy = pltpu.make_async_copy(src, dst, r.loc.at[sem])
        copy.start()
        return copy

    own_mix = [load(r.mixsh.at[k, :, jcols], r.qpre.at[k * S:(k + 1) * S], k) for k in range(5)]
    if p.FD:
        stage = [r.gact.at[0:F, m * S:(m + 1) * S] for m in range(3)]
        own_ff = [load(r.shsh if m == 0 else r.exsh.at[m - 1], stage[m], 5 + m) for m in range(3)]
    else:
        own_ff = [load(r.exsh.at[m], r.ffw.at[m, rows_of(i, S)], 5 + m) for m in range(3)]
    load_x = load(r.x, r.xv, 8)
    load_og = load(r.og, r.up, 9)

    def enter():
        barrier = pltpu.get_barrier_semaphore()
        for d in range(1, n):
            pl.semaphore_signal(barrier, inc=1, device_id={"dp": lax.rem(i + d, n)}, device_id_type=MESH)
        for d in range(1, mp):
            pl.semaphore_signal(barrier, inc=1, device_id={"mp": lax.rem(j + d, mp)}, device_id_type=MESH)
        pl.semaphore_wait(barrier, n - 1 + mp - 1)

    def slot(k, device):
        rows = rows_of(device, S)
        if k == 4:
            return r.wo.at[rows, jcols]
        if k < 4:
            return r.mixw.at[k, rows]
        m, half = FF_ORDER[(k - 5) // 2], (k - 5) % 2
        if p.FD:
            return r.ffw.at[m, half * F // 2:(half + 1) * F // 2, rows]
        return r.ffw.at[m, pl.ds(pl.multiple_of(device * S + half * S // 2, S // 2), S // 2)]

    def gather_ready(k):
        if k < 5:
            own_mix[k].wait()
            slot(k, i)[...] = r.qpre[k * S:(k + 1) * S, :].astype(BF)
        else:
            m, half = FF_ORDER[(k - 5) // 2], (k - 5) % 2
            if half == 0:
                own_ff[m].wait()
            if p.FD:
                slot(k, i)[...] = stage[m][half * F // 2:(half + 1) * F // 2, :].astype(BF)

    relays = HI == 4
    next_to_end = (zi == 1) | (zi == 2)

    def along_z(block, ssem, rsem):
        for d in range(1, HI):
            to = lax.rem(zi + d, HI)
            near = (jnp.abs(to - zi) < 3) if relays else None
            go(block, block, ssem.at[d - 1], rsem.at[d - 1], when=near, dp=to * LO + yi)

    def hand_on(block, ssem, rsem):
        if relays:
            end = jnp.where(zi == 2, 3, 0)
            go(block, block, ssem, rsem.at[jnp.where(zi == 2, 2, 0)], when=next_to_end, dp=end * LO + yi)

    def from_z_source(k, d, y):
        return slot(k, lax.rem(zi - d + HI, HI) * LO + y)

    WAYS = [2, 1, *range(3, HI)]

    def gather_send(k):
        src = slot(k, i)
        along_z(src, r.zs.at[k], r.zr.at[k])
        go(src, src, r.ys.at[k, 0], r.yr.at[k, 0], dp=zi * LO + 1 - yi)

    def gather_forward(k):
        if k - 1 in Y_FIRST:
            b = Y_FIRST.index(k - 1)
            block = from_z_source(k - 1, 2, 1 - yi)
            arrived(block, r.ur.at[b, 1])
            hand_on(block, r.yp.at[b], r.ur.at[b])
        if k in Y_FIRST:
            b = Y_FIRST.index(k)
            peers = slot(k, zi * LO + 1 - yi)
            arrived(peers, r.yr.at[k, 0])
            along_z(peers, r.us.at[b], r.ur.at[b])
        for d in WAYS:
            block = from_z_source(k, d, yi)
            arrived(block, r.zr.at[k, d - 1])
            if d == 2:
                hand_on(block, r.zp.at[k], r.zr.at[k])
            if k not in Y_FIRST:
                go(block, block, r.ys.at[k, d], r.yr.at[k, d], dp=zi * LO + 1 - yi)

    def gather_wait(k):
        for d in range(HI):
            if k not in Y_FIRST:
                arrived(from_z_source(k, d, 1 - yi), r.yr.at[k, d])
            elif d in (1, 3) or d > 3:
                arrived(from_z_source(k, d, 1 - yi), r.ur.at[Y_FIRST.index(k), d - 1])

    def share_send(s, block, src=None):
        own = block(j)
        src = own if src is None else src
        for d in range(1, X):
            go(src, own, r.xs.at[s, d - 1], r.xr.at[s, d - 1], mp=lax.rem(xi + d, X) * 2 + ci)
        go(src, own, r.cs.at[s, 0], r.cr.at[s, 0], mp=xi * 2 + 1 - ci)

    def share_forward(s, block):
        for d in range(1, X):
            part = block(lax.rem(xi - d + X, X) * 2 + ci)
            arrived(part, r.xr.at[s, d - 1])
            go(part, part, r.cs.at[s, d], r.cr.at[s, d], mp=xi * 2 + 1 - ci)

    def share_wait(s, block):
        for d in range(X):
            arrived(block(lax.rem(xi - d + X, X) * 2 + 1 - ci), r.cr.at[s, d])

    def sum_begin(s, b, compute):
        sent = []
        for d in [*range(1, X), 0]:
            to = lax.rem(xi + d, X)
            compute(to, 1 - ci)
            sent.append(go(
                r.part.at[to, 1 - ci], r.recc.at[b, to], r.acs.at[s, d], r.acr.at[s, d], mp=xi * 2 + 1 - ci
            ))
        for d in range(1, X):
            to = lax.rem(xi + d, X)
            compute(to, ci)
            arrived(r.recc.at[b, to], r.acr.at[s, d])
            for t in range(NT):
                q = slice(t * 128, (t + 1) * 128)
                r.part[to, ci, q] = (
                    r.part[to, ci, q].astype(F32) + r.recc[b, to, q].astype(F32)
                ).astype(BF)
                sent.append(go(
                    r.part.at[to, ci, q], r.recx.at[b, d - 1, q], r.axs.at[s, d - 1, t], r.axr.at[s, d - 1, t],
                    mp=to * 2 + ci,
                ))
        compute(xi, ci)
        return sent

    def sum_arrived(s, b, t):
        if t == 0:
            arrived(r.recc.at[b, xi], r.acr.at[s, 0])
        for d in range(1, X):
            arrived(r.recx.at[b, d - 1, t * 128:(t + 1) * 128], r.axr.at[s, d - 1, t])

    def sum_tile(b, q):
        total = r.part[xi, ci, q].astype(F32) + r.recc[b, xi, q].astype(F32)
        for d in range(1, X):
            total = total + r.recx[b, d - 1, q].astype(F32)
        return total

    flat = p.FD

    def half_of(k):
        size = (F if flat else S) // 2
        return (k - 5) // 2, slice((k - 5) % 2 * size, ((k - 5) % 2 + 1) * size)

    def block_of(k, z, y):
        if k < 5:
            return r.gm.at[k, z, y]
        m, rows = half_of(k)
        return r.gf.at[m, y, rows, rows_of(z, S)] if flat else r.gf.at[m, z, y, rows]

    def from_y(k):
        if k < 5:
            return r.rym.at[k]
        m, rows = half_of(k)
        return r.ryf.at[m, rows] if flat else r.ryf.at[m, :, rows]

    def from_y_block(k, z):
        ref = from_y(k)
        return ref.at[:, rows_of(z, S)] if flat and k >= 5 else ref.at[z]

    def to_y(k):
        if k < 5:
            return r.gm.at[k, :, 1 - yi]
        m, rows = half_of(k)
        return r.gf.at[m, 1 - yi, rows] if flat else r.gf.at[m, :, 1 - yi, rows]

    def from_z(k, d, own=True):
        if not own:
            return (r.othm if k < 5 else r.othf).at[d - 1]
        if k < 5:
            return r.rzm.at[k, d - 1]
        m, rows = half_of(k)
        return r.rzf.at[m, d - 1, rows]

    def handed(k, own=True):
        if not own:
            return (r.othm if k < 5 else r.othf).at[HI - 1]
        if k < 5:
            return r.relm.at[max(k - 2, 0)]
        m, rows = half_of(k)
        return r.relf.at[m, rows]

    def z_sems(k, own):
        if own:
            return r.bzs.at[k], r.bzr.at[k], r.bts.at[k], r.btr.at[k]
        o = Z_FIRST.index(k)
        return r.ozs.at[o], r.ozr.at[o], r.ots.at[o], r.otr.at[o]

    def stepped(k):
        return relays and k not in STRAIGHT

    def far(d, back=False):
        other = lax.rem(zi + (HI - d if back else d), HI)
        return jnp.abs(other - zi) == 3

    def z_send(k, own, ways):
        y = yi if own else 1 - yi
        ssem, rsem, tsem, trsem = z_sems(k, own)
        for d in ways:
            to = lax.rem(zi + d, HI)
            block, dst = block_of(k, to, y), from_z(k, d, own)
            if stepped(k) and d != 2:
                go(block, handed(k, own), tsem, trsem, when=far(d), dp=jnp.where(zi == 0, 1, 2) * LO + yi)
                go(block, dst, ssem.at[d - 1], rsem.at[d - 1], when=jnp.logical_not(far(d)), dp=to * LO + yi)
            else:
                go(block, dst, ssem.at[d - 1], rsem.at[d - 1], dp=to * LO + yi)

    def z_send_handed(k, own):
        block = block_of(k, lax.rem(zi + 2, HI), yi if own else 1 - yi)

        @pl.when(next_to_end)
        def _():
            arrived(handed(k, own), z_sems(k, own)[3])
            block[...] = (block[...].astype(F32) + handed(k, own)[...].astype(F32)).astype(BF)

        z_send(k, own, [2])

    def z_total(k, own):
        for d in range(1, HI):
            wait = partial(arrived, from_z(k, d, own), z_sems(k, own)[1].at[d - 1])
            guarded(jnp.logical_not(far(d, back=True)) if stepped(k) and d != 2 else None, wait)
        total = block_of(k, zi, yi if own else 1 - yi)[...].astype(F32)
        for d in range(1, HI):
            total = total + from_z(k, d, own)[...].astype(F32)
        return total

    def clear_far_places():
        if not relays:
            return
        for d in (1, 3):
            @pl.when(far(d, back=True))
            def _(d=d):
                r.rzm[:, d - 1] = jnp.zeros((5, S, C), BF)
                for m in range(3):
                    r.rzf[m, d - 1] = jnp.zeros(r.rzf.shape[2:], BF)
                r.othm[d - 1] = jnp.zeros(r.othm.shape[1:], BF)
                r.othf[d - 1] = jnp.zeros(r.othf.shape[1:], BF)

    def near_ways(k):
        return [3, 1] if stepped(k) else list(range(1, HI))

    def scatter_first(*pieces):
        for k in pieces:
            if k in Z_FIRST:
                for own in (False, True):
                    z_send(k, own, near_ways(k))
            else:
                go(to_y(k), from_y(k), r.bys.at[k], r.byr.at[k], dp=zi * LO + 1 - yi)

    def scatter_second(*pieces):
        for k in pieces:
            if k in Z_FIRST:
                block = block_of(k, zi, 1 - yi)
                block[...] = z_total(k, False).astype(BF)
                go(block, from_y_block(k, zi), r.bys.at[k], r.byr.at[k], dp=zi * LO + 1 - yi)
                continue
            arrived(from_y(k), r.byr.at[k])
            for d in range(1, HI):
                to = lax.rem(zi + d, HI)
                block = block_of(k, to, yi)
                block[...] = (block[...].astype(F32) + from_y_block(k, to)[...].astype(F32)).astype(BF)
            z_send(k, True, near_ways(k))

    def scatter_handed(*pieces):
        for k in pieces:
            if stepped(k):
                if k in Z_FIRST:
                    z_send_handed(k, False)
                z_send_handed(k, True)

    def scatter_total(k):
        if k in Z_FIRST:
            arrived(from_y_block(k, zi), r.byr.at[k])
        return z_total(k, True) + from_y_block(k, zi)[...].astype(F32)

    def squares_of(total):
        squared = total * total
        if squared.shape[-1] % 128:
            corner = (lax.broadcasted_iota(jnp.int32, (8, 128), 0) + lax.broadcasted_iota(jnp.int32, (8, 128), 1)) == 0
            return jnp.where(corner, jnp.sum(squared), 0.0)
        folded = jnp.sum(squared.reshape(-1, 8, squared.shape[-1]), axis=0)
        return sum(folded[:, c:c + 128] for c in range(0, folded.shape[-1], 128))

    def finish_ff(*pieces):
        for k in pieces:
            m, rows = half_of(k)
            total = scatter_total(k)
            if m == 0:
                r.gso[rows] = total
            else:
                r.geo[m - 1, rows] = total
            r.sqs[...] += squares_of(total)

    def put_grad(k, lhs, rhs, turned=False):
        g = r.gm.at[k] if k < 5 else r.gf.at[k - 5]
        per = TT // (LO * S)

        def tile(t):
            if turned:
                out = dot_nn(lhs[rows_of(t, TT), :], rhs[...])
            else:
                out = dot_tn(lhs[:, rows_of(t, TT)], rhs[...])
            g[pl.ds(t * per, per)] = out.astype(BF).reshape(per, LO, S, out.shape[-1])

        each(D // TT, tile)

    def put_ff_grad(m, units, model):
        if not flat:
            return put_grad(5 + m, model, units)
        for f in range(0, F, 384):
            q = slice(f, min(f + 384, F))
            out = dot_tn(units[:, q], model[...]).astype(BF)
            for y in range(LO):
                for z in range(HI):
                    r.gf[m, y, q, z * S:(z + 1) * S] = out[:, (z * LO + y) * S:(z * LO + y + 1) * S]

    def to_units(a, m):
        return dot_nt(a, r.ffw[m]) if flat else dot_nn(a, r.ffw[m])

    def to_model(a, m):
        return dot_nn(a, r.ffw[m]) if flat else dot_nt(a, r.ffw[m])

    gather_ready(0)
    gather_ready(1)
    enter()
    gather_send(0)
    gather_send(1)
    gather_ready(2)
    gather_send(2)
    r.sqs[...] = jnp.zeros_like(r.sqs)
    clear_far_places()

    length = r.live[0]
    load_x.wait()

    def norm_tile(t):
        q = rows_of(t, 128)
        v = r.xv[q, :].astype(F32)
        r.nin[q, :] = (v * lax.rsqrt(jnp.mean(v * v, axis=-1, keepdims=True) + EPSILON)).astype(BF)

    each(T // 128, norm_tile)
    for k in range(3, 11):
        gather_ready(k)
    load_x_own = load(r.x.at[rows_of(j, TB)], r.xown, 8)
    load_og.wait()
    load_cos = load(r.cos, r.cosv, 0)
    load_sin = load(r.sin, r.sinv, 1)

    def live_tile(t):
        q = rows_of(t, 128)
        place = lax.broadcasted_iota(jnp.int32, (128, D), 0) + t * 128
        r.up[q, :] = jnp.where(place < length, r.up[q, :].astype(F32), 0.0).astype(BF)

    each(T // 128, live_tile)

    place = lax.broadcasted_iota(jnp.int32, (1, T), 1)
    segment = r.seg[...].astype(F32)
    r.segk[...] = jnp.broadcast_to(jnp.where(place < length, segment, -2.0), (8, T))
    seg_q = jnp.where(place < length, segment, -1.0)
    for t in range(T // 128):
        q = slice(t * 128, t * 128 + 128)
        r.segq[q, :] = jnp.transpose(jnp.broadcast_to(seg_q[:, q], (128, 128)))

    down = lax.broadcasted_iota(jnp.int32, (B, B), 0)
    over = lax.broadcasted_iota(jnp.int32, (B, B), 1)
    heads = D // HEAD

    def rate_of(h):
        return -(8.0 * (j * H + h).astype(F32) / heads) * (1.0 - LAYER_PLACE)

    for h in range(H):
        rate = rate_of(h)
        for o in range(2):
            distance = down - over + o * B
            fade = jnp.exp(rate * jnp.maximum(distance, 0).astype(F32))
            r.dec[o, h] = jnp.where(distance >= 0, fade, 0.0)

    for t in range(D // 128):
        q = slice(t * 128, t * 128 + 128)
        r.nint[q, :] = jnp.transpose(r.nin[:, q])
    load_cos.wait()
    load_sin.wait()
    load_x_own.wait()

    def turn_into(pre_ref, rot_ref, k):
        def tile(t):
            q = rows_of(t, TT)
            pre = dot_nn(r.nin[q, :], r.mixw[k])
            pre_ref[q, :] = pre
            act = pre * jax.nn.sigmoid(pre)
            c, s = r.cosv[q, :], r.sinv[q, :]
            for h in range(H):
                a = act[:, h * HEAD:(h + 1) * HEAD]
                rot_ref[q, 2 * h * HEAD:(2 * h + 1) * HEAD] = (a * c).astype(BF)
                rot_ref[q, (2 * h + 1) * HEAD:(2 * h + 2) * HEAD] = (a * s).astype(BF)

        each(T // TT, tile)

    def project_into(ref, k):
        def tile(t):
            q = rows_of(t, TT)
            ref[q, :] = dot_nn(r.nin[q, :], r.mixw[k]).astype(ref.dtype)

        each(T // TT, tile)

    gather_forward(0)
    gather_send(3)
    gather_forward(1)
    gather_send(4)
    gather_wait(0)
    turn_into(r.qpre, r.qrot, 0)
    gather_forward(2)
    gather_send(5)
    gather_wait(1)
    turn_into(r.kpre, r.krot, 1)
    gather_forward(3)
    gather_send(6)
    gather_wait(2)
    project_into(r.val, 2)
    gather_forward(4)
    gather_send(7)
    gather_wait(3)
    project_into(r.gpre, 3)

    def wo_block(owner):
        return r.wo.at[:, pl.ds(pl.multiple_of(owner * C, C), C)]


    NB = T // B
    REACH = LONGEST // B

    def keys_of(qb):
        return slice(max(0, qb - REACH) * B, (qb + 1) * B)

    def weights_of(qb, h):
        key = keys_of(qb)
        width = key.stop - key.start
        fades = [r.dec[min(o, 1), h] for o in range(width // B - 1, -1, -1)]
        for o in range(2, width // B):
            fades[width // B - 1 - o] *= jnp.exp(rate_of(h) * ((o - 1) * B))
        seen = jnp.broadcast_to(r.segk[0:1, key], (B, width))
        same = widen(r.segq[qb * B:(qb + 1) * B, :], width) == seen
        return jnp.where(same, jnp.concatenate(fades, axis=1), 0.0)

    def u_block(qb):
        return lambda owner: r.ufull.at[qb * B:(qb + 1) * B, pl.ds(pl.multiple_of(owner * C, C), C)]

    def attend(qb):
        q = slice(qb * B, (qb + 1) * B)
        squares = jnp.zeros((B, 1), F32)
        for h in range(H):
            rot = slice(2 * h * HEAD, 2 * (h + 1) * HEAD)
            chan = slice(h * HEAD, (h + 1) * HEAD)
            key = keys_of(qb)
            scores = dot_nt(r.qrot[q, rot], r.krot[key, rot]) * weights_of(qb, h)
            total = dot_nn(scores.astype(BF), r.val[key, chan])
            r.mixed[q, chan] = total
            squares = squares + jnp.sum(total * total, axis=-1, keepdims=True)
            r.ufull[q, pl.ds(pl.multiple_of(j * C + h * HEAD, HEAD), HEAD)] = (
                total * r.gpre[q, chan]
            ).astype(BF)
        r.ss[j, :, q] = jnp.transpose(jnp.broadcast_to(squares, (B, 128)))[0:8, :]

    def ss_block(owner):
        return r.ss.at[owner]

    for qb in range(NB):
        attend(qb)
        share_send(1 + qb, u_block(qb))
        if qb == NB - 1:
            share_send(1 + NB, ss_block)
        if qb == 0:
            gather_forward(5)
            gather_send(8)
        if qb == 1:
            gather_wait(4)
            share_send(0, wo_block)
        if qb == 3:
            share_forward(0, wo_block)
        if qb == 2:
            gather_forward(6)
            gather_send(9)
        if qb > 0:
            share_forward(qb, u_block(qb - 1))
    share_forward(NB, u_block(NB - 1))
    share_forward(1 + NB, ss_block)
    gather_forward(7)
    gather_send(10)
    gather_forward(8)
    share_wait(0, wo_block)
    for qb in range(NB):
        share_wait(1 + qb, u_block(qb))
    share_wait(1 + NB, ss_block)
    early = [copy for copy, when in pending]

    total_ss = r.ss[0]
    for owner in range(1, mp):
        total_ss = total_ss + r.ss[owner]
    inverse = lax.rsqrt(total_ss * (1.0 / D) + EPSILON)
    for t in range(T // 128):
        q = slice(t * 128, t * 128 + 128)
        r.rcol[q, :] = jnp.transpose(jnp.broadcast_to(inverse[0:1, q], (128, 128)))

    def hidden_tile(t):
        q = rows_of(t, TB)
        out = widen(r.rcol[q, :], D) * dot_nn(r.ufull[q, :], r.wo[...])
        hidden = r.xv[q, :].astype(F32) + out
        scale = lax.rsqrt(jnp.mean(hidden * hidden, axis=-1, keepdims=True) + EPSILON)
        r.nmid[q, :] = (hidden * scale).astype(BF)

        @pl.when(t == j)
        def _():
            r.hown[...] = hidden

    each(T // TB, hidden_tile)
    gather_wait(5)
    gather_wait(6)

    def gate_tile(t):
        q = rows_of(t, TT)
        r.gact[q, 0:F] = to_units(r.nmid[q, :], 1)

    each(T // TT, gate_tile)
    gather_forward(9)
    gather_wait(7)
    gather_wait(8)

    def up_tile(t):
        q = rows_of(t, TT)
        upper = to_units(r.nmid[q, :], 2)
        r.uact[q, :] = upper.astype(BF)
        r.prod[q, :] = (r.gact[q, 0:F] * upper).astype(BF)

    each(T // TT, up_tile)
    put_ff_grad(0, r.prod, r.up)
    gather_forward(10)
    scatter_first(5, 6)
    gather_wait(9)
    gather_wait(10)

    def mid_block(x, c):
        q = rows_of(x * 2 + c, TB)
        g = to_units(r.up[q, :], 0)
        grad_gate, grad_up = (g * r.uact[q, :].astype(F32)).astype(BF), (g * r.gact[q, 0:F]).astype(BF)
        r.ggate[q, :] = grad_gate
        r.gup[q, :] = grad_up
        r.part[x, c] = (to_model(grad_gate, 1) + to_model(grad_up, 2)).astype(BF)

    used = sum_begin(0, 0, mid_block)
    scatter_handed(5)
    scatter_second(6)
    put_ff_grad(1, r.ggate, r.nmid)
    scatter_first(7, 8)
    scatter_handed(6)

    def back_tile(t):
        q = rows_of(t, 128)
        here = rows_of(j * (TB // 128) + t, 128)
        grad = sum_tile(0, q)
        hidden = r.hown[q, :]
        scale = lax.rsqrt(jnp.mean(hidden * hidden, axis=-1, keepdims=True) + EPSILON)
        normed = hidden * scale
        inner = jnp.mean(grad * normed, axis=-1, keepdims=True)
        out = r.up[here, :].astype(F32) + scale * (grad - normed * inner)
        low = out.astype(BF)
        r.hlow[here, :] = low
        mixer_out = hidden - r.xown[q, :].astype(F32)
        product = jnp.sum(low.astype(F32) * mixer_out, axis=-1, keepdims=True) * (1.0 / D)
        r.inn[j, :, q] = jnp.transpose(jnp.broadcast_to(product, (128, 128)))[0:8, :]

    def token_block(ref):
        return lambda owner: ref.at[rows_of(owner, TB)]

    BO, IN, GM, HL, IG = 2 + NB, 3 + NB, 4 + NB, 9 + NB, 9 + NB + NT

    def inn_block(owner):
        return r.inn.at[owner]

    def half_block(ref, t):
        return lambda owner: ref.at[rows_of(owner * NT + t, 128)]

    for t in range(NT):
        sum_arrived(0, 0, t)
        back_tile(t)
        share_send(HL + t, half_block(r.hlow, t))
    share_send(IN, inn_block)
    put_ff_grad(2, r.gup, r.nmid)
    scatter_first(9, 10)
    scatter_second(5)
    scatter_second(7)
    for t in range(NT):
        share_forward(HL + t, half_block(r.hlow, t))
    share_forward(IN, inn_block)
    for copy in used:
        settle(copy)

    def expand_block(x, c):
        q = rows_of(x * 2 + c, TB)
        r.part[x, c] = to_model(r.prod[q, :], 0).astype(BF)

    scatter_handed(7)
    scatter_second(8)
    used = sum_begin(1, 1, expand_block)
    for t in range(NT):
        share_wait(HL + t, half_block(r.hlow, t))
    share_wait(IN, inn_block)
    for owner in range(mp):
        for t in range(TB // 128):
            row = r.inn[owner, 0:1, t * 128:(t + 1) * 128]
            q = slice(owner * TB + t * 128, owner * TB + (t + 1) * 128)
            r.icol[q, :] = jnp.transpose(jnp.broadcast_to(row, (128, 128)))

    wo_rows = rows_of(j, C)

    def gated_tile(t):
        q = rows_of(t, TT)
        low = r.hlow[q, :]
        grad = dot_nt(low, r.wo[wo_rows, :])
        inner = widen(r.icol[q, :], C)
        inverse = widen(r.rcol[q, :], C)
        normed = r.mixed[q, :] * inverse
        r.gproj[3][q, :] = (grad * normed).astype(BF)
        r.gmix[q, :] = (inverse * (grad * r.gpre[q, :] - normed * inner)).astype(BF)
        r.rh[q, :] = (inverse * r.hlow[q, jcols].astype(F32)).astype(BF)

    each(T // TT, gated_tile)
    put_grad(4, r.ufull, r.rh)
    scatter_first(4)
    scatter_handed(8)

    def swish_back(pre, grad):
        gate = jax.nn.sigmoid(pre)
        return grad * (gate * (1.0 + pre * (1.0 - gate)))

    def attend_back(qb):
        q, key = slice(qb * B, (qb + 1) * B), keys_of(qb)
        for h in range(H):
            rot = slice(2 * h * HEAD, 2 * (h + 1) * HEAD)
            chan = slice(h * HEAD, (h + 1) * HEAD)
            weights = weights_of(qb, h)
            scores = (dot_nt(r.qrot[q, rot], r.krot[key, rot]) * weights).astype(BF)
            back = (dot_nt(r.gmix[q, chan], r.val[key, chan]) * weights).astype(BF)
            dq = dot_nn(back, r.krot[key, rot])
            turned = dq[:, :HEAD] * r.cosv[q, :] + dq[:, HEAD:] * r.sinv[q, :]
            r.gproj[0][q, chan] = swish_back(r.qpre[q, chan], turned).astype(BF)
            dk = dot_tn(back, r.qrot[q, rot])
            dv = dot_tn(scores, r.gmix[q, chan])
            for kb in range(key.start // B, qb + 1):
                at = slice(kb * B - key.start, (kb + 1) * B - key.start)
                rows = slice(kb * B, (kb + 1) * B)
                dkb, dvb = dk[at], dv[at]
                if qb < min(kb + REACH, NB - 1):
                    dkb, dvb = dkb + r.dk[rows, rot], dvb + r.dv[rows, chan]
                if kb < qb:
                    r.dk[rows, rot], r.dv[rows, chan] = dkb, dvb
                else:
                    turned = dkb[:, :HEAD] * r.cosv[q, :] + dkb[:, HEAD:] * r.sinv[q, :]
                    r.gproj[1][q, chan] = swish_back(r.kpre[q, chan], turned).astype(BF)
                    r.gproj[2][q, chan] = dvb.astype(BF)

    def output_tile(t):
        q = rows_of(t, 128)
        r.bov[rows_of(j * NT + t, 128), :] = (r.hown[q, :] + sum_tile(1, q)).astype(BF)

    def late_core(x):
        return pltpu.make_async_remote_copy(
            src_ref=r.part.at[x, 1 - ci], dst_ref=r.recc.at[0, x], send_sem=r.acs.at[2, x], recv_sem=r.acr.at[2, x],
            device_id={"mp": xi * 2 + 1 - ci}, device_id_type=MESH,
        )

    def late_chip(x, d, t):
        q = slice(t * 128, (t + 1) * 128)
        return pltpu.make_async_remote_copy(
            src_ref=r.part.at[x, ci, q], dst_ref=r.recx.at[0, d - 1, q], send_sem=r.axs.at[2, d - 1, t],
            recv_sem=r.axr.at[2, d - 1, t], device_id={"mp": x * 2 + ci}, device_id_type=MESH,
        )

    def blocks_in(qb):
        return [divmod(at, 2) for at in range(qb * B // TB, (qb + 1) * B // TB)]

    def late_begin(x, c):
        q = slice((x * 2 + c) * TB, (x * 2 + c + 1) * TB)
        out = dot_nt(r.gproj[0][q, :], r.mixw[0])
        for k in range(1, 4):
            out = out + dot_nt(r.gproj[k][q, :], r.mixw[k])
        r.part[x, c] = out.astype(BF)

        @pl.when(ci != c)
        def _():
            late_core(x).start()

    def late_pass(x, c):
        @pl.when(ci == c)
        def _():
            arrived(r.recc.at[0, x], r.acr.at[2, x])

        @pl.when((ci == c) & (xi != x))
        def _():
            for t in range(NT):
                q = slice(t * 128, (t + 1) * 128)
                r.part[x, c, q] = (r.part[x, c, q].astype(F32) + r.recc[0, x, q].astype(F32)).astype(BF)
                late_chip(x, lax.rem(x - xi + X, X), t).start()

    put_grad(3, r.nint, r.gproj[3], turned=True)
    scatter_first(3)
    scatter_second(9)
    for qb in range(NB - 1, -1, -1):
        attend_back(qb)
        if qb == NB - 1:
            for t in range(NT):
                sum_arrived(1, 1, t)
            each(TB // 128, output_tile)
            share_send(BO, token_block(r.bov))
            for copy in used + early:
                settle(copy)
        for x, c in blocks_in(qb):
            late_begin(x, c)
        if qb < NB - 1:
            for x, c in blocks_in(qb + 1):
                late_pass(x, c)
        if qb == NB - 1:
            scatter_handed(9)
            scatter_second(10)
            finish_ff(5)
        if qb == max(NB - 2, 0):
            scatter_handed(4, 10)
            scatter_second(3)
            share_forward(BO, token_block(r.bov))
            finish_ff(6)
        if qb == max(NB - 3, 0):
            scatter_second(4)
            scatter_handed(3)
            finish_ff(7)
    for x, c in blocks_in(0):
        late_pass(x, c)
    pending.extend((late_core(x), None) for x in range(X))
    pending.extend((late_chip(lax.rem(xi + d, X), d, t), None) for d in range(1, X) for t in range(NT))
    for k in (2, 0):
        put_grad(k, r.nint, r.gproj[k], turned=True)
        scatter_first(k)
    finish_ff(8)
    scatter_second(2)
    put_grad(1, r.nint, r.gproj[1], turned=True)
    scatter_first(1)
    scatter_handed(2)
    finish_ff(9, 10)

    def input_tile(t):
        q = rows_of(t, 128)
        grad = sum_tile(0, q)
        v = r.xown[q, :].astype(F32)
        scale = lax.rsqrt(jnp.mean(v * v, axis=-1, keepdims=True) + EPSILON)
        normed = v * scale
        inner = jnp.mean(grad * normed, axis=-1, keepdims=True)
        r.igv[rows_of(j * NT + t, 128), :] = (r.hlow[rows_of(j * NT + t, 128), :].astype(F32) + scale * (grad - normed * inner)).astype(BF)

    for t in range(NT):
        for d in range(1, X):
            arrived(r.recx.at[0, d - 1, t * 128:(t + 1) * 128], r.axr.at[2, d - 1, t])
        input_tile(t)
        share_send(IG + t, half_block(r.igv, t))
    scatter_second(0, 1)
    share_wait(BO, token_block(r.bov))
    stores = [load(r.bov, r.bo, 0)]

    def grad_block(k):
        return lambda owner: r.gmv.at[k * S:(k + 1) * S, pl.ds(pl.multiple_of(owner * C, C), C)]

    for k in (4, 3, 2, 0, 1):
        total = scatter_total(k).astype(BF)
        r.gmv[k * S:(k + 1) * S, jcols] = total
        r.sqs[...] += squares_of(total.astype(F32))
        share_send(GM + k, grad_block(k))

    r.s1[j] = r.sqs[...]
    for d in range(1, mp):
        go(r.s1.at[j], r.s1.at[j], r.q1s.at[d], r.q1r.at[d], mp=lax.rem(j + d, mp))
    for t in range(NT):
        share_forward(IG + t, half_block(r.igv, t))
    for d in range(1, mp):
        arrived(r.s1.at[lax.rem(j - d + mp, mp)], r.q1r.at[d])
    total = r.s1[0]
    for owner in range(1, mp):
        total = total + r.s1[owner]
    r.s2[i] = total
    for d in range(1, n):
        go(r.s2.at[i], r.s2.at[i], r.q2s.at[d], r.q2r.at[d], dp=lax.rem(i + d, n))
    for k in (4, 3, 2, 0, 1):
        share_forward(GM + k, grad_block(k))
    for d in range(1, n):
        arrived(r.s2.at[lax.rem(i - d + n, n)], r.q2r.at[d])
    total = r.s2[0]
    for owner in range(1, n):
        total = total + r.s2[owner]
    r.sqo[...] = total

    for t in range(NT):
        share_wait(IG + t, half_block(r.igv, t))
    stores.append(load(r.igv, r.ig, 1))
    for k in (4, 3, 2, 0, 1):
        share_wait(GM + k, grad_block(k))
        stores.append(load(r.gmv.at[k * S:(k + 1) * S], r.gmo.at[k], 2 + k))
    for copy in stores:
        copy.wait()
    for copy, when in pending:
        guarded(when, copy.wait_send)


def fused(p, *operands):
    scratch = scratch_of(p)
    names = IN_NAMES + OUT_NAMES + tuple(scratch)
    anywhere = pl.BlockSpec(memory_space=pl.ANY)
    vmem = pl.BlockSpec(memory_space=pltpu.VMEM)
    smem = pl.BlockSpec(memory_space=pltpu.SMEM)
    return pl.pallas_call(
        partial(body, p, names),
        out_shape=(
            jax.ShapeDtypeStruct((p.T, p.D), BF),
            jax.ShapeDtypeStruct((p.T, p.D), BF),
            jax.ShapeDtypeStruct((5, p.S, p.D), BF),
            jax.ShapeDtypeStruct((2, p.F, p.S) if p.FD else (2, p.S, p.F), F32),
            jax.ShapeDtypeStruct((p.F, p.S) if p.FD else (p.S, p.F), F32),
            jax.ShapeDtypeStruct((8, 128), F32),
        ),
        in_specs=[anywhere, anywhere, vmem, smem] + [anywhere] * 5,
        out_specs=(anywhere, anywhere, anywhere, vmem, vmem, vmem),
        scratch_shapes=list(scratch.values()),
        compiler_params=pltpu.CompilerParams(
            collective_id=0, has_side_effects=True, vmem_limit_bytes=VMEM_LIMIT
        ),
    )(*operands)


VMEM_LIMIT = 64 * 2**20 - 2**18


def renew(weight, momentum, shadow, grad, clip_factor):
    clipped = grad * clip_factor
    velocity = MOMENTUM * momentum + clipped
    updated = weight - LEARN_RATE * (clipped + MOMENTUM * velocity)
    average = SHADOW_DECAY * shadow + (1.0 - SHADOW_DECAY) * updated
    return (velocity, average, updated)


def update_body(cuts, *refs):
    kinds, pieces = len(cuts), sum(len(c) for c in cuts)
    sq, carried = refs[0], refs[1:3]
    ins = [refs[3 + 4 * w:7 + 4 * w] for w in range(kinds)]
    refs = refs[3 + 4 * kinds:]
    norm_out, carried_out = refs[0], refs[1:3]
    outs = [refs[3 + 3 * w:6 + 3 * w] for w in range(kinds)]
    refs = refs[3 + 3 * kinds:]
    held = [refs[4 * w:4 * w + 4] for w in range(kinds)]
    made = [refs[4 * kinds + 3 * w:4 * kinds + 3 * w + 3] for w in range(kinds)]
    bounce, (in_sem, out_sem, carry_sem) = refs[7 * kinds:7 * kinds + 2], refs[7 * kinds + 2:]
    loads, order = {}, [(w, c) for w in range(kinds) for c in range(len(cuts[w]))]
    for at, (w, c) in enumerate(order):
        for a in range(4):
            cut = cuts[w][c]
            loads[at, a] = pltpu.make_async_copy(ins[w][a].at[cut], held[w][a].at[cut], in_sem.at[at, a])
            loads[at, a].start()
    carry = [pltpu.make_async_copy(carried[a], bounce[a], carry_sem.at[a]) for a in range(2)]
    for copy in carry:
        copy.start()
    copies = []
    norm = jnp.sqrt(jnp.broadcast_to(jnp.sum(sq[...]), (8, 128)))
    norm_out[...] = norm
    clip_factor = 1.0 / jnp.maximum(jnp.max(norm), 1.0)
    for at, (w, c) in enumerate(order):
        cut = cuts[w][c]
        for a in range(4):
            loads[at, a].wait()
        new = renew(*[held[w][a][cut] for a in range(3)], held[w][3][cut].astype(F32), clip_factor)
        for a in range(3):
            made[w][a][cut] = new[a]
            copy = pltpu.make_async_copy(made[w][a].at[cut], outs[w][a].at[cut], out_sem.at[at, a])
            copy.start()
            copies.append(copy)
    for a in range(2):
        carry[a].wait()
        copy = pltpu.make_async_copy(bounce[a], carried_out[a], carry_sem.at[2 + a])
        copy.start()
        copies.append(copy)
    for copy in copies:
        copy.wait()


def update(sq, carried, weights):
    cuts = [[c for c in range(g[0].shape[0])] if g[0].ndim == 3 else [slice(None)] for g in weights]
    pieces = sum(len(c) for c in cuts)
    anywhere = pl.BlockSpec(memory_space=pl.ANY)
    vmem = pl.BlockSpec(memory_space=pltpu.VMEM)
    flat_in = [a for group in weights for a in group]
    flat_out = [a for group in weights for a in group[:3]]
    dma = pltpu.SemaphoreType.DMA
    size = sum(a.size * a.dtype.itemsize for a in flat_in + flat_out + 2 * list(carried))
    return pl.pallas_call(
        partial(update_body, cuts),
        out_shape=[jax.ShapeDtypeStruct(a.shape, a.dtype) for a in [sq, *carried, *flat_out]],
        in_specs=[vmem] + [anywhere] * (2 + len(flat_in)),
        out_specs=[vmem] + [anywhere] * (2 + len(flat_out)),
        scratch_shapes=[pltpu.VMEM(a.shape, a.dtype) for a in flat_in + flat_out + list(carried)]
        + [dma((pieces, 4)), dma((pieces, 3)), dma((4,))],
        cost_estimate=pl.CostEstimate(flops=size, bytes_accessed=size, transcendentals=0),
        compiler_params=pltpu.CompilerParams(vmem_limit_bytes=VMEM_LIMIT),
    )(sq, *carried, *flat_in)


def turn_tables(tokens):
    theta = np.float32(10000.0) ** (-np.arange(HEAD, dtype=np.float32) / np.float32(HEAD))
    angle = np.arange(tokens, dtype=np.float32)[:, None] * theta.astype(np.float32)[None, :]
    angle = angle.astype(np.float64)
    return np.cos(angle).astype(np.float32), np.sin(angle).astype(np.float32)


def per_device(mesh, block_input, segment_ids, live_length, output_grad, mixer_weight, mixer_momentum, mixer_shadow,
               expand_weight, expand_momentum, expand_shadow, shrink_weight, shrink_momentum, shrink_shadow):
    rows, length, width = block_input.shape
    p = plan_of(mesh, length, width, shrink_weight.shape[0])
    turn = (lambda v: jnp.swapaxes(v, -1, -2)) if p.FD else (lambda v: v)
    if p.FD:
        shards = (turn(expand_weight), shrink_weight)
    else:
        shards = (jnp.concatenate([shrink_weight.T[None], expand_weight], axis=0).astype(BF), shrink_weight)
    cos, sin = turn_tables(length)
    out, grad_in, gm, ge, gs, sq = fused(
        p, block_input[0], output_grad[0], segment_ids, live_length, jnp.asarray(cos), jnp.asarray(sin), mixer_weight, *shards
    )
    new = update(sq, (out, grad_in), (
        (mixer_weight, mixer_momentum, mixer_shadow, gm),
        (turn(expand_weight), turn(expand_momentum), turn(expand_shadow), ge),
        (shrink_weight, shrink_momentum, shrink_shadow, gs if p.FD else gs.T),
    ))
    norm, out, grad_in = new[:3]
    return (out[None], grad_in[None], norm[0, 0], *new[3:6], *(turn(v) for v in new[6:9]), *new[9:12])


def solution(mesh):
    row, mixer, expand, shrink = P("dp", None, None), P(None, "dp", None), P(None, "dp", "mp"), P("mp", "dp")
    return jax.shard_map(
        partial(per_device, mesh),
        mesh=mesh,
        in_specs=(row, P("dp", None), P("dp"), row) + (mixer,) * 3 + (expand,) * 3 + (shrink,) * 3,
        out_specs=(row, row, P()) + (mixer,) * 3 + (expand,) * 3 + (shrink,) * 3,
        check_vma=False,
    )
```

```python
from functools import partial
from types import SimpleNamespace

import jax
import jax.numpy as jnp
import numpy as np
from jax import lax
from jax.experimental import pallas as pl
from jax.experimental.pallas import tpu as pltpu
from jax.sharding import PartitionSpec as P

HEAD = 128
EPSILON = 1e-06
LEARN_RATE = 32.0
MOMENTUM = 0.5
SHADOW_DECAY = 0.5
LAYER_PLACE = 12.0 / 24.0
LONGEST = 512
FF_ORDER = (1, 2, 0)
Y_FIRST = (4, 6)
Z_FIRST = (5, 2)
STRAIGHT = (0, 1)
MESH = pl.DeviceIdType.MESH
BF = jnp.bfloat16
F32 = jnp.float32


def dot_nn(a, b):
    return lax.dot_general(a, b, (((1,), (0,)), ((), ())), preferred_element_type=F32)


def dot_nt(a, b):
    return lax.dot_general(a, b, (((1,), (1,)), ((), ())), preferred_element_type=F32)


def dot_tn(a, b):
    return lax.dot_general(a, b, (((0,), (0,)), ((), ())), preferred_element_type=F32)


def rows_of(index, size):
    return pl.ds(pl.multiple_of(index * size, size), size)


def each(count, body):
    def step(t, carry):
        body(t)
        return carry

    lax.fori_loop(0, count, step, 0)


def widen(column, width):
    return jnp.concatenate([column] * (width // 128), axis=1)


def plan_of(mesh, tokens, width, inner):
    n, mp = mesh.shape["dp"], mesh.shape["mp"]
    lo, core = 2, 2
    return SimpleNamespace(
        n=n, mp=mp, LO=lo, HI=n // lo, X=mp // core, T=tokens, D=width, C=width // mp, F=inner,
        S=width // n, H=width // mp // HEAD, TB=tokens // mp, B=min(256, tokens),
        NT=tokens // mp // 128, FD=(width // n) % 128 == 0,
    )


def scratch_of(p):
    T, D, C, F, S, HI, LO, X, TB, B = p.T, p.D, p.C, p.F, p.S, p.HI, p.LO, p.X, p.TB, p.B
    dma = pltpu.SemaphoreType.DMA
    v = pltpu.VMEM
    return dict(
        mixw=v((4, D, C), BF), wo=v((D, D), BF), ffw=v((3, F, D) if p.FD else (3, D, F), BF),
        xown=v((TB, D), BF), nin=v((T, D), BF), nint=v((D, T), BF), up=v((T, D), BF),
        cosv=v((T, HEAD), F32), sinv=v((T, HEAD), F32),
        segq=v((T, 128), F32), segk=v((8, T), F32), dec=v((2, p.H, B, B), F32),
        qpre=v((T, C), F32), kpre=v((T, C), F32), gpre=v((T, C), F32), val=v((T, C), BF),
        qrot=v((T, 2 * C), BF), krot=v((T, 2 * C), BF), mixed=v((T, C), F32),
        ufull=v((T, D), BF), ss=v((p.mp, 8, T), F32), rcol=v((T, 128), F32),
        inn=v((p.mp, 8, TB), F32), hown=v((TB, D), F32),
        gact=v((T, max(F, 2 * C + HEAD)), F32), uact=v((T, F), BF), prod=v((T, F), BF), ggate=v((T, F), BF), gup=v((T, F), BF),
        part=v((X, 2, TB, D), BF), recc=v((2, X, TB, D), BF), recx=v((2, X - 1, TB, D), BF),
        xv=v((T, D), BF),
        gm=v((5, HI, LO, S, C), BF), rym=v((5, HI, S, C), BF), rzm=v((5, HI - 1, S, C), BF),
        gf=v((3, LO, F, HI * S) if p.FD else (3, HI, LO, S, F), BF),
        ryf=v((3, F, HI * S) if p.FD else (3, HI, S, F), BF),
        rzf=v((3, HI - 1, F, S) if p.FD else (3, HI - 1, S, F), BF),
        relm=v((3, S, C), BF), relf=v((3, F, S) if p.FD else (3, S, F), BF),
        othm=v((HI, S, C), BF), othf=v((HI, F // 2, S) if p.FD else (HI, S // 2, F), BF),
        sqs=v((8, 128), F32), s1=v((p.mp, 8, 128), F32), s2=v((p.n, 8, 128), F32),
        loc=dma((10,)),
        zs=dma((11, HI - 1)), zr=dma((11, HI - 1)), us=dma((len(Y_FIRST), HI - 1)), ur=dma((len(Y_FIRST), HI - 1)),
        zp=dma((11,)), yp=dma((len(Y_FIRST),)), ys=dma((11, HI)), yr=dma((11, HI)),
        xs=dma((20, X - 1)), xr=dma((20, X - 1)), cs=dma((20, X)), cr=dma((20, X)),
        acs=dma((3, X)), acr=dma((3, X)), axs=dma((3, X - 1, p.NT)), axr=dma((3, X - 1, p.NT)),
        bys=dma((11,)), byr=dma((11,)), bzs=dma((11, HI - 1)), bzr=dma((11, HI - 1)),
        bts=dma((11,)), btr=dma((11,)), ozs=dma((2, HI - 1)), ozr=dma((2, HI - 1)), ots=dma((2,)), otr=dma((2,)),
        ags=dma((p.NT, p.mp)), agr=dma((p.NT, p.mp)), ahs=dma((2, p.mp)), ahr=dma((2, p.mp)),
        q1s=dma((p.mp,)), q1r=dma((p.mp,)), q2s=dma((p.n,)), q2r=dma((p.n,)),
    )


IN_NAMES = ("x", "og", "seg", "live", "cos", "sin", "mixsh", "exsh", "shsh")
OUT_NAMES = ("bo", "ig", "gmo", "geo", "gso", "sqo")


def body(p, names, *refs):
    r = SimpleNamespace(**dict(zip(names, refs)))
    n, mp, LO, HI, X, T, D, C, F, S, H, TB, B = (
        p.n, p.mp, p.LO, p.HI, p.X, p.T, p.D, p.C, p.F, p.S, p.H, p.TB, p.B,
    )
    NT, TT = p.NT, min(512, p.T)
    i, j = lax.axis_index("dp"), lax.axis_index("mp")
    zi, yi = i // LO, lax.rem(i, LO)
    xi, ci = j // 2, lax.rem(j, 2)
    jcols = pl.ds(pl.multiple_of(j * C, C), C)
    pending = []
    r.nmid = r.nin
    r.bov, r.igv, r.gmv = r.up, r.ufull, r.wo
    r.dk, r.icol, r.dv = r.gact.at[:, 0:2 * C], r.gact.at[:, 2 * C:2 * C + HEAD], r.mixed
    r.gproj = [r.ggate.at[:, 0:C], r.ggate.at[:, C:2 * C], r.gup.at[:, 0:C], r.gup.at[:, C:2 * C]]
    r.ggated, r.hcols, r.gmix, r.rh = [r.xv.at[:, a * C:(a + 1) * C] for a in range(4)]
    r.hsend, r.gsend = r.uact.at[:, 0:C], r.uact.at[:, C:2 * C]

    def go(src, dst, ssem, rsem, when=None, **device):
        copy = pltpu.make_async_remote_copy(
            src_ref=src, dst_ref=dst, send_sem=ssem, recv_sem=rsem,
            device_id=device, device_id_type=MESH,
        )
        guarded(when, copy.start)
        pending.append((copy, when))
        return copy

    def guarded(when, act):
        if when is None:
            act()
        else:
            pl.when(when)(lambda: act())

    def arrived(dst, sem):
        pltpu.make_async_copy(dst, dst, sem).wait()

    def settle(copy):
        for other, when in pending:
            if other is copy:
                guarded(when, copy.wait_send)
        pending[:] = [entry for entry in pending if entry[0] is not copy]

    def load(src, dst, sem):
        copy = pltpu.make_async_copy(src, dst, r.loc.at[sem])
        copy.start()
        return copy

    own_mix = [load(r.mixsh.at[k, :, jcols], r.qpre.at[k * S:(k + 1) * S], k) for k in range(5)]
    if p.FD:
        stage = [r.gact.at[0:F, m * S:(m + 1) * S] for m in range(3)]
        own_ff = [load(r.shsh if m == 0 else r.exsh.at[m - 1], stage[m], 5 + m) for m in range(3)]
    else:
        own_ff = [load(r.exsh.at[m], r.ffw.at[m, rows_of(i, S)], 5 + m) for m in range(3)]
    load_x = load(r.x, r.xv, 8)
    load_og = load(r.og, r.up, 9)

    def enter():
        barrier = pltpu.get_barrier_semaphore()
        for d in range(1, n):
            pl.semaphore_signal(barrier, inc=1, device_id={"dp": lax.rem(i + d, n)}, device_id_type=MESH)
        for d in range(1, mp):
            pl.semaphore_signal(barrier, inc=1, device_id={"mp": lax.rem(j + d, mp)}, device_id_type=MESH)
        pl.semaphore_wait(barrier, n - 1 + mp - 1)

    def slot(k, device):
        rows = rows_of(device, S)
        if k == 4:
            return r.wo.at[rows, jcols]
        if k < 4:
            return r.mixw.at[k, rows]
        m, half = FF_ORDER[(k - 5) // 2], (k - 5) % 2
        if p.FD:
            return r.ffw.at[m, half * F // 2:(half + 1) * F // 2, rows]
        return r.ffw.at[m, pl.ds(pl.multiple_of(device * S + half * S // 2, S // 2), S // 2)]

    def gather_ready(k):
        if k < 5:
            own_mix[k].wait()
            slot(k, i)[...] = r.qpre[k * S:(k + 1) * S, :].astype(BF)
        else:
            m, half = FF_ORDER[(k - 5) // 2], (k - 5) % 2
            if half == 0:
                own_ff[m].wait()
            if p.FD:
                slot(k, i)[...] = stage[m][half * F // 2:(half + 1) * F // 2, :].astype(BF)

    relays = HI == 4
    next_to_end = (zi == 1) | (zi == 2)

    def along_z(block, ssem, rsem):
        for d in range(1, HI):
            to = lax.rem(zi + d, HI)
            near = (jnp.abs(to - zi) < 3) if relays else None
            go(block, block, ssem.at[d - 1], rsem.at[d - 1], when=near, dp=to * LO + yi)

    def hand_on(block, ssem, rsem):
        if relays:
            end = jnp.where(zi == 2, 3, 0)
            go(block, block, ssem, rsem.at[jnp.where(zi == 2, 2, 0)], when=next_to_end, dp=end * LO + yi)

    def from_z_source(k, d, y):
        return slot(k, lax.rem(zi - d + HI, HI) * LO + y)

    WAYS = [2, 1, *range(3, HI)]

    def gather_send(k):
        src = slot(k, i)
        along_z(src, r.zs.at[k], r.zr.at[k])
        go(src, src, r.ys.at[k, 0], r.yr.at[k, 0], dp=zi * LO + 1 - yi)

    def gather_forward(k):
        if k - 1 in Y_FIRST:
            b = Y_FIRST.index(k - 1)
            block = from_z_source(k - 1, 2, 1 - yi)
            arrived(block, r.ur.at[b, 1])
            hand_on(block, r.yp.at[b], r.ur.at[b])
        if k in Y_FIRST:
            b = Y_FIRST.index(k)
            peers = slot(k, zi * LO + 1 - yi)
            arrived(peers, r.yr.at[k, 0])
            along_z(peers, r.us.at[b], r.ur.at[b])
        for d in WAYS:
            block = from_z_source(k, d, yi)
            arrived(block, r.zr.at[k, d - 1])
            if d == 2:
                hand_on(block, r.zp.at[k], r.zr.at[k])
            if k not in Y_FIRST:
                go(block, block, r.ys.at[k, d], r.yr.at[k, d], dp=zi * LO + 1 - yi)

    def gather_wait(k):
        for d in range(HI):
            if k not in Y_FIRST:
                arrived(from_z_source(k, d, 1 - yi), r.yr.at[k, d])
            elif d in (1, 3) or d > 3:
                arrived(from_z_source(k, d, 1 - yi), r.ur.at[Y_FIRST.index(k), d - 1])

    def share_send(s, block, src=None):
        own = block(j)
        src = own if src is None else src
        for d in range(1, X):
            go(src, own, r.xs.at[s, d - 1], r.xr.at[s, d - 1], mp=lax.rem(xi + d, X) * 2 + ci)
        go(src, own, r.cs.at[s, 0], r.cr.at[s, 0], mp=xi * 2 + 1 - ci)

    def share_forward(s, block):
        for d in range(1, X):
            part = block(lax.rem(xi - d + X, X) * 2 + ci)
            arrived(part, r.xr.at[s, d - 1])
            go(part, part, r.cs.at[s, d], r.cr.at[s, d], mp=xi * 2 + 1 - ci)

    def share_wait(s, block):
        for d in range(X):
            arrived(block(lax.rem(xi - d + X, X) * 2 + 1 - ci), r.cr.at[s, d])

    def sum_begin(s, b, compute):
        sent = []

        def to_sibling(d):
            to = lax.rem(xi + d, X)
            compute(to, 1 - ci)
            sent.append(go(
                r.part.at[to, 1 - ci], r.recc.at[b, to], r.acs.at[s, d], r.acr.at[s, d], mp=xi * 2 + 1 - ci
            ))

        for d in range(1, X):
            to_sibling(d)
        for d in range(1, X):
            to = lax.rem(xi + d, X)
            compute(to, ci)
            arrived(r.recc.at[b, to], r.acr.at[s, d])
            for t in range(NT):
                q = slice(t * 128, (t + 1) * 128)
                r.part[to, ci, q] = (
                    r.part[to, ci, q].astype(F32) + r.recc[b, to, q].astype(F32)
                ).astype(BF)
                sent.append(go(
                    r.part.at[to, ci, q], r.recx.at[b, d - 1, q], r.axs.at[s, d - 1, t], r.axr.at[s, d - 1, t],
                    mp=to * 2 + ci,
                ))
        to_sibling(0)
        compute(xi, ci)
        return sent

    def sum_arrived(s, b, t):
        if t == 0:
            arrived(r.recc.at[b, xi], r.acr.at[s, 0])
        for d in range(1, X):
            arrived(r.recx.at[b, d - 1, t * 128:(t + 1) * 128], r.axr.at[s, d - 1, t])

    def sum_tile(b, q):
        total = r.part[xi, ci, q].astype(F32) + r.recc[b, xi, q].astype(F32)
        for d in range(1, X):
            total = total + r.recx[b, d - 1, q].astype(F32)
        return total

    flat = p.FD

    def half_of(k):
        size = (F if flat else S) // 2
        return (k - 5) // 2, slice((k - 5) % 2 * size, ((k - 5) % 2 + 1) * size)

    def block_of(k, z, y):
        if k < 5:
            return r.gm.at[k, z, y]
        m, rows = half_of(k)
        return r.gf.at[m, y, rows, rows_of(z, S)] if flat else r.gf.at[m, z, y, rows]

    def from_y(k):
        if k < 5:
            return r.rym.at[k]
        m, rows = half_of(k)
        return r.ryf.at[m, rows] if flat else r.ryf.at[m, :, rows]

    def from_y_block(k, z):
        ref = from_y(k)
        return ref.at[:, rows_of(z, S)] if flat and k >= 5 else ref.at[z]

    def to_y(k):
        if k < 5:
            return r.gm.at[k, :, 1 - yi]
        m, rows = half_of(k)
        return r.gf.at[m, 1 - yi, rows] if flat else r.gf.at[m, :, 1 - yi, rows]

    def from_z(k, d, own=True):
        if not own:
            return (r.othm if k < 5 else r.othf).at[d - 1]
        if k < 5:
            return r.rzm.at[k, d - 1]
        m, rows = half_of(k)
        return r.rzf.at[m, d - 1, rows]

    def handed(k, own=True):
        if not own:
            return (r.othm if k < 5 else r.othf).at[HI - 1]
        if k < 5:
            return r.relm.at[max(k - 2, 0)]
        m, rows = half_of(k)
        return r.relf.at[m, rows]

    def z_sems(k, own):
        if own:
            return r.bzs.at[k], r.bzr.at[k], r.bts.at[k], r.btr.at[k]
        o = Z_FIRST.index(k)
        return r.ozs.at[o], r.ozr.at[o], r.ots.at[o], r.otr.at[o]

    def stepped(k):
        return relays and k not in STRAIGHT

    def far(d, back=False):
        other = lax.rem(zi + (HI - d if back else d), HI)
        return jnp.abs(other - zi) == 3

    def z_send(k, own, ways):
        y = yi if own else 1 - yi
        ssem, rsem, tsem, trsem = z_sems(k, own)
        for d in ways:
            to = lax.rem(zi + d, HI)
            block, dst = block_of(k, to, y), from_z(k, d, own)
            if stepped(k) and d != 2:
                go(block, handed(k, own), tsem, trsem, when=far(d), dp=jnp.where(zi == 0, 1, 2) * LO + yi)
                go(block, dst, ssem.at[d - 1], rsem.at[d - 1], when=jnp.logical_not(far(d)), dp=to * LO + yi)
            else:
                go(block, dst, ssem.at[d - 1], rsem.at[d - 1], dp=to * LO + yi)

    def z_send_handed(k, own):
        block = block_of(k, lax.rem(zi + 2, HI), yi if own else 1 - yi)

        @pl.when(next_to_end)
        def _():
            arrived(handed(k, own), z_sems(k, own)[3])
            block[...] = (block[...].astype(F32) + handed(k, own)[...].astype(F32)).astype(BF)

        z_send(k, own, [2])

    def z_total(k, own):
        for d in range(1, HI):
            wait = partial(arrived, from_z(k, d, own), z_sems(k, own)[1].at[d - 1])
            guarded(jnp.logical_not(far(d, back=True)) if stepped(k) and d != 2 else None, wait)
        total = block_of(k, zi, yi if own else 1 - yi)[...].astype(F32)
        for d in range(1, HI):
            total = total + from_z(k, d, own)[...].astype(F32)
        return total

    def clear_far_places():
        if not relays:
            return
        for d in (1, 3):
            @pl.when(far(d, back=True))
            def _(d=d):
                r.rzm[:, d - 1] = jnp.zeros((5, S, C), BF)
                for m in range(3):
                    r.rzf[m, d - 1] = jnp.zeros(r.rzf.shape[2:], BF)
                r.othm[d - 1] = jnp.zeros(r.othm.shape[1:], BF)
                r.othf[d - 1] = jnp.zeros(r.othf.shape[1:], BF)

    def near_ways(k):
        return [3, 1] if stepped(k) else list(range(1, HI))

    def scatter_first(*pieces):
        for k in pieces:
            if k in Z_FIRST:
                for own in (False, True):
                    z_send(k, own, near_ways(k))
            else:
                go(to_y(k), from_y(k), r.bys.at[k], r.byr.at[k], dp=zi * LO + 1 - yi)

    def scatter_second(*pieces):
        for k in pieces:
            if k in Z_FIRST:
                block = block_of(k, zi, 1 - yi)
                block[...] = z_total(k, False).astype(BF)
                go(block, from_y_block(k, zi), r.bys.at[k], r.byr.at[k], dp=zi * LO + 1 - yi)
                continue
            arrived(from_y(k), r.byr.at[k])
            for d in range(1, HI):
                to = lax.rem(zi + d, HI)
                block = block_of(k, to, yi)
                block[...] = (block[...].astype(F32) + from_y_block(k, to)[...].astype(F32)).astype(BF)
            z_send(k, True, near_ways(k))

    def scatter_handed(*pieces):
        for k in pieces:
            if stepped(k):
                if k in Z_FIRST:
                    z_send_handed(k, False)
                z_send_handed(k, True)

    def scatter_total(k):
        if k in Z_FIRST:
            arrived(from_y_block(k, zi), r.byr.at[k])
        return z_total(k, True) + from_y_block(k, zi)[...].astype(F32)

    def squares_of(total):
        squared = total * total
        if squared.shape[-1] % 128:
            corner = (lax.broadcasted_iota(jnp.int32, (8, 128), 0) + lax.broadcasted_iota(jnp.int32, (8, 128), 1)) == 0
            return jnp.where(corner, jnp.sum(squared), 0.0)
        folded = jnp.sum(squared.reshape(-1, 8, squared.shape[-1]), axis=0)
        return sum(folded[:, c:c + 128] for c in range(0, folded.shape[-1], 128))

    def finish_ff(*pieces):
        for k in pieces:
            m, rows = half_of(k)
            total = scatter_total(k)
            if m == 0:
                r.gso[rows] = total
            else:
                r.geo[m - 1, rows] = total
            r.sqs[...] += squares_of(total)

    def put_grad(k, lhs, rhs, turned=False):
        g = r.gm.at[k] if k < 5 else r.gf.at[k - 5]
        per = TT // (LO * S)

        def tile(t):
            if turned:
                out = dot_nn(lhs[rows_of(t, TT), :], rhs[...])
            else:
                out = dot_tn(lhs[:, rows_of(t, TT)], rhs[...])
            g[pl.ds(t * per, per)] = out.astype(BF).reshape(per, LO, S, out.shape[-1])

        each(D // TT, tile)

    def put_ff_grad(m, units, model):
        if not flat:
            return put_grad(5 + m, model, units)
        for f in range(0, F, 384):
            q = slice(f, min(f + 384, F))
            out = dot_tn(units[:, q], model[...]).astype(BF)
            for y in range(LO):
                for z in range(HI):
                    r.gf[m, y, q, z * S:(z + 1) * S] = out[:, (z * LO + y) * S:(z * LO + y + 1) * S]

    def to_units(a, m):
        return dot_nt(a, r.ffw[m]) if flat else dot_nn(a, r.ffw[m])

    def to_model(a, m):
        return dot_nn(a, r.ffw[m]) if flat else dot_nt(a, r.ffw[m])

    gather_ready(0)
    gather_ready(1)
    enter()
    gather_send(0)
    gather_send(1)
    gather_ready(2)
    gather_send(2)
    r.sqs[...] = jnp.zeros_like(r.sqs)
    clear_far_places()

    length = r.live[0]
    load_x.wait()

    def norm_tile(t):
        q = rows_of(t, 128)
        v = r.xv[q, :].astype(F32)
        r.nin[q, :] = (v * lax.rsqrt(jnp.mean(v * v, axis=-1, keepdims=True) + EPSILON)).astype(BF)

    each(T // 128, norm_tile)
    for k in range(3, 11):
        gather_ready(k)
    load_x_own = load(r.x.at[rows_of(j, TB)], r.xown, 8)
    load_og.wait()
    load_cos = load(r.cos, r.cosv, 0)
    load_sin = load(r.sin, r.sinv, 1)

    def live_tile(t):
        q = rows_of(t, 128)
        place = lax.broadcasted_iota(jnp.int32, (128, D), 0) + t * 128
        r.up[q, :] = jnp.where(place < length, r.up[q, :].astype(F32), 0.0).astype(BF)

    each(T // 128, live_tile)

    place = lax.broadcasted_iota(jnp.int32, (1, T), 1)
    segment = r.seg[...].astype(F32)
    r.segk[...] = jnp.broadcast_to(jnp.where(place < length, segment, -2.0), (8, T))
    seg_q = jnp.where(place < length, segment, -1.0)
    for t in range(T // 128):
        q = slice(t * 128, t * 128 + 128)
        r.segq[q, :] = jnp.transpose(jnp.broadcast_to(seg_q[:, q], (128, 128)))

    down = lax.broadcasted_iota(jnp.int32, (B, B), 0)
    over = lax.broadcasted_iota(jnp.int32, (B, B), 1)
    heads = D // HEAD

    def rate_of(h):
        return -(8.0 * (j * H + h).astype(F32) / heads) * (1.0 - LAYER_PLACE)

    for h in range(H):
        rate = rate_of(h)
        for o in range(2):
            distance = down - over + o * B
            fade = jnp.exp(rate * jnp.maximum(distance, 0).astype(F32))
            r.dec[o, h] = jnp.where(distance >= 0, fade, 0.0)

    for t in range(D // 128):
        q = slice(t * 128, t * 128 + 128)
        r.nint[q, :] = jnp.transpose(r.nin[:, q])
    load_cos.wait()
    load_sin.wait()
    load_x_own.wait()

    def turn_into(pre_ref, rot_ref, k):
        def tile(t):
            q = rows_of(t, TT)
            pre = dot_nn(r.nin[q, :], r.mixw[k])
            pre_ref[q, :] = pre
            act = pre * jax.nn.sigmoid(pre)
            c, s = r.cosv[q, :], r.sinv[q, :]
            for h in range(H):
                a = act[:, h * HEAD:(h + 1) * HEAD]
                rot_ref[q, 2 * h * HEAD:(2 * h + 1) * HEAD] = (a * c).astype(BF)
                rot_ref[q, (2 * h + 1) * HEAD:(2 * h + 2) * HEAD] = (a * s).astype(BF)

        each(T // TT, tile)

    def project_into(ref, k):
        def tile(t):
            q = rows_of(t, TT)
            ref[q, :] = dot_nn(r.nin[q, :], r.mixw[k]).astype(ref.dtype)

        each(T // TT, tile)

    gather_forward(0)
    gather_send(3)
    gather_forward(1)
    gather_send(4)
    gather_wait(0)
    turn_into(r.qpre, r.qrot, 0)
    gather_forward(2)
    gather_send(5)
    gather_wait(1)
    turn_into(r.kpre, r.krot, 1)
    gather_forward(3)
    gather_send(6)
    gather_wait(2)
    project_into(r.val, 2)
    gather_forward(4)
    gather_send(7)
    gather_wait(3)
    project_into(r.gpre, 3)

    def wo_block(owner):
        return r.wo.at[:, pl.ds(pl.multiple_of(owner * C, C), C)]


    NB = T // B
    REACH = LONGEST // B

    def keys_of(qb):
        return slice(max(0, qb - REACH) * B, (qb + 1) * B)

    def weights_of(qb, h):
        key = keys_of(qb)
        width = key.stop - key.start
        fades = [r.dec[min(o, 1), h] for o in range(width // B - 1, -1, -1)]
        for o in range(2, width // B):
            fades[width // B - 1 - o] *= jnp.exp(rate_of(h) * ((o - 1) * B))
        seen = jnp.broadcast_to(r.segk[0:1, key], (B, width))
        same = widen(r.segq[qb * B:(qb + 1) * B, :], width) == seen
        return jnp.where(same, jnp.concatenate(fades, axis=1), 0.0)

    def u_block(qb):
        return lambda owner: r.ufull.at[qb * B:(qb + 1) * B, pl.ds(pl.multiple_of(owner * C, C), C)]

    def attend(qb):
        q = slice(qb * B, (qb + 1) * B)
        squares = jnp.zeros((B, 1), F32)
        for h in range(H):
            rot = slice(2 * h * HEAD, 2 * (h + 1) * HEAD)
            chan = slice(h * HEAD, (h + 1) * HEAD)
            key = keys_of(qb)
            scores = dot_nt(r.qrot[q, rot], r.krot[key, rot]) * weights_of(qb, h)
            total = dot_nn(scores.astype(BF), r.val[key, chan])
            r.mixed[q, chan] = total
            squares = squares + jnp.sum(total * total, axis=-1, keepdims=True)
            r.ufull[q, pl.ds(pl.multiple_of(j * C + h * HEAD, HEAD), HEAD)] = (
                total * r.gpre[q, chan]
            ).astype(BF)
        r.ss[j, :, q] = jnp.transpose(jnp.broadcast_to(squares, (B, 128)))[0:8, :]

    def ss_block(owner):
        return r.ss.at[owner]

    for qb in range(NB):
        attend(qb)
        share_send(1 + qb, u_block(qb))
        if qb == NB - 1:
            share_send(1 + NB, ss_block)
        if qb == 0:
            gather_forward(5)
            gather_send(8)
        if qb == 1:
            gather_wait(4)
            share_send(0, wo_block)
        if qb == 3:
            share_forward(0, wo_block)
        if qb == 2:
            gather_forward(6)
            gather_send(9)
        if qb > 0:
            share_forward(qb, u_block(qb - 1))
    share_forward(NB, u_block(NB - 1))
    share_forward(1 + NB, ss_block)
    gather_forward(7)
    gather_send(10)
    gather_forward(8)
    share_wait(0, wo_block)
    for qb in range(NB):
        share_wait(1 + qb, u_block(qb))
    share_wait(1 + NB, ss_block)
    early = [copy for copy, when in pending]

    total_ss = r.ss[0]
    for owner in range(1, mp):
        total_ss = total_ss + r.ss[owner]
    inverse = lax.rsqrt(total_ss * (1.0 / D) + EPSILON)
    for t in range(T // 128):
        q = slice(t * 128, t * 128 + 128)
        r.rcol[q, :] = jnp.transpose(jnp.broadcast_to(inverse[0:1, q], (128, 128)))

    def hidden_tile(t):
        q = rows_of(t, TB)
        out = widen(r.rcol[q, :], D) * dot_nn(r.ufull[q, :], r.wo[...])
        hidden = r.xv[q, :].astype(F32) + out
        scale = lax.rsqrt(jnp.mean(hidden * hidden, axis=-1, keepdims=True) + EPSILON)
        r.nmid[q, :] = (hidden * scale).astype(BF)

        @pl.when(t == j)
        def _():
            r.hown[...] = hidden

    each(T // TB, hidden_tile)
    gather_wait(5)
    gather_wait(6)

    def gate_tile(t):
        q = rows_of(t, TT)
        r.gact[q, 0:F] = to_units(r.nmid[q, :], 1)

    each(T // TT, gate_tile)
    gather_forward(9)
    gather_wait(7)
    gather_wait(8)

    def up_tile(t):
        q = rows_of(t, TT)
        upper = to_units(r.nmid[q, :], 2)
        r.uact[q, :] = upper.astype(BF)
        r.prod[q, :] = (r.gact[q, 0:F] * upper).astype(BF)

    each(T // TT, up_tile)
    put_ff_grad(0, r.prod, r.up)
    gather_forward(10)
    scatter_first(5, 6)
    gather_wait(9)
    gather_wait(10)

    def mid_block(x, c):
        q = rows_of(x * 2 + c, TB)
        g = to_units(r.up[q, :], 0)
        grad_gate, grad_up = (g * r.uact[q, :].astype(F32)).astype(BF), (g * r.gact[q, 0:F]).astype(BF)
        r.ggate[q, :] = grad_gate
        r.gup[q, :] = grad_up
        r.part[x, c] = (to_model(grad_gate, 1) + to_model(grad_up, 2)).astype(BF)

    used = sum_begin(0, 0, mid_block)
    scatter_handed(5)
    scatter_second(6)
    put_ff_grad(1, r.ggate, r.nmid)
    scatter_first(7, 8)
    scatter_handed(6)

    def back_tile(t):
        q = rows_of(t, 128)
        here = rows_of(j * (TB // 128) + t, 128)
        grad = sum_tile(0, q)
        hidden = r.hown[q, :]
        scale = lax.rsqrt(jnp.mean(hidden * hidden, axis=-1, keepdims=True) + EPSILON)
        normed = hidden * scale
        inner = jnp.mean(grad * normed, axis=-1, keepdims=True)
        out = r.up[here, :].astype(F32) + scale * (grad - normed * inner)
        low = out.astype(BF)
        grad_gated = dot_nt(low, r.wo[...]).astype(BF)
        for owner in range(mp):
            rows, cols = slice(owner * TB + t * 128, owner * TB + (t + 1) * 128), slice(owner * C, (owner + 1) * C)
            r.gsend[rows, :] = grad_gated[:, cols]
            r.hsend[rows, :] = low[:, cols]
        r.ggated[here, :] = r.gsend[here, :]
        r.hcols[here, :] = r.hsend[here, :]
        mixer_out = hidden - r.xown[q, :].astype(F32)
        product = jnp.sum(low.astype(F32) * mixer_out, axis=-1, keepdims=True) * (1.0 / D)
        r.inn[j, :, q] = jnp.transpose(jnp.broadcast_to(product, (128, 128)))[0:8, :]

    def token_block(ref):
        return lambda owner: ref.at[rows_of(owner, TB)]

    BO, GM, IG = 2 + NB, 3 + NB, 8 + NB

    def half_block(ref, t):
        return lambda owner: ref.at[rows_of(owner * NT + t, 128)]

    def peers():
        return [(d, lax.rem(j + d, mp), lax.rem(j - d + mp, mp)) for d in range(1, mp)]

    for t in range(NT):
        sum_arrived(0, 0, t)
        back_tile(t)
        for d, to, source in peers():
            go(half_block(r.gsend, t)(to), half_block(r.ggated, t)(j), r.ags.at[t, d], r.agr.at[t, d], mp=to)
    for d, to, source in peers():
        go(r.inn.at[j], r.inn.at[j], r.ahs.at[0, d], r.ahr.at[0, d], mp=to)
    for d, to, source in peers():
        go(token_block(r.hsend)(to), token_block(r.hcols)(j), r.ahs.at[1, d], r.ahr.at[1, d], mp=to)
    put_ff_grad(2, r.gup, r.nmid)
    scatter_first(9, 10)
    scatter_second(5)
    scatter_second(7)
    for copy in used:
        settle(copy)

    def expand_tile(t):
        r.part[t // 2, lax.rem(t, 2)] = to_model(r.prod[rows_of(t, TB), :], 0).astype(BF)

    each(mp, expand_tile)
    used = [
        go(r.part.at[to, 1 - ci], r.recc.at[1, to], r.acs.at[1, d], r.acr.at[1, d], mp=xi * 2 + 1 - ci)
        for d, to in [(d, lax.rem(xi + d, X)) for d in range(X)]
    ]
    scatter_handed(7)
    for d, to, source in peers():
        for t in range(NT):
            arrived(half_block(r.ggated, t)(source), r.agr.at[t, d])
        arrived(r.inn.at[source], r.ahr.at[0, d])
    for owner in range(mp):
        for t in range(TB // 128):
            row = r.inn[owner, 0:1, t * 128:(t + 1) * 128]
            q = slice(owner * TB + t * 128, owner * TB + (t + 1) * 128)
            r.icol[q, :] = jnp.transpose(jnp.broadcast_to(row, (128, 128)))

    def gated_tile(t):
        q = rows_of(t, TT)
        grad = r.ggated[q, :].astype(F32)
        inner = widen(r.icol[q, :], C)
        inverse = widen(r.rcol[q, :], C)
        normed = r.mixed[q, :] * inverse
        r.gproj[3][q, :] = (grad * normed).astype(BF)
        r.gmix[q, :] = (inverse * (grad * r.gpre[q, :] - normed * inner)).astype(BF)

    each(T // TT, gated_tile)

    for d in [*range(1, X), 0]:
        to = lax.rem(xi + d, X)
        arrived(r.recc.at[1, to], r.acr.at[1, d])
        for t in range(NT):
            q = slice(t * 128, (t + 1) * 128)
            r.recc[1, to, q] = (r.part[to, ci, q].astype(F32) + r.recc[1, to, q].astype(F32)).astype(BF)
            if d:
                go(r.recc.at[1, to, q], r.recx.at[1, d - 1, q], r.axs.at[1, d - 1, t], r.axr.at[1, d - 1, t], mp=to * 2 + ci)
    scatter_second(8)

    def output_grad_tile(t):
        q = rows_of(t, TT)
        r.rh[q, :] = (widen(r.rcol[q, :], C) * r.hcols[q, :].astype(F32)).astype(BF)

    def swish_back(pre, grad):
        gate = jax.nn.sigmoid(pre)
        return grad * (gate * (1.0 + pre * (1.0 - gate)))

    def attend_back(qb):
        q, key = slice(qb * B, (qb + 1) * B), keys_of(qb)
        for h in range(H):
            rot = slice(2 * h * HEAD, 2 * (h + 1) * HEAD)
            chan = slice(h * HEAD, (h + 1) * HEAD)
            weights = weights_of(qb, h)
            scores = (dot_nt(r.qrot[q, rot], r.krot[key, rot]) * weights).astype(BF)
            back = (dot_nt(r.gmix[q, chan], r.val[key, chan]) * weights).astype(BF)
            dq = dot_nn(back, r.krot[key, rot])
            turned = dq[:, :HEAD] * r.cosv[q, :] + dq[:, HEAD:] * r.sinv[q, :]
            r.gproj[0][q, chan] = swish_back(r.qpre[q, chan], turned).astype(BF)
            dk = dot_tn(back, r.qrot[q, rot])
            dv = dot_tn(scores, r.gmix[q, chan])
            for kb in range(key.start // B, qb + 1):
                at = slice(kb * B - key.start, (kb + 1) * B - key.start)
                rows = slice(kb * B, (kb + 1) * B)
                dkb, dvb = dk[at], dv[at]
                if qb < min(kb + REACH, NB - 1):
                    dkb, dvb = dkb + r.dk[rows, rot], dvb + r.dv[rows, chan]
                if kb < qb:
                    r.dk[rows, rot], r.dv[rows, chan] = dkb, dvb
                else:
                    turned = dkb[:, :HEAD] * r.cosv[q, :] + dkb[:, HEAD:] * r.sinv[q, :]
                    r.gproj[1][q, chan] = swish_back(r.kpre[q, chan], turned).astype(BF)
                    r.gproj[2][q, chan] = dvb.astype(BF)

    def output_tile(t):
        q = rows_of(t, 128)
        total = r.recc[1, xi, q].astype(F32)
        for d in range(1, X):
            total = total + r.recx[1, d - 1, q].astype(F32)
        r.bov[rows_of(j * NT + t, 128), :] = (r.hown[q, :] + total).astype(BF)

    def late_core(x):
        return pltpu.make_async_remote_copy(
            src_ref=r.part.at[x, 1 - ci], dst_ref=r.recc.at[0, x], send_sem=r.acs.at[2, x], recv_sem=r.acr.at[2, x],
            device_id={"mp": xi * 2 + 1 - ci}, device_id_type=MESH,
        )

    def late_chip(x, d, t):
        q = slice(t * 128, (t + 1) * 128)
        return pltpu.make_async_remote_copy(
            src_ref=r.part.at[x, ci, q], dst_ref=r.recx.at[0, d - 1, q], send_sem=r.axs.at[2, d - 1, t],
            recv_sem=r.axr.at[2, d - 1, t], device_id={"mp": x * 2 + ci}, device_id_type=MESH,
        )

    def blocks_in(qb):
        return [divmod(at, 2) for at in range(qb * B // TB, (qb + 1) * B // TB)]

    def late_begin(x, c):
        q = slice((x * 2 + c) * TB, (x * 2 + c + 1) * TB)
        out = dot_nt(r.gproj[0][q, :], r.mixw[0])
        for k in range(1, 4):
            out = out + dot_nt(r.gproj[k][q, :], r.mixw[k])
        r.part[x, c] = out.astype(BF)

        @pl.when(ci != c)
        def _():
            late_core(x).start()

    def late_pass(x, c):
        @pl.when(ci == c)
        def _():
            arrived(r.recc.at[0, x], r.acr.at[2, x])

        @pl.when((ci == c) & (xi != x))
        def _():
            for t in range(NT):
                q = slice(t * 128, (t + 1) * 128)
                r.part[x, c, q] = (r.part[x, c, q].astype(F32) + r.recc[0, x, q].astype(F32)).astype(BF)
                late_chip(x, lax.rem(x - xi + X, X), t).start()

    put_grad(3, r.nint, r.gproj[3], turned=True)
    scatter_first(3)
    scatter_second(9)
    for qb in range(NB - 1, -1, -1):
        attend_back(qb)
        if qb == NB - 1:
            for copy in used + early:
                settle(copy)
        for x, c in blocks_in(qb):
            late_begin(x, c)
        if qb < NB - 1:
            for x, c in blocks_in(qb + 1):
                late_pass(x, c)
        if qb == NB - 1:
            for d, to, source in peers():
                arrived(token_block(r.hcols)(source), r.ahr.at[1, d])
            each(T // TT, output_grad_tile)
            put_grad(4, r.ufull, r.rh)
            scatter_first(4)
            scatter_handed(8, 9)
            scatter_second(10)
            finish_ff(5)
        if qb == max(NB - 2, 0):
            scatter_handed(10)
            scatter_second(3)
            for t in range(NT):
                for d in range(1, X):
                    arrived(r.recx.at[1, d - 1, t * 128:(t + 1) * 128], r.axr.at[1, d - 1, t])
            each(TB // 128, output_tile)
            share_send(BO, token_block(r.bov))
            finish_ff(6)
        if qb == max(NB - 3, 0):
            scatter_second(4)
            scatter_handed(3)
            share_forward(BO, token_block(r.bov))
            finish_ff(7)
    for x, c in blocks_in(0):
        late_pass(x, c)
    pending.extend((late_core(x), None) for x in range(X))
    pending.extend((late_chip(lax.rem(xi + d, X), d, t), None) for d in range(1, X) for t in range(NT))
    for k in (2, 0):
        put_grad(k, r.nint, r.gproj[k], turned=True)
        scatter_first(k)
    scatter_handed(4)
    put_grad(1, r.nint, r.gproj[1], turned=True)
    scatter_first(1)
    scatter_handed(2)
    finish_ff(8, 9, 10)
    scatter_second(0, 2)

    def input_tile(t):
        q = slice(t * 128, (t + 1) * 128)
        low = jnp.concatenate(
            [r.hsend[owner * TB + t * 128:owner * TB + (t + 1) * 128, :] for owner in range(mp)], axis=1
        ).astype(F32)
        grad = sum_tile(0, q)
        v = r.xown[q, :].astype(F32)
        scale = lax.rsqrt(jnp.mean(v * v, axis=-1, keepdims=True) + EPSILON)
        normed = v * scale
        inner = jnp.mean(grad * normed, axis=-1, keepdims=True)
        r.igv[rows_of(j * NT + t, 128), :] = (low + scale * (grad - normed * inner)).astype(BF)

    for t in range(NT):
        for d in range(1, X):
            arrived(r.recx.at[0, d - 1, t * 128:(t + 1) * 128], r.axr.at[2, d - 1, t])
        input_tile(t)
        share_send(IG + t, half_block(r.igv, t))
    scatter_second(1)
    share_wait(BO, token_block(r.bov))
    stores = [load(r.bov, r.bo, 0)]

    def grad_block(k):
        return lambda owner: r.gmv.at[k * S:(k + 1) * S, pl.ds(pl.multiple_of(owner * C, C), C)]

    for k in (4, 3, 0, 2, 1):
        total = scatter_total(k).astype(BF)
        r.gmv[k * S:(k + 1) * S, jcols] = total
        r.sqs[...] += squares_of(total.astype(F32))
        share_send(GM + k, grad_block(k))

    r.s1[j] = r.sqs[...]
    for d in range(1, mp):
        go(r.s1.at[j], r.s1.at[j], r.q1s.at[d], r.q1r.at[d], mp=lax.rem(j + d, mp))
    for t in range(NT):
        share_forward(IG + t, half_block(r.igv, t))
    for d in range(1, mp):
        arrived(r.s1.at[lax.rem(j - d + mp, mp)], r.q1r.at[d])
    total = r.s1[0]
    for owner in range(1, mp):
        total = total + r.s1[owner]
    r.s2[i] = total
    for d in range(1, n):
        go(r.s2.at[i], r.s2.at[i], r.q2s.at[d], r.q2r.at[d], dp=lax.rem(i + d, n))
    for k in (4, 3, 2, 0, 1):
        share_forward(GM + k, grad_block(k))
    for d in range(1, n):
        arrived(r.s2.at[lax.rem(i - d + n, n)], r.q2r.at[d])
    total = r.s2[0]
    for owner in range(1, n):
        total = total + r.s2[owner]
    r.sqo[...] = total

    for t in range(NT):
        share_wait(IG + t, half_block(r.igv, t))
    stores.append(load(r.igv, r.ig, 1))
    for k in (4, 3, 2, 0, 1):
        share_wait(GM + k, grad_block(k))
        stores.append(load(r.gmv.at[k * S:(k + 1) * S], r.gmo.at[k], 2 + k))
    for copy in stores:
        copy.wait()
    for copy, when in pending:
        guarded(when, copy.wait_send)


def fused(p, *operands):
    scratch = scratch_of(p)
    names = IN_NAMES + OUT_NAMES + tuple(scratch)
    anywhere = pl.BlockSpec(memory_space=pl.ANY)
    vmem = pl.BlockSpec(memory_space=pltpu.VMEM)
    smem = pl.BlockSpec(memory_space=pltpu.SMEM)
    return pl.pallas_call(
        partial(body, p, names),
        out_shape=(
            jax.ShapeDtypeStruct((p.T, p.D), BF),
            jax.ShapeDtypeStruct((p.T, p.D), BF),
            jax.ShapeDtypeStruct((5, p.S, p.D), BF),
            jax.ShapeDtypeStruct((2, p.F, p.S) if p.FD else (2, p.S, p.F), F32),
            jax.ShapeDtypeStruct((p.F, p.S) if p.FD else (p.S, p.F), F32),
            jax.ShapeDtypeStruct((8, 128), F32),
        ),
        in_specs=[anywhere, anywhere, vmem, smem] + [anywhere] * 5,
        out_specs=(anywhere, anywhere, anywhere, vmem, vmem, vmem),
        scratch_shapes=list(scratch.values()),
        compiler_params=pltpu.CompilerParams(
            collective_id=0, has_side_effects=True, vmem_limit_bytes=VMEM_LIMIT
        ),
    )(*operands)


VMEM_LIMIT = 64 * 2**20 - 2**18


def renew(weight, momentum, shadow, grad, clip_factor):
    clipped = grad * clip_factor
    velocity = MOMENTUM * momentum + clipped
    updated = weight - LEARN_RATE * (clipped + MOMENTUM * velocity)
    average = SHADOW_DECAY * shadow + (1.0 - SHADOW_DECAY) * updated
    return (velocity, average, updated)


def update_body(cuts, *refs):
    kinds, pieces = len(cuts), sum(len(c) for c in cuts)
    sq, carried = refs[0], refs[1:3]
    ins = [refs[3 + 4 * w:7 + 4 * w] for w in range(kinds)]
    refs = refs[3 + 4 * kinds:]
    norm_out, carried_out = refs[0], refs[1:3]
    outs = [refs[3 + 3 * w:6 + 3 * w] for w in range(kinds)]
    refs = refs[3 + 3 * kinds:]
    held = [refs[4 * w:4 * w + 4] for w in range(kinds)]
    made = [refs[4 * kinds + 3 * w:4 * kinds + 3 * w + 3] for w in range(kinds)]
    bounce, (in_sem, out_sem, carry_sem) = refs[7 * kinds:7 * kinds + 2], refs[7 * kinds + 2:]
    loads, order = {}, [(w, c) for w in range(kinds) for c in range(len(cuts[w]))]
    for at, (w, c) in enumerate(order):
        for a in range(4):
            cut = cuts[w][c]
            loads[at, a] = pltpu.make_async_copy(ins[w][a].at[cut], held[w][a].at[cut], in_sem.at[at, a])
            loads[at, a].start()
    carry = [pltpu.make_async_copy(carried[a], bounce[a], carry_sem.at[a]) for a in range(2)]
    for copy in carry:
        copy.start()
    copies = []
    norm = jnp.sqrt(jnp.broadcast_to(jnp.sum(sq[...]), (8, 128)))
    norm_out[...] = norm
    clip_factor = 1.0 / jnp.maximum(jnp.max(norm), 1.0)
    for at, (w, c) in enumerate(order):
        cut = cuts[w][c]
        for a in range(4):
            loads[at, a].wait()
        new = renew(*[held[w][a][cut] for a in range(3)], held[w][3][cut].astype(F32), clip_factor)
        for a in range(3):
            made[w][a][cut] = new[a]
            copy = pltpu.make_async_copy(made[w][a].at[cut], outs[w][a].at[cut], out_sem.at[at, a])
            copy.start()
            copies.append(copy)
    for a in range(2):
        carry[a].wait()
        copy = pltpu.make_async_copy(bounce[a], carried_out[a], carry_sem.at[2 + a])
        copy.start()
        copies.append(copy)
    for copy in copies:
        copy.wait()


def update(sq, carried, weights):
    cuts = [[c for c in range(g[0].shape[0])] if g[0].ndim == 3 else [slice(None)] for g in weights]
    pieces = sum(len(c) for c in cuts)
    anywhere = pl.BlockSpec(memory_space=pl.ANY)
    vmem = pl.BlockSpec(memory_space=pltpu.VMEM)
    flat_in = [a for group in weights for a in group]
    flat_out = [a for group in weights for a in group[:3]]
    dma = pltpu.SemaphoreType.DMA
    size = sum(a.size * a.dtype.itemsize for a in flat_in + flat_out + 2 * list(carried))
    return pl.pallas_call(
        partial(update_body, cuts),
        out_shape=[jax.ShapeDtypeStruct(a.shape, a.dtype) for a in [sq, *carried, *flat_out]],
        in_specs=[vmem] + [anywhere] * (2 + len(flat_in)),
        out_specs=[vmem] + [anywhere] * (2 + len(flat_out)),
        scratch_shapes=[pltpu.VMEM(a.shape, a.dtype) for a in flat_in + flat_out + list(carried)]
        + [dma((pieces, 4)), dma((pieces, 3)), dma((4,))],
        cost_estimate=pl.CostEstimate(flops=size, bytes_accessed=size, transcendentals=0),
        compiler_params=pltpu.CompilerParams(vmem_limit_bytes=VMEM_LIMIT),
    )(sq, *carried, *flat_in)


def turn_tables(tokens):
    theta = np.float32(10000.0) ** (-np.arange(HEAD, dtype=np.float32) / np.float32(HEAD))
    angle = np.arange(tokens, dtype=np.float32)[:, None] * theta.astype(np.float32)[None, :]
    angle = angle.astype(np.float64)
    return np.cos(angle).astype(np.float32), np.sin(angle).astype(np.float32)


def per_device(mesh, block_input, segment_ids, live_length, output_grad, mixer_weight, mixer_momentum, mixer_shadow,
               expand_weight, expand_momentum, expand_shadow, shrink_weight, shrink_momentum, shrink_shadow):
    rows, length, width = block_input.shape
    p = plan_of(mesh, length, width, shrink_weight.shape[0])
    turn = (lambda v: jnp.swapaxes(v, -1, -2)) if p.FD else (lambda v: v)
    if p.FD:
        shards = (turn(expand_weight), shrink_weight)
    else:
        shards = (jnp.concatenate([shrink_weight.T[None], expand_weight], axis=0).astype(BF), shrink_weight)
    cos, sin = turn_tables(length)
    out, grad_in, gm, ge, gs, sq = fused(
        p, block_input[0], output_grad[0], segment_ids, live_length, jnp.asarray(cos), jnp.asarray(sin), mixer_weight, *shards
    )
    new = update(sq, (out, grad_in), (
        (mixer_weight, mixer_momentum, mixer_shadow, gm),
        (turn(expand_weight), turn(expand_momentum), turn(expand_shadow), ge),
        (shrink_weight, shrink_momentum, shrink_shadow, gs if p.FD else gs.T),
    ))
    norm, out, grad_in = new[:3]
    return (out[None], grad_in[None], norm[0, 0], *new[3:6], *(turn(v) for v in new[6:9]), *new[9:12])


def solution(mesh):
    row, mixer, expand, shrink = P("dp", None, None), P(None, "dp", None), P(None, "dp", "mp"), P("mp", "dp")
    return jax.shard_map(
        partial(per_device, mesh),
        mesh=mesh,
        in_specs=(row, P("dp", None), P("dp"), row) + (mixer,) * 3 + (expand,) * 3 + (shrink,) * 3,
        out_specs=(row, row, P()) + (mixer,) * 3 + (expand,) * 3 + (shrink,) * 3,
        check_vma=False,
    )
```

```python
from functools import partial
from types import SimpleNamespace

import jax
import jax.numpy as jnp
import numpy as np
from jax import lax
from jax.experimental import pallas as pl
from jax.experimental.pallas import tpu as pltpu
from jax.sharding import PartitionSpec as P

HEAD = 128
EPSILON = 1e-06
LEARN_RATE = 32.0
MOMENTUM = 0.5
SHADOW_DECAY = 0.5
LAYER_PLACE = 12.0 / 24.0
LONGEST = 512
FF_ORDER = (1, 2, 0)
Y_FIRST = (4, 6)
Z_FIRST = (9, 4)
STRAIGHT = (2, 0, 1)
MESH = pl.DeviceIdType.MESH
BF = jnp.bfloat16
F32 = jnp.float32


def dot_nn(a, b):
    return lax.dot_general(a, b, (((1,), (0,)), ((), ())), preferred_element_type=F32)


def dot_nt(a, b):
    return lax.dot_general(a, b, (((1,), (1,)), ((), ())), preferred_element_type=F32)


def dot_tn(a, b):
    return lax.dot_general(a, b, (((0,), (0,)), ((), ())), preferred_element_type=F32)


def rows_of(index, size):
    return pl.ds(pl.multiple_of(index * size, size), size)


def each(count, body):
    def step(t, carry):
        body(t)
        return carry

    lax.fori_loop(0, count, step, 0)


def widen(column, width):
    return jnp.concatenate([column] * (width // 128), axis=1)


def plan_of(mesh, tokens, width, inner):
    n, mp = mesh.shape["dp"], mesh.shape["mp"]
    lo, core = 2, 2
    return SimpleNamespace(
        n=n, mp=mp, LO=lo, HI=n // lo, X=mp // core, T=tokens, D=width, C=width // mp, F=inner,
        S=width // n, H=width // mp // HEAD, TB=tokens // mp, B=min(256, tokens),
        NT=tokens // mp // 128, FD=(width // n) % 128 == 0,
    )


def scratch_of(p):
    T, D, C, F, S, HI, LO, X, TB, B = p.T, p.D, p.C, p.F, p.S, p.HI, p.LO, p.X, p.TB, p.B
    dma = pltpu.SemaphoreType.DMA
    v = pltpu.VMEM
    return dict(
        mixw=v((4, D, C), BF), wo=v((D, D), BF), ffw=v((3, F, D) if p.FD else (3, D, F), BF),
        xown=v((TB, D), BF), nin=v((T, D), BF), nint=v((D, T), BF), up=v((T, D), BF),
        cosv=v((T, HEAD), F32), sinv=v((T, HEAD), F32),
        segq=v((T, 128), F32), segk=v((8, T), F32), dec=v((2, p.H, B, B), F32),
        qpre=v((T, C), F32), kpre=v((T, C), F32), gpre=v((T, C), F32), val=v((T, C), BF),
        qrot=v((T, 2 * C), BF), krot=v((T, 2 * C), BF), mixed=v((T, C), F32),
        ufull=v((T, D), BF), ss=v((p.mp, 8, T), F32), rcol=v((T, 128), F32),
        inn=v((p.mp, 8, TB), F32), hown=v((TB, D), F32),
        gact=v((T, max(F, 2 * C + HEAD)), F32), uact=v((T, F), BF), prod=v((T, F), BF), ggate=v((T, F), BF), gup=v((T, F), BF),
        part=v((X, 2, TB, D), BF), recc=v((2, X, TB, D), BF), recx=v((2, X - 1, TB, D), BF),
        xv=v((T, D), BF),
        gm=v((5, HI, LO, S, C), BF), rym=v((5, HI, S, C), BF), rzm=v((5, HI - 1, S, C), BF),
        gf=v((3, LO, F, HI * S) if p.FD else (3, HI, LO, S, F), BF),
        ryf=v((3, F, HI * S) if p.FD else (3, HI, S, F), BF),
        rzf=v((3, HI - 1, F, S) if p.FD else (3, HI - 1, S, F), BF),
        relm=v((2, S, C), BF), relf=v((3, F, S) if p.FD else (3, S, F), BF),
        othm=v((HI, S, C), BF), othf=v((HI, F // 2, S) if p.FD else (HI, S // 2, F), BF),
        sqs=v((8, 128), F32), s1=v((p.mp, 8, 128), F32), s2=v((p.n, 8, 128), F32),
        loc=dma((10,)),
        zs=dma((11, HI - 1)), zr=dma((11, HI - 1)), us=dma((len(Y_FIRST), HI - 1)), ur=dma((len(Y_FIRST), HI - 1)),
        zp=dma((11,)), yp=dma((len(Y_FIRST),)), ys=dma((11, HI)), yr=dma((11, HI)),
        xs=dma((20, X - 1)), xr=dma((20, X - 1)), cs=dma((20, X)), cr=dma((20, X)),
        acs=dma((3, X)), acr=dma((3, X)), axs=dma((3, X - 1, p.NT)), axr=dma((3, X - 1, p.NT)),
        bys=dma((11,)), byr=dma((11,)), bzs=dma((11, HI - 1)), bzr=dma((11, HI - 1)),
        bts=dma((11,)), btr=dma((11,)), ozs=dma((2, HI - 1)), ozr=dma((2, HI - 1)), ots=dma((2,)), otr=dma((2,)),
        ags=dma((p.NT, p.mp)), agr=dma((p.NT, p.mp)), ahs=dma((2, p.mp)), ahr=dma((2, p.mp)),
        q1s=dma((p.mp,)), q1r=dma((p.mp,)), q2s=dma((p.n,)), q2r=dma((p.n,)),
    )


IN_NAMES = ("x", "og", "seg", "live", "cos", "sin", "mixsh", "exsh", "shsh")
OUT_NAMES = ("bo", "ig", "gmo", "geo", "gso", "sqo")


def body(p, names, *refs):
    r = SimpleNamespace(**dict(zip(names, refs)))
    n, mp, LO, HI, X, T, D, C, F, S, H, TB, B = (
        p.n, p.mp, p.LO, p.HI, p.X, p.T, p.D, p.C, p.F, p.S, p.H, p.TB, p.B,
    )
    NT, TT = p.NT, min(512, p.T)
    i, j = lax.axis_index("dp"), lax.axis_index("mp")
    zi, yi = i // LO, lax.rem(i, LO)
    xi, ci = j // 2, lax.rem(j, 2)
    jcols = pl.ds(pl.multiple_of(j * C, C), C)
    pending = []
    r.nmid = r.nin
    r.bov, r.igv, r.gmv = r.up, r.ufull, r.wo
    r.dk, r.icol, r.dv = r.gact.at[:, 0:2 * C], r.gact.at[:, 2 * C:2 * C + HEAD], r.mixed
    r.gproj = [r.ggate.at[:, 0:C], r.ggate.at[:, C:2 * C], r.gup.at[:, 0:C], r.gup.at[:, C:2 * C]]
    r.ggated, r.hcols, r.gmix, r.rh = [r.xv.at[:, a * C:(a + 1) * C] for a in range(4)]
    r.hsend, r.gsend = r.uact.at[:, 0:C], r.uact.at[:, C:2 * C]

    def go(src, dst, ssem, rsem, when=None, **device):
        copy = pltpu.make_async_remote_copy(
            src_ref=src, dst_ref=dst, send_sem=ssem, recv_sem=rsem,
            device_id=device, device_id_type=MESH,
        )
        guarded(when, copy.start)
        pending.append((copy, when))
        return copy

    def guarded(when, act):
        if when is None:
            act()
        else:
            pl.when(when)(lambda: act())

    def arrived(dst, sem):
        pltpu.make_async_copy(dst, dst, sem).wait()

    def settle(copy):
        for other, when in pending:
            if other is copy:
                guarded(when, copy.wait_send)
        pending[:] = [entry for entry in pending if entry[0] is not copy]

    def load(src, dst, sem):
        copy = pltpu.make_async_copy(src, dst, r.loc.at[sem])
        copy.start()
        return copy

    own_mix = [load(r.mixsh.at[k, :, jcols], r.qpre.at[k * S:(k + 1) * S], k) for k in range(5)]
    if p.FD:
        stage = [r.gact.at[0:F, m * S:(m + 1) * S] for m in range(3)]
        own_ff = [load(r.shsh if m == 0 else r.exsh.at[m - 1], stage[m], 5 + m) for m in range(3)]
    else:
        own_ff = [load(r.exsh.at[m], r.ffw.at[m, rows_of(i, S)], 5 + m) for m in range(3)]
    load_x = load(r.x, r.xv, 8)
    load_og = load(r.og, r.up, 9)

    def enter():
        barrier = pltpu.get_barrier_semaphore()
        for d in range(1, n):
            pl.semaphore_signal(barrier, inc=1, device_id={"dp": lax.rem(i + d, n)}, device_id_type=MESH)
        for d in range(1, mp):
            pl.semaphore_signal(barrier, inc=1, device_id={"mp": lax.rem(j + d, mp)}, device_id_type=MESH)
        pl.semaphore_wait(barrier, n - 1 + mp - 1)

    def slot(k, device):
        rows = rows_of(device, S)
        if k == 4:
            return r.wo.at[rows, jcols]
        if k < 4:
            return r.mixw.at[k, rows]
        m, half = FF_ORDER[(k - 5) // 2], (k - 5) % 2
        if p.FD:
            return r.ffw.at[m, half * F // 2:(half + 1) * F // 2, rows]
        return r.ffw.at[m, pl.ds(pl.multiple_of(device * S + half * S // 2, S // 2), S // 2)]

    def gather_ready(k):
        if k < 5:
            own_mix[k].wait()
            slot(k, i)[...] = r.qpre[k * S:(k + 1) * S, :].astype(BF)
        else:
            m, half = FF_ORDER[(k - 5) // 2], (k - 5) % 2
            if half == 0:
                own_ff[m].wait()
            if p.FD:
                slot(k, i)[...] = stage[m][half * F // 2:(half + 1) * F // 2, :].astype(BF)

    relays = HI == 4
    next_to_end = (zi == 1) | (zi == 2)

    def along_z(block, ssem, rsem):
        for d in range(1, HI):
            to = lax.rem(zi + d, HI)
            near = (jnp.abs(to - zi) < 3) if relays else None
            go(block, block, ssem.at[d - 1], rsem.at[d - 1], when=near, dp=to * LO + yi)

    def hand_on(block, ssem, rsem):
        if relays:
            end = jnp.where(zi == 2, 3, 0)
            go(block, block, ssem, rsem.at[jnp.where(zi == 2, 2, 0)], when=next_to_end, dp=end * LO + yi)

    def from_z_source(k, d, y):
        return slot(k, lax.rem(zi - d + HI, HI) * LO + y)

    WAYS = [2, 1, *range(3, HI)]

    def gather_send(k):
        src = slot(k, i)
        along_z(src, r.zs.at[k], r.zr.at[k])
        go(src, src, r.ys.at[k, 0], r.yr.at[k, 0], dp=zi * LO + 1 - yi)

    def gather_forward(k):
        if k - 1 in Y_FIRST:
            b = Y_FIRST.index(k - 1)
            block = from_z_source(k - 1, 2, 1 - yi)
            arrived(block, r.ur.at[b, 1])
            hand_on(block, r.yp.at[b], r.ur.at[b])
        if k in Y_FIRST:
            b = Y_FIRST.index(k)
            peers = slot(k, zi * LO + 1 - yi)
            arrived(peers, r.yr.at[k, 0])
            along_z(peers, r.us.at[b], r.ur.at[b])
        for d in WAYS:
            block = from_z_source(k, d, yi)
            arrived(block, r.zr.at[k, d - 1])
            if d == 2:
                hand_on(block, r.zp.at[k], r.zr.at[k])
            if k not in Y_FIRST:
                go(block, block, r.ys.at[k, d], r.yr.at[k, d], dp=zi * LO + 1 - yi)

    def gather_wait(k):
        for d in range(HI):
            if k not in Y_FIRST:
                arrived(from_z_source(k, d, 1 - yi), r.yr.at[k, d])
            elif d in (1, 3) or d > 3:
                arrived(from_z_source(k, d, 1 - yi), r.ur.at[Y_FIRST.index(k), d - 1])

    def share_send(s, block, src=None):
        own = block(j)
        src = own if src is None else src
        for d in range(1, X):
            go(src, own, r.xs.at[s, d - 1], r.xr.at[s, d - 1], mp=lax.rem(xi + d, X) * 2 + ci)
        go(src, own, r.cs.at[s, 0], r.cr.at[s, 0], mp=xi * 2 + 1 - ci)

    def share_forward(s, block):
        for d in range(1, X):
            part = block(lax.rem(xi - d + X, X) * 2 + ci)
            arrived(part, r.xr.at[s, d - 1])
            go(part, part, r.cs.at[s, d], r.cr.at[s, d], mp=xi * 2 + 1 - ci)

    def share_wait(s, block):
        for d in range(X):
            arrived(block(lax.rem(xi - d + X, X) * 2 + 1 - ci), r.cr.at[s, d])

    def sum_begin(s, b, compute, between):
        sent = []

        def pair(d):
            to = lax.rem(xi + d, X)
            compute(to)
            sent.append(go(
                r.part.at[to, 1 - ci], r.recc.at[b, to], r.acs.at[s, d], r.acr.at[s, d], mp=xi * 2 + 1 - ci
            ))

        for d in range(1, X):
            pair(d)
        between()
        for d in range(1, X):
            to = lax.rem(xi + d, X)
            arrived(r.recc.at[b, to], r.acr.at[s, d])
            for t in range(NT):
                q = slice(t * 128, (t + 1) * 128)
                r.part[to, ci, q] = (
                    r.part[to, ci, q].astype(F32) + r.recc[b, to, q].astype(F32)
                ).astype(BF)
                sent.append(go(
                    r.part.at[to, ci, q], r.recx.at[b, d - 1, q], r.axs.at[s, d - 1, t], r.axr.at[s, d - 1, t],
                    mp=to * 2 + ci,
                ))
        pair(0)
        return sent

    def sum_arrived(s, b, t):
        if t == 0:
            arrived(r.recc.at[b, xi], r.acr.at[s, 0])
        for d in range(1, X):
            arrived(r.recx.at[b, d - 1, t * 128:(t + 1) * 128], r.axr.at[s, d - 1, t])

    def sum_tile(b, q):
        total = r.part[xi, ci, q].astype(F32) + r.recc[b, xi, q].astype(F32)
        for d in range(1, X):
            total = total + r.recx[b, d - 1, q].astype(F32)
        return total

    flat = p.FD

    def half_of(k):
        size = (F if flat else S) // 2
        return (k - 5) // 2, slice((k - 5) % 2 * size, ((k - 5) % 2 + 1) * size)

    def block_of(k, z, y):
        if k < 5:
            return r.gm.at[k, z, y]
        m, rows = half_of(k)
        return r.gf.at[m, y, rows, rows_of(z, S)] if flat else r.gf.at[m, z, y, rows]

    def from_y(k):
        if k < 5:
            return r.rym.at[k]
        m, rows = half_of(k)
        return r.ryf.at[m, rows] if flat else r.ryf.at[m, :, rows]

    def from_y_block(k, z):
        ref = from_y(k)
        return ref.at[:, rows_of(z, S)] if flat and k >= 5 else ref.at[z]

    def to_y(k):
        if k < 5:
            return r.gm.at[k, :, 1 - yi]
        m, rows = half_of(k)
        return r.gf.at[m, 1 - yi, rows] if flat else r.gf.at[m, :, 1 - yi, rows]

    def from_z(k, d, own=True):
        if not own:
            return (r.othm if k < 5 else r.othf).at[d - 1]
        if k < 5:
            return r.rzm.at[k, d - 1]
        m, rows = half_of(k)
        return r.rzf.at[m, d - 1, rows]

    def handed(k, own=True):
        if not own:
            return (r.othm if k < 5 else r.othf).at[HI - 1]
        if k < 5:
            return r.relm.at[max(k - 3, 0)]
        m, rows = half_of(k)
        return r.relf.at[m, rows]

    def z_sems(k, own):
        if own:
            return r.bzs.at[k], r.bzr.at[k], r.bts.at[k], r.btr.at[k]
        o = Z_FIRST.index(k)
        return r.ozs.at[o], r.ozr.at[o], r.ots.at[o], r.otr.at[o]

    def stepped(k):
        return relays and k not in STRAIGHT

    def far(d, back=False):
        other = lax.rem(zi + (HI - d if back else d), HI)
        return jnp.abs(other - zi) == 3

    def z_send(k, own, ways):
        y = yi if own else 1 - yi
        ssem, rsem, tsem, trsem = z_sems(k, own)
        for d in ways:
            to = lax.rem(zi + d, HI)
            block, dst = block_of(k, to, y), from_z(k, d, own)
            if stepped(k) and d != 2:
                go(block, handed(k, own), tsem, trsem, when=far(d), dp=jnp.where(zi == 0, 1, 2) * LO + yi)
                go(block, dst, ssem.at[d - 1], rsem.at[d - 1], when=jnp.logical_not(far(d)), dp=to * LO + yi)
            else:
                go(block, dst, ssem.at[d - 1], rsem.at[d - 1], dp=to * LO + yi)

    def z_send_handed(k, own):
        block = block_of(k, lax.rem(zi + 2, HI), yi if own else 1 - yi)

        @pl.when(next_to_end)
        def _():
            arrived(handed(k, own), z_sems(k, own)[3])
            block[...] = (block[...].astype(F32) + handed(k, own)[...].astype(F32)).astype(BF)

        z_send(k, own, [2])

    def z_total(k, own):
        for d in range(1, HI):
            wait = partial(arrived, from_z(k, d, own), z_sems(k, own)[1].at[d - 1])
            guarded(jnp.logical_not(far(d, back=True)) if stepped(k) and d != 2 else None, wait)
        total = block_of(k, zi, yi if own else 1 - yi)[...].astype(F32)
        for d in range(1, HI):
            total = total + from_z(k, d, own)[...].astype(F32)
        return total

    def clear_far_places():
        if not relays:
            return
        for d in (1, 3):
            @pl.when(far(d, back=True))
            def _(d=d):
                r.rzm[:, d - 1] = jnp.zeros((5, S, C), BF)
                for m in range(3):
                    r.rzf[m, d - 1] = jnp.zeros(r.rzf.shape[2:], BF)
                r.othm[d - 1] = jnp.zeros(r.othm.shape[1:], BF)
                r.othf[d - 1] = jnp.zeros(r.othf.shape[1:], BF)

    def near_ways(k):
        return [3, 1] if stepped(k) else list(range(1, HI))

    def scatter_first(*pieces):
        for k in pieces:
            if k in Z_FIRST:
                for own in (False, True):
                    z_send(k, own, near_ways(k))
            else:
                go(to_y(k), from_y(k), r.bys.at[k], r.byr.at[k], dp=zi * LO + 1 - yi)

    def scatter_second(*pieces):
        for k in pieces:
            if k in Z_FIRST:
                block = block_of(k, zi, 1 - yi)
                block[...] = z_total(k, False).astype(BF)
                go(block, from_y_block(k, zi), r.bys.at[k], r.byr.at[k], dp=zi * LO + 1 - yi)
                continue
            arrived(from_y(k), r.byr.at[k])
            for d in range(1, HI):
                to = lax.rem(zi + d, HI)
                block = block_of(k, to, yi)
                block[...] = (block[...].astype(F32) + from_y_block(k, to)[...].astype(F32)).astype(BF)
            z_send(k, True, near_ways(k))

    def scatter_handed(*pieces):
        for k in pieces:
            if stepped(k):
                if k in Z_FIRST:
                    z_send_handed(k, False)
                z_send_handed(k, True)

    def scatter_total(k):
        if k in Z_FIRST:
            arrived(from_y_block(k, zi), r.byr.at[k])
        return z_total(k, True) + from_y_block(k, zi)[...].astype(F32)

    def squares_of(total):
        squared = total * total
        if squared.shape[-1] % 128:
            corner = (lax.broadcasted_iota(jnp.int32, (8, 128), 0) + lax.broadcasted_iota(jnp.int32, (8, 128), 1)) == 0
            return jnp.where(corner, jnp.sum(squared), 0.0)
        folded = jnp.sum(squared.reshape(-1, 8, squared.shape[-1]), axis=0)
        return sum(folded[:, c:c + 128] for c in range(0, folded.shape[-1], 128))

    def finish_ff(*pieces):
        for k in pieces:
            m, rows = half_of(k)
            total = scatter_total(k)
            if m == 0:
                r.gso[rows] = total
            else:
                r.geo[m - 1, rows] = total
            r.sqs[...] += squares_of(total)

    def put_grad(k, lhs, rhs, turned=False):
        g = r.gm.at[k] if k < 5 else r.gf.at[k - 5]
        per = TT // (LO * S)

        def tile(t):
            if turned:
                out = dot_nn(lhs[rows_of(t, TT), :], rhs[...])
            else:
                out = dot_tn(lhs[:, rows_of(t, TT)], rhs[...])
            g[pl.ds(t * per, per)] = out.astype(BF).reshape(per, LO, S, out.shape[-1])

        each(D // TT, tile)

    def put_ff_grad(m, units, model):
        if not flat:
            return put_grad(5 + m, model, units)
        for f in range(0, F, 384):
            q = slice(f, min(f + 384, F))
            out = dot_tn(units[:, q], model[...]).astype(BF)
            for y in range(LO):
                for z in range(HI):
                    r.gf[m, y, q, z * S:(z + 1) * S] = out[:, (z * LO + y) * S:(z * LO + y + 1) * S]

    def to_units(a, m):
        return dot_nt(a, r.ffw[m]) if flat else dot_nn(a, r.ffw[m])

    def to_model(a, m):
        return dot_nn(a, r.ffw[m]) if flat else dot_nt(a, r.ffw[m])

    gather_ready(0)
    gather_ready(1)
    enter()
    gather_send(0)
    gather_send(1)
    gather_ready(2)
    gather_send(2)
    r.sqs[...] = jnp.zeros_like(r.sqs)
    clear_far_places()

    length = r.live[0]
    load_x.wait()

    def norm_tile(t):
        q = rows_of(t, 128)
        v = r.xv[q, :].astype(F32)
        r.nin[q, :] = (v * lax.rsqrt(jnp.mean(v * v, axis=-1, keepdims=True) + EPSILON)).astype(BF)

    each(T // 128, norm_tile)
    for k in range(3, 11):
        gather_ready(k)
    load_x_own = load(r.x.at[rows_of(j, TB)], r.xown, 8)
    load_og.wait()
    load_cos = load(r.cos, r.cosv, 0)
    load_sin = load(r.sin, r.sinv, 1)

    def live_tile(t):
        q = rows_of(t, 128)
        place = lax.broadcasted_iota(jnp.int32, (128, D), 0) + t * 128
        r.up[q, :] = jnp.where(place < length, r.up[q, :].astype(F32), 0.0).astype(BF)

    each(T // 128, live_tile)

    place = lax.broadcasted_iota(jnp.int32, (1, T), 1)
    segment = r.seg[...].astype(F32)
    r.segk[...] = jnp.broadcast_to(jnp.where(place < length, segment, -2.0), (8, T))
    seg_q = jnp.where(place < length, segment, -1.0)
    for t in range(T // 128):
        q = slice(t * 128, t * 128 + 128)
        r.segq[q, :] = jnp.transpose(jnp.broadcast_to(seg_q[:, q], (128, 128)))

    down = lax.broadcasted_iota(jnp.int32, (B, B), 0)
    over = lax.broadcasted_iota(jnp.int32, (B, B), 1)
    heads = D // HEAD

    def rate_of(h):
        return -(8.0 * (j * H + h).astype(F32) / heads) * (1.0 - LAYER_PLACE)

    for h in range(H):
        rate = rate_of(h)
        for o in range(2):
            distance = down - over + o * B
            fade = jnp.exp(rate * jnp.maximum(distance, 0).astype(F32))
            r.dec[o, h] = jnp.where(distance >= 0, fade, 0.0)

    for t in range(D // 128):
        q = slice(t * 128, t * 128 + 128)
        r.nint[q, :] = jnp.transpose(r.nin[:, q])
    load_cos.wait()
    load_sin.wait()
    load_x_own.wait()

    def turn_into(pre_ref, rot_ref, k):
        def tile(t):
            q = rows_of(t, TT)
            pre = dot_nn(r.nin[q, :], r.mixw[k])
            pre_ref[q, :] = pre
            act = pre * jax.nn.sigmoid(pre)
            c, s = r.cosv[q, :], r.sinv[q, :]
            for h in range(H):
                a = act[:, h * HEAD:(h + 1) * HEAD]
                rot_ref[q, 2 * h * HEAD:(2 * h + 1) * HEAD] = (a * c).astype(BF)
                rot_ref[q, (2 * h + 1) * HEAD:(2 * h + 2) * HEAD] = (a * s).astype(BF)

        each(T // TT, tile)

    def project_into(ref, k):
        def tile(t):
            q = rows_of(t, TT)
            ref[q, :] = dot_nn(r.nin[q, :], r.mixw[k]).astype(ref.dtype)

        each(T // TT, tile)

    gather_forward(0)
    gather_send(3)
    gather_forward(1)
    gather_send(4)
    gather_wait(0)
    turn_into(r.qpre, r.qrot, 0)
    gather_forward(2)
    gather_send(5)
    gather_wait(1)
    turn_into(r.kpre, r.krot, 1)
    gather_forward(3)
    gather_send(6)
    gather_wait(2)
    project_into(r.val, 2)
    gather_forward(4)
    gather_send(7)
    gather_wait(3)
    project_into(r.gpre, 3)

    def wo_block(owner):
        return r.wo.at[:, pl.ds(pl.multiple_of(owner * C, C), C)]


    NB = T // B
    REACH = LONGEST // B

    def keys_of(qb):
        return slice(max(0, qb - REACH) * B, (qb + 1) * B)

    def weights_of(qb, h):
        key = keys_of(qb)
        width = key.stop - key.start
        fades = [r.dec[min(o, 1), h] for o in range(width // B - 1, -1, -1)]
        for o in range(2, width // B):
            fades[width // B - 1 - o] *= jnp.exp(rate_of(h) * ((o - 1) * B))
        seen = jnp.broadcast_to(r.segk[0:1, key], (B, width))
        same = widen(r.segq[qb * B:(qb + 1) * B, :], width) == seen
        return jnp.where(same, jnp.concatenate(fades, axis=1), 0.0)

    def u_block(qb):
        return lambda owner: r.ufull.at[qb * B:(qb + 1) * B, pl.ds(pl.multiple_of(owner * C, C), C)]

    def attend(qb):
        q = slice(qb * B, (qb + 1) * B)
        squares = jnp.zeros((B, 1), F32)
        for h in range(H):
            rot = slice(2 * h * HEAD, 2 * (h + 1) * HEAD)
            chan = slice(h * HEAD, (h + 1) * HEAD)
            key = keys_of(qb)
            scores = dot_nt(r.qrot[q, rot], r.krot[key, rot]) * weights_of(qb, h)
            total = dot_nn(scores.astype(BF), r.val[key, chan])
            r.mixed[q, chan] = total
            squares = squares + jnp.sum(total * total, axis=-1, keepdims=True)
            r.ufull[q, pl.ds(pl.multiple_of(j * C + h * HEAD, HEAD), HEAD)] = (
                total * r.gpre[q, chan]
            ).astype(BF)
        r.ss[j, :, q] = jnp.transpose(jnp.broadcast_to(squares, (B, 128)))[0:8, :]

    def ss_block(owner):
        return r.ss.at[owner]

    for qb in range(NB):
        attend(qb)
        share_send(1 + qb, u_block(qb))
        if qb == NB - 1:
            share_send(1 + NB, ss_block)
        if qb == 0:
            gather_forward(5)
            gather_send(8)
        if qb == 1:
            gather_wait(4)
            share_send(0, wo_block)
        if qb == 3:
            share_forward(0, wo_block)
        if qb == 2:
            gather_forward(6)
            gather_send(9)
        if qb > 0:
            share_forward(qb, u_block(qb - 1))
    share_forward(NB, u_block(NB - 1))
    share_forward(1 + NB, ss_block)
    gather_forward(7)
    gather_send(10)
    gather_forward(8)
    share_wait(0, wo_block)
    for qb in range(NB):
        share_wait(1 + qb, u_block(qb))
    share_wait(1 + NB, ss_block)
    early = [copy for copy, when in pending]

    total_ss = r.ss[0]
    for owner in range(1, mp):
        total_ss = total_ss + r.ss[owner]
    inverse = lax.rsqrt(total_ss * (1.0 / D) + EPSILON)
    for t in range(T // 128):
        q = slice(t * 128, t * 128 + 128)
        r.rcol[q, :] = jnp.transpose(jnp.broadcast_to(inverse[0:1, q], (128, 128)))

    def hidden_tile(t):
        q = rows_of(t, TB)
        out = widen(r.rcol[q, :], D) * dot_nn(r.ufull[q, :], r.wo[...])
        hidden = r.xv[q, :].astype(F32) + out
        scale = lax.rsqrt(jnp.mean(hidden * hidden, axis=-1, keepdims=True) + EPSILON)
        r.nmid[q, :] = (hidden * scale).astype(BF)

        @pl.when(t == j)
        def _():
            r.hown[...] = hidden

    each(T // TB, hidden_tile)
    gather_wait(5)
    gather_wait(6)

    def gate_tile(t):
        q = rows_of(t, TT)
        r.gact[q, 0:F] = to_units(r.nmid[q, :], 1)

    each(T // TT, gate_tile)
    gather_forward(9)
    gather_wait(7)
    gather_wait(8)

    def up_tile(t):
        q = rows_of(t, TT)
        upper = to_units(r.nmid[q, :], 2)
        r.uact[q, :] = upper.astype(BF)
        r.prod[q, :] = (r.gact[q, 0:F] * upper).astype(BF)

    each(T // TT, up_tile)
    put_ff_grad(0, r.prod, r.up)
    gather_forward(10)
    scatter_first(5, 6)
    gather_wait(9)
    gather_wait(10)

    def mid_pair(x):
        q = rows_of(x, 2 * TB)
        g = to_units(r.up[q, :], 0)
        grad_gate, grad_up = (g * r.uact[q, :].astype(F32)).astype(BF), (g * r.gact[q, 0:F]).astype(BF)
        r.ggate[q, :] = grad_gate
        r.gup[q, :] = grad_up
        r.part[x] = (to_model(grad_gate, 1) + to_model(grad_up, 2)).astype(BF).reshape(2, TB, D)

    used = sum_begin(0, 0, mid_pair, partial(scatter_second, 5))
    put_ff_grad(1, r.ggate, r.nmid)
    scatter_first(7, 8)
    scatter_handed(5)
    scatter_second(6)

    def back_tile(t):
        q = slice(t * 128, (t + 1) * 128)
        here = rows_of(j * (TB // 128) + t, 128)
        grad = sum_tile(0, q)
        hidden = r.hown[q, :]
        scale = lax.rsqrt(jnp.mean(hidden * hidden, axis=-1, keepdims=True) + EPSILON)
        normed = hidden * scale
        inner = jnp.mean(grad * normed, axis=-1, keepdims=True)
        out = r.up[here, :].astype(F32) + scale * (grad - normed * inner)
        low = out.astype(BF)
        for owner in range(mp):
            r.hsend[owner * TB + t * 128:owner * TB + (t + 1) * 128, :] = low[:, owner * C:(owner + 1) * C]
        mixer_out = hidden - r.xown[q, :].astype(F32)
        product = jnp.sum(low.astype(F32) * mixer_out, axis=-1, keepdims=True) * (1.0 / D)
        r.inn[j, :, q] = jnp.transpose(jnp.broadcast_to(product, (128, 128)))[0:8, :]

    def token_block(ref):
        return lambda owner: ref.at[rows_of(owner, TB)]

    BO, GM, IG = 2 + NB, 3 + NB, 8 + NB

    def half_block(ref, t):
        return lambda owner: ref.at[rows_of(owner * NT + t, 128)]

    def peers():
        return [(d, lax.rem(j + d, mp), lax.rem(j - d + mp, mp)) for d in range(1, mp)]

    for t in range(NT):
        sum_arrived(0, 0, t)
        back_tile(t)
    low = jnp.concatenate([r.hsend[owner * TB:(owner + 1) * TB, :] for owner in range(mp)], axis=1)
    grad_gated = dot_nt(low, r.wo[...]).astype(BF)
    for owner in range(mp):
        r.gsend[owner * TB:(owner + 1) * TB, :] = grad_gated[:, owner * C:(owner + 1) * C]
    for d, to, source in peers():
        go(token_block(r.gsend)(to), token_block(r.ggated)(j), r.ags.at[0, d], r.agr.at[0, d], mp=to)
    own_rows = rows_of(j, TB)
    r.ggated[own_rows, :] = r.gsend[own_rows, :]
    r.hcols[own_rows, :] = r.hsend[own_rows, :]
    for d, to, source in peers():
        go(r.inn.at[j], r.inn.at[j], r.ahs.at[0, d], r.ahr.at[0, d], mp=to)
    for d, to, source in peers():
        go(token_block(r.hsend)(to), token_block(r.hcols)(j), r.ahs.at[1, d], r.ahr.at[1, d], mp=to)
    put_ff_grad(2, r.gup, r.nmid)
    scatter_first(9, 10)
    scatter_handed(6)
    scatter_second(7)
    for copy in used:
        settle(copy)

    def expand_tile(t):
        r.part[t // 2, lax.rem(t, 2)] = to_model(r.prod[rows_of(t, TB), :], 0).astype(BF)

    each(mp, expand_tile)
    used = [
        go(r.part.at[to, 1 - ci], r.recc.at[1, to], r.acs.at[1, d], r.acr.at[1, d], mp=xi * 2 + 1 - ci)
        for d, to in [(d, lax.rem(xi + d, X)) for d in range(X)]
    ]
    for d, to, source in peers():
        arrived(token_block(r.ggated)(source), r.agr.at[0, d])
        arrived(r.inn.at[source], r.ahr.at[0, d])
    for owner in range(mp):
        for t in range(TB // 128):
            row = r.inn[owner, 0:1, t * 128:(t + 1) * 128]
            q = slice(owner * TB + t * 128, owner * TB + (t + 1) * 128)
            r.icol[q, :] = jnp.transpose(jnp.broadcast_to(row, (128, 128)))

    def gated_tile(t):
        q = rows_of(t, TT)
        grad = r.ggated[q, :].astype(F32)
        inner = widen(r.icol[q, :], C)
        inverse = widen(r.rcol[q, :], C)
        normed = r.mixed[q, :] * inverse
        r.gproj[3][q, :] = (grad * normed).astype(BF)
        r.gmix[q, :] = (inverse * (grad * r.gpre[q, :] - normed * inner)).astype(BF)

    each(T // TT, gated_tile)

    for d in [*range(1, X), 0]:
        to = lax.rem(xi + d, X)
        arrived(r.recc.at[1, to], r.acr.at[1, d])
        for t in range(NT):
            q = slice(t * 128, (t + 1) * 128)
            r.recc[1, to, q] = (r.part[to, ci, q].astype(F32) + r.recc[1, to, q].astype(F32)).astype(BF)
            if d:
                go(r.recc.at[1, to, q], r.recx.at[1, d - 1, q], r.axs.at[1, d - 1, t], r.axr.at[1, d - 1, t], mp=to * 2 + ci)
    scatter_second(8)

    def output_grad_tile(t):
        q = rows_of(t, TT)
        r.rh[q, :] = (widen(r.rcol[q, :], C) * r.hcols[q, :].astype(F32)).astype(BF)

    def swish_back(pre, grad):
        gate = jax.nn.sigmoid(pre)
        return grad * (gate * (1.0 + pre * (1.0 - gate)))

    def attend_back(qb):
        q, key = slice(qb * B, (qb + 1) * B), keys_of(qb)
        for h in range(H):
            rot = slice(2 * h * HEAD, 2 * (h + 1) * HEAD)
            chan = slice(h * HEAD, (h + 1) * HEAD)
            weights = weights_of(qb, h)
            scores = (dot_nt(r.qrot[q, rot], r.krot[key, rot]) * weights).astype(BF)
            back = (dot_nt(r.gmix[q, chan], r.val[key, chan]) * weights).astype(BF)
            dq = dot_nn(back, r.krot[key, rot])
            turned = dq[:, :HEAD] * r.cosv[q, :] + dq[:, HEAD:] * r.sinv[q, :]
            r.gproj[0][q, chan] = swish_back(r.qpre[q, chan], turned).astype(BF)
            dk = dot_tn(back, r.qrot[q, rot])
            dv = dot_tn(scores, r.gmix[q, chan])
            for kb in range(key.start // B, qb + 1):
                at = slice(kb * B - key.start, (kb + 1) * B - key.start)
                rows = slice(kb * B, (kb + 1) * B)
                dkb, dvb = dk[at], dv[at]
                if qb < min(kb + REACH, NB - 1):
                    dkb, dvb = dkb + r.dk[rows, rot], dvb + r.dv[rows, chan]
                if kb < qb:
                    r.dk[rows, rot], r.dv[rows, chan] = dkb, dvb
                else:
                    turned = dkb[:, :HEAD] * r.cosv[q, :] + dkb[:, HEAD:] * r.sinv[q, :]
                    r.gproj[1][q, chan] = swish_back(r.kpre[q, chan], turned).astype(BF)
                    r.gproj[2][q, chan] = dvb.astype(BF)

    def output_tile(t):
        q = rows_of(t, 128)
        total = r.recc[1, xi, q].astype(F32)
        for d in range(1, X):
            total = total + r.recx[1, d - 1, q].astype(F32)
        r.bov[rows_of(j * NT + t, 128), :] = (r.hown[q, :] + total).astype(BF)

    def late_core(x):
        return pltpu.make_async_remote_copy(
            src_ref=r.part.at[x, 1 - ci], dst_ref=r.recc.at[0, x], send_sem=r.acs.at[2, x], recv_sem=r.acr.at[2, x],
            device_id={"mp": xi * 2 + 1 - ci}, device_id_type=MESH,
        )

    def late_chip(x, d, t):
        q = slice(t * 128, (t + 1) * 128)
        return pltpu.make_async_remote_copy(
            src_ref=r.part.at[x, ci, q], dst_ref=r.recx.at[0, d - 1, q], send_sem=r.axs.at[2, d - 1, t],
            recv_sem=r.axr.at[2, d - 1, t], device_id={"mp": x * 2 + ci}, device_id_type=MESH,
        )

    def blocks_in(qb):
        return [divmod(at, 2) for at in range(qb * B // TB, (qb + 1) * B // TB)]

    def late_begin(x, c):
        q = slice((x * 2 + c) * TB, (x * 2 + c + 1) * TB)
        out = dot_nt(r.gproj[0][q, :], r.mixw[0])
        for k in range(1, 4):
            out = out + dot_nt(r.gproj[k][q, :], r.mixw[k])
        r.part[x, c] = out.astype(BF)

        @pl.when(ci != c)
        def _():
            late_core(x).start()

    def late_pass(x, c):
        @pl.when(ci == c)
        def _():
            arrived(r.recc.at[0, x], r.acr.at[2, x])

        @pl.when((ci == c) & (xi != x))
        def _():
            for t in range(NT):
                q = slice(t * 128, (t + 1) * 128)
                r.part[x, c, q] = (r.part[x, c, q].astype(F32) + r.recc[0, x, q].astype(F32)).astype(BF)
                late_chip(x, lax.rem(x - xi + X, X), t).start()

    put_grad(3, r.nint, r.gproj[3], turned=True)
    scatter_first(3)
    for qb in range(NB - 1, -1, -1):
        attend_back(qb)
        if qb == NB - 1:
            for copy in used + early:
                settle(copy)
        for x, c in blocks_in(qb):
            late_begin(x, c)
        if qb < NB - 1:
            for x, c in blocks_in(qb + 1):
                late_pass(x, c)
        if qb == NB - 1:
            for d, to, source in peers():
                arrived(token_block(r.hcols)(source), r.ahr.at[1, d])
            each(T // TT, output_grad_tile)
            put_grad(4, r.ufull, r.rh)
            scatter_first(4)
            scatter_handed(7, 8, 9)
            scatter_second(10)
            finish_ff(5)
        if qb == max(NB - 2, 0):
            scatter_handed(10)
            scatter_second(3, 9)
            for t in range(NT):
                for d in range(1, X):
                    arrived(r.recx.at[1, d - 1, t * 128:(t + 1) * 128], r.axr.at[1, d - 1, t])
            each(TB // 128, output_tile)
            share_send(BO, token_block(r.bov))
            finish_ff(6)
        if qb == max(NB - 3, 0):
            scatter_handed(4, 3)
            share_forward(BO, token_block(r.bov))
            finish_ff(7)
    for x, c in blocks_in(0):
        late_pass(x, c)
    pending.extend((late_core(x), None) for x in range(X))
    pending.extend((late_chip(lax.rem(xi + d, X), d, t), None) for d in range(1, X) for t in range(NT))
    for k in (2, 0):
        put_grad(k, r.nint, r.gproj[k], turned=True)
        scatter_first(k)
    scatter_second(4)
    put_grad(1, r.nint, r.gproj[1], turned=True)
    scatter_first(1)
    finish_ff(8, 9, 10)
    scatter_second(2, 0)

    def input_tile(t):
        q = slice(t * 128, (t + 1) * 128)
        low = jnp.concatenate(
            [r.hsend[owner * TB + t * 128:owner * TB + (t + 1) * 128, :] for owner in range(mp)], axis=1
        ).astype(F32)
        grad = sum_tile(0, q)
        v = r.xown[q, :].astype(F32)
        scale = lax.rsqrt(jnp.mean(v * v, axis=-1, keepdims=True) + EPSILON)
        normed = v * scale
        inner = jnp.mean(grad * normed, axis=-1, keepdims=True)
        r.igv[rows_of(j * NT + t, 128), :] = (low + scale * (grad - normed * inner)).astype(BF)

    for t in range(NT):
        for d in range(1, X):
            arrived(r.recx.at[0, d - 1, t * 128:(t + 1) * 128], r.axr.at[2, d - 1, t])
        input_tile(t)
        share_send(IG + t, half_block(r.igv, t))
    scatter_second(1)
    scatter_handed(2)
    share_wait(BO, token_block(r.bov))
    stores = [load(r.bov, r.bo, 0)]

    def grad_block(k):
        return lambda owner: r.gmv.at[k * S:(k + 1) * S, pl.ds(pl.multiple_of(owner * C, C), C)]

    for k in (4, 3, 2, 0, 1):
        total = scatter_total(k).astype(BF)
        r.gmv[k * S:(k + 1) * S, jcols] = total
        r.sqs[...] += squares_of(total.astype(F32))
        share_send(GM + k, grad_block(k))

    r.s1[j] = r.sqs[...]
    for d in range(1, mp):
        go(r.s1.at[j], r.s1.at[j], r.q1s.at[d], r.q1r.at[d], mp=lax.rem(j + d, mp))
    for t in range(NT):
        share_forward(IG + t, half_block(r.igv, t))
    for d in range(1, mp):
        arrived(r.s1.at[lax.rem(j - d + mp, mp)], r.q1r.at[d])
    total = r.s1[0]
    for owner in range(1, mp):
        total = total + r.s1[owner]
    r.s2[i] = total
    for d in range(1, n):
        go(r.s2.at[i], r.s2.at[i], r.q2s.at[d], r.q2r.at[d], dp=lax.rem(i + d, n))
    for k in (4, 3, 2, 0, 1):
        share_forward(GM + k, grad_block(k))
    for d in range(1, n):
        arrived(r.s2.at[lax.rem(i - d + n, n)], r.q2r.at[d])
    total = r.s2[0]
    for owner in range(1, n):
        total = total + r.s2[owner]
    r.sqo[...] = total

    for t in range(NT):
        share_wait(IG + t, half_block(r.igv, t))
    stores.append(load(r.igv, r.ig, 1))
    for k in (4, 3, 2, 0, 1):
        share_wait(GM + k, grad_block(k))
        stores.append(load(r.gmv.at[k * S:(k + 1) * S], r.gmo.at[k], 2 + k))
    for copy in stores:
        copy.wait()
    for copy, when in pending:
        guarded(when, copy.wait_send)


def fused(p, *operands):
    scratch = scratch_of(p)
    names = IN_NAMES + OUT_NAMES + tuple(scratch)
    anywhere = pl.BlockSpec(memory_space=pl.ANY)
    vmem = pl.BlockSpec(memory_space=pltpu.VMEM)
    smem = pl.BlockSpec(memory_space=pltpu.SMEM)
    return pl.pallas_call(
        partial(body, p, names),
        out_shape=(
            jax.ShapeDtypeStruct((p.T, p.D), BF),
            jax.ShapeDtypeStruct((p.T, p.D), BF),
            jax.ShapeDtypeStruct((5, p.S, p.D), BF),
            jax.ShapeDtypeStruct((2, p.F, p.S) if p.FD else (2, p.S, p.F), F32),
            jax.ShapeDtypeStruct((p.F, p.S) if p.FD else (p.S, p.F), F32),
            jax.ShapeDtypeStruct((8, 128), F32),
        ),
        in_specs=[anywhere, anywhere, vmem, smem] + [anywhere] * 5,
        out_specs=(anywhere, anywhere, anywhere, vmem, vmem, vmem),
        scratch_shapes=list(scratch.values()),
        compiler_params=pltpu.CompilerParams(
            collective_id=0, has_side_effects=True, vmem_limit_bytes=VMEM_LIMIT
        ),
    )(*operands)


VMEM_LIMIT = 64 * 2**20 - 2**18


def renew(weight, momentum, shadow, grad, clip_factor):
    clipped = grad * clip_factor
    velocity = MOMENTUM * momentum + clipped
    updated = weight - LEARN_RATE * (clipped + MOMENTUM * velocity)
    average = SHADOW_DECAY * shadow + (1.0 - SHADOW_DECAY) * updated
    return (velocity, average, updated)


def update_body(cuts, *refs):
    kinds, pieces = len(cuts), sum(len(c) for c in cuts)
    sq, carried = refs[0], refs[1:3]
    ins = [refs[3 + 4 * w:7 + 4 * w] for w in range(kinds)]
    refs = refs[3 + 4 * kinds:]
    norm_out, carried_out = refs[0], refs[1:3]
    outs = [refs[3 + 3 * w:6 + 3 * w] for w in range(kinds)]
    refs = refs[3 + 3 * kinds:]
    held = [refs[4 * w:4 * w + 4] for w in range(kinds)]
    made = [refs[4 * kinds + 3 * w:4 * kinds + 3 * w + 3] for w in range(kinds)]
    bounce, (in_sem, out_sem, carry_sem) = refs[7 * kinds:7 * kinds + 2], refs[7 * kinds + 2:]
    loads, order = {}, [(w, c) for w in range(kinds) for c in range(len(cuts[w]))]
    for at, (w, c) in enumerate(order):
        for a in range(4):
            cut = cuts[w][c]
            loads[at, a] = pltpu.make_async_copy(ins[w][a].at[cut], held[w][a].at[cut], in_sem.at[at, a])
            loads[at, a].start()
    carry = [pltpu.make_async_copy(carried[a], bounce[a], carry_sem.at[a]) for a in range(2)]
    for copy in carry:
        copy.start()
    copies = []
    norm = jnp.sqrt(jnp.broadcast_to(jnp.sum(sq[...]), (8, 128)))
    norm_out[...] = norm
    clip_factor = 1.0 / jnp.maximum(jnp.max(norm), 1.0)
    for at, (w, c) in enumerate(order):
        cut = cuts[w][c]
        for a in range(4):
            loads[at, a].wait()
        new = renew(*[held[w][a][cut] for a in range(3)], held[w][3][cut].astype(F32), clip_factor)
        for a in range(3):
            made[w][a][cut] = new[a]
            copy = pltpu.make_async_copy(made[w][a].at[cut], outs[w][a].at[cut], out_sem.at[at, a])
            copy.start()
            copies.append(copy)
    for a in range(2):
        carry[a].wait()
        copy = pltpu.make_async_copy(bounce[a], carried_out[a], carry_sem.at[2 + a])
        copy.start()
        copies.append(copy)
    for copy in copies:
        copy.wait()


def update(sq, carried, weights):
    cuts = [[c for c in range(g[0].shape[0])] if g[0].ndim == 3 else [slice(None)] for g in weights]
    pieces = sum(len(c) for c in cuts)
    anywhere = pl.BlockSpec(memory_space=pl.ANY)
    vmem = pl.BlockSpec(memory_space=pltpu.VMEM)
    flat_in = [a for group in weights for a in group]
    flat_out = [a for group in weights for a in group[:3]]
    dma = pltpu.SemaphoreType.DMA
    size = sum(a.size * a.dtype.itemsize for a in flat_in + flat_out + 2 * list(carried))
    return pl.pallas_call(
        partial(update_body, cuts),
        out_shape=[jax.ShapeDtypeStruct(a.shape, a.dtype) for a in [sq, *carried, *flat_out]],
        in_specs=[vmem] + [anywhere] * (2 + len(flat_in)),
        out_specs=[vmem] + [anywhere] * (2 + len(flat_out)),
        scratch_shapes=[pltpu.VMEM(a.shape, a.dtype) for a in flat_in + flat_out + list(carried)]
        + [dma((pieces, 4)), dma((pieces, 3)), dma((4,))],
        cost_estimate=pl.CostEstimate(flops=size, bytes_accessed=size, transcendentals=0),
        compiler_params=pltpu.CompilerParams(vmem_limit_bytes=VMEM_LIMIT),
    )(sq, *carried, *flat_in)


def turn_tables(tokens):
    theta = np.float32(10000.0) ** (-np.arange(HEAD, dtype=np.float32) / np.float32(HEAD))
    angle = np.arange(tokens, dtype=np.float32)[:, None] * theta.astype(np.float32)[None, :]
    angle = angle.astype(np.float64)
    return np.cos(angle).astype(np.float32), np.sin(angle).astype(np.float32)


def per_device(mesh, block_input, segment_ids, live_length, output_grad, mixer_weight, mixer_momentum, mixer_shadow,
               expand_weight, expand_momentum, expand_shadow, shrink_weight, shrink_momentum, shrink_shadow):
    rows, length, width = block_input.shape
    p = plan_of(mesh, length, width, shrink_weight.shape[0])
    turn = (lambda v: jnp.swapaxes(v, -1, -2)) if p.FD else (lambda v: v)
    if p.FD:
        shards = (turn(expand_weight), shrink_weight)
    else:
        shards = (jnp.concatenate([shrink_weight.T[None], expand_weight], axis=0).astype(BF), shrink_weight)
    cos, sin = turn_tables(length)
    out, grad_in, gm, ge, gs, sq = fused(
        p, block_input[0], output_grad[0], segment_ids, live_length, jnp.asarray(cos), jnp.asarray(sin), mixer_weight, *shards
    )
    new = update(sq, (out, grad_in), (
        (mixer_weight, mixer_momentum, mixer_shadow, gm),
        (turn(expand_weight), turn(expand_momentum), turn(expand_shadow), ge),
        (shrink_weight, shrink_momentum, shrink_shadow, gs if p.FD else gs.T),
    ))
    norm, out, grad_in = new[:3]
    return (out[None], grad_in[None], norm[0, 0], *new[3:6], *(turn(v) for v in new[6:9]), *new[9:12])


def solution(mesh):
    row, mixer, expand, shrink = P("dp", None, None), P(None, "dp", None), P(None, "dp", "mp"), P("mp", "dp")
    return jax.shard_map(
        partial(per_device, mesh),
        mesh=mesh,
        in_specs=(row, P("dp", None), P("dp"), row) + (mixer,) * 3 + (expand,) * 3 + (shrink,) * 3,
        out_specs=(row, row, P()) + (mixer,) * 3 + (expand,) * 3 + (shrink,) * 3,
        check_vma=False,
    )
```

```python
from functools import partial
from types import SimpleNamespace

import jax
import jax.numpy as jnp
import numpy as np
from jax import lax
from jax.experimental import pallas as pl
from jax.experimental.pallas import tpu as pltpu
from jax.sharding import PartitionSpec as P

HEAD = 128
EPSILON = 1e-06
LEARN_RATE = 32.0
MOMENTUM = 0.5
SHADOW_DECAY = 0.5
LAYER_PLACE = 12.0 / 24.0
LONGEST = 512
FF_ORDER = (1, 2, 0)
Y_FIRST = (4, 6)
Z_FIRST = (9, 4)
STRAIGHT = (2, 0, 1)
MESH = pl.DeviceIdType.MESH
BF = jnp.bfloat16
F32 = jnp.float32


def dot_nn(a, b):
    return lax.dot_general(a, b, (((1,), (0,)), ((), ())), preferred_element_type=F32)


def dot_nt(a, b):
    return lax.dot_general(a, b, (((1,), (1,)), ((), ())), preferred_element_type=F32)


def dot_tn(a, b):
    return lax.dot_general(a, b, (((0,), (0,)), ((), ())), preferred_element_type=F32)


def rows_of(index, size):
    return pl.ds(pl.multiple_of(index * size, size), size)


def each(count, body):
    def step(t, carry):
        body(t)
        return carry

    lax.fori_loop(0, count, step, 0)


def widen(column, width):
    return jnp.concatenate([column] * (width // 128), axis=1)


def plan_of(mesh, tokens, width, inner):
    n, mp = mesh.shape["dp"], mesh.shape["mp"]
    lo, core = 2, 2
    return SimpleNamespace(
        n=n, mp=mp, LO=lo, HI=n // lo, X=mp // core, T=tokens, D=width, C=width // mp, F=inner,
        S=width // n, H=width // mp // HEAD, TB=tokens // mp, B=min(256, tokens),
        NT=tokens // mp // 128, FD=(width // n) % 128 == 0,
    )


def scratch_of(p):
    T, D, C, F, S, HI, LO, X, TB, B = p.T, p.D, p.C, p.F, p.S, p.HI, p.LO, p.X, p.TB, p.B
    dma = pltpu.SemaphoreType.DMA
    v = pltpu.VMEM
    return dict(
        mixw=v((4, D, C), BF), wo=v((D, D), BF), ffw=v((3, F, D) if p.FD else (3, D, F), BF),
        xown=v((TB, D), BF), nin=v((T, D), BF), nint=v((D, T), BF), up=v((T, D), BF),
        cosv=v((T, HEAD), F32), sinv=v((T, HEAD), F32),
        segq=v((T, 128), F32), segk=v((8, T), F32), dec=v((2, p.H, B, B), F32),
        qpre=v((T, C), F32), kpre=v((T, C), F32), gpre=v((T, C), F32), val=v((T, C), BF),
        qrot=v((T, 2 * C), BF), krot=v((T, 2 * C), BF), mixed=v((T, C), F32),
        ufull=v((T, D), BF), ss=v((p.mp, 8, T), F32), rcol=v((T, 128), F32),
        inn=v((p.mp, 8, TB), F32), hown=v((TB, D), F32),
        gact=v((T, max(F, 2 * C + HEAD)), F32), uact=v((T, F), BF), prod=v((T, F), BF), ggate=v((T, F), BF), gup=v((T, F), BF),
        part=v((X, 2, TB, D), BF), recc=v((2, X, TB, D), BF), recx=v((2, X - 1, TB, D), BF),
        xv=v((T, D), BF),
        gm=v((5, HI, LO, S, C), BF), rym=v((5, HI, S, C), BF), rzm=v((5, HI - 1, S, C), BF),
        gf=v((3, LO, F, HI * S) if p.FD else (3, HI, LO, S, F), BF),
        ryf=v((3, F, HI * S) if p.FD else (3, HI, S, F), BF),
        rzf=v((3, HI - 1, F, S) if p.FD else (3, HI - 1, S, F), BF),
        relm=v((2, S, C), BF), relf=v((3, F, S) if p.FD else (3, S, F), BF),
        othm=v((HI, S, C), BF), othf=v((HI, F // 2, S) if p.FD else (HI, S // 2, F), BF),
        sqs=v((8, 128), F32), s1=v((p.mp, 8, 128), F32), s2=v((p.n, 8, 128), F32),
        loc=dma((10,)),
        zs=dma((11, HI - 1)), zr=dma((11, HI - 1)), us=dma((len(Y_FIRST), HI - 1)), ur=dma((len(Y_FIRST), HI - 1)),
        zp=dma((11,)), yp=dma((len(Y_FIRST),)), ys=dma((11, HI)), yr=dma((11, HI)),
        xs=dma((20, X - 1)), xr=dma((20, X - 1)), cs=dma((20, X)), cr=dma((20, X)),
        acs=dma((3, X)), acr=dma((3, X)), axs=dma((3, X - 1, p.NT)), axr=dma((3, X - 1, p.NT)),
        bys=dma((11,)), byr=dma((11,)), bzs=dma((11, HI - 1)), bzr=dma((11, HI - 1)),
        bts=dma((11,)), btr=dma((11,)), ozs=dma((2, HI - 1)), ozr=dma((2, HI - 1)), ots=dma((2,)), otr=dma((2,)),
        ags=dma((p.NT, p.mp)), agr=dma((p.NT, p.mp)), ahs=dma((2, p.mp)), ahr=dma((2, p.mp)),
        q1s=dma((p.mp,)), q1r=dma((p.mp,)), q2s=dma((p.n,)), q2r=dma((p.n,)),
    )


IN_NAMES = ("x", "og", "seg", "live", "cos", "sin", "mixsh", "exsh", "shsh")
OUT_NAMES = ("bo", "ig", "gmo", "geo", "gso", "sqo")


def body(p, names, *refs):
    r = SimpleNamespace(**dict(zip(names, refs)))
    n, mp, LO, HI, X, T, D, C, F, S, H, TB, B = (
        p.n, p.mp, p.LO, p.HI, p.X, p.T, p.D, p.C, p.F, p.S, p.H, p.TB, p.B,
    )
    NT, TT = p.NT, min(512, p.T)
    i, j = lax.axis_index("dp"), lax.axis_index("mp")
    zi, yi = i // LO, lax.rem(i, LO)
    xi, ci = j // 2, lax.rem(j, 2)
    jcols = pl.ds(pl.multiple_of(j * C, C), C)
    pending = []
    r.nmid = r.nin
    r.bov, r.igv, r.gmv = r.up, r.ufull, r.wo
    r.dk, r.icol, r.dv = r.gact.at[:, 0:2 * C], r.gact.at[:, 2 * C:2 * C + HEAD], r.mixed
    r.gproj = [r.ggate.at[:, 0:C], r.ggate.at[:, C:2 * C], r.gup.at[:, 0:C], r.gup.at[:, C:2 * C]]
    r.ggated, r.hcols, r.gmix, r.rh = [r.xv.at[:, a * C:(a + 1) * C] for a in range(4)]
    r.hsend, r.gsend = r.uact.at[:, 0:C], r.uact.at[:, C:2 * C]

    def go(src, dst, ssem, rsem, when=None, **device):
        copy = pltpu.make_async_remote_copy(
            src_ref=src, dst_ref=dst, send_sem=ssem, recv_sem=rsem,
            device_id=device, device_id_type=MESH,
        )
        guarded(when, copy.start)
        pending.append((copy, when))
        return copy

    def guarded(when, act):
        if when is None:
            act()
        else:
            pl.when(when)(lambda: act())

    def arrived(dst, sem):
        pltpu.make_async_copy(dst, dst, sem).wait()

    def settle(copy):
        for other, when in pending:
            if other is copy:
                guarded(when, copy.wait_send)
        pending[:] = [entry for entry in pending if entry[0] is not copy]

    def load(src, dst, sem):
        copy = pltpu.make_async_copy(src, dst, r.loc.at[sem])
        copy.start()
        return copy

    own_mix = [load(r.mixsh.at[k, :, jcols], r.qpre.at[k * S:(k + 1) * S], k) for k in range(5)]
    if p.FD:
        stage = [r.gact.at[0:F, m * S:(m + 1) * S] for m in range(3)]
        own_ff = [load(r.shsh if m == 0 else r.exsh.at[m - 1], stage[m], 5 + m) for m in range(3)]
    else:
        own_ff = [load(r.exsh.at[m], r.ffw.at[m, rows_of(i, S)], 5 + m) for m in range(3)]
    load_x = load(r.x, r.xv, 8)
    load_og = load(r.og, r.up, 9)

    def enter():
        barrier = pltpu.get_barrier_semaphore()
        for d in range(1, n):
            pl.semaphore_signal(barrier, inc=1, device_id={"dp": lax.rem(i + d, n)}, device_id_type=MESH)
        for d in range(1, mp):
            pl.semaphore_signal(barrier, inc=1, device_id={"mp": lax.rem(j + d, mp)}, device_id_type=MESH)
        pl.semaphore_wait(barrier, n - 1 + mp - 1)

    def slot(k, device):
        rows = rows_of(device, S)
        if k == 4:
            return r.wo.at[rows, jcols]
        if k < 4:
            return r.mixw.at[k, rows]
        m, half = FF_ORDER[(k - 5) // 2], (k - 5) % 2
        if p.FD:
            return r.ffw.at[m, half * F // 2:(half + 1) * F // 2, rows]
        return r.ffw.at[m, pl.ds(pl.multiple_of(device * S + half * S // 2, S // 2), S // 2)]

    def gather_ready(k):
        if k < 5:
            own_mix[k].wait()
            slot(k, i)[...] = r.qpre[k * S:(k + 1) * S, :].astype(BF)
        else:
            m, half = FF_ORDER[(k - 5) // 2], (k - 5) % 2
            if half == 0:
                own_ff[m].wait()
            if p.FD:
                slot(k, i)[...] = stage[m][half * F // 2:(half + 1) * F // 2, :].astype(BF)

    relays = HI == 4
    next_to_end = (zi == 1) | (zi == 2)

    def along_z(block, ssem, rsem):
        for d in range(1, HI):
            to = lax.rem(zi + d, HI)
            near = (jnp.abs(to - zi) < 3) if relays else None
            go(block, block, ssem.at[d - 1], rsem.at[d - 1], when=near, dp=to * LO + yi)

    def hand_on(block, ssem, rsem):
        if relays:
            end = jnp.where(zi == 2, 3, 0)
            go(block, block, ssem, rsem.at[jnp.where(zi == 2, 2, 0)], when=next_to_end, dp=end * LO + yi)

    def from_z_source(k, d, y):
        return slot(k, lax.rem(zi - d + HI, HI) * LO + y)

    WAYS = [2, 1, *range(3, HI)]

    def gather_send(k):
        src = slot(k, i)
        along_z(src, r.zs.at[k], r.zr.at[k])
        go(src, src, r.ys.at[k, 0], r.yr.at[k, 0], dp=zi * LO + 1 - yi)

    def gather_forward(k):
        if k - 1 in Y_FIRST:
            b = Y_FIRST.index(k - 1)
            block = from_z_source(k - 1, 2, 1 - yi)
            arrived(block, r.ur.at[b, 1])
            hand_on(block, r.yp.at[b], r.ur.at[b])
        if k in Y_FIRST:
            b = Y_FIRST.index(k)
            peers = slot(k, zi * LO + 1 - yi)
            arrived(peers, r.yr.at[k, 0])
            along_z(peers, r.us.at[b], r.ur.at[b])
        for d in WAYS:
            block = from_z_source(k, d, yi)
            arrived(block, r.zr.at[k, d - 1])
            if d == 2:
                hand_on(block, r.zp.at[k], r.zr.at[k])
            if k not in Y_FIRST:
                go(block, block, r.ys.at[k, d], r.yr.at[k, d], dp=zi * LO + 1 - yi)

    def gather_wait(k):
        for d in range(HI):
            if k not in Y_FIRST:
                arrived(from_z_source(k, d, 1 - yi), r.yr.at[k, d])
            elif d in (1, 3) or d > 3:
                arrived(from_z_source(k, d, 1 - yi), r.ur.at[Y_FIRST.index(k), d - 1])

    def share_send(s, block, src=None):
        own = block(j)
        src = own if src is None else src
        for d in range(1, X):
            go(src, own, r.xs.at[s, d - 1], r.xr.at[s, d - 1], mp=lax.rem(xi + d, X) * 2 + ci)
        go(src, own, r.cs.at[s, 0], r.cr.at[s, 0], mp=xi * 2 + 1 - ci)

    def share_forward(s, block):
        for d in range(1, X):
            part = block(lax.rem(xi - d + X, X) * 2 + ci)
            arrived(part, r.xr.at[s, d - 1])
            go(part, part, r.cs.at[s, d], r.cr.at[s, d], mp=xi * 2 + 1 - ci)

    def share_wait(s, block):
        for d in range(X):
            arrived(block(lax.rem(xi - d + X, X) * 2 + 1 - ci), r.cr.at[s, d])

    def sum_begin(s, b, compute, between):
        sent = []

        def pair(d):
            to = lax.rem(xi + d, X)
            compute(to)
            sent.append(go(
                r.part.at[to, 1 - ci], r.recc.at[b, to], r.acs.at[s, d], r.acr.at[s, d], mp=xi * 2 + 1 - ci
            ))

        for d in range(1, X):
            pair(d)
        between()
        for d in range(1, X):
            to = lax.rem(xi + d, X)
            arrived(r.recc.at[b, to], r.acr.at[s, d])
            for t in range(NT):
                q = slice(t * 128, (t + 1) * 128)
                r.part[to, ci, q] = (
                    r.part[to, ci, q].astype(F32) + r.recc[b, to, q].astype(F32)
                ).astype(BF)
                sent.append(go(
                    r.part.at[to, ci, q], r.recx.at[b, d - 1, q], r.axs.at[s, d - 1, t], r.axr.at[s, d - 1, t],
                    mp=to * 2 + ci,
                ))
        pair(0)
        return sent

    def sum_arrived(s, b, t):
        if t == 0:
            arrived(r.recc.at[b, xi], r.acr.at[s, 0])
        for d in range(1, X):
            arrived(r.recx.at[b, d - 1, t * 128:(t + 1) * 128], r.axr.at[s, d - 1, t])

    def sum_tile(b, q):
        total = r.part[xi, ci, q].astype(F32) + r.recc[b, xi, q].astype(F32)
        for d in range(1, X):
            total = total + r.recx[b, d - 1, q].astype(F32)
        return total

    flat = p.FD

    def half_of(k):
        size = (F if flat else S) // 2
        return (k - 5) // 2, slice((k - 5) % 2 * size, ((k - 5) % 2 + 1) * size)

    def block_of(k, z, y):
        if k < 5:
            return r.gm.at[k, z, y]
        m, rows = half_of(k)
        return r.gf.at[m, y, rows, rows_of(z, S)] if flat else r.gf.at[m, z, y, rows]

    def from_y(k):
        if k < 5:
            return r.rym.at[k]
        m, rows = half_of(k)
        return r.ryf.at[m, rows] if flat else r.ryf.at[m, :, rows]

    def from_y_block(k, z):
        ref = from_y(k)
        return ref.at[:, rows_of(z, S)] if flat and k >= 5 else ref.at[z]

    def to_y(k):
        if k < 5:
            return r.gm.at[k, :, 1 - yi]
        m, rows = half_of(k)
        return r.gf.at[m, 1 - yi, rows] if flat else r.gf.at[m, :, 1 - yi, rows]

    def from_z(k, d, own=True):
        if not own:
            return (r.othm if k < 5 else r.othf).at[d - 1]
        if k < 5:
            return r.rzm.at[k, d - 1]
        m, rows = half_of(k)
        return r.rzf.at[m, d - 1, rows]

    def handed(k, own=True):
        if not own:
            return (r.othm if k < 5 else r.othf).at[HI - 1]
        if k < 5:
            return r.relm.at[max(k - 3, 0)]
        m, rows = half_of(k)
        return r.relf.at[m, rows]

    def z_sems(k, own):
        if own:
            return r.bzs.at[k], r.bzr.at[k], r.bts.at[k], r.btr.at[k]
        o = Z_FIRST.index(k)
        return r.ozs.at[o], r.ozr.at[o], r.ots.at[o], r.otr.at[o]

    def stepped(k):
        return relays and k not in STRAIGHT

    def far(d, back=False):
        other = lax.rem(zi + (HI - d if back else d), HI)
        return jnp.abs(other - zi) == 3

    def z_send(k, own, ways):
        y = yi if own else 1 - yi
        ssem, rsem, tsem, trsem = z_sems(k, own)
        for d in ways:
            to = lax.rem(zi + d, HI)
            block, dst = block_of(k, to, y), from_z(k, d, own)
            if stepped(k) and d != 2:
                go(block, handed(k, own), tsem, trsem, when=far(d), dp=jnp.where(zi == 0, 1, 2) * LO + yi)
                go(block, dst, ssem.at[d - 1], rsem.at[d - 1], when=jnp.logical_not(far(d)), dp=to * LO + yi)
            else:
                go(block, dst, ssem.at[d - 1], rsem.at[d - 1], dp=to * LO + yi)

    def z_send_handed(k, own):
        block = block_of(k, lax.rem(zi + 2, HI), yi if own else 1 - yi)

        @pl.when(next_to_end)
        def _():
            arrived(handed(k, own), z_sems(k, own)[3])
            block[...] = (block[...].astype(F32) + handed(k, own)[...].astype(F32)).astype(BF)

        z_send(k, own, [2])

    def z_total(k, own):
        for d in range(1, HI):
            wait = partial(arrived, from_z(k, d, own), z_sems(k, own)[1].at[d - 1])
            guarded(jnp.logical_not(far(d, back=True)) if stepped(k) and d != 2 else None, wait)
        total = block_of(k, zi, yi if own else 1 - yi)[...].astype(F32)
        for d in range(1, HI):
            total = total + from_z(k, d, own)[...].astype(F32)
        return total

    def clear_far_places():
        if not relays:
            return
        for d in (1, 3):
            @pl.when(far(d, back=True))
            def _(d=d):
                r.rzm[:, d - 1] = jnp.zeros((5, S, C), BF)
                for m in range(3):
                    r.rzf[m, d - 1] = jnp.zeros(r.rzf.shape[2:], BF)
                r.othm[d - 1] = jnp.zeros(r.othm.shape[1:], BF)
                r.othf[d - 1] = jnp.zeros(r.othf.shape[1:], BF)

    def near_ways(k):
        return [3, 1] if stepped(k) else list(range(1, HI))

    def scatter_first(*pieces):
        for k in pieces:
            if k in Z_FIRST:
                for own in (False, True):
                    z_send(k, own, near_ways(k))
            else:
                go(to_y(k), from_y(k), r.bys.at[k], r.byr.at[k], dp=zi * LO + 1 - yi)

    def scatter_second(*pieces):
        for k in pieces:
            if k in Z_FIRST:
                block = block_of(k, zi, 1 - yi)
                block[...] = z_total(k, False).astype(BF)
                go(block, from_y_block(k, zi), r.bys.at[k], r.byr.at[k], dp=zi * LO + 1 - yi)
                continue
            arrived(from_y(k), r.byr.at[k])
            for d in range(1, HI):
                to = lax.rem(zi + d, HI)
                block = block_of(k, to, yi)
                block[...] = (block[...].astype(F32) + from_y_block(k, to)[...].astype(F32)).astype(BF)
            z_send(k, True, near_ways(k))

    def scatter_handed(*pieces):
        for k in pieces:
            if stepped(k):
                if k in Z_FIRST:
                    z_send_handed(k, False)
                z_send_handed(k, True)

    def scatter_total(k):
        if k in Z_FIRST:
            arrived(from_y_block(k, zi), r.byr.at[k])
        return z_total(k, True) + from_y_block(k, zi)[...].astype(F32)

    def squares_of(total):
        squared = total * total
        if squared.shape[-1] % 128:
            corner = (lax.broadcasted_iota(jnp.int32, (8, 128), 0) + lax.broadcasted_iota(jnp.int32, (8, 128), 1)) == 0
            return jnp.where(corner, jnp.sum(squared), 0.0)
        folded = jnp.sum(squared.reshape(-1, 8, squared.shape[-1]), axis=0)
        return sum(folded[:, c:c + 128] for c in range(0, folded.shape[-1], 128))

    def finish_ff(*pieces):
        for k in pieces:
            m, rows = half_of(k)
            total = scatter_total(k)
            if m == 0:
                r.gso[rows] = total
            else:
                r.geo[m - 1, rows] = total
            r.sqs[...] += squares_of(total)

    def put_grad(k, lhs, rhs, turned=False):
        g = r.gm.at[k] if k < 5 else r.gf.at[k - 5]
        per = TT // (LO * S)

        def tile(t):
            if turned:
                out = dot_nn(lhs[rows_of(t, TT), :], rhs[...])
            else:
                out = dot_tn(lhs[:, rows_of(t, TT)], rhs[...])
            g[pl.ds(t * per, per)] = out.astype(BF).reshape(per, LO, S, out.shape[-1])

        each(D // TT, tile)

    def put_ff_grad(m, units, model):
        if not flat:
            return put_grad(5 + m, model, units)
        for f in range(0, F, 384):
            q = slice(f, min(f + 384, F))
            out = dot_tn(units[:, q], model[...]).astype(BF)
            for y in range(LO):
                for z in range(HI):
                    r.gf[m, y, q, z * S:(z + 1) * S] = out[:, (z * LO + y) * S:(z * LO + y + 1) * S]

    def to_units(a, m):
        return dot_nt(a, r.ffw[m]) if flat else dot_nn(a, r.ffw[m])

    def to_model(a, m):
        return dot_nn(a, r.ffw[m]) if flat else dot_nt(a, r.ffw[m])

    gather_ready(0)
    gather_ready(1)
    enter()
    gather_send(0)
    gather_send(1)
    r.sqs[...] = jnp.zeros_like(r.sqs)

    length = r.live[0]
    load_x.wait()

    def norm_tile(t):
        q = rows_of(t, 128)
        v = r.xv[q, :].astype(F32)
        r.nin[q, :] = (v * lax.rsqrt(jnp.mean(v * v, axis=-1, keepdims=True) + EPSILON)).astype(BF)

    each(T // 128, norm_tile)
    for k in range(2, 5):
        gather_ready(k)
    load_x_own = load(r.x.at[rows_of(j, TB)], r.xown, 8)
    load_cos = load(r.cos, r.cosv, 0)
    load_sin = load(r.sin, r.sinv, 1)

    load_cos.wait()
    load_sin.wait()
    load_x_own.wait()

    def turn_into(pre_ref, rot_ref, k):
        def tile(t):
            q = rows_of(t, TT)
            pre = dot_nn(r.nin[q, :], r.mixw[k])
            pre_ref[q, :] = pre
            act = pre * jax.nn.sigmoid(pre)
            c, s = r.cosv[q, :], r.sinv[q, :]
            for h in range(H):
                a = act[:, h * HEAD:(h + 1) * HEAD]
                rot_ref[q, 2 * h * HEAD:(2 * h + 1) * HEAD] = (a * c).astype(BF)
                rot_ref[q, (2 * h + 1) * HEAD:(2 * h + 2) * HEAD] = (a * s).astype(BF)

        each(T // TT, tile)

    def project_into(ref, k):
        def tile(t):
            q = rows_of(t, TT)
            ref[q, :] = dot_nn(r.nin[q, :], r.mixw[k]).astype(ref.dtype)

        each(T // TT, tile)

    gather_forward(0)
    gather_send(2)
    gather_forward(1)
    gather_send(3)
    gather_wait(0)
    turn_into(r.qpre, r.qrot, 0)
    gather_ready(5)
    gather_ready(6)
    gather_forward(2)
    gather_send(4)
    gather_wait(1)
    turn_into(r.kpre, r.krot, 1)
    gather_forward(3)
    gather_send(5)
    gather_send(6)
    gather_wait(2)
    project_into(r.val, 2)
    for k in range(7, 11):
        gather_ready(k)
    place = lax.broadcasted_iota(jnp.int32, (1, T), 1)
    segment = r.seg[...].astype(F32)
    r.segk[...] = jnp.broadcast_to(jnp.where(place < length, segment, -2.0), (8, T))
    seg_q = jnp.where(place < length, segment, -1.0)
    for t in range(T // 128):
        q = slice(t * 128, t * 128 + 128)
        r.segq[q, :] = jnp.transpose(jnp.broadcast_to(seg_q[:, q], (128, 128)))

    down = lax.broadcasted_iota(jnp.int32, (B, B), 0)
    over = lax.broadcasted_iota(jnp.int32, (B, B), 1)
    heads = D // HEAD

    def rate_of(h):
        return -(8.0 * (j * H + h).astype(F32) / heads) * (1.0 - LAYER_PLACE)

    for h in range(H):
        rate = rate_of(h)
        for o in range(2):
            distance = down - over + o * B
            fade = jnp.exp(rate * jnp.maximum(distance, 0).astype(F32))
            r.dec[o, h] = jnp.where(distance >= 0, fade, 0.0)

    gather_forward(4)
    gather_send(7)
    gather_wait(3)
    project_into(r.gpre, 3)

    def wo_block(owner):
        return r.wo.at[:, pl.ds(pl.multiple_of(owner * C, C), C)]


    NB = T // B
    REACH = LONGEST // B

    def keys_of(qb):
        return slice(max(0, qb - REACH) * B, (qb + 1) * B)

    def weights_of(qb, h):
        key = keys_of(qb)
        width = key.stop - key.start
        fades = [r.dec[min(o, 1), h] for o in range(width // B - 1, -1, -1)]
        for o in range(2, width // B):
            fades[width // B - 1 - o] *= jnp.exp(rate_of(h) * ((o - 1) * B))
        seen = jnp.broadcast_to(r.segk[0:1, key], (B, width))
        same = widen(r.segq[qb * B:(qb + 1) * B, :], width) == seen
        return jnp.where(same, jnp.concatenate(fades, axis=1), 0.0)

    def u_block(qb):
        return lambda owner: r.ufull.at[qb * B:(qb + 1) * B, pl.ds(pl.multiple_of(owner * C, C), C)]

    def attend(qb):
        q = slice(qb * B, (qb + 1) * B)
        squares = jnp.zeros((B, 1), F32)
        for h in range(H):
            rot = slice(2 * h * HEAD, 2 * (h + 1) * HEAD)
            chan = slice(h * HEAD, (h + 1) * HEAD)
            key = keys_of(qb)
            scores = dot_nt(r.qrot[q, rot], r.krot[key, rot]) * weights_of(qb, h)
            total = dot_nn(scores.astype(BF), r.val[key, chan])
            r.mixed[q, chan] = total
            squares = squares + jnp.sum(total * total, axis=-1, keepdims=True)
            r.ufull[q, pl.ds(pl.multiple_of(j * C + h * HEAD, HEAD), HEAD)] = (
                total * r.gpre[q, chan]
            ).astype(BF)
        r.ss[j, :, q] = jnp.transpose(jnp.broadcast_to(squares, (B, 128)))[0:8, :]

    def ss_block(owner):
        return r.ss.at[owner]

    for qb in range(NB):
        attend(qb)
        share_send(1 + qb, u_block(qb))
        if qb == NB - 1:
            share_send(1 + NB, ss_block)
        if qb == 0:
            gather_forward(5)
            gather_send(8)
        if qb == 1:
            gather_wait(4)
            share_send(0, wo_block)
        if qb == 3:
            share_forward(0, wo_block)
        if qb == 2:
            gather_forward(6)
            gather_send(9)
        if qb > 0:
            share_forward(qb, u_block(qb - 1))
    share_forward(NB, u_block(NB - 1))
    share_forward(1 + NB, ss_block)
    gather_forward(7)
    gather_send(10)
    load_og.wait()

    def live_tile(t):
        q = rows_of(t, 128)
        place = lax.broadcasted_iota(jnp.int32, (128, D), 0) + t * 128
        r.up[q, :] = jnp.where(place < length, r.up[q, :].astype(F32), 0.0).astype(BF)

    each(T // 128, live_tile)

    for t in range(D // 128):
        q = slice(t * 128, t * 128 + 128)
        r.nint[q, :] = jnp.transpose(r.nin[:, q])
    clear_far_places()
    gather_forward(8)
    share_wait(0, wo_block)
    for qb in range(NB):
        share_wait(1 + qb, u_block(qb))
    share_wait(1 + NB, ss_block)
    early = [copy for copy, when in pending]

    total_ss = r.ss[0]
    for owner in range(1, mp):
        total_ss = total_ss + r.ss[owner]
    inverse = lax.rsqrt(total_ss * (1.0 / D) + EPSILON)
    for t in range(T // 128):
        q = slice(t * 128, t * 128 + 128)
        r.rcol[q, :] = jnp.transpose(jnp.broadcast_to(inverse[0:1, q], (128, 128)))

    def hidden_tile(t):
        q = rows_of(t, TB)
        out = widen(r.rcol[q, :], D) * dot_nn(r.ufull[q, :], r.wo[...])
        hidden = r.xv[q, :].astype(F32) + out
        scale = lax.rsqrt(jnp.mean(hidden * hidden, axis=-1, keepdims=True) + EPSILON)
        r.nmid[q, :] = (hidden * scale).astype(BF)

        @pl.when(t == j)
        def _():
            r.hown[...] = hidden

    each(T // TB, hidden_tile)
    gather_forward(9)
    gather_wait(5)
    gather_wait(6)

    def gate_tile(t):
        q = rows_of(t, TT)
        r.gact[q, 0:F] = to_units(r.nmid[q, :], 1)

    each(T // TT, gate_tile)
    gather_forward(10)
    gather_wait(7)
    gather_wait(8)

    def up_tile(t):
        q = rows_of(t, TT)
        upper = to_units(r.nmid[q, :], 2)
        r.uact[q, :] = upper.astype(BF)
        r.prod[q, :] = (r.gact[q, 0:F] * upper).astype(BF)

    each(T // TT, up_tile)
    put_ff_grad(0, r.prod, r.up)
    scatter_first(5, 6)
    gather_wait(9)
    gather_wait(10)

    def mid_pair(x):
        q = rows_of(x, 2 * TB)
        g = to_units(r.up[q, :], 0)
        grad_gate, grad_up = (g * r.uact[q, :].astype(F32)).astype(BF), (g * r.gact[q, 0:F]).astype(BF)
        r.ggate[q, :] = grad_gate
        r.gup[q, :] = grad_up
        r.part[x] = (to_model(grad_gate, 1) + to_model(grad_up, 2)).astype(BF).reshape(2, TB, D)

    used = sum_begin(0, 0, mid_pair, partial(scatter_second, 5))
    put_ff_grad(1, r.ggate, r.nmid)
    scatter_first(7, 8)
    scatter_handed(5)
    scatter_second(6)

    def back_tile(t):
        q = slice(t * 128, (t + 1) * 128)
        here = rows_of(j * (TB // 128) + t, 128)
        grad = sum_tile(0, q)
        hidden = r.hown[q, :]
        scale = lax.rsqrt(jnp.mean(hidden * hidden, axis=-1, keepdims=True) + EPSILON)
        normed = hidden * scale
        inner = jnp.mean(grad * normed, axis=-1, keepdims=True)
        out = r.up[here, :].astype(F32) + scale * (grad - normed * inner)
        low = out.astype(BF)
        for owner in range(mp):
            r.hsend[owner * TB + t * 128:owner * TB + (t + 1) * 128, :] = low[:, owner * C:(owner + 1) * C]
        mixer_out = hidden - r.xown[q, :].astype(F32)
        product = jnp.sum(low.astype(F32) * mixer_out, axis=-1, keepdims=True) * (1.0 / D)
        r.inn[j, :, q] = jnp.transpose(jnp.broadcast_to(product, (128, 128)))[0:8, :]

    def token_block(ref):
        return lambda owner: ref.at[rows_of(owner, TB)]

    BO, GM, IG = 2 + NB, 3 + NB, 8 + NB

    def half_block(ref, t):
        return lambda owner: ref.at[rows_of(owner * NT + t, 128)]

    def peers():
        return [(d, lax.rem(j + d, mp), lax.rem(j - d + mp, mp)) for d in range(1, mp)]

    for t in range(NT):
        sum_arrived(0, 0, t)
        back_tile(t)
    low = jnp.concatenate([r.hsend[owner * TB:(owner + 1) * TB, :] for owner in range(mp)], axis=1)
    grad_gated = dot_nt(low, r.wo[...]).astype(BF)
    for owner in range(mp):
        r.gsend[owner * TB:(owner + 1) * TB, :] = grad_gated[:, owner * C:(owner + 1) * C]
    for d, to, source in peers():
        go(token_block(r.gsend)(to), token_block(r.ggated)(j), r.ags.at[0, d], r.agr.at[0, d], mp=to)
    own_rows = rows_of(j, TB)
    r.ggated[own_rows, :] = r.gsend[own_rows, :]
    r.hcols[own_rows, :] = r.hsend[own_rows, :]
    for d, to, source in peers():
        go(r.inn.at[j], r.inn.at[j], r.ahs.at[0, d], r.ahr.at[0, d], mp=to)
    for d, to, source in peers():
        go(token_block(r.hsend)(to), token_block(r.hcols)(j), r.ahs.at[1, d], r.ahr.at[1, d], mp=to)
    put_ff_grad(2, r.gup, r.nmid)
    scatter_first(9, 10)
    scatter_handed(6)
    scatter_second(7)
    for copy in used:
        settle(copy)

    def expand_tile(t):
        r.part[t // 2, lax.rem(t, 2)] = to_model(r.prod[rows_of(t, TB), :], 0).astype(BF)

    each(mp, expand_tile)
    used = [
        go(r.part.at[to, 1 - ci], r.recc.at[1, to], r.acs.at[1, d], r.acr.at[1, d], mp=xi * 2 + 1 - ci)
        for d, to in [(d, lax.rem(xi + d, X)) for d in range(X)]
    ]
    for d, to, source in peers():
        arrived(token_block(r.ggated)(source), r.agr.at[0, d])
        arrived(r.inn.at[source], r.ahr.at[0, d])
    for owner in range(mp):
        for t in range(TB // 128):
            row = r.inn[owner, 0:1, t * 128:(t + 1) * 128]
            q = slice(owner * TB + t * 128, owner * TB + (t + 1) * 128)
            r.icol[q, :] = jnp.transpose(jnp.broadcast_to(row, (128, 128)))

    def gated_tile(t):
        q = rows_of(t, TT)
        grad = r.ggated[q, :].astype(F32)
        inner = widen(r.icol[q, :], C)
        inverse = widen(r.rcol[q, :], C)
        normed = r.mixed[q, :] * inverse
        r.gproj[3][q, :] = (grad * normed).astype(BF)
        r.gmix[q, :] = (inverse * (grad * r.gpre[q, :] - normed * inner)).astype(BF)

    each(T // TT, gated_tile)

    for d in [*range(1, X), 0]:
        to = lax.rem(xi + d, X)
        arrived(r.recc.at[1, to], r.acr.at[1, d])
        for t in range(NT):
            q = slice(t * 128, (t + 1) * 128)
            r.recc[1, to, q] = (r.part[to, ci, q].astype(F32) + r.recc[1, to, q].astype(F32)).astype(BF)
            if d:
                go(r.recc.at[1, to, q], r.recx.at[1, d - 1, q], r.axs.at[1, d - 1, t], r.axr.at[1, d - 1, t], mp=to * 2 + ci)
    scatter_second(8)

    def output_grad_tile(t):
        q = rows_of(t, TT)
        r.rh[q, :] = (widen(r.rcol[q, :], C) * r.hcols[q, :].astype(F32)).astype(BF)

    def swish_back(pre, grad):
        gate = jax.nn.sigmoid(pre)
        return grad * (gate * (1.0 + pre * (1.0 - gate)))

    def attend_back(qb):
        q, key = slice(qb * B, (qb + 1) * B), keys_of(qb)
        for h in range(H):
            rot = slice(2 * h * HEAD, 2 * (h + 1) * HEAD)
            chan = slice(h * HEAD, (h + 1) * HEAD)
            weights = weights_of(qb, h)
            scores = (dot_nt(r.qrot[q, rot], r.krot[key, rot]) * weights).astype(BF)
            back = (dot_nt(r.gmix[q, chan], r.val[key, chan]) * weights).astype(BF)
            dq = dot_nn(back, r.krot[key, rot])
            turned = dq[:, :HEAD] * r.cosv[q, :] + dq[:, HEAD:] * r.sinv[q, :]
            r.gproj[0][q, chan] = swish_back(r.qpre[q, chan], turned).astype(BF)
            dk = dot_tn(back, r.qrot[q, rot])
            dv = dot_tn(scores, r.gmix[q, chan])
            for kb in range(key.start // B, qb + 1):
                at = slice(kb * B - key.start, (kb + 1) * B - key.start)
                rows = slice(kb * B, (kb + 1) * B)
                dkb, dvb = dk[at], dv[at]
                if qb < min(kb + REACH, NB - 1):
                    dkb, dvb = dkb + r.dk[rows, rot], dvb + r.dv[rows, chan]
                if kb < qb:
                    r.dk[rows, rot], r.dv[rows, chan] = dkb, dvb
                else:
                    turned = dkb[:, :HEAD] * r.cosv[q, :] + dkb[:, HEAD:] * r.sinv[q, :]
                    r.gproj[1][q, chan] = swish_back(r.kpre[q, chan], turned).astype(BF)
                    r.gproj[2][q, chan] = dvb.astype(BF)

    def output_tile(t):
        q = rows_of(t, 128)
        total = r.recc[1, xi, q].astype(F32)
        for d in range(1, X):
            total = total + r.recx[1, d - 1, q].astype(F32)
        r.bov[rows_of(j * NT + t, 128), :] = (r.hown[q, :] + total).astype(BF)

    def late_core(x):
        return pltpu.make_async_remote_copy(
            src_ref=r.part.at[x, 1 - ci], dst_ref=r.recc.at[0, x], send_sem=r.acs.at[2, x], recv_sem=r.acr.at[2, x],
            device_id={"mp": xi * 2 + 1 - ci}, device_id_type=MESH,
        )

    def late_chip(x, d, t):
        q = slice(t * 128, (t + 1) * 128)
        return pltpu.make_async_remote_copy(
            src_ref=r.part.at[x, ci, q], dst_ref=r.recx.at[0, d - 1, q], send_sem=r.axs.at[2, d - 1, t],
            recv_sem=r.axr.at[2, d - 1, t], device_id={"mp": x * 2 + ci}, device_id_type=MESH,
        )

    def blocks_in(qb):
        return [divmod(at, 2) for at in range(qb * B // TB, (qb + 1) * B // TB)]

    def late_begin(x, c):
        q = slice((x * 2 + c) * TB, (x * 2 + c + 1) * TB)
        out = dot_nt(r.gproj[0][q, :], r.mixw[0])
        for k in range(1, 4):
            out = out + dot_nt(r.gproj[k][q, :], r.mixw[k])
        r.part[x, c] = out.astype(BF)

        @pl.when(ci != c)
        def _():
            late_core(x).start()

    def late_pass(x, c):
        @pl.when(ci == c)
        def _():
            arrived(r.recc.at[0, x], r.acr.at[2, x])

        @pl.when((ci == c) & (xi != x))
        def _():
            for t in range(NT):
                q = slice(t * 128, (t + 1) * 128)
                r.part[x, c, q] = (r.part[x, c, q].astype(F32) + r.recc[0, x, q].astype(F32)).astype(BF)
                late_chip(x, lax.rem(x - xi + X, X), t).start()

    put_grad(3, r.nint, r.gproj[3], turned=True)
    scatter_first(3)
    for qb in range(NB - 1, -1, -1):
        attend_back(qb)
        if qb == NB - 1:
            for copy in used + early:
                settle(copy)
        for x, c in blocks_in(qb):
            late_begin(x, c)
        if qb < NB - 1:
            for x, c in blocks_in(qb + 1):
                late_pass(x, c)
        if qb == NB - 1:
            for d, to, source in peers():
                arrived(token_block(r.hcols)(source), r.ahr.at[1, d])
            each(T // TT, output_grad_tile)
            put_grad(4, r.ufull, r.rh)
            scatter_first(4)
            scatter_handed(7, 8, 9)
            scatter_second(10)
            finish_ff(5)
        if qb == max(NB - 2, 0):
            scatter_handed(10)
            scatter_second(3, 9)
            for t in range(NT):
                for d in range(1, X):
                    arrived(r.recx.at[1, d - 1, t * 128:(t + 1) * 128], r.axr.at[1, d - 1, t])
            each(TB // 128, output_tile)
            share_send(BO, token_block(r.bov))
            finish_ff(6)
        if qb == max(NB - 3, 0):
            scatter_handed(4, 3)
            share_forward(BO, token_block(r.bov))
            finish_ff(7)
    for x, c in blocks_in(0):
        late_pass(x, c)
    pending.extend((late_core(x), None) for x in range(X))
    pending.extend((late_chip(lax.rem(xi + d, X), d, t), None) for d in range(1, X) for t in range(NT))
    for k in (2, 0):
        put_grad(k, r.nint, r.gproj[k], turned=True)
        scatter_first(k)
    scatter_second(4)
    put_grad(1, r.nint, r.gproj[1], turned=True)
    scatter_first(1)
    finish_ff(8, 9, 10)
    scatter_second(2, 0)

    def input_tile(t):
        q = slice(t * 128, (t + 1) * 128)
        low = jnp.concatenate(
            [r.hsend[owner * TB + t * 128:owner * TB + (t + 1) * 128, :] for owner in range(mp)], axis=1
        ).astype(F32)
        grad = sum_tile(0, q)
        v = r.xown[q, :].astype(F32)
        scale = lax.rsqrt(jnp.mean(v * v, axis=-1, keepdims=True) + EPSILON)
        normed = v * scale
        inner = jnp.mean(grad * normed, axis=-1, keepdims=True)
        r.igv[rows_of(j * NT + t, 128), :] = (low + scale * (grad - normed * inner)).astype(BF)

    for t in range(NT):
        for d in range(1, X):
            arrived(r.recx.at[0, d - 1, t * 128:(t + 1) * 128], r.axr.at[2, d - 1, t])
        input_tile(t)
        share_send(IG + t, half_block(r.igv, t))
    scatter_second(1)
    scatter_handed(2)
    share_wait(BO, token_block(r.bov))
    stores = [load(r.bov, r.bo, 0)]

    def grad_block(k):
        return lambda owner: r.gmv.at[k * S:(k + 1) * S, pl.ds(pl.multiple_of(owner * C, C), C)]

    for k in (4, 3, 2, 0, 1):
        total = scatter_total(k).astype(BF)
        r.gmv[k * S:(k + 1) * S, jcols] = total
        r.sqs[...] += squares_of(total.astype(F32))
        share_send(GM + k, grad_block(k))

    r.s1[j] = r.sqs[...]
    for d in range(1, mp):
        go(r.s1.at[j], r.s1.at[j], r.q1s.at[d], r.q1r.at[d], mp=lax.rem(j + d, mp))
    for t in range(NT):
        share_forward(IG + t, half_block(r.igv, t))
    for d in range(1, mp):
        arrived(r.s1.at[lax.rem(j - d + mp, mp)], r.q1r.at[d])
    total = r.s1[0]
    for owner in range(1, mp):
        total = total + r.s1[owner]
    r.s2[i] = total
    for d in range(1, n):
        go(r.s2.at[i], r.s2.at[i], r.q2s.at[d], r.q2r.at[d], dp=lax.rem(i + d, n))
    for k in (4, 3, 2, 0, 1):
        share_forward(GM + k, grad_block(k))
    for d in range(1, n):
        arrived(r.s2.at[lax.rem(i - d + n, n)], r.q2r.at[d])
    total = r.s2[0]
    for owner in range(1, n):
        total = total + r.s2[owner]
    r.sqo[...] = total

    for t in range(NT):
        share_wait(IG + t, half_block(r.igv, t))
    stores.append(load(r.igv, r.ig, 1))
    for k in (4, 3, 2, 0, 1):
        share_wait(GM + k, grad_block(k))
        stores.append(load(r.gmv.at[k * S:(k + 1) * S], r.gmo.at[k], 2 + k))
    for copy in stores:
        copy.wait()
    for copy, when in pending:
        guarded(when, copy.wait_send)


def fused(p, *operands):
    scratch = scratch_of(p)
    names = IN_NAMES + OUT_NAMES + tuple(scratch)
    anywhere = pl.BlockSpec(memory_space=pl.ANY)
    vmem = pl.BlockSpec(memory_space=pltpu.VMEM)
    smem = pl.BlockSpec(memory_space=pltpu.SMEM)
    return pl.pallas_call(
        partial(body, p, names),
        out_shape=(
            jax.ShapeDtypeStruct((p.T, p.D), BF),
            jax.ShapeDtypeStruct((p.T, p.D), BF),
            jax.ShapeDtypeStruct((5, p.S, p.D), BF),
            jax.ShapeDtypeStruct((2, p.F, p.S) if p.FD else (2, p.S, p.F), F32),
            jax.ShapeDtypeStruct((p.F, p.S) if p.FD else (p.S, p.F), F32),
            jax.ShapeDtypeStruct((8, 128), F32),
        ),
        in_specs=[anywhere, anywhere, vmem, smem] + [anywhere] * 5,
        out_specs=(anywhere, anywhere, anywhere, vmem, vmem, vmem),
        scratch_shapes=list(scratch.values()),
        compiler_params=pltpu.CompilerParams(
            collective_id=0, has_side_effects=True, vmem_limit_bytes=VMEM_LIMIT
        ),
    )(*operands)


VMEM_LIMIT = 64 * 2**20 - 2**18


def renew(weight, momentum, shadow, grad, clip_factor):
    clipped = grad * clip_factor
    velocity = MOMENTUM * momentum + clipped
    updated = weight - LEARN_RATE * (clipped + MOMENTUM * velocity)
    average = SHADOW_DECAY * shadow + (1.0 - SHADOW_DECAY) * updated
    return (velocity, average, updated)


def update_body(cuts, *refs):
    kinds, pieces = len(cuts), sum(len(c) for c in cuts)
    sq, carried = refs[0], refs[1:3]
    ins = [refs[3 + 4 * w:7 + 4 * w] for w in range(kinds)]
    refs = refs[3 + 4 * kinds:]
    norm_out, carried_out = refs[0], refs[1:3]
    outs = [refs[3 + 3 * w:6 + 3 * w] for w in range(kinds)]
    refs = refs[3 + 3 * kinds:]
    held = [refs[4 * w:4 * w + 4] for w in range(kinds)]
    made = [refs[4 * kinds + 3 * w:4 * kinds + 3 * w + 3] for w in range(kinds)]
    bounce, (in_sem, out_sem, carry_sem) = refs[7 * kinds:7 * kinds + 2], refs[7 * kinds + 2:]
    loads, order = {}, [(w, c) for w in range(kinds) for c in range(len(cuts[w]))]
    for at, (w, c) in enumerate(order):
        for a in range(4):
            cut = cuts[w][c]
            loads[at, a] = pltpu.make_async_copy(ins[w][a].at[cut], held[w][a].at[cut], in_sem.at[at, a])
            loads[at, a].start()
    carry = [pltpu.make_async_copy(carried[a], bounce[a], carry_sem.at[a]) for a in range(2)]
    for copy in carry:
        copy.start()
    copies = []
    norm = jnp.sqrt(jnp.broadcast_to(jnp.sum(sq[...]), (8, 128)))
    norm_out[...] = norm
    clip_factor = 1.0 / jnp.maximum(jnp.max(norm), 1.0)
    for at, (w, c) in enumerate(order):
        cut = cuts[w][c]
        for a in range(4):
            loads[at, a].wait()
        new = renew(*[held[w][a][cut] for a in range(3)], held[w][3][cut].astype(F32), clip_factor)
        for a in range(3):
            made[w][a][cut] = new[a]
            copy = pltpu.make_async_copy(made[w][a].at[cut], outs[w][a].at[cut], out_sem.at[at, a])
            copy.start()
            copies.append(copy)
    for a in range(2):
        carry[a].wait()
        copy = pltpu.make_async_copy(bounce[a], carried_out[a], carry_sem.at[2 + a])
        copy.start()
        copies.append(copy)
    for copy in copies:
        copy.wait()


def update(sq, carried, weights):
    cuts = [[c for c in range(g[0].shape[0])] if g[0].ndim == 3 else [slice(None)] for g in weights]
    pieces = sum(len(c) for c in cuts)
    anywhere = pl.BlockSpec(memory_space=pl.ANY)
    vmem = pl.BlockSpec(memory_space=pltpu.VMEM)
    flat_in = [a for group in weights for a in group]
    flat_out = [a for group in weights for a in group[:3]]
    dma = pltpu.SemaphoreType.DMA
    size = sum(a.size * a.dtype.itemsize for a in flat_in + flat_out + 2 * list(carried))
    return pl.pallas_call(
        partial(update_body, cuts),
        out_shape=[jax.ShapeDtypeStruct(a.shape, a.dtype) for a in [sq, *carried, *flat_out]],
        in_specs=[vmem] + [anywhere] * (2 + len(flat_in)),
        out_specs=[vmem] + [anywhere] * (2 + len(flat_out)),
        scratch_shapes=[pltpu.VMEM(a.shape, a.dtype) for a in flat_in + flat_out + list(carried)]
        + [dma((pieces, 4)), dma((pieces, 3)), dma((4,))],
        cost_estimate=pl.CostEstimate(flops=size, bytes_accessed=size, transcendentals=0),
        compiler_params=pltpu.CompilerParams(vmem_limit_bytes=VMEM_LIMIT),
    )(sq, *carried, *flat_in)


def turn_tables(tokens):
    theta = np.float32(10000.0) ** (-np.arange(HEAD, dtype=np.float32) / np.float32(HEAD))
    angle = np.arange(tokens, dtype=np.float32)[:, None] * theta.astype(np.float32)[None, :]
    angle = angle.astype(np.float64)
    return np.cos(angle).astype(np.float32), np.sin(angle).astype(np.float32)


def per_device(mesh, block_input, segment_ids, live_length, output_grad, mixer_weight, mixer_momentum, mixer_shadow,
               expand_weight, expand_momentum, expand_shadow, shrink_weight, shrink_momentum, shrink_shadow):
    rows, length, width = block_input.shape
    p = plan_of(mesh, length, width, shrink_weight.shape[0])
    turn = (lambda v: jnp.swapaxes(v, -1, -2)) if p.FD else (lambda v: v)
    if p.FD:
        shards = (turn(expand_weight), shrink_weight)
    else:
        shards = (jnp.concatenate([shrink_weight.T[None], expand_weight], axis=0).astype(BF), shrink_weight)
    cos, sin = turn_tables(length)
    out, grad_in, gm, ge, gs, sq = fused(
        p, block_input[0], output_grad[0], segment_ids, live_length, jnp.asarray(cos), jnp.asarray(sin), mixer_weight, *shards
    )
    new = update(sq, (out, grad_in), (
        (mixer_weight, mixer_momentum, mixer_shadow, gm),
        (turn(expand_weight), turn(expand_momentum), turn(expand_shadow), ge),
        (shrink_weight, shrink_momentum, shrink_shadow, gs if p.FD else gs.T),
    ))
    norm, out, grad_in = new[:3]
    return (out[None], grad_in[None], norm[0, 0], *new[3:6], *(turn(v) for v in new[6:9]), *new[9:12])


def solution(mesh):
    row, mixer, expand, shrink = P("dp", None, None), P(None, "dp", None), P(None, "dp", "mp"), P("mp", "dp")
    return jax.shard_map(
        partial(per_device, mesh),
        mesh=mesh,
        in_specs=(row, P("dp", None), P("dp"), row) + (mixer,) * 3 + (expand,) * 3 + (shrink,) * 3,
        out_specs=(row, row, P()) + (mixer,) * 3 + (expand,) * 3 + (shrink,) * 3,
        check_vma=False,
    )
```

```python
from functools import partial
from types import SimpleNamespace

import jax
import jax.numpy as jnp
import numpy as np
from jax import lax
from jax.experimental import pallas as pl
from jax.experimental.pallas import tpu as pltpu
from jax.sharding import PartitionSpec as P

HEAD = 128
EPSILON = 1e-06
LEARN_RATE = 32.0
MOMENTUM = 0.5
SHADOW_DECAY = 0.5
LAYER_PLACE = 12.0 / 24.0
LONGEST = 512
FF_ORDER = (1, 2, 0)
Y_FIRST = (4, 6)
Z_FIRST = (9, 4)
STRAIGHT = (2, 0, 1)
MESH = pl.DeviceIdType.MESH
BF = jnp.bfloat16
F32 = jnp.float32


def dot_nn(a, b):
    return lax.dot_general(a, b, (((1,), (0,)), ((), ())), preferred_element_type=F32)


def dot_nt(a, b):
    return lax.dot_general(a, b, (((1,), (1,)), ((), ())), preferred_element_type=F32)


def dot_tn(a, b):
    return lax.dot_general(a, b, (((0,), (0,)), ((), ())), preferred_element_type=F32)


def rows_of(index, size):
    return pl.ds(pl.multiple_of(index * size, size), size)


def each(count, body):
    def step(t, carry):
        body(t)
        return carry

    lax.fori_loop(0, count, step, 0)


def widen(column, width):
    return jnp.concatenate([column] * (width // 128), axis=1)


def plan_of(mesh, tokens, width, inner):
    n, mp = mesh.shape["dp"], mesh.shape["mp"]
    lo, core = 2, 2
    return SimpleNamespace(
        n=n, mp=mp, LO=lo, HI=n // lo, X=mp // core, T=tokens, D=width, C=width // mp, F=inner,
        S=width // n, H=width // mp // HEAD, TB=tokens // mp, B=min(256, tokens),
        NT=tokens // mp // 128, FD=(width // n) % 128 == 0,
    )


def scratch_of(p):
    T, D, C, F, S, HI, LO, X, TB, B = p.T, p.D, p.C, p.F, p.S, p.HI, p.LO, p.X, p.TB, p.B
    dma = pltpu.SemaphoreType.DMA
    v = pltpu.VMEM
    return dict(
        mixw=v((4, D, C), BF), wo=v((D, D), BF), ffw=v((3, F, D) if p.FD else (3, D, F), BF),
        xown=v((TB, D), BF), nin=v((T, D), BF), nint=v((D, T), BF), up=v((T, D), BF),
        cosv=v((T, HEAD), F32), sinv=v((T, HEAD), F32),
        segq=v((T, 128), F32), segk=v((8, T), F32), dec=v((2, p.H, B, B), F32),
        qpre=v((T, C), F32), kpre=v((T, C), F32), gpre=v((T, C), F32), val=v((T, C), BF),
        qrot=v((T, 2 * C), BF), krot=v((T, 2 * C), BF), mixed=v((T, C), F32),
        ufull=v((T, D), BF), ss=v((p.mp, 8, T), F32), rcol=v((T, 128), F32),
        inn=v((p.mp, 8, TB), F32), hown=v((TB, D), F32),
        gact=v((T, max(F, 2 * C + HEAD)), F32), uact=v((T, F), BF), prod=v((T, F), BF), ggate=v((T, F), BF), gup=v((T, F), BF),
        part=v((X, 2, TB, D), BF), recc=v((2, X, TB, D), BF), recx=v((2, X - 1, TB, D), BF),
        xv=v((T, D), BF),
        gm=v((5, HI, LO, S, C), BF), rym=v((5, HI, S, C), BF), rzm=v((5, HI - 1, S, C), BF),
        gf=v((3, LO, F, HI * S) if p.FD else (3, HI, LO, S, F), BF),
        ryf=v((3, F, HI * S) if p.FD else (3, HI, S, F), BF),
        rzf=v((3, HI - 1, F, S) if p.FD else (3, HI - 1, S, F), BF),
        relm=v((2, S, C), BF), relf=v((3, F, S) if p.FD else (3, S, F), BF),
        othm=v((HI, S, C), BF), othf=v((HI, F // 2, S) if p.FD else (HI, S // 2, F), BF),
        sqs=v((8, 128), F32), s1=v((p.mp, 8, 128), F32), s2=v((p.n, 8, 128), F32),
        loc=dma((10,)),
        zs=dma((11, HI - 1)), zr=dma((11, HI - 1)), us=dma((len(Y_FIRST), HI - 1)), ur=dma((len(Y_FIRST), HI - 1)),
        zp=dma((11,)), yp=dma((len(Y_FIRST),)), ys=dma((11, HI)), yr=dma((11, HI)),
        xs=dma((20, X - 1)), xr=dma((20, X - 1)), cs=dma((20, X)), cr=dma((20, X)),
        acs=dma((3, X)), acr=dma((3, X)), axs=dma((3, X - 1, p.NT)), axr=dma((3, X - 1, p.NT)),
        bys=dma((11,)), byr=dma((11,)), bzs=dma((11, HI - 1)), bzr=dma((11, HI - 1)),
        bts=dma((11,)), btr=dma((11,)), ozs=dma((2, HI - 1)), ozr=dma((2, HI - 1)), ots=dma((2,)), otr=dma((2,)),
        ags=dma((p.NT, p.mp)), agr=dma((p.NT, p.mp)), ahs=dma((2, p.mp)), ahr=dma((2, p.mp)),
        q1s=dma((p.mp,)), q1r=dma((p.mp,)), q2s=dma((p.n,)), q2r=dma((p.n,)),
    )


IN_NAMES = ("x", "og", "seg", "live", "cos", "sin", "mixsh", "exsh", "shsh")
OUT_NAMES = ("bo", "ig", "gmo", "geo", "gso", "sqo")


def body(p, names, *refs):
    r = SimpleNamespace(**dict(zip(names, refs)))
    n, mp, LO, HI, X, T, D, C, F, S, H, TB, B = (
        p.n, p.mp, p.LO, p.HI, p.X, p.T, p.D, p.C, p.F, p.S, p.H, p.TB, p.B,
    )
    NT, TT = p.NT, min(512, p.T)
    i, j = lax.axis_index("dp"), lax.axis_index("mp")
    zi, yi = i // LO, lax.rem(i, LO)
    xi, ci = j // 2, lax.rem(j, 2)
    jcols = pl.ds(pl.multiple_of(j * C, C), C)
    pending, tagged, tag = [], [], [None]
    r.nmid = r.nin
    r.bov, r.igv, r.gmv = r.up, r.ufull, r.wo
    r.dk, r.icol, r.dv = r.gact.at[:, 0:2 * C], r.gact.at[:, 2 * C:2 * C + HEAD], r.mixed
    r.gproj = [r.ggate.at[:, 0:C], r.ggate.at[:, C:2 * C], r.gup.at[:, 0:C], r.gup.at[:, C:2 * C]]
    r.ggated, r.hcols, r.gmix, r.rh = [r.xv.at[:, a * C:(a + 1) * C] for a in range(4)]
    r.hsend, r.gsend = r.uact.at[:, 0:C], r.uact.at[:, C:2 * C]

    def go(src, dst, ssem, rsem, when=None, **device):
        copy = pltpu.make_async_remote_copy(
            src_ref=src, dst_ref=dst, send_sem=ssem, recv_sem=rsem,
            device_id=device, device_id_type=MESH,
        )
        guarded(when, copy.start)
        pending.append((copy, when))
        tagged.append((tag[0], copy))
        return copy

    def guarded(when, act):
        if when is None:
            act()
        else:
            pl.when(when)(lambda: act())

    def arrived(dst, sem):
        pltpu.make_async_copy(dst, dst, sem).wait()

    def settle(copy):
        for other, when in pending:
            if other is copy:
                guarded(when, copy.wait_send)
        pending[:] = [entry for entry in pending if entry[0] is not copy]

    def settle_tags(*tags):
        for other, copy in tagged:
            if other in tags:
                settle(copy)

    def load(src, dst, sem):
        copy = pltpu.make_async_copy(src, dst, r.loc.at[sem])
        copy.start()
        return copy

    own_mix = [load(r.mixsh.at[k, :, jcols], r.qpre.at[k * S:(k + 1) * S], k) for k in range(5)]
    if p.FD:
        stage = [r.gact.at[0:F, m * S:(m + 1) * S] for m in range(3)]
        own_ff = [load(r.shsh if m == 0 else r.exsh.at[m - 1], stage[m], 5 + m) for m in range(3)]
    else:
        own_ff = [load(r.exsh.at[m], r.ffw.at[m, rows_of(i, S)], 5 + m) for m in range(3)]
    load_x = load(r.x, r.xv, 8)
    load_og = load(r.og, r.up, 9)

    def enter():
        barrier = pltpu.get_barrier_semaphore()
        for d in range(1, n):
            pl.semaphore_signal(barrier, inc=1, device_id={"dp": lax.rem(i + d, n)}, device_id_type=MESH)
        for d in range(1, mp):
            pl.semaphore_signal(barrier, inc=1, device_id={"mp": lax.rem(j + d, mp)}, device_id_type=MESH)
        pl.semaphore_wait(barrier, n - 1 + mp - 1)

    def slot(k, device):
        rows = rows_of(device, S)
        if k == 4:
            return r.wo.at[rows, jcols]
        if k < 4:
            return r.mixw.at[k, rows]
        m, half = FF_ORDER[(k - 5) // 2], (k - 5) % 2
        if p.FD:
            return r.ffw.at[m, half * F // 2:(half + 1) * F // 2, rows]
        return r.ffw.at[m, pl.ds(pl.multiple_of(device * S + half * S // 2, S // 2), S // 2)]

    def gather_ready(k):
        if k < 5:
            own_mix[k].wait()
            slot(k, i)[...] = r.qpre[k * S:(k + 1) * S, :].astype(BF)
        else:
            m, half = FF_ORDER[(k - 5) // 2], (k - 5) % 2
            if half == 0:
                own_ff[m].wait()
            if p.FD:
                slot(k, i)[...] = stage[m][half * F // 2:(half + 1) * F // 2, :].astype(BF)

    relays = HI == 4
    next_to_end = (zi == 1) | (zi == 2)

    def along_z(block, ssem, rsem):
        for d in range(1, HI):
            to = lax.rem(zi + d, HI)
            near = (jnp.abs(to - zi) < 3) if relays else None
            go(block, block, ssem.at[d - 1], rsem.at[d - 1], when=near, dp=to * LO + yi)

    def hand_on(block, ssem, rsem):
        if relays:
            end = jnp.where(zi == 2, 3, 0)
            go(block, block, ssem, rsem.at[jnp.where(zi == 2, 2, 0)], when=next_to_end, dp=end * LO + yi)

    def from_z_source(k, d, y):
        return slot(k, lax.rem(zi - d + HI, HI) * LO + y)

    WAYS = [2, 1, *range(3, HI)]

    def gather_send(k):
        tag[0] = k
        src = slot(k, i)
        along_z(src, r.zs.at[k], r.zr.at[k])
        go(src, src, r.ys.at[k, 0], r.yr.at[k, 0], dp=zi * LO + 1 - yi)

    def gather_forward(k):
        tag[0] = k - 1
        if k - 1 in Y_FIRST:
            b = Y_FIRST.index(k - 1)
            block = from_z_source(k - 1, 2, 1 - yi)
            arrived(block, r.ur.at[b, 1])
            hand_on(block, r.yp.at[b], r.ur.at[b])
        tag[0] = k
        if k in Y_FIRST:
            b = Y_FIRST.index(k)
            peers = slot(k, zi * LO + 1 - yi)
            arrived(peers, r.yr.at[k, 0])
            along_z(peers, r.us.at[b], r.ur.at[b])
        for d in WAYS:
            block = from_z_source(k, d, yi)
            arrived(block, r.zr.at[k, d - 1])
            if d == 2:
                hand_on(block, r.zp.at[k], r.zr.at[k])
            if k not in Y_FIRST:
                go(block, block, r.ys.at[k, d], r.yr.at[k, d], dp=zi * LO + 1 - yi)

    def gather_wait(k):
        for d in range(HI):
            if k not in Y_FIRST:
                arrived(from_z_source(k, d, 1 - yi), r.yr.at[k, d])
            elif d in (1, 3) or d > 3:
                arrived(from_z_source(k, d, 1 - yi), r.ur.at[Y_FIRST.index(k), d - 1])

    def share_send(s, block, src=None):
        tag[0] = 100 + s
        own = block(j)
        src = own if src is None else src
        for d in range(1, X):
            go(src, own, r.xs.at[s, d - 1], r.xr.at[s, d - 1], mp=lax.rem(xi + d, X) * 2 + ci)
        go(src, own, r.cs.at[s, 0], r.cr.at[s, 0], mp=xi * 2 + 1 - ci)

    def share_forward(s, block):
        tag[0] = 100 + s
        for d in range(1, X):
            part = block(lax.rem(xi - d + X, X) * 2 + ci)
            arrived(part, r.xr.at[s, d - 1])
            go(part, part, r.cs.at[s, d], r.cr.at[s, d], mp=xi * 2 + 1 - ci)

    def share_wait(s, block):
        for d in range(X):
            arrived(block(lax.rem(xi - d + X, X) * 2 + 1 - ci), r.cr.at[s, d])

    def sum_begin(s, b, compute, between):
        tag[0] = None
        sent = []

        def pair(d):
            to = lax.rem(xi + d, X)
            compute(to)
            sent.append(go(
                r.part.at[to, 1 - ci], r.recc.at[b, to], r.acs.at[s, d], r.acr.at[s, d], mp=xi * 2 + 1 - ci
            ))

        for d in range(1, X):
            pair(d)
        between()
        for d in range(1, X):
            to = lax.rem(xi + d, X)
            arrived(r.recc.at[b, to], r.acr.at[s, d])
            for t in range(NT):
                q = slice(t * 128, (t + 1) * 128)
                r.part[to, ci, q] = (
                    r.part[to, ci, q].astype(F32) + r.recc[b, to, q].astype(F32)
                ).astype(BF)
                sent.append(go(
                    r.part.at[to, ci, q], r.recx.at[b, d - 1, q], r.axs.at[s, d - 1, t], r.axr.at[s, d - 1, t],
                    mp=to * 2 + ci,
                ))
        pair(0)
        return sent

    def sum_arrived(s, b, t):
        if t == 0:
            arrived(r.recc.at[b, xi], r.acr.at[s, 0])
        for d in range(1, X):
            arrived(r.recx.at[b, d - 1, t * 128:(t + 1) * 128], r.axr.at[s, d - 1, t])

    def sum_tile(b, q):
        total = r.part[xi, ci, q].astype(F32) + r.recc[b, xi, q].astype(F32)
        for d in range(1, X):
            total = total + r.recx[b, d - 1, q].astype(F32)
        return total

    flat = p.FD

    def half_of(k):
        size = (F if flat else S) // 2
        return (k - 5) // 2, slice((k - 5) % 2 * size, ((k - 5) % 2 + 1) * size)

    def block_of(k, z, y):
        if k < 5:
            return r.gm.at[k, z, y]
        m, rows = half_of(k)
        return r.gf.at[m, y, rows, rows_of(z, S)] if flat else r.gf.at[m, z, y, rows]

    def from_y(k):
        if k < 5:
            return r.rym.at[k]
        m, rows = half_of(k)
        return r.ryf.at[m, rows] if flat else r.ryf.at[m, :, rows]

    def from_y_block(k, z):
        ref = from_y(k)
        return ref.at[:, rows_of(z, S)] if flat and k >= 5 else ref.at[z]

    def to_y(k):
        if k < 5:
            return r.gm.at[k, :, 1 - yi]
        m, rows = half_of(k)
        return r.gf.at[m, 1 - yi, rows] if flat else r.gf.at[m, :, 1 - yi, rows]

    def from_z(k, d, own=True):
        if not own:
            return (r.othm if k < 5 else r.othf).at[d - 1]
        if k < 5:
            return r.rzm.at[k, d - 1]
        m, rows = half_of(k)
        return r.rzf.at[m, d - 1, rows]

    def handed(k, own=True):
        if not own:
            return (r.othm if k < 5 else r.othf).at[HI - 1]
        if k < 5:
            return r.relm.at[max(k - 3, 0)]
        m, rows = half_of(k)
        return r.relf.at[m, rows]

    def z_sems(k, own):
        if own:
            return r.bzs.at[k], r.bzr.at[k], r.bts.at[k], r.btr.at[k]
        o = Z_FIRST.index(k)
        return r.ozs.at[o], r.ozr.at[o], r.ots.at[o], r.otr.at[o]

    def stepped(k):
        return relays and k not in STRAIGHT

    def far(d, back=False):
        other = lax.rem(zi + (HI - d if back else d), HI)
        return jnp.abs(other - zi) == 3

    def z_send(k, own, ways):
        y = yi if own else 1 - yi
        ssem, rsem, tsem, trsem = z_sems(k, own)
        for d in ways:
            to = lax.rem(zi + d, HI)
            block, dst = block_of(k, to, y), from_z(k, d, own)
            if stepped(k) and d != 2:
                go(block, handed(k, own), tsem, trsem, when=far(d), dp=jnp.where(zi == 0, 1, 2) * LO + yi)
                go(block, dst, ssem.at[d - 1], rsem.at[d - 1], when=jnp.logical_not(far(d)), dp=to * LO + yi)
            else:
                go(block, dst, ssem.at[d - 1], rsem.at[d - 1], dp=to * LO + yi)

    def z_send_handed(k, own):
        block = block_of(k, lax.rem(zi + 2, HI), yi if own else 1 - yi)

        @pl.when(next_to_end)
        def _():
            arrived(handed(k, own), z_sems(k, own)[3])
            block[...] = (block[...].astype(F32) + handed(k, own)[...].astype(F32)).astype(BF)

        z_send(k, own, [2])

    def z_total(k, own):
        for d in range(1, HI):
            wait = partial(arrived, from_z(k, d, own), z_sems(k, own)[1].at[d - 1])
            guarded(jnp.logical_not(far(d, back=True)) if stepped(k) and d != 2 else None, wait)
        total = block_of(k, zi, yi if own else 1 - yi)[...].astype(F32)
        for d in range(1, HI):
            total = total + from_z(k, d, own)[...].astype(F32)
        return total

    def clear_far_places():
        if not relays:
            return
        for d in (1, 3):
            @pl.when(far(d, back=True))
            def _(d=d):
                r.rzm[:, d - 1] = jnp.zeros((5, S, C), BF)
                for m in range(3):
                    r.rzf[m, d - 1] = jnp.zeros(r.rzf.shape[2:], BF)
                r.othm[d - 1] = jnp.zeros(r.othm.shape[1:], BF)
                r.othf[d - 1] = jnp.zeros(r.othf.shape[1:], BF)

    def near_ways(k):
        return [3, 1] if stepped(k) else list(range(1, HI))

    def scatter_first(*pieces):
        for k in pieces:
            if k in Z_FIRST:
                for own in (False, True):
                    z_send(k, own, near_ways(k))
            else:
                go(to_y(k), from_y(k), r.bys.at[k], r.byr.at[k], dp=zi * LO + 1 - yi)

    def scatter_second(*pieces):
        for k in pieces:
            if k in Z_FIRST:
                block = block_of(k, zi, 1 - yi)
                block[...] = z_total(k, False).astype(BF)
                go(block, from_y_block(k, zi), r.bys.at[k], r.byr.at[k], dp=zi * LO + 1 - yi)
                continue
            arrived(from_y(k), r.byr.at[k])
            for d in range(1, HI):
                to = lax.rem(zi + d, HI)
                block = block_of(k, to, yi)
                block[...] = (block[...].astype(F32) + from_y_block(k, to)[...].astype(F32)).astype(BF)
            z_send(k, True, near_ways(k))

    def scatter_handed(*pieces):
        for k in pieces:
            if stepped(k):
                if k in Z_FIRST:
                    z_send_handed(k, False)
                z_send_handed(k, True)

    def scatter_total(k):
        if k in Z_FIRST:
            arrived(from_y_block(k, zi), r.byr.at[k])
        return z_total(k, True) + from_y_block(k, zi)[...].astype(F32)

    def squares_of(total):
        squared = total * total
        if squared.shape[-1] % 128:
            corner = (lax.broadcasted_iota(jnp.int32, (8, 128), 0) + lax.broadcasted_iota(jnp.int32, (8, 128), 1)) == 0
            return jnp.where(corner, jnp.sum(squared), 0.0)
        folded = jnp.sum(squared.reshape(-1, 8, squared.shape[-1]), axis=0)
        return sum(folded[:, c:c + 128] for c in range(0, folded.shape[-1], 128))

    def finish_ff(*pieces):
        for k in pieces:
            m, rows = half_of(k)
            total = scatter_total(k)
            if m == 0:
                r.gso[rows] = total
            else:
                r.geo[m - 1, rows] = total
            r.sqs[...] += squares_of(total)

    def put_grad(k, lhs, rhs, turned=False):
        g = r.gm.at[k] if k < 5 else r.gf.at[k - 5]
        per = TT // (LO * S)

        def tile(t):
            if turned:
                out = dot_nn(lhs[rows_of(t, TT), :], rhs[...])
            else:
                out = dot_tn(lhs[:, rows_of(t, TT)], rhs[...])
            g[pl.ds(t * per, per)] = out.astype(BF).reshape(per, LO, S, out.shape[-1])

        each(D // TT, tile)

    def flip(ref, size):
        def row(t):
            rows = rows_of(t, size)
            for c in range(0, ref.shape[1], size):
                ref[rows, c:c + size] = jnp.transpose(ref[rows, c:c + size])

        each(ref.shape[0] // size, row)

    def put_grad_flipped(k, lhs, rhs):
        g = r.gm.at[k]
        per = B // (LO * S)

        def tile(t):
            cols = rows_of(t, B)
            out = dot_nn(lhs[0:B, cols], rhs[0:B, :])
            for b in range(B, T, B):
                out = out + dot_nn(lhs[b:b + B, cols], rhs[b:b + B, :])
            g[pl.ds(t * per, per)] = out.astype(BF).reshape(per, LO, S, out.shape[-1])

        each(D // B, tile)

    def put_ff_grad(m, units, model):
        if not flat:
            return put_grad(5 + m, model, units)
        for f in range(0, F, 384):
            q = slice(f, min(f + 384, F))
            out = dot_tn(units[:, q], model[...]).astype(BF)
            for y in range(LO):
                for z in range(HI):
                    r.gf[m, y, q, z * S:(z + 1) * S] = out[:, (z * LO + y) * S:(z * LO + y + 1) * S]

    def to_units(a, m):
        return dot_nt(a, r.ffw[m]) if flat else dot_nn(a, r.ffw[m])

    def to_model(a, m):
        return dot_nn(a, r.ffw[m]) if flat else dot_nt(a, r.ffw[m])

    gather_ready(0)
    gather_ready(1)
    enter()
    gather_send(0)
    gather_send(1)
    r.sqs[...] = jnp.zeros_like(r.sqs)

    length = r.live[0]
    load_x.wait()

    def norm_tile(t):
        q = rows_of(t, 128)
        v = r.xv[q, :].astype(F32)
        r.nin[q, :] = (v * lax.rsqrt(jnp.mean(v * v, axis=-1, keepdims=True) + EPSILON)).astype(BF)

    each(T // 128, norm_tile)
    for k in range(2, 5):
        gather_ready(k)
    load_x_own = load(r.x.at[rows_of(j, TB)], r.xown, 8)
    load_cos = load(r.cos, r.cosv, 0)
    load_sin = load(r.sin, r.sinv, 1)

    load_cos.wait()
    load_sin.wait()
    load_x_own.wait()

    def turn_into(pre_ref, rot_ref, k):
        def tile(t):
            q = rows_of(t, TT)
            pre = dot_nn(r.nin[q, :], r.mixw[k])
            pre_ref[q, :] = pre
            act = pre * jax.nn.sigmoid(pre)
            c, s = r.cosv[q, :], r.sinv[q, :]
            for h in range(H):
                a = act[:, h * HEAD:(h + 1) * HEAD]
                rot_ref[q, 2 * h * HEAD:(2 * h + 1) * HEAD] = (a * c).astype(BF)
                rot_ref[q, (2 * h + 1) * HEAD:(2 * h + 2) * HEAD] = (a * s).astype(BF)

        each(T // TT, tile)

    def project_into(ref, k):
        def tile(t):
            q = rows_of(t, TT)
            ref[q, :] = dot_nn(r.nin[q, :], r.mixw[k]).astype(ref.dtype)

        each(T // TT, tile)

    gather_forward(0)
    gather_send(2)
    gather_forward(1)
    gather_send(3)
    gather_wait(0)
    turn_into(r.qpre, r.qrot, 0)
    gather_ready(5)
    gather_ready(6)
    gather_forward(2)
    gather_send(4)
    gather_wait(1)
    turn_into(r.kpre, r.krot, 1)
    gather_forward(3)
    gather_send(5)
    gather_send(6)
    gather_wait(2)
    project_into(r.val, 2)
    for k in range(7, 11):
        gather_ready(k)
    place = lax.broadcasted_iota(jnp.int32, (1, T), 1)
    segment = r.seg[...].astype(F32)
    r.segk[...] = jnp.broadcast_to(jnp.where(place < length, segment, -2.0), (8, T))
    seg_q = jnp.where(place < length, segment, -1.0)
    for t in range(T // 128):
        q = slice(t * 128, t * 128 + 128)
        r.segq[q, :] = jnp.transpose(jnp.broadcast_to(seg_q[:, q], (128, 128)))

    down = lax.broadcasted_iota(jnp.int32, (B, B), 0)
    over = lax.broadcasted_iota(jnp.int32, (B, B), 1)
    heads = D // HEAD

    def rate_of(h):
        return -(8.0 * (j * H + h).astype(F32) / heads) * (1.0 - LAYER_PLACE)

    for h in range(H):
        rate = rate_of(h)
        for o in range(2):
            distance = down - over + o * B
            fade = jnp.exp(rate * jnp.maximum(distance, 0).astype(F32))
            r.dec[o, h] = jnp.where(distance >= 0, fade, 0.0)

    gather_forward(4)
    gather_send(7)
    gather_wait(3)
    project_into(r.gpre, 3)

    def wo_block(owner):
        return r.wo.at[:, pl.ds(pl.multiple_of(owner * C, C), C)]


    NB = T // B
    REACH = LONGEST // B

    def keys_of(qb):
        return slice(max(0, qb - REACH) * B, (qb + 1) * B)

    def weights_of(qb, h):
        key = keys_of(qb)
        width = key.stop - key.start
        fades = [r.dec[min(o, 1), h] for o in range(width // B - 1, -1, -1)]
        for o in range(2, width // B):
            fades[width // B - 1 - o] *= jnp.exp(rate_of(h) * ((o - 1) * B))
        seen = jnp.broadcast_to(r.segk[0:1, key], (B, width))
        same = widen(r.segq[qb * B:(qb + 1) * B, :], width) == seen
        return jnp.where(same, jnp.concatenate(fades, axis=1), 0.0)

    def u_block(qb):
        return lambda owner: r.ufull.at[qb * B:(qb + 1) * B, pl.ds(pl.multiple_of(owner * C, C), C)]

    def attend(qb):
        q = slice(qb * B, (qb + 1) * B)
        squares = jnp.zeros((B, 1), F32)
        for h in range(H):
            rot = slice(2 * h * HEAD, 2 * (h + 1) * HEAD)
            chan = slice(h * HEAD, (h + 1) * HEAD)
            key = keys_of(qb)
            scores = dot_nt(r.qrot[q, rot], r.krot[key, rot]) * weights_of(qb, h)
            total = dot_nn(scores.astype(BF), r.val[key, chan])
            r.mixed[q, chan] = total
            squares = squares + jnp.sum(total * total, axis=-1, keepdims=True)
            r.ufull[q, pl.ds(pl.multiple_of(j * C + h * HEAD, HEAD), HEAD)] = (
                total * r.gpre[q, chan]
            ).astype(BF)
        r.ss[j, :, q] = jnp.transpose(jnp.broadcast_to(squares, (B, 128)))[0:8, :]

    def ss_block(owner):
        return r.ss.at[owner]

    for qb in range(NB):
        attend(qb)
        share_send(1 + qb, u_block(qb))
        if qb == NB - 1:
            share_send(1 + NB, ss_block)
        if qb == 0:
            gather_forward(5)
            gather_send(8)
        if qb == 1:
            gather_wait(4)
            share_send(0, wo_block)
        if qb == 3:
            share_forward(0, wo_block)
        if qb == 2:
            gather_forward(6)
            gather_send(9)
        if qb > 0:
            share_forward(qb, u_block(qb - 1))
    share_forward(NB, u_block(NB - 1))
    share_forward(1 + NB, ss_block)
    gather_forward(7)
    gather_send(10)
    load_og.wait()

    def live_tile(t):
        q = rows_of(t, 128)
        place = lax.broadcasted_iota(jnp.int32, (128, D), 0) + t * 128
        r.up[q, :] = jnp.where(place < length, r.up[q, :].astype(F32), 0.0).astype(BF)

    each(T // 128, live_tile)

    for t in range(D // 128):
        q = slice(t * 128, t * 128 + 128)
        r.nint[q, :] = jnp.transpose(r.nin[:, q])
    clear_far_places()
    settle_tags(0, 1, 2, 3)
    for k in range(4):
        flip(r.mixw.at[k], C)
    gather_forward(8)
    share_wait(0, wo_block)
    for qb in range(NB):
        share_wait(1 + qb, u_block(qb))
    share_wait(1 + NB, ss_block)
    early = [copy for copy, when in pending]

    total_ss = r.ss[0]
    for owner in range(1, mp):
        total_ss = total_ss + r.ss[owner]
    inverse = lax.rsqrt(total_ss * (1.0 / D) + EPSILON)
    for t in range(T // 128):
        q = slice(t * 128, t * 128 + 128)
        r.rcol[q, :] = jnp.transpose(jnp.broadcast_to(inverse[0:1, q], (128, 128)))

    def hidden_tile(t):
        q = rows_of(t, TB)
        out = widen(r.rcol[q, :], D) * dot_nn(r.ufull[q, :], r.wo[...])
        hidden = r.xv[q, :].astype(F32) + out
        scale = lax.rsqrt(jnp.mean(hidden * hidden, axis=-1, keepdims=True) + EPSILON)
        r.nmid[q, :] = (hidden * scale).astype(BF)

        @pl.when(t == j)
        def _():
            r.hown[...] = hidden

    each(T // TB, hidden_tile)
    gather_forward(9)
    settle_tags(4, *range(100, 101 + NB))
    flip(r.wo, B)
    flip(r.ufull, B)
    gather_wait(5)
    gather_wait(6)

    def gate_tile(t):
        q = rows_of(t, TT)
        r.gact[q, 0:F] = to_units(r.nmid[q, :], 1)

    each(T // TT, gate_tile)
    gather_forward(10)
    gather_wait(7)
    gather_wait(8)

    def up_tile(t):
        q = rows_of(t, TT)
        upper = to_units(r.nmid[q, :], 2)
        r.uact[q, :] = upper.astype(BF)
        r.prod[q, :] = (r.gact[q, 0:F] * upper).astype(BF)

    each(T // TT, up_tile)
    put_ff_grad(0, r.prod, r.up)
    scatter_first(5, 6)
    gather_wait(9)
    gather_wait(10)

    def mid_pair(x):
        q = rows_of(x, 2 * TB)
        g = to_units(r.up[q, :], 0)
        grad_gate, grad_up = (g * r.uact[q, :].astype(F32)).astype(BF), (g * r.gact[q, 0:F]).astype(BF)
        r.ggate[q, :] = grad_gate
        r.gup[q, :] = grad_up
        r.part[x] = (to_model(grad_gate, 1) + to_model(grad_up, 2)).astype(BF).reshape(2, TB, D)

    used = sum_begin(0, 0, mid_pair, partial(scatter_second, 5))
    put_ff_grad(1, r.ggate, r.nmid)
    scatter_first(7, 8)
    scatter_handed(5)
    scatter_second(6)

    def back_tile(t):
        q = slice(t * 128, (t + 1) * 128)
        here = rows_of(j * (TB // 128) + t, 128)
        grad = sum_tile(0, q)
        hidden = r.hown[q, :]
        scale = lax.rsqrt(jnp.mean(hidden * hidden, axis=-1, keepdims=True) + EPSILON)
        normed = hidden * scale
        inner = jnp.mean(grad * normed, axis=-1, keepdims=True)
        out = r.up[here, :].astype(F32) + scale * (grad - normed * inner)
        low = out.astype(BF)
        for owner in range(mp):
            r.hsend[owner * TB + t * 128:owner * TB + (t + 1) * 128, :] = low[:, owner * C:(owner + 1) * C]
        mixer_out = hidden - r.xown[q, :].astype(F32)
        product = jnp.sum(low.astype(F32) * mixer_out, axis=-1, keepdims=True) * (1.0 / D)
        r.inn[j, :, q] = jnp.transpose(jnp.broadcast_to(product, (128, 128)))[0:8, :]

    def token_block(ref):
        return lambda owner: ref.at[rows_of(owner, TB)]

    BO, GM, IG = 2 + NB, 3 + NB, 8 + NB

    def half_block(ref, t):
        return lambda owner: ref.at[rows_of(owner * NT + t, 128)]

    def peers():
        return [(d, lax.rem(j + d, mp), lax.rem(j - d + mp, mp)) for d in range(1, mp)]

    for t in range(NT):
        sum_arrived(0, 0, t)
        back_tile(t)
    low = jnp.concatenate([r.hsend[owner * TB:(owner + 1) * TB, :] for owner in range(mp)], axis=1)
    for e in range(0, D, B):
        out = dot_nn(low[:, 0:B], r.wo[e:e + B, 0:B])
        for d in range(B, D, B):
            out = out + dot_nn(low[:, d:d + B], r.wo[e:e + B, d:d + B])
        for c in range(0, B, C):
            owner = (e + c) // C
            r.gsend[owner * TB:(owner + 1) * TB, :] = out[:, c:c + C].astype(BF)
    for d, to, source in peers():
        go(token_block(r.gsend)(to), token_block(r.ggated)(j), r.ags.at[0, d], r.agr.at[0, d], mp=to)
    own_rows = rows_of(j, TB)
    r.ggated[own_rows, :] = r.gsend[own_rows, :]
    r.hcols[own_rows, :] = r.hsend[own_rows, :]
    for d, to, source in peers():
        go(r.inn.at[j], r.inn.at[j], r.ahs.at[0, d], r.ahr.at[0, d], mp=to)
    for d, to, source in peers():
        go(token_block(r.hsend)(to), token_block(r.hcols)(j), r.ahs.at[1, d], r.ahr.at[1, d], mp=to)
    put_ff_grad(2, r.gup, r.nmid)
    scatter_first(9, 10)
    scatter_handed(6)
    scatter_second(7)
    for copy in used:
        settle(copy)

    def expand_tile(t):
        r.part[t // 2, lax.rem(t, 2)] = to_model(r.prod[rows_of(t, TB), :], 0).astype(BF)

    each(mp, expand_tile)
    used = [
        go(r.part.at[to, 1 - ci], r.recc.at[1, to], r.acs.at[1, d], r.acr.at[1, d], mp=xi * 2 + 1 - ci)
        for d, to in [(d, lax.rem(xi + d, X)) for d in range(X)]
    ]
    for d, to, source in peers():
        arrived(token_block(r.ggated)(source), r.agr.at[0, d])
        arrived(r.inn.at[source], r.ahr.at[0, d])
    for owner in range(mp):
        for t in range(TB // 128):
            row = r.inn[owner, 0:1, t * 128:(t + 1) * 128]
            q = slice(owner * TB + t * 128, owner * TB + (t + 1) * 128)
            r.icol[q, :] = jnp.transpose(jnp.broadcast_to(row, (128, 128)))

    def gated_tile(t):
        q = rows_of(t, TT)
        grad = r.ggated[q, :].astype(F32)
        inner = widen(r.icol[q, :], C)
        inverse = widen(r.rcol[q, :], C)
        normed = r.mixed[q, :] * inverse
        r.gproj[3][q, :] = (grad * normed).astype(BF)
        r.gmix[q, :] = (inverse * (grad * r.gpre[q, :] - normed * inner)).astype(BF)

    each(T // TT, gated_tile)

    for d in [*range(1, X), 0]:
        to = lax.rem(xi + d, X)
        arrived(r.recc.at[1, to], r.acr.at[1, d])
        for t in range(NT):
            q = slice(t * 128, (t + 1) * 128)
            r.recc[1, to, q] = (r.part[to, ci, q].astype(F32) + r.recc[1, to, q].astype(F32)).astype(BF)
            if d:
                go(r.recc.at[1, to, q], r.recx.at[1, d - 1, q], r.axs.at[1, d - 1, t], r.axr.at[1, d - 1, t], mp=to * 2 + ci)
    scatter_second(8)

    def output_grad_tile(t):
        q = rows_of(t, TT)
        r.rh[q, :] = (widen(r.rcol[q, :], C) * r.hcols[q, :].astype(F32)).astype(BF)

    def swish_back(pre, grad):
        gate = jax.nn.sigmoid(pre)
        return grad * (gate * (1.0 + pre * (1.0 - gate)))

    def attend_back(qb):
        q, key = slice(qb * B, (qb + 1) * B), keys_of(qb)
        for h in range(H):
            rot = slice(2 * h * HEAD, 2 * (h + 1) * HEAD)
            chan = slice(h * HEAD, (h + 1) * HEAD)
            weights = weights_of(qb, h)
            scores = (dot_nt(r.qrot[q, rot], r.krot[key, rot]) * weights).astype(BF)
            back = (dot_nt(r.gmix[q, chan], r.val[key, chan]) * weights).astype(BF)
            dq = dot_nn(back, r.krot[key, rot])
            turned = dq[:, :HEAD] * r.cosv[q, :] + dq[:, HEAD:] * r.sinv[q, :]
            r.gproj[0][q, chan] = swish_back(r.qpre[q, chan], turned).astype(BF)
            dk = dot_tn(back, r.qrot[q, rot])
            dv = dot_tn(scores, r.gmix[q, chan])
            for kb in range(key.start // B, qb + 1):
                at = slice(kb * B - key.start, (kb + 1) * B - key.start)
                rows = slice(kb * B, (kb + 1) * B)
                dkb, dvb = dk[at], dv[at]
                if qb < min(kb + REACH, NB - 1):
                    dkb, dvb = dkb + r.dk[rows, rot], dvb + r.dv[rows, chan]
                if kb < qb:
                    r.dk[rows, rot], r.dv[rows, chan] = dkb, dvb
                else:
                    turned = dkb[:, :HEAD] * r.cosv[q, :] + dkb[:, HEAD:] * r.sinv[q, :]
                    r.gproj[1][q, chan] = swish_back(r.kpre[q, chan], turned).astype(BF)
                    r.gproj[2][q, chan] = dvb.astype(BF)

    def output_tile(t):
        q = rows_of(t, 128)
        total = r.recc[1, xi, q].astype(F32)
        for d in range(1, X):
            total = total + r.recx[1, d - 1, q].astype(F32)
        r.bov[rows_of(j * NT + t, 128), :] = (r.hown[q, :] + total).astype(BF)

    def late_core(x):
        return pltpu.make_async_remote_copy(
            src_ref=r.part.at[x, 1 - ci], dst_ref=r.recc.at[0, x], send_sem=r.acs.at[2, x], recv_sem=r.acr.at[2, x],
            device_id={"mp": xi * 2 + 1 - ci}, device_id_type=MESH,
        )

    def late_chip(x, d, t):
        q = slice(t * 128, (t + 1) * 128)
        return pltpu.make_async_remote_copy(
            src_ref=r.part.at[x, ci, q], dst_ref=r.recx.at[0, d - 1, q], send_sem=r.axs.at[2, d - 1, t],
            recv_sem=r.axr.at[2, d - 1, t], device_id={"mp": x * 2 + ci}, device_id_type=MESH,
        )

    def blocks_in(qb):
        return [divmod(at, 2) for at in range(qb * B // TB, (qb + 1) * B // TB)]

    def late_begin(x, c):
        q = slice((x * 2 + c) * TB, (x * 2 + c + 1) * TB)
        for d in range(0, D, C):
            out = dot_nn(r.gproj[0][q, :], r.mixw[0, d:d + C, :])
            for k in range(1, 4):
                out = out + dot_nn(r.gproj[k][q, :], r.mixw[k, d:d + C, :])
            r.part[x, c, :, d:d + C] = out.astype(BF)

        @pl.when(ci != c)
        def _():
            late_core(x).start()

    def late_pass(x, c):
        @pl.when(ci == c)
        def _():
            arrived(r.recc.at[0, x], r.acr.at[2, x])

        @pl.when((ci == c) & (xi != x))
        def _():
            for t in range(NT):
                q = slice(t * 128, (t + 1) * 128)
                r.part[x, c, q] = (r.part[x, c, q].astype(F32) + r.recc[0, x, q].astype(F32)).astype(BF)
                late_chip(x, lax.rem(x - xi + X, X), t).start()

    put_grad(3, r.nint, r.gproj[3], turned=True)
    scatter_first(3)
    for qb in range(NB - 1, -1, -1):
        attend_back(qb)
        if qb == NB - 1:
            for copy in used + early:
                settle(copy)
        for x, c in blocks_in(qb):
            late_begin(x, c)
        if qb < NB - 1:
            for x, c in blocks_in(qb + 1):
                late_pass(x, c)
        if qb == NB - 1:
            for d, to, source in peers():
                arrived(token_block(r.hcols)(source), r.ahr.at[1, d])
            each(T // TT, output_grad_tile)
            put_grad_flipped(4, r.ufull, r.rh)
            scatter_first(4)
            scatter_handed(7, 8, 9)
            scatter_second(10)
            finish_ff(5)
        if qb == max(NB - 2, 0):
            scatter_handed(10)
            scatter_second(3, 9)
            for t in range(NT):
                for d in range(1, X):
                    arrived(r.recx.at[1, d - 1, t * 128:(t + 1) * 128], r.axr.at[1, d - 1, t])
            each(TB // 128, output_tile)
            share_send(BO, token_block(r.bov))
            finish_ff(6)
        if qb == max(NB - 3, 0):
            scatter_handed(4, 3)
            share_forward(BO, token_block(r.bov))
            finish_ff(7)
    for x, c in blocks_in(0):
        late_pass(x, c)
    pending.extend((late_core(x), None) for x in range(X))
    pending.extend((late_chip(lax.rem(xi + d, X), d, t), None) for d in range(1, X) for t in range(NT))
    for k in (2, 0):
        put_grad(k, r.nint, r.gproj[k], turned=True)
        scatter_first(k)
    scatter_second(4)
    put_grad(1, r.nint, r.gproj[1], turned=True)
    scatter_first(1)
    finish_ff(8, 9, 10)
    scatter_second(2, 0)

    def input_tile(t):
        q = slice(t * 128, (t + 1) * 128)
        low = jnp.concatenate(
            [r.hsend[owner * TB + t * 128:owner * TB + (t + 1) * 128, :] for owner in range(mp)], axis=1
        ).astype(F32)
        grad = sum_tile(0, q)
        v = r.xown[q, :].astype(F32)
        scale = lax.rsqrt(jnp.mean(v * v, axis=-1, keepdims=True) + EPSILON)
        normed = v * scale
        inner = jnp.mean(grad * normed, axis=-1, keepdims=True)
        r.igv[rows_of(j * NT + t, 128), :] = (low + scale * (grad - normed * inner)).astype(BF)

    for t in range(NT):
        for d in range(1, X):
            arrived(r.recx.at[0, d - 1, t * 128:(t + 1) * 128], r.axr.at[2, d - 1, t])
        input_tile(t)
        share_send(IG + t, half_block(r.igv, t))
    scatter_second(1)
    scatter_handed(2)
    share_wait(BO, token_block(r.bov))
    stores = [load(r.bov, r.bo, 0)]

    def grad_block(k):
        return lambda owner: r.gmv.at[k * S:(k + 1) * S, pl.ds(pl.multiple_of(owner * C, C), C)]

    for k in (4, 3, 2, 0, 1):
        total = scatter_total(k).astype(BF)
        r.gmv[k * S:(k + 1) * S, jcols] = total
        r.sqs[...] += squares_of(total.astype(F32))
        share_send(GM + k, grad_block(k))

    r.s1[j] = r.sqs[...]
    for d in range(1, mp):
        go(r.s1.at[j], r.s1.at[j], r.q1s.at[d], r.q1r.at[d], mp=lax.rem(j + d, mp))
    for t in range(NT):
        share_forward(IG + t, half_block(r.igv, t))
    for d in range(1, mp):
        arrived(r.s1.at[lax.rem(j - d + mp, mp)], r.q1r.at[d])
    total = r.s1[0]
    for owner in range(1, mp):
        total = total + r.s1[owner]
    r.s2[i] = total
    for d in range(1, n):
        go(r.s2.at[i], r.s2.at[i], r.q2s.at[d], r.q2r.at[d], dp=lax.rem(i + d, n))
    for k in (4, 3, 2, 0, 1):
        share_forward(GM + k, grad_block(k))
    for d in range(1, n):
        arrived(r.s2.at[lax.rem(i - d + n, n)], r.q2r.at[d])
    total = r.s2[0]
    for owner in range(1, n):
        total = total + r.s2[owner]
    r.sqo[...] = total

    for t in range(NT):
        share_wait(IG + t, half_block(r.igv, t))
    stores.append(load(r.igv, r.ig, 1))
    for k in (4, 3, 2, 0, 1):
        share_wait(GM + k, grad_block(k))
        stores.append(load(r.gmv.at[k * S:(k + 1) * S], r.gmo.at[k], 2 + k))
    for copy in stores:
        copy.wait()
    for copy, when in pending:
        guarded(when, copy.wait_send)


def fused(p, *operands):
    scratch = scratch_of(p)
    names = IN_NAMES + OUT_NAMES + tuple(scratch)
    anywhere = pl.BlockSpec(memory_space=pl.ANY)
    vmem = pl.BlockSpec(memory_space=pltpu.VMEM)
    smem = pl.BlockSpec(memory_space=pltpu.SMEM)
    return pl.pallas_call(
        partial(body, p, names),
        out_shape=(
            jax.ShapeDtypeStruct((p.T, p.D), BF),
            jax.ShapeDtypeStruct((p.T, p.D), BF),
            jax.ShapeDtypeStruct((5, p.S, p.D), BF),
            jax.ShapeDtypeStruct((2, p.F, p.S) if p.FD else (2, p.S, p.F), F32),
            jax.ShapeDtypeStruct((p.F, p.S) if p.FD else (p.S, p.F), F32),
            jax.ShapeDtypeStruct((8, 128), F32),
        ),
        in_specs=[anywhere, anywhere, vmem, smem] + [anywhere] * 5,
        out_specs=(anywhere, anywhere, anywhere, vmem, vmem, vmem),
        scratch_shapes=list(scratch.values()),
        compiler_params=pltpu.CompilerParams(
            collective_id=0, has_side_effects=True, vmem_limit_bytes=VMEM_LIMIT
        ),
    )(*operands)


VMEM_LIMIT = 64 * 2**20 - 2**18


def renew(weight, momentum, shadow, grad, clip_factor):
    clipped = grad * clip_factor
    velocity = MOMENTUM * momentum + clipped
    updated = weight - LEARN_RATE * (clipped + MOMENTUM * velocity)
    average = SHADOW_DECAY * shadow + (1.0 - SHADOW_DECAY) * updated
    return (velocity, average, updated)


def update_body(cuts, *refs):
    kinds, pieces = len(cuts), sum(len(c) for c in cuts)
    sq, carried = refs[0], refs[1:3]
    ins = [refs[3 + 4 * w:7 + 4 * w] for w in range(kinds)]
    refs = refs[3 + 4 * kinds:]
    norm_out, carried_out = refs[0], refs[1:3]
    outs = [refs[3 + 3 * w:6 + 3 * w] for w in range(kinds)]
    refs = refs[3 + 3 * kinds:]
    held = [refs[4 * w:4 * w + 4] for w in range(kinds)]
    made = [refs[4 * kinds + 3 * w:4 * kinds + 3 * w + 3] for w in range(kinds)]
    bounce, (in_sem, out_sem, carry_sem) = refs[7 * kinds:7 * kinds + 2], refs[7 * kinds + 2:]
    loads, order = {}, [(w, c) for w in range(kinds) for c in range(len(cuts[w]))]
    for at, (w, c) in enumerate(order):
        for a in range(4):
            cut = cuts[w][c]
            loads[at, a] = pltpu.make_async_copy(ins[w][a].at[cut], held[w][a].at[cut], in_sem.at[at, a])
            loads[at, a].start()
    carry = [pltpu.make_async_copy(carried[a], bounce[a], carry_sem.at[a]) for a in range(2)]
    for copy in carry:
        copy.start()
    copies = []
    norm = jnp.sqrt(jnp.broadcast_to(jnp.sum(sq[...]), (8, 128)))
    norm_out[...] = norm
    clip_factor = 1.0 / jnp.maximum(jnp.max(norm), 1.0)
    for at, (w, c) in enumerate(order):
        cut = cuts[w][c]
        for a in range(4):
            loads[at, a].wait()
        new = renew(*[held[w][a][cut] for a in range(3)], held[w][3][cut].astype(F32), clip_factor)
        for a in range(3):
            made[w][a][cut] = new[a]
            copy = pltpu.make_async_copy(made[w][a].at[cut], outs[w][a].at[cut], out_sem.at[at, a])
            copy.start()
            copies.append(copy)
    for a in range(2):
        carry[a].wait()
        copy = pltpu.make_async_copy(bounce[a], carried_out[a], carry_sem.at[2 + a])
        copy.start()
        copies.append(copy)
    for copy in copies:
        copy.wait()


def update(sq, carried, weights):
    cuts = [[c for c in range(g[0].shape[0])] if g[0].ndim == 3 else [slice(None)] for g in weights]
    pieces = sum(len(c) for c in cuts)
    anywhere = pl.BlockSpec(memory_space=pl.ANY)
    vmem = pl.BlockSpec(memory_space=pltpu.VMEM)
    flat_in = [a for group in weights for a in group]
    flat_out = [a for group in weights for a in group[:3]]
    dma = pltpu.SemaphoreType.DMA
    size = sum(a.size * a.dtype.itemsize for a in flat_in + flat_out + 2 * list(carried))
    return pl.pallas_call(
        partial(update_body, cuts),
        out_shape=[jax.ShapeDtypeStruct(a.shape, a.dtype) for a in [sq, *carried, *flat_out]],
        in_specs=[vmem] + [anywhere] * (2 + len(flat_in)),
        out_specs=[vmem] + [anywhere] * (2 + len(flat_out)),
        scratch_shapes=[pltpu.VMEM(a.shape, a.dtype) for a in flat_in + flat_out + list(carried)]
        + [dma((pieces, 4)), dma((pieces, 3)), dma((4,))],
        cost_estimate=pl.CostEstimate(flops=size, bytes_accessed=size, transcendentals=0),
        compiler_params=pltpu.CompilerParams(vmem_limit_bytes=VMEM_LIMIT),
    )(sq, *carried, *flat_in)


def turn_tables(tokens):
    theta = np.float32(10000.0) ** (-np.arange(HEAD, dtype=np.float32) / np.float32(HEAD))
    angle = np.arange(tokens, dtype=np.float32)[:, None] * theta.astype(np.float32)[None, :]
    angle = angle.astype(np.float64)
    return np.cos(angle).astype(np.float32), np.sin(angle).astype(np.float32)


def per_device(mesh, block_input, segment_ids, live_length, output_grad, mixer_weight, mixer_momentum, mixer_shadow,
               expand_weight, expand_momentum, expand_shadow, shrink_weight, shrink_momentum, shrink_shadow):
    rows, length, width = block_input.shape
    p = plan_of(mesh, length, width, shrink_weight.shape[0])
    turn = (lambda v: jnp.swapaxes(v, -1, -2)) if p.FD else (lambda v: v)
    if p.FD:
        shards = (turn(expand_weight), shrink_weight)
    else:
        shards = (jnp.concatenate([shrink_weight.T[None], expand_weight], axis=0).astype(BF), shrink_weight)
    cos, sin = turn_tables(length)
    out, grad_in, gm, ge, gs, sq = fused(
        p, block_input[0], output_grad[0], segment_ids, live_length, jnp.asarray(cos), jnp.asarray(sin), mixer_weight, *shards
    )
    new = update(sq, (out, grad_in), (
        (mixer_weight, mixer_momentum, mixer_shadow, gm),
        (turn(expand_weight), turn(expand_momentum), turn(expand_shadow), ge),
        (shrink_weight, shrink_momentum, shrink_shadow, gs if p.FD else gs.T),
    ))
    norm, out, grad_in = new[:3]
    return (out[None], grad_in[None], norm[0, 0], *new[3:6], *(turn(v) for v in new[6:9]), *new[9:12])


def solution(mesh):
    row, mixer, expand, shrink = P("dp", None, None), P(None, "dp", None), P(None, "dp", "mp"), P("mp", "dp")
    return jax.shard_map(
        partial(per_device, mesh),
        mesh=mesh,
        in_specs=(row, P("dp", None), P("dp"), row) + (mixer,) * 3 + (expand,) * 3 + (shrink,) * 3,
        out_specs=(row, row, P()) + (mixer,) * 3 + (expand,) * 3 + (shrink,) * 3,
        check_vma=False,
    )
```

```python
from functools import partial
from types import SimpleNamespace

import jax
import jax.numpy as jnp
import numpy as np
from jax import lax
from jax.experimental import pallas as pl
from jax.experimental.pallas import tpu as pltpu
from jax.sharding import PartitionSpec as P

HEAD = 128
EPSILON = 1e-06
LEARN_RATE = 32.0
MOMENTUM = 0.5
SHADOW_DECAY = 0.5
LAYER_PLACE = 12.0 / 24.0
LONGEST = 512
FF_ORDER = (1, 2, 0)
Y_FIRST = (4, 6)
Z_FIRST = (9, 4)
STRAIGHT = (2, 0, 1)
MESH = pl.DeviceIdType.MESH
BF = jnp.bfloat16
F32 = jnp.float32


def dot_nn(a, b):
    return lax.dot_general(a, b, (((1,), (0,)), ((), ())), preferred_element_type=F32)


def dot_nt(a, b):
    return lax.dot_general(a, b, (((1,), (1,)), ((), ())), preferred_element_type=F32)


def dot_tn(a, b):
    return lax.dot_general(a, b, (((0,), (0,)), ((), ())), preferred_element_type=F32)


def rows_of(index, size):
    return pl.ds(pl.multiple_of(index * size, size), size)


def each(count, body):
    def step(t, carry):
        body(t)
        return carry

    lax.fori_loop(0, count, step, 0)


def widen(column, width):
    return jnp.concatenate([column] * (width // 128), axis=1)


def plan_of(mesh, tokens, width, inner):
    n, mp = mesh.shape["dp"], mesh.shape["mp"]
    lo, core = 2, 2
    return SimpleNamespace(
        n=n, mp=mp, LO=lo, HI=n // lo, X=mp // core, T=tokens, D=width, C=width // mp, F=inner,
        S=width // n, H=width // mp // HEAD, TB=tokens // mp, B=min(256, tokens),
        N=n * mp if n * mp <= 32 else 1, NT=tokens // mp // 128, FD=(width // n) % 128 == 0,
    )


def scratch_of(p):
    T, D, C, F, S, HI, LO, X, TB, B = p.T, p.D, p.C, p.F, p.S, p.HI, p.LO, p.X, p.TB, p.B
    dma = pltpu.SemaphoreType.DMA
    v = pltpu.VMEM
    return dict(
        mixw=v((4, D, C), BF), wo=v((D, D), BF), ffw=v((3, F, D) if p.FD else (3, D, F), BF),
        xown=v((TB, D), BF), nin=v((T, D), BF), nint=v((D, T), BF), up=v((T, D), BF),
        cosv=v((T, HEAD), F32), sinv=v((T, HEAD), F32),
        segq=v((T, 128), F32), segk=v((8, T), F32), dec=v((2, p.H, B, B), F32),
        qpre=v((T, C), F32), kpre=v((T, C), F32), gpre=v((T, C), F32), val=v((T, C), BF),
        qrot=v((T, 2 * C), BF), krot=v((T, 2 * C), BF), mixed=v((T, C), F32),
        ufull=v((T, D), BF), ss=v((p.mp, 8, T), F32), rcol=v((T, 128), F32),
        inn=v((p.mp, 8, TB), F32), hown=v((TB, D), F32),
        gact=v((T, max(F, 2 * C + HEAD)), F32), uact=v((T, F), BF), prod=v((T, F), BF), ggate=v((T, F), BF), gup=v((T, F), BF),
        part=v((X, 2, TB, D), BF), recc=v((2, X, TB, D), BF), recx=v((2, X - 1, TB, D), BF),
        xv=v((T, D), BF),
        gm=v((5, HI, LO, S, C), BF), rym=v((5, HI, S, C), BF), rzm=v((5, HI - 1, S, C), BF),
        gf=v((3, LO, F, HI * S) if p.FD else (3, HI, LO, S, F), BF),
        ryf=v((3, F, HI * S) if p.FD else (3, HI, S, F), BF),
        rzf=v((3, HI - 1, F, S) if p.FD else (3, HI - 1, S, F), BF),
        relm=v((2, S, C), BF), relf=v((3, F, S) if p.FD else (3, S, F), BF),
        othm=v((HI, S, C), BF), othf=v((HI, F // 2, S) if p.FD else (HI, S // 2, F), BF),
        sqs=v((8, 128), F32), sall=v((p.N, 8, 128), F32), s1=v((p.mp if p.N == 1 else 1, 8, 128), F32), s2=v((p.n if p.N == 1 else 1, 8, 128), F32),
        loc=dma((10,)),
        zs=dma((11, HI - 1)), zr=dma((11, HI - 1)), us=dma((len(Y_FIRST), HI - 1)), ur=dma((len(Y_FIRST), HI - 1)),
        zp=dma((11,)), yp=dma((len(Y_FIRST),)), ys=dma((11, HI)), yr=dma((11, HI)),
        xs=dma((20, X - 1)), xr=dma((20, X - 1)), cs=dma((20, X)), cr=dma((20, X)),
        acs=dma((3, X)), acr=dma((3, X)), axs=dma((3, X - 1, p.NT)), axr=dma((3, X - 1, p.NT)),
        bys=dma((11,)), byr=dma((11,)), bzs=dma((11, HI - 1)), bzr=dma((11, HI - 1)),
        bts=dma((11,)), btr=dma((11,)), ozs=dma((2, HI - 1)), ozr=dma((2, HI - 1)), ots=dma((2,)), otr=dma((2,)),
        ags=dma((p.NT, p.mp)), agr=dma((p.NT, p.mp)), ahs=dma((2, p.mp)), ahr=dma((2, p.mp)),
        gms=dma((5, p.mp)), gmr=dma((5, p.mp)), qs=dma((p.N,)), qr=dma((p.N,)),
        q1s=dma((p.mp,)), q1r=dma((p.mp,)), q2s=dma((p.n,)), q2r=dma((p.n,)),
    )


IN_NAMES = ("x", "og", "seg", "live", "cos", "sin", "mixsh", "exsh", "shsh")
OUT_NAMES = ("bo", "ig", "gmo", "geo", "gso", "sqo")


def body(p, names, *refs):
    r = SimpleNamespace(**dict(zip(names, refs)))
    n, mp, LO, HI, X, T, D, C, F, S, H, TB, B = (
        p.n, p.mp, p.LO, p.HI, p.X, p.T, p.D, p.C, p.F, p.S, p.H, p.TB, p.B,
    )
    NT, TT = p.NT, min(512, p.T)
    i, j = lax.axis_index("dp"), lax.axis_index("mp")
    zi, yi = i // LO, lax.rem(i, LO)
    xi, ci = j // 2, lax.rem(j, 2)
    jcols = pl.ds(pl.multiple_of(j * C, C), C)
    pending = []
    r.nmid = r.nin
    r.bov, r.igv, r.gmv = r.up, r.ufull, r.wo
    r.dk, r.icol, r.dv = r.gact.at[:, 0:2 * C], r.gact.at[:, 2 * C:2 * C + HEAD], r.mixed
    r.gproj = [r.ggate.at[:, 0:C], r.ggate.at[:, C:2 * C], r.gup.at[:, 0:C], r.gup.at[:, C:2 * C]]
    r.ggated, r.hcols, r.gmix, r.rh = [r.xv.at[:, a * C:(a + 1) * C] for a in range(4)]
    r.hsend, r.gsend = r.uact.at[:, 0:C], r.uact.at[:, C:2 * C]

    def go(src, dst, ssem, rsem, when=None, **device):
        copy = pltpu.make_async_remote_copy(
            src_ref=src, dst_ref=dst, send_sem=ssem, recv_sem=rsem,
            device_id=device, device_id_type=MESH,
        )
        guarded(when, copy.start)
        pending.append((copy, when))
        return copy

    def guarded(when, act):
        if when is None:
            act()
        else:
            pl.when(when)(lambda: act())

    def arrived(dst, sem):
        pltpu.make_async_copy(dst, dst, sem).wait()

    def settle(copy):
        for other, when in pending:
            if other is copy:
                guarded(when, copy.wait_send)
        pending[:] = [entry for entry in pending if entry[0] is not copy]

    def load(src, dst, sem):
        copy = pltpu.make_async_copy(src, dst, r.loc.at[sem])
        copy.start()
        return copy

    own_mix = [load(r.mixsh.at[k, :, jcols], r.qpre.at[k * S:(k + 1) * S], k) for k in range(5)]
    if p.FD:
        stage = [r.gact.at[0:F, m * S:(m + 1) * S] for m in range(3)]
        own_ff = [load(r.shsh if m == 0 else r.exsh.at[m - 1], stage[m], 5 + m) for m in range(3)]
    else:
        own_ff = [load(r.exsh.at[m], r.ffw.at[m, rows_of(i, S)], 5 + m) for m in range(3)]
    load_x = load(r.x, r.xv, 8)
    load_og = load(r.og, r.up, 9)

    def enter():
        barrier = pltpu.get_barrier_semaphore()
        if p.N > 1:
            others = [whole(d) for d in range(1, p.N)]
        else:
            others = [{"dp": lax.rem(i + d, n)} for d in range(1, n)] + [{"mp": lax.rem(j + d, mp)} for d in range(1, mp)]
        for other in others:
            pl.semaphore_signal(barrier, inc=1, device_id=other, device_id_type=MESH)
        pl.semaphore_wait(barrier, len(others))

    def whole(d):
        at = lax.rem(i * mp + j + d, p.N)
        return {"dp": at // mp, "mp": lax.rem(at, mp)}

    def slot(k, device):
        rows = rows_of(device, S)
        if k == 4:
            return r.wo.at[rows, jcols]
        if k < 4:
            return r.mixw.at[k, rows]
        m, half = FF_ORDER[(k - 5) // 2], (k - 5) % 2
        if p.FD:
            return r.ffw.at[m, half * F // 2:(half + 1) * F // 2, rows]
        return r.ffw.at[m, pl.ds(pl.multiple_of(device * S + half * S // 2, S // 2), S // 2)]

    def gather_ready(k):
        if k < 5:
            own_mix[k].wait()
            slot(k, i)[...] = r.qpre[k * S:(k + 1) * S, :].astype(BF)
        else:
            m, half = FF_ORDER[(k - 5) // 2], (k - 5) % 2
            if half == 0:
                own_ff[m].wait()
            if p.FD:
                slot(k, i)[...] = stage[m][half * F // 2:(half + 1) * F // 2, :].astype(BF)

    relays = HI == 4
    next_to_end = (zi == 1) | (zi == 2)

    def along_z(block, ssem, rsem):
        for d in range(1, HI):
            to = lax.rem(zi + d, HI)
            near = (jnp.abs(to - zi) < 3) if relays else None
            go(block, block, ssem.at[d - 1], rsem.at[d - 1], when=near, dp=to * LO + yi)

    def hand_on(block, ssem, rsem):
        if relays:
            end = jnp.where(zi == 2, 3, 0)
            go(block, block, ssem, rsem.at[jnp.where(zi == 2, 2, 0)], when=next_to_end, dp=end * LO + yi)

    def from_z_source(k, d, y):
        return slot(k, lax.rem(zi - d + HI, HI) * LO + y)

    WAYS = [2, 1, *range(3, HI)]

    def gather_send(k):
        src = slot(k, i)
        along_z(src, r.zs.at[k], r.zr.at[k])
        go(src, src, r.ys.at[k, 0], r.yr.at[k, 0], dp=zi * LO + 1 - yi)

    def gather_forward(k):
        if k - 1 in Y_FIRST:
            b = Y_FIRST.index(k - 1)
            block = from_z_source(k - 1, 2, 1 - yi)
            arrived(block, r.ur.at[b, 1])
            hand_on(block, r.yp.at[b], r.ur.at[b])
        if k in Y_FIRST:
            b = Y_FIRST.index(k)
            peers = slot(k, zi * LO + 1 - yi)
            arrived(peers, r.yr.at[k, 0])
            along_z(peers, r.us.at[b], r.ur.at[b])
        for d in WAYS:
            block = from_z_source(k, d, yi)
            arrived(block, r.zr.at[k, d - 1])
            if d == 2:
                hand_on(block, r.zp.at[k], r.zr.at[k])
            if k not in Y_FIRST:
                go(block, block, r.ys.at[k, d], r.yr.at[k, d], dp=zi * LO + 1 - yi)

    def gather_wait(k):
        for d in range(HI):
            if k not in Y_FIRST:
                arrived(from_z_source(k, d, 1 - yi), r.yr.at[k, d])
            elif d in (1, 3) or d > 3:
                arrived(from_z_source(k, d, 1 - yi), r.ur.at[Y_FIRST.index(k), d - 1])

    def share_send(s, block, src=None):
        own = block(j)
        src = own if src is None else src
        for d in range(1, X):
            go(src, own, r.xs.at[s, d - 1], r.xr.at[s, d - 1], mp=lax.rem(xi + d, X) * 2 + ci)
        go(src, own, r.cs.at[s, 0], r.cr.at[s, 0], mp=xi * 2 + 1 - ci)

    def share_forward(s, block):
        for d in range(1, X):
            part = block(lax.rem(xi - d + X, X) * 2 + ci)
            arrived(part, r.xr.at[s, d - 1])
            go(part, part, r.cs.at[s, d], r.cr.at[s, d], mp=xi * 2 + 1 - ci)

    def share_wait(s, block):
        for d in range(X):
            arrived(block(lax.rem(xi - d + X, X) * 2 + 1 - ci), r.cr.at[s, d])

    def sum_begin(s, b, compute, between):
        sent = []

        def pair(d):
            to = lax.rem(xi + d, X)
            compute(to)
            sent.append(go(
                r.part.at[to, 1 - ci], r.recc.at[b, to], r.acs.at[s, d], r.acr.at[s, d], mp=xi * 2 + 1 - ci
            ))

        for d in range(1, X):
            pair(d)
        between()
        for d in range(1, X):
            to = lax.rem(xi + d, X)
            arrived(r.recc.at[b, to], r.acr.at[s, d])
            for t in range(NT):
                q = slice(t * 128, (t + 1) * 128)
                r.part[to, ci, q] = (
                    r.part[to, ci, q].astype(F32) + r.recc[b, to, q].astype(F32)
                ).astype(BF)
                sent.append(go(
                    r.part.at[to, ci, q], r.recx.at[b, d - 1, q], r.axs.at[s, d - 1, t], r.axr.at[s, d - 1, t],
                    mp=to * 2 + ci,
                ))
        pair(0)
        return sent

    def sum_arrived(s, b, t):
        if t == 0:
            arrived(r.recc.at[b, xi], r.acr.at[s, 0])
        for d in range(1, X):
            arrived(r.recx.at[b, d - 1, t * 128:(t + 1) * 128], r.axr.at[s, d - 1, t])

    def sum_tile(b, q):
        total = r.part[xi, ci, q].astype(F32) + r.recc[b, xi, q].astype(F32)
        for d in range(1, X):
            total = total + r.recx[b, d - 1, q].astype(F32)
        return total

    flat = p.FD

    def half_of(k):
        size = (F if flat else S) // 2
        return (k - 5) // 2, slice((k - 5) % 2 * size, ((k - 5) % 2 + 1) * size)

    def block_of(k, z, y):
        if k < 5:
            return r.gm.at[k, z, y]
        m, rows = half_of(k)
        return r.gf.at[m, y, rows, rows_of(z, S)] if flat else r.gf.at[m, z, y, rows]

    def from_y(k):
        if k < 5:
            return r.rym.at[k]
        m, rows = half_of(k)
        return r.ryf.at[m, rows] if flat else r.ryf.at[m, :, rows]

    def from_y_block(k, z):
        ref = from_y(k)
        return ref.at[:, rows_of(z, S)] if flat and k >= 5 else ref.at[z]

    def to_y(k):
        if k < 5:
            return r.gm.at[k, :, 1 - yi]
        m, rows = half_of(k)
        return r.gf.at[m, 1 - yi, rows] if flat else r.gf.at[m, :, 1 - yi, rows]

    def from_z(k, d, own=True):
        if not own:
            return (r.othm if k < 5 else r.othf).at[d - 1]
        if k < 5:
            return r.rzm.at[k, d - 1]
        m, rows = half_of(k)
        return r.rzf.at[m, d - 1, rows]

    def handed(k, own=True):
        if not own:
            return (r.othm if k < 5 else r.othf).at[HI - 1]
        if k < 5:
            return r.relm.at[max(k - 3, 0)]
        m, rows = half_of(k)
        return r.relf.at[m, rows]

    def z_sems(k, own):
        if own:
            return r.bzs.at[k], r.bzr.at[k], r.bts.at[k], r.btr.at[k]
        o = Z_FIRST.index(k)
        return r.ozs.at[o], r.ozr.at[o], r.ots.at[o], r.otr.at[o]

    def stepped(k):
        return relays and k not in STRAIGHT

    def far(d, back=False):
        other = lax.rem(zi + (HI - d if back else d), HI)
        return jnp.abs(other - zi) == 3

    def z_send(k, own, ways):
        y = yi if own else 1 - yi
        ssem, rsem, tsem, trsem = z_sems(k, own)
        for d in ways:
            to = lax.rem(zi + d, HI)
            block, dst = block_of(k, to, y), from_z(k, d, own)
            if stepped(k) and d != 2:
                go(block, handed(k, own), tsem, trsem, when=far(d), dp=jnp.where(zi == 0, 1, 2) * LO + yi)
                go(block, dst, ssem.at[d - 1], rsem.at[d - 1], when=jnp.logical_not(far(d)), dp=to * LO + yi)
            else:
                go(block, dst, ssem.at[d - 1], rsem.at[d - 1], dp=to * LO + yi)

    def z_send_handed(k, own):
        block = block_of(k, lax.rem(zi + 2, HI), yi if own else 1 - yi)

        @pl.when(next_to_end)
        def _():
            arrived(handed(k, own), z_sems(k, own)[3])
            block[...] = (block[...].astype(F32) + handed(k, own)[...].astype(F32)).astype(BF)

        z_send(k, own, [2])

    def z_total(k, own):
        for d in range(1, HI):
            wait = partial(arrived, from_z(k, d, own), z_sems(k, own)[1].at[d - 1])
            guarded(jnp.logical_not(far(d, back=True)) if stepped(k) and d != 2 else None, wait)
        total = block_of(k, zi, yi if own else 1 - yi)[...].astype(F32)
        for d in range(1, HI):
            total = total + from_z(k, d, own)[...].astype(F32)
        return total

    def clear_far_places():
        if not relays:
            return
        for d in (1, 3):
            @pl.when(far(d, back=True))
            def _(d=d):
                r.rzm[:, d - 1] = jnp.zeros((5, S, C), BF)
                for m in range(3):
                    r.rzf[m, d - 1] = jnp.zeros(r.rzf.shape[2:], BF)
                r.othm[d - 1] = jnp.zeros(r.othm.shape[1:], BF)
                r.othf[d - 1] = jnp.zeros(r.othf.shape[1:], BF)

    def near_ways(k):
        return [3, 1] if stepped(k) else list(range(1, HI))

    def scatter_first(*pieces):
        for k in pieces:
            if k in Z_FIRST:
                for own in (False, True):
                    z_send(k, own, near_ways(k))
            else:
                go(to_y(k), from_y(k), r.bys.at[k], r.byr.at[k], dp=zi * LO + 1 - yi)

    def scatter_second(*pieces):
        for k in pieces:
            if k in Z_FIRST:
                block = block_of(k, zi, 1 - yi)
                block[...] = z_total(k, False).astype(BF)
                go(block, from_y_block(k, zi), r.bys.at[k], r.byr.at[k], dp=zi * LO + 1 - yi)
                continue
            arrived(from_y(k), r.byr.at[k])
            for d in range(1, HI):
                to = lax.rem(zi + d, HI)
                block = block_of(k, to, yi)
                block[...] = (block[...].astype(F32) + from_y_block(k, to)[...].astype(F32)).astype(BF)
            z_send(k, True, near_ways(k))

    def scatter_handed(*pieces):
        for k in pieces:
            if stepped(k):
                if k in Z_FIRST:
                    z_send_handed(k, False)
                z_send_handed(k, True)

    def scatter_total(k):
        if k in Z_FIRST:
            arrived(from_y_block(k, zi), r.byr.at[k])
        return z_total(k, True) + from_y_block(k, zi)[...].astype(F32)

    def squares_of(total):
        squared = total * total
        if squared.shape[-1] % 128:
            corner = (lax.broadcasted_iota(jnp.int32, (8, 128), 0) + lax.broadcasted_iota(jnp.int32, (8, 128), 1)) == 0
            return jnp.where(corner, jnp.sum(squared), 0.0)
        folded = jnp.sum(squared.reshape(-1, 8, squared.shape[-1]), axis=0)
        return sum(folded[:, c:c + 128] for c in range(0, folded.shape[-1], 128))

    def finish_ff(*pieces):
        for k in pieces:
            m, rows = half_of(k)
            total = scatter_total(k)
            if m == 0:
                r.gso[rows] = total
            else:
                r.geo[m - 1, rows] = total
            r.sqs[...] += squares_of(total)

    def put_grad(k, lhs, rhs, turned=False):
        g = r.gm.at[k] if k < 5 else r.gf.at[k - 5]
        per = TT // (LO * S)

        def tile(t):
            if turned:
                out = dot_nn(lhs[rows_of(t, TT), :], rhs[...])
            else:
                out = dot_tn(lhs[:, rows_of(t, TT)], rhs[...])
            g[pl.ds(t * per, per)] = out.astype(BF).reshape(per, LO, S, out.shape[-1])

        each(D // TT, tile)

    def put_ff_grad(m, units, model):
        if not flat:
            return put_grad(5 + m, model, units)
        for f in range(0, F, 384):
            q = slice(f, min(f + 384, F))
            out = dot_tn(units[:, q], model[...]).astype(BF)
            for y in range(LO):
                for z in range(HI):
                    r.gf[m, y, q, z * S:(z + 1) * S] = out[:, (z * LO + y) * S:(z * LO + y + 1) * S]

    def to_units(a, m):
        return dot_nt(a, r.ffw[m]) if flat else dot_nn(a, r.ffw[m])

    def to_model(a, m):
        return dot_nn(a, r.ffw[m]) if flat else dot_nt(a, r.ffw[m])

    gather_ready(0)
    gather_ready(1)
    enter()
    gather_send(0)
    gather_send(1)
    gather_ready(2)
    gather_send(2)
    r.sqs[...] = jnp.zeros_like(r.sqs)
    clear_far_places()

    length = r.live[0]
    load_x.wait()

    def norm_tile(t):
        q = rows_of(t, 128)
        v = r.xv[q, :].astype(F32)
        r.nin[q, :] = (v * lax.rsqrt(jnp.mean(v * v, axis=-1, keepdims=True) + EPSILON)).astype(BF)

    each(T // 128, norm_tile)
    for k in range(3, 11):
        gather_ready(k)
    load_x_own = load(r.x.at[rows_of(j, TB)], r.xown, 8)
    load_og.wait()
    load_cos = load(r.cos, r.cosv, 0)
    load_sin = load(r.sin, r.sinv, 1)

    def live_tile(t):
        q = rows_of(t, 128)
        place = lax.broadcasted_iota(jnp.int32, (128, D), 0) + t * 128
        r.up[q, :] = jnp.where(place < length, r.up[q, :].astype(F32), 0.0).astype(BF)

    each(T // 128, live_tile)

    place = lax.broadcasted_iota(jnp.int32, (1, T), 1)
    segment = r.seg[...].astype(F32)
    r.segk[...] = jnp.broadcast_to(jnp.where(place < length, segment, -2.0), (8, T))
    seg_q = jnp.where(place < length, segment, -1.0)
    for t in range(T // 128):
        q = slice(t * 128, t * 128 + 128)
        r.segq[q, :] = jnp.transpose(jnp.broadcast_to(seg_q[:, q], (128, 128)))

    down = lax.broadcasted_iota(jnp.int32, (B, B), 0)
    over = lax.broadcasted_iota(jnp.int32, (B, B), 1)
    heads = D // HEAD

    def rate_of(h):
        return -(8.0 * (j * H + h).astype(F32) / heads) * (1.0 - LAYER_PLACE)

    for h in range(H):
        rate = rate_of(h)
        for o in range(2):
            distance = down - over + o * B
            fade = jnp.exp(rate * jnp.maximum(distance, 0).astype(F32))
            r.dec[o, h] = jnp.where(distance >= 0, fade, 0.0)

    for t in range(D // 128):
        q = slice(t * 128, t * 128 + 128)
        r.nint[q, :] = jnp.transpose(r.nin[:, q])
    load_cos.wait()
    load_sin.wait()
    load_x_own.wait()

    def turn_into(pre_ref, rot_ref, k):
        def tile(t):
            q = rows_of(t, TT)
            pre = dot_nn(r.nin[q, :], r.mixw[k])
            pre_ref[q, :] = pre
            act = pre * jax.nn.sigmoid(pre)
            c, s = r.cosv[q, :], r.sinv[q, :]
            for h in range(H):
                a = act[:, h * HEAD:(h + 1) * HEAD]
                rot_ref[q, 2 * h * HEAD:(2 * h + 1) * HEAD] = (a * c).astype(BF)
                rot_ref[q, (2 * h + 1) * HEAD:(2 * h + 2) * HEAD] = (a * s).astype(BF)

        each(T // TT, tile)

    def project_into(ref, k):
        def tile(t):
            q = rows_of(t, TT)
            ref[q, :] = dot_nn(r.nin[q, :], r.mixw[k]).astype(ref.dtype)

        each(T // TT, tile)

    gather_forward(0)
    gather_send(3)
    gather_forward(1)
    gather_send(4)
    gather_wait(0)
    turn_into(r.qpre, r.qrot, 0)
    gather_forward(2)
    gather_send(5)
    gather_wait(1)
    turn_into(r.kpre, r.krot, 1)
    gather_forward(3)
    gather_send(6)
    gather_wait(2)
    project_into(r.val, 2)
    gather_forward(4)
    gather_send(7)
    gather_wait(3)
    project_into(r.gpre, 3)

    def wo_block(owner):
        return r.wo.at[:, pl.ds(pl.multiple_of(owner * C, C), C)]


    NB = T // B
    REACH = LONGEST // B

    def keys_of(qb):
        return slice(max(0, qb - REACH) * B, (qb + 1) * B)

    def weights_of(qb, h):
        key = keys_of(qb)
        width = key.stop - key.start
        fades = [r.dec[min(o, 1), h] for o in range(width // B - 1, -1, -1)]
        for o in range(2, width // B):
            fades[width // B - 1 - o] *= jnp.exp(rate_of(h) * ((o - 1) * B))
        seen = jnp.broadcast_to(r.segk[0:1, key], (B, width))
        same = widen(r.segq[qb * B:(qb + 1) * B, :], width) == seen
        return jnp.where(same, jnp.concatenate(fades, axis=1), 0.0)

    def u_block(qb):
        return lambda owner: r.ufull.at[qb * B:(qb + 1) * B, pl.ds(pl.multiple_of(owner * C, C), C)]

    def attend(qb):
        q = slice(qb * B, (qb + 1) * B)
        squares = jnp.zeros((B, 1), F32)
        for h in range(H):
            rot = slice(2 * h * HEAD, 2 * (h + 1) * HEAD)
            chan = slice(h * HEAD, (h + 1) * HEAD)
            key = keys_of(qb)
            scores = dot_nt(r.qrot[q, rot], r.krot[key, rot]) * weights_of(qb, h)
            total = dot_nn(scores.astype(BF), r.val[key, chan])
            r.mixed[q, chan] = total
            squares = squares + jnp.sum(total * total, axis=-1, keepdims=True)
            r.ufull[q, pl.ds(pl.multiple_of(j * C + h * HEAD, HEAD), HEAD)] = (
                total * r.gpre[q, chan]
            ).astype(BF)
        r.ss[j, :, q] = jnp.transpose(jnp.broadcast_to(squares, (B, 128)))[0:8, :]

    def ss_block(owner):
        return r.ss.at[owner]

    for qb in range(NB):
        attend(qb)
        share_send(1 + qb, u_block(qb))
        if qb == NB - 1:
            share_send(1 + NB, ss_block)
        if qb == 0:
            gather_forward(5)
            gather_send(8)
        if qb == 1:
            gather_wait(4)
            share_send(0, wo_block)
        if qb == 3:
            share_forward(0, wo_block)
        if qb == 2:
            gather_forward(6)
            gather_send(9)
        if qb > 0:
            share_forward(qb, u_block(qb - 1))
    share_forward(NB, u_block(NB - 1))
    share_forward(1 + NB, ss_block)
    gather_forward(7)
    gather_send(10)
    gather_forward(8)
    share_wait(0, wo_block)
    for qb in range(NB):
        share_wait(1 + qb, u_block(qb))
    share_wait(1 + NB, ss_block)
    early = [copy for copy, when in pending]

    total_ss = r.ss[0]
    for owner in range(1, mp):
        total_ss = total_ss + r.ss[owner]
    inverse = lax.rsqrt(total_ss * (1.0 / D) + EPSILON)
    for t in range(T // 128):
        q = slice(t * 128, t * 128 + 128)
        r.rcol[q, :] = jnp.transpose(jnp.broadcast_to(inverse[0:1, q], (128, 128)))

    def hidden_tile(t):
        q = rows_of(t, TB)
        out = widen(r.rcol[q, :], D) * dot_nn(r.ufull[q, :], r.wo[...])
        hidden = r.xv[q, :].astype(F32) + out
        scale = lax.rsqrt(jnp.mean(hidden * hidden, axis=-1, keepdims=True) + EPSILON)
        r.nmid[q, :] = (hidden * scale).astype(BF)

        @pl.when(t == j)
        def _():
            r.hown[...] = hidden

    each(T // TB, hidden_tile)
    gather_wait(5)
    gather_wait(6)

    def gate_tile(t):
        q = rows_of(t, TT)
        r.gact[q, 0:F] = to_units(r.nmid[q, :], 1)

    each(T // TT, gate_tile)
    gather_forward(9)
    gather_wait(7)
    gather_wait(8)

    def up_tile(t):
        q = rows_of(t, TT)
        upper = to_units(r.nmid[q, :], 2)
        r.uact[q, :] = upper.astype(BF)
        r.prod[q, :] = (r.gact[q, 0:F] * upper).astype(BF)

    each(T // TT, up_tile)
    put_ff_grad(0, r.prod, r.up)
    gather_forward(10)
    scatter_first(5, 6)
    for copy in early:
        settle(copy)
    gather_wait(9)
    gather_wait(10)

    def mid_pair(x):
        q = rows_of(x, 2 * TB)
        g = to_units(r.up[q, :], 0)
        grad_gate, grad_up = (g * r.uact[q, :].astype(F32)).astype(BF), (g * r.gact[q, 0:F]).astype(BF)
        r.ggate[q, :] = grad_gate
        r.gup[q, :] = grad_up
        r.part[x] = (to_model(grad_gate, 1) + to_model(grad_up, 2)).astype(BF).reshape(2, TB, D)

    used = sum_begin(0, 0, mid_pair, partial(scatter_second, 5))
    put_ff_grad(1, r.ggate, r.nmid)
    scatter_first(7, 8)
    scatter_handed(5)
    scatter_second(6)

    def back_tile(t):
        q = slice(t * 128, (t + 1) * 128)
        here = rows_of(j * (TB // 128) + t, 128)
        grad = sum_tile(0, q)
        hidden = r.hown[q, :]
        scale = lax.rsqrt(jnp.mean(hidden * hidden, axis=-1, keepdims=True) + EPSILON)
        normed = hidden * scale
        inner = jnp.mean(grad * normed, axis=-1, keepdims=True)
        out = r.up[here, :].astype(F32) + scale * (grad - normed * inner)
        low = out.astype(BF)
        for owner in range(mp):
            r.hsend[owner * TB + t * 128:owner * TB + (t + 1) * 128, :] = low[:, owner * C:(owner + 1) * C]
        mixer_out = hidden - r.xown[q, :].astype(F32)
        product = jnp.sum(low.astype(F32) * mixer_out, axis=-1, keepdims=True) * (1.0 / D)
        r.inn[j, :, q] = jnp.transpose(jnp.broadcast_to(product, (128, 128)))[0:8, :]

    def token_block(ref):
        return lambda owner: ref.at[rows_of(owner, TB)]

    BO, GM, IG = 2 + NB, 3 + NB, 8 + NB

    def half_block(ref, t):
        return lambda owner: ref.at[rows_of(owner * NT + t, 128)]

    def peers():
        return [(d, lax.rem(j + d, mp), lax.rem(j - d + mp, mp)) for d in range(1, mp)]

    for t in range(NT):
        sum_arrived(0, 0, t)
        back_tile(t)
    low = jnp.concatenate([r.hsend[owner * TB:(owner + 1) * TB, :] for owner in range(mp)], axis=1)
    grad_gated = dot_nt(low, r.wo[...]).astype(BF)
    for owner in range(mp):
        r.gsend[owner * TB:(owner + 1) * TB, :] = grad_gated[:, owner * C:(owner + 1) * C]
    for d, to, source in peers():
        go(token_block(r.gsend)(to), token_block(r.ggated)(j), r.ags.at[0, d], r.agr.at[0, d], mp=to)
    own_rows = rows_of(j, TB)
    r.ggated[own_rows, :] = r.gsend[own_rows, :]
    r.hcols[own_rows, :] = r.hsend[own_rows, :]
    for d, to, source in peers():
        go(r.inn.at[j], r.inn.at[j], r.ahs.at[0, d], r.ahr.at[0, d], mp=to)
    for d, to, source in peers():
        go(token_block(r.hsend)(to), token_block(r.hcols)(j), r.ahs.at[1, d], r.ahr.at[1, d], mp=to)
    put_ff_grad(2, r.gup, r.nmid)
    scatter_first(9, 10)
    scatter_handed(6)
    scatter_second(7)
    for copy in used:
        settle(copy)

    def expand_tile(t):
        r.part[t // 2, lax.rem(t, 2)] = to_model(r.prod[rows_of(t, TB), :], 0).astype(BF)

    each(mp, expand_tile)
    used = [
        go(r.part.at[to, 1 - ci], r.recc.at[1, to], r.acs.at[1, d], r.acr.at[1, d], mp=xi * 2 + 1 - ci)
        for d, to in [(d, lax.rem(xi + d, X)) for d in range(X)]
    ]
    for d, to, source in peers():
        arrived(token_block(r.ggated)(source), r.agr.at[0, d])
        arrived(r.inn.at[source], r.ahr.at[0, d])
    for owner in range(mp):
        for t in range(TB // 128):
            row = r.inn[owner, 0:1, t * 128:(t + 1) * 128]
            q = slice(owner * TB + t * 128, owner * TB + (t + 1) * 128)
            r.icol[q, :] = jnp.transpose(jnp.broadcast_to(row, (128, 128)))

    def gated_tile(t):
        q = rows_of(t, TT)
        grad = r.ggated[q, :].astype(F32)
        inner = widen(r.icol[q, :], C)
        inverse = widen(r.rcol[q, :], C)
        normed = r.mixed[q, :] * inverse
        r.gproj[3][q, :] = (grad * normed).astype(BF)
        r.gmix[q, :] = (inverse * (grad * r.gpre[q, :] - normed * inner)).astype(BF)

    each(T // TT, gated_tile)

    for d in [*range(1, X), 0]:
        to = lax.rem(xi + d, X)
        arrived(r.recc.at[1, to], r.acr.at[1, d])
        for t in range(NT):
            q = slice(t * 128, (t + 1) * 128)
            r.recc[1, to, q] = (r.part[to, ci, q].astype(F32) + r.recc[1, to, q].astype(F32)).astype(BF)
            if d:
                go(r.recc.at[1, to, q], r.recx.at[1, d - 1, q], r.axs.at[1, d - 1, t], r.axr.at[1, d - 1, t], mp=to * 2 + ci)
    scatter_second(8)

    def output_grad_tile(t):
        q = rows_of(t, TT)
        r.rh[q, :] = (widen(r.rcol[q, :], C) * r.hcols[q, :].astype(F32)).astype(BF)

    def swish_back(pre, grad):
        gate = jax.nn.sigmoid(pre)
        return grad * (gate * (1.0 + pre * (1.0 - gate)))

    def attend_back(qb):
        q, key = slice(qb * B, (qb + 1) * B), keys_of(qb)
        for h in range(H):
            rot = slice(2 * h * HEAD, 2 * (h + 1) * HEAD)
            chan = slice(h * HEAD, (h + 1) * HEAD)
            weights = weights_of(qb, h)
            scores = (dot_nt(r.qrot[q, rot], r.krot[key, rot]) * weights).astype(BF)
            back = (dot_nt(r.gmix[q, chan], r.val[key, chan]) * weights).astype(BF)
            dq = dot_nn(back, r.krot[key, rot])
            turned = dq[:, :HEAD] * r.cosv[q, :] + dq[:, HEAD:] * r.sinv[q, :]
            r.gproj[0][q, chan] = swish_back(r.qpre[q, chan], turned).astype(BF)
            dk = dot_tn(back, r.qrot[q, rot])
            dv = dot_tn(scores, r.gmix[q, chan])
            for kb in range(key.start // B, qb + 1):
                at = slice(kb * B - key.start, (kb + 1) * B - key.start)
                rows = slice(kb * B, (kb + 1) * B)
                dkb, dvb = dk[at], dv[at]
                if qb < min(kb + REACH, NB - 1):
                    dkb, dvb = dkb + r.dk[rows, rot], dvb + r.dv[rows, chan]
                if kb < qb:
                    r.dk[rows, rot], r.dv[rows, chan] = dkb, dvb
                else:
                    turned = dkb[:, :HEAD] * r.cosv[q, :] + dkb[:, HEAD:] * r.sinv[q, :]
                    r.gproj[1][q, chan] = swish_back(r.kpre[q, chan], turned).astype(BF)
                    r.gproj[2][q, chan] = dvb.astype(BF)

    def output_tile(t):
        q = rows_of(t, 128)
        total = r.recc[1, xi, q].astype(F32)
        for d in range(1, X):
            total = total + r.recx[1, d - 1, q].astype(F32)
        r.bov[rows_of(j * NT + t, 128), :] = (r.hown[q, :] + total).astype(BF)

    def late_core(x):
        return pltpu.make_async_remote_copy(
            src_ref=r.part.at[x, 1 - ci], dst_ref=r.recc.at[0, x], send_sem=r.acs.at[2, x], recv_sem=r.acr.at[2, x],
            device_id={"mp": xi * 2 + 1 - ci}, device_id_type=MESH,
        )

    def late_chip(x, d, t):
        q = slice(t * 128, (t + 1) * 128)
        return pltpu.make_async_remote_copy(
            src_ref=r.part.at[x, ci, q], dst_ref=r.recx.at[0, d - 1, q], send_sem=r.axs.at[2, d - 1, t],
            recv_sem=r.axr.at[2, d - 1, t], device_id={"mp": x * 2 + ci}, device_id_type=MESH,
        )

    def blocks_in(qb):
        return [divmod(at, 2) for at in range(qb * B // TB, (qb + 1) * B // TB)]

    def late_begin(x, c):
        q = slice((x * 2 + c) * TB, (x * 2 + c + 1) * TB)
        out = dot_nt(r.gproj[0][q, :], r.mixw[0])
        for k in range(1, 4):
            out = out + dot_nt(r.gproj[k][q, :], r.mixw[k])
        r.part[x, c] = out.astype(BF)

        @pl.when(ci != c)
        def _():
            late_core(x).start()

    def late_pass(x, c):
        @pl.when(ci == c)
        def _():
            arrived(r.recc.at[0, x], r.acr.at[2, x])

        @pl.when((ci == c) & (xi != x))
        def _():
            for t in range(NT):
                q = slice(t * 128, (t + 1) * 128)
                r.part[x, c, q] = (r.part[x, c, q].astype(F32) + r.recc[0, x, q].astype(F32)).astype(BF)
                late_chip(x, lax.rem(x - xi + X, X), t).start()

    put_grad(3, r.nint, r.gproj[3], turned=True)
    scatter_first(3)
    for qb in range(NB - 1, -1, -1):
        attend_back(qb)
        if qb == NB - 1:
            for copy in used:
                settle(copy)
        for x, c in blocks_in(qb):
            late_begin(x, c)
        if qb < NB - 1:
            for x, c in blocks_in(qb + 1):
                late_pass(x, c)
        if qb == NB - 1:
            for d, to, source in peers():
                arrived(token_block(r.hcols)(source), r.ahr.at[1, d])
            each(T // TT, output_grad_tile)
            put_grad(4, r.ufull, r.rh)
            scatter_first(4)
            scatter_handed(7, 8, 9)
            scatter_second(10)
            finish_ff(5)
        if qb == max(NB - 2, 0):
            scatter_handed(10)
            scatter_second(3, 9)
            for t in range(NT):
                for d in range(1, X):
                    arrived(r.recx.at[1, d - 1, t * 128:(t + 1) * 128], r.axr.at[1, d - 1, t])
            each(TB // 128, output_tile)
            share_send(BO, token_block(r.bov))
            finish_ff(6)
        if qb == max(NB - 3, 0):
            scatter_handed(4, 3)
            share_forward(BO, token_block(r.bov))
            finish_ff(7)
    for x, c in blocks_in(0):
        late_pass(x, c)
    pending.extend((late_core(x), None) for x in range(X))
    pending.extend((late_chip(lax.rem(xi + d, X), d, t), None) for d in range(1, X) for t in range(NT))
    for k in (2, 0):
        put_grad(k, r.nint, r.gproj[k], turned=True)
        scatter_first(k)
    scatter_second(4)
    put_grad(1, r.nint, r.gproj[1], turned=True)
    scatter_first(1)
    finish_ff(8, 9, 10)
    scatter_second(2, 0)

    def input_tile(t):
        q = slice(t * 128, (t + 1) * 128)
        low = jnp.concatenate(
            [r.hsend[owner * TB + t * 128:owner * TB + (t + 1) * 128, :] for owner in range(mp)], axis=1
        ).astype(F32)
        grad = sum_tile(0, q)
        v = r.xown[q, :].astype(F32)
        scale = lax.rsqrt(jnp.mean(v * v, axis=-1, keepdims=True) + EPSILON)
        normed = v * scale
        inner = jnp.mean(grad * normed, axis=-1, keepdims=True)
        r.igv[rows_of(j * NT + t, 128), :] = (low + scale * (grad - normed * inner)).astype(BF)

    for t in range(NT):
        for d in range(1, X):
            arrived(r.recx.at[0, d - 1, t * 128:(t + 1) * 128], r.axr.at[2, d - 1, t])
        input_tile(t)
        share_send(IG + t, half_block(r.igv, t))
    done = [copy for copy, when in pending]
    scatter_second(1)
    scatter_handed(2)
    for copy in done:
        settle(copy)
    share_wait(BO, token_block(r.bov))
    stores = [load(r.bov, r.bo, 0)]

    def grad_block(k):
        return lambda owner: r.gmv.at[k * S:(k + 1) * S, pl.ds(pl.multiple_of(owner * C, C), C)]

    for k in (4, 3, 2, 0, 1):
        total = scatter_total(k).astype(BF)
        r.gmv[k * S:(k + 1) * S, jcols] = total
        r.sqs[...] += squares_of(total.astype(F32))
        for d, to, source in peers():
            go(grad_block(k)(j), grad_block(k)(j), r.gms.at[k, d], r.gmr.at[k, d], mp=to)

    if p.N > 1:
        at = i * mp + j
        r.sall[at] = r.sqs[...]
        for d in range(1, p.N):
            go(r.sall.at[at], r.sall.at[at], r.qs.at[d], r.qr.at[d], **whole(d))
        for t in range(NT):
            share_forward(IG + t, half_block(r.igv, t))
        for d in range(1, p.N):
            arrived(r.sall.at[lax.rem(at - d + p.N, p.N)], r.qr.at[d])
        r.sqo[...] = jnp.sum(r.sall[...], axis=0)
    else:
        r.s1[j] = r.sqs[...]
        for d, to, source in peers():
            go(r.s1.at[j], r.s1.at[j], r.q1s.at[d], r.q1r.at[d], mp=to)
        for t in range(NT):
            share_forward(IG + t, half_block(r.igv, t))
        for d, to, source in peers():
            arrived(r.s1.at[source], r.q1r.at[d])
        r.s2[i] = jnp.sum(r.s1[...], axis=0)
        for d in range(1, n):
            go(r.s2.at[i], r.s2.at[i], r.q2s.at[d], r.q2r.at[d], dp=lax.rem(i + d, n))
        for d in range(1, n):
            arrived(r.s2.at[lax.rem(i - d + n, n)], r.q2r.at[d])
        r.sqo[...] = jnp.sum(r.s2[...], axis=0)

    for t in range(NT):
        share_wait(IG + t, half_block(r.igv, t))
    stores.append(load(r.igv, r.ig, 1))
    for k in (4, 3, 2, 0, 1):
        for d, to, source in peers():
            arrived(grad_block(k)(source), r.gmr.at[k, d])
        stores.append(load(r.gmv.at[k * S:(k + 1) * S], r.gmo.at[k], 2 + k))
    for copy in stores:
        copy.wait()
    for copy, when in pending:
        guarded(when, copy.wait_send)


def fused(p, *operands):
    scratch = scratch_of(p)
    names = IN_NAMES + OUT_NAMES + tuple(scratch)
    anywhere = pl.BlockSpec(memory_space=pl.ANY)
    vmem = pl.BlockSpec(memory_space=pltpu.VMEM)
    smem = pl.BlockSpec(memory_space=pltpu.SMEM)
    return pl.pallas_call(
        partial(body, p, names),
        out_shape=(
            jax.ShapeDtypeStruct((p.T, p.D), BF),
            jax.ShapeDtypeStruct((p.T, p.D), BF),
            jax.ShapeDtypeStruct((5, p.S, p.D), BF),
            jax.ShapeDtypeStruct((2, p.F, p.S) if p.FD else (2, p.S, p.F), F32),
            jax.ShapeDtypeStruct((p.F, p.S) if p.FD else (p.S, p.F), F32),
            jax.ShapeDtypeStruct((8, 128), F32),
        ),
        in_specs=[anywhere, anywhere, vmem, smem] + [anywhere] * 5,
        out_specs=(anywhere, anywhere, anywhere, vmem, vmem, vmem),
        scratch_shapes=list(scratch.values()),
        compiler_params=pltpu.CompilerParams(
            collective_id=0, has_side_effects=True, vmem_limit_bytes=VMEM_LIMIT
        ),
    )(*operands)


VMEM_LIMIT = 64 * 2**20 - 2**18


def renew(weight, momentum, shadow, grad, clip_factor):
    clipped = grad * clip_factor
    velocity = MOMENTUM * momentum + clipped
    updated = weight - LEARN_RATE * (clipped + MOMENTUM * velocity)
    average = SHADOW_DECAY * shadow + (1.0 - SHADOW_DECAY) * updated
    return (velocity, average, updated)


def update_body(cuts, *refs):
    kinds, pieces = len(cuts), sum(len(c) for c in cuts)
    sq, carried = refs[0], refs[1:3]
    ins = [refs[3 + 4 * w:7 + 4 * w] for w in range(kinds)]
    refs = refs[3 + 4 * kinds:]
    norm_out, carried_out = refs[0], refs[1:3]
    outs = [refs[3 + 3 * w:6 + 3 * w] for w in range(kinds)]
    refs = refs[3 + 3 * kinds:]
    held = [refs[4 * w:4 * w + 4] for w in range(kinds)]
    made = [refs[4 * kinds + 3 * w:4 * kinds + 3 * w + 3] for w in range(kinds)]
    bounce, (in_sem, out_sem, carry_sem) = refs[7 * kinds:7 * kinds + 2], refs[7 * kinds + 2:]
    order = [(w, c) for w in range(kinds) for c in range(len(cuts[w]))]
    loads, copies = {}, []

    def load_piece(at):
        if at < len(order):
            w, c = order[at]
            loads[at] = [
                pltpu.make_async_copy(ins[w][a].at[cuts[w][c]], held[w][a].at[cuts[w][c]], in_sem.at[at, a]) for a in range(4)
            ]
            for copy in loads[at]:
                copy.start()

    def store(src, dst, sem):
        copies.append(pltpu.make_async_copy(src, dst, sem))
        copies[-1].start()

    for at in range(AHEAD):
        load_piece(at)
    carry = [pltpu.make_async_copy(carried[a], bounce[a], carry_sem.at[a]) for a in range(2)]
    carry[0].start()
    norm = jnp.sqrt(jnp.broadcast_to(jnp.sum(sq[...]), (8, 128)))
    norm_out[0, 0] = jnp.max(norm)
    clip_factor = 1.0 / jnp.maximum(jnp.max(norm), 1.0)
    for at, (w, c) in enumerate(order):
        cut = cuts[w][c]
        for copy in loads[at]:
            copy.wait()
        new = renew(*[held[w][a][cut] for a in range(3)], held[w][3][cut].astype(F32), clip_factor)
        for a in range(3):
            made[w][a][cut] = new[a]
            store(made[w][a].at[cut], outs[w][a].at[cut], out_sem.at[at, a])
        load_piece(at + AHEAD)
        if at in (1, 3):
            a = at // 2
            carry[a].wait()
            store(bounce[a], carried_out[a], carry_sem.at[2 + a])
            if a == 0:
                carry[1].start()
    for copy in copies:
        copy.wait()


AHEAD = 3


def update(sq, carried, weights):
    cuts = [[c for c in range(g[0].shape[0])] if g[0].ndim == 3 else [slice(None)] for g in weights]
    pieces = sum(len(c) for c in cuts)
    anywhere = pl.BlockSpec(memory_space=pl.ANY)
    vmem = pl.BlockSpec(memory_space=pltpu.VMEM)
    flat_in = [a for group in weights for a in group]
    flat_out = [a for group in weights for a in group[:3]]
    dma = pltpu.SemaphoreType.DMA
    size = sum(a.size * a.dtype.itemsize for a in flat_in + flat_out + 2 * list(carried))
    return pl.pallas_call(
        partial(update_body, cuts),
        out_shape=[jax.ShapeDtypeStruct((1, 1), F32)] + [jax.ShapeDtypeStruct(a.shape, a.dtype) for a in [*carried, *flat_out]],
        in_specs=[vmem] + [anywhere] * (2 + len(flat_in)),
        out_specs=[pl.BlockSpec(memory_space=pltpu.SMEM)] + [anywhere] * (2 + len(flat_out)),
        scratch_shapes=[pltpu.VMEM(a.shape, a.dtype) for a in flat_in + flat_out + list(carried)]
        + [dma((pieces, 4)), dma((pieces, 3)), dma((4,))],
        cost_estimate=pl.CostEstimate(flops=size, bytes_accessed=size, transcendentals=0),
        compiler_params=pltpu.CompilerParams(vmem_limit_bytes=VMEM_LIMIT),
    )(sq, *carried, *flat_in)


def turn_tables(tokens):
    theta = np.float32(10000.0) ** (-np.arange(HEAD, dtype=np.float32) / np.float32(HEAD))
    angle = np.arange(tokens, dtype=np.float32)[:, None] * theta.astype(np.float32)[None, :]
    angle = angle.astype(np.float64)
    return np.cos(angle).astype(np.float32), np.sin(angle).astype(np.float32)


def per_device(mesh, block_input, segment_ids, live_length, output_grad, mixer_weight, mixer_momentum, mixer_shadow,
               expand_weight, expand_momentum, expand_shadow, shrink_weight, shrink_momentum, shrink_shadow):
    rows, length, width = block_input.shape
    p = plan_of(mesh, length, width, shrink_weight.shape[0])
    turn = (lambda v: jnp.swapaxes(v, -1, -2)) if p.FD else (lambda v: v)
    if p.FD:
        shards = (turn(expand_weight), shrink_weight)
    else:
        shards = (jnp.concatenate([shrink_weight.T[None], expand_weight], axis=0).astype(BF), shrink_weight)
    cos, sin = turn_tables(length)
    out, grad_in, gm, ge, gs, sq = fused(
        p, block_input[0], output_grad[0], segment_ids, live_length, jnp.asarray(cos), jnp.asarray(sin), mixer_weight, *shards
    )
    new = update(sq, (out, grad_in), (
        (mixer_weight, mixer_momentum, mixer_shadow, gm),
        (turn(expand_weight), turn(expand_momentum), turn(expand_shadow), ge),
        (shrink_weight, shrink_momentum, shrink_shadow, gs if p.FD else gs.T),
    ))
    norm, out, grad_in = new[:3]
    return (out[None], grad_in[None], norm[0, 0], *new[3:6], *(turn(v) for v in new[6:9]), *new[9:12])


def solution(mesh):
    row, mixer, expand, shrink = P("dp", None, None), P(None, "dp", None), P(None, "dp", "mp"), P("mp", "dp")
    return jax.shard_map(
        partial(per_device, mesh),
        mesh=mesh,
        in_specs=(row, P("dp", None), P("dp"), row) + (mixer,) * 3 + (expand,) * 3 + (shrink,) * 3,
        out_specs=(row, row, P()) + (mixer,) * 3 + (expand,) * 3 + (shrink,) * 3,
        check_vma=False,
    )
```

```python
from functools import partial
from types import SimpleNamespace

import jax
import jax.numpy as jnp
import numpy as np
from jax import lax
from jax.experimental import pallas as pl
from jax.experimental.pallas import tpu as pltpu
from jax.sharding import PartitionSpec as P

HEAD = 128
EPSILON = 1e-06
LEARN_RATE = 32.0
MOMENTUM = 0.5
SHADOW_DECAY = 0.5
LAYER_PLACE = 12.0 / 24.0
LONGEST = 512
FF_ORDER = (1, 2, 0)
Y_FIRST = (4, 6)
Z_FIRST = (9, 4)
STRAIGHT = (2, 0, 1)
MESH = pl.DeviceIdType.MESH
BF = jnp.bfloat16
F32 = jnp.float32


def dot_nn(a, b):
    return lax.dot_general(a, b, (((1,), (0,)), ((), ())), preferred_element_type=F32)


def dot_nt(a, b):
    return lax.dot_general(a, b, (((1,), (1,)), ((), ())), preferred_element_type=F32)


def dot_tn(a, b):
    return lax.dot_general(a, b, (((0,), (0,)), ((), ())), preferred_element_type=F32)


def rows_of(index, size):
    return pl.ds(pl.multiple_of(index * size, size), size)


def each(count, body):
    def step(t, carry):
        body(t)
        return carry

    lax.fori_loop(0, count, step, 0)


def widen(column, width):
    return jnp.concatenate([column] * (width // 128), axis=1)


def plan_of(mesh, tokens, width, inner):
    n, mp = mesh.shape["dp"], mesh.shape["mp"]
    lo, core = 2, 2
    return SimpleNamespace(
        n=n, mp=mp, LO=lo, HI=n // lo, X=mp // core, T=tokens, D=width, C=width // mp, F=inner,
        S=width // n, H=width // mp // HEAD, TB=tokens // mp, B=min(256, tokens),
        N=n * mp if n * mp <= 32 else 1, NT=tokens // mp // 128, FD=(width // n) % 128 == 0,
    )


def scratch_of(p):
    T, D, C, F, S, HI, LO, X, TB, B = p.T, p.D, p.C, p.F, p.S, p.HI, p.LO, p.X, p.TB, p.B
    dma = pltpu.SemaphoreType.DMA
    v = pltpu.VMEM
    return dict(
        mixw=v((4, D, C), BF), wo=v((D, D), BF), ffw=v((3, F, D) if p.FD else (3, D, F), BF),
        xown=v((TB, D), BF), nin=v((T, D), BF), nint=v((D, T), BF), up=v((T, D), BF),
        cosv=v((T, HEAD), F32), sinv=v((T, HEAD), F32),
        segq=v((T, 128), F32), segk=v((8, T), F32), dec=v((2, p.H, B, B), F32),
        qpre=v((T, C), F32), kpre=v((T, C), F32), gpre=v((T, C), F32), val=v((T, C), BF),
        qrot=v((T, 2 * C), BF), krot=v((T, 2 * C), BF), mixed=v((T, C), F32),
        ufull=v((T, D), BF), ss=v((p.mp, 8, T), F32), rcol=v((T, 128), F32),
        inn=v((p.mp, 8, TB), F32), hown=v((TB, D), F32),
        gact=v((T, max(F, 2 * C + HEAD)), F32), uact=v((T, F), BF), prod=v((T, F), BF), ggate=v((T, F), BF), gup=v((T, F), BF),
        part=v((X, 2, TB, D), BF), recc=v((2, X, TB, D), BF), recx=v((2, X - 1, TB, D), BF),
        xv=v((T, D), BF),
        gm=v((5, HI, LO, S, C), BF), rym=v((5, HI, S, C), BF), rzm=v((5, HI - 1, S, C), BF),
        gf=v((3, LO, F, HI * S) if p.FD else (3, HI, LO, S, F), BF),
        ryf=v((3, F, HI * S) if p.FD else (3, HI, S, F), BF),
        rzf=v((3, HI - 1, F, S) if p.FD else (3, HI - 1, S, F), BF),
        relm=v((2, S, C), BF), relf=v((3, F, S) if p.FD else (3, S, F), BF),
        othm=v((HI, S, C), BF), othf=v((HI, F // 2, S) if p.FD else (HI, S // 2, F), BF),
        sqs=v((8, 128), F32), sall=v((p.N, 8, 128), F32), s1=v((p.mp if p.N == 1 else 1, 8, 128), F32), s2=v((p.n if p.N == 1 else 1, 8, 128), F32),
        loc=dma((10,)),
        zs=dma((11, HI - 1)), zr=dma((11, HI - 1)), us=dma((len(Y_FIRST), HI - 1)), ur=dma((len(Y_FIRST), HI - 1)),
        zp=dma((11,)), yp=dma((len(Y_FIRST),)), ys=dma((11, HI)), yr=dma((11, HI)),
        xs=dma((20, X - 1)), xr=dma((20, X - 1)), cs=dma((20, X)), cr=dma((20, X)),
        acs=dma((3, X)), acr=dma((3, X)), axs=dma((3, X - 1, p.NT)), axr=dma((3, X - 1, p.NT)),
        bys=dma((11,)), byr=dma((11,)), bzs=dma((11, HI - 1)), bzr=dma((11, HI - 1)),
        bts=dma((11,)), btr=dma((11,)), ozs=dma((2, HI - 1)), ozr=dma((2, HI - 1)), ots=dma((2,)), otr=dma((2,)),
        ags=dma((p.NT, p.mp)), agr=dma((p.NT, p.mp)), ahs=dma((2, p.mp)), ahr=dma((2, p.mp)),
        gms=dma((5, p.mp)), gmr=dma((5, p.mp)), qs=dma((p.N,)), qr=dma((p.N,)),
        q1s=dma((p.mp,)), q1r=dma((p.mp,)), q2s=dma((p.n,)), q2r=dma((p.n,)),
    )


IN_NAMES = ("x", "og", "seg", "live", "cos", "sin", "mixsh", "exsh", "shsh")
OUT_NAMES = ("bo", "ig", "gmo", "geo", "gso", "sqo")


def body(p, names, *refs):
    r = SimpleNamespace(**dict(zip(names, refs)))
    n, mp, LO, HI, X, T, D, C, F, S, H, TB, B = (
        p.n, p.mp, p.LO, p.HI, p.X, p.T, p.D, p.C, p.F, p.S, p.H, p.TB, p.B,
    )
    NT, TT = p.NT, min(512, p.T)
    i, j = lax.axis_index("dp"), lax.axis_index("mp")
    zi, yi = i // LO, lax.rem(i, LO)
    xi, ci = j // 2, lax.rem(j, 2)
    jcols = pl.ds(pl.multiple_of(j * C, C), C)
    pending = []
    r.nmid = r.nin
    r.bov, r.igv, r.gmv = r.up, r.ufull, r.wo
    r.dk, r.icol, r.dv = r.gact.at[:, 0:2 * C], r.gact.at[:, 2 * C:2 * C + HEAD], r.mixed
    r.gproj = [r.ggate.at[:, 0:C], r.ggate.at[:, C:2 * C], r.gup.at[:, 0:C], r.gup.at[:, C:2 * C]]
    r.ggated, r.hcols, r.gmix, r.rh = [r.xv.at[:, a * C:(a + 1) * C] for a in range(4)]
    r.hsend, r.gsend = r.uact.at[:, 0:C], r.uact.at[:, C:2 * C]

    def go(src, dst, ssem, rsem, when=None, **device):
        copy = pltpu.make_async_remote_copy(
            src_ref=src, dst_ref=dst, send_sem=ssem, recv_sem=rsem,
            device_id=device, device_id_type=MESH,
        )
        guarded(when, copy.start)
        pending.append((copy, when))
        return copy

    def guarded(when, act):
        if when is None:
            act()
        else:
            pl.when(when)(lambda: act())

    def arrived(dst, sem):
        pltpu.make_async_copy(dst, dst, sem).wait()

    def settle(copy):
        for other, when in pending:
            if other is copy:
                guarded(when, copy.wait_send)
        pending[:] = [entry for entry in pending if entry[0] is not copy]

    def load(src, dst, sem):
        copy = pltpu.make_async_copy(src, dst, r.loc.at[sem])
        copy.start()
        return copy

    own_mix = [load(r.mixsh.at[k, :, jcols], r.qpre.at[k * S:(k + 1) * S], k) for k in range(5)]
    if p.FD:
        stage = [r.gact.at[0:F, m * S:(m + 1) * S] for m in range(3)]
        own_ff = [load(r.shsh if m == 0 else r.exsh.at[m - 1], stage[m], 5 + m) for m in range(3)]
    else:
        own_ff = [load(r.exsh.at[m], r.ffw.at[m, rows_of(i, S)], 5 + m) for m in range(3)]
    load_x = load(r.x, r.xv, 8)
    load_og = load(r.og, r.up, 9)

    def enter():
        barrier = pltpu.get_barrier_semaphore()
        if p.N > 1:
            others = [whole(d) for d in range(1, p.N)]
        else:
            others = [{"dp": lax.rem(i + d, n)} for d in range(1, n)] + [{"mp": lax.rem(j + d, mp)} for d in range(1, mp)]
        for other in others:
            pl.semaphore_signal(barrier, inc=1, device_id=other, device_id_type=MESH)
        pl.semaphore_wait(barrier, len(others))

    def whole(d):
        at = lax.rem(i * mp + j + d, p.N)
        return {"dp": at // mp, "mp": lax.rem(at, mp)}

    def slot(k, device):
        rows = rows_of(device, S)
        if k == 4:
            return r.wo.at[rows, jcols]
        if k < 4:
            return r.mixw.at[k, rows]
        m, half = FF_ORDER[(k - 5) // 2], (k - 5) % 2
        if p.FD:
            return r.ffw.at[m, half * F // 2:(half + 1) * F // 2, rows]
        return r.ffw.at[m, pl.ds(pl.multiple_of(device * S + half * S // 2, S // 2), S // 2)]

    def gather_ready(k):
        if k < 5:
            own_mix[k].wait()
            slot(k, i)[...] = r.qpre[k * S:(k + 1) * S, :].astype(BF)
        else:
            m, half = FF_ORDER[(k - 5) // 2], (k - 5) % 2
            if half == 0:
                own_ff[m].wait()
            if p.FD:
                slot(k, i)[...] = stage[m][half * F // 2:(half + 1) * F // 2, :].astype(BF)

    relays = HI == 4
    next_to_end = (zi == 1) | (zi == 2)

    def along_z(block, ssem, rsem):
        for d in range(1, HI):
            to = lax.rem(zi + d, HI)
            near = (jnp.abs(to - zi) < 3) if relays else None
            go(block, block, ssem.at[d - 1], rsem.at[d - 1], when=near, dp=to * LO + yi)

    def hand_on(block, ssem, rsem):
        if relays:
            end = jnp.where(zi == 2, 3, 0)
            go(block, block, ssem, rsem.at[jnp.where(zi == 2, 2, 0)], when=next_to_end, dp=end * LO + yi)

    def from_z_source(k, d, y):
        return slot(k, lax.rem(zi - d + HI, HI) * LO + y)

    WAYS = [2, 1, *range(3, HI)]

    def gather_send(k):
        src = slot(k, i)
        along_z(src, r.zs.at[k], r.zr.at[k])
        go(src, src, r.ys.at[k, 0], r.yr.at[k, 0], dp=zi * LO + 1 - yi)

    def gather_forward(k):
        if k - 1 in Y_FIRST:
            b = Y_FIRST.index(k - 1)
            block = from_z_source(k - 1, 2, 1 - yi)
            arrived(block, r.ur.at[b, 1])
            hand_on(block, r.yp.at[b], r.ur.at[b])
        if k in Y_FIRST:
            b = Y_FIRST.index(k)
            peers = slot(k, zi * LO + 1 - yi)
            arrived(peers, r.yr.at[k, 0])
            along_z(peers, r.us.at[b], r.ur.at[b])
        for d in WAYS:
            block = from_z_source(k, d, yi)
            arrived(block, r.zr.at[k, d - 1])
            if d == 2:
                hand_on(block, r.zp.at[k], r.zr.at[k])
            if k not in Y_FIRST:
                go(block, block, r.ys.at[k, d], r.yr.at[k, d], dp=zi * LO + 1 - yi)

    def gather_wait(k):
        for d in range(HI):
            if k not in Y_FIRST:
                arrived(from_z_source(k, d, 1 - yi), r.yr.at[k, d])
            elif d in (1, 3) or d > 3:
                arrived(from_z_source(k, d, 1 - yi), r.ur.at[Y_FIRST.index(k), d - 1])

    def share_send(s, block, src=None):
        own = block(j)
        src = own if src is None else src
        for d in range(1, X):
            go(src, own, r.xs.at[s, d - 1], r.xr.at[s, d - 1], mp=lax.rem(xi + d, X) * 2 + ci)
        go(src, own, r.cs.at[s, 0], r.cr.at[s, 0], mp=xi * 2 + 1 - ci)

    def share_forward(s, block):
        for d in range(1, X):
            part = block(lax.rem(xi - d + X, X) * 2 + ci)
            arrived(part, r.xr.at[s, d - 1])
            go(part, part, r.cs.at[s, d], r.cr.at[s, d], mp=xi * 2 + 1 - ci)

    def share_wait(s, block):
        for d in range(X):
            arrived(block(lax.rem(xi - d + X, X) * 2 + 1 - ci), r.cr.at[s, d])

    def sum_begin(s, b, compute, between):
        sent = []

        def pair(d):
            to = lax.rem(xi + d, X)
            compute(to)
            sent.append(go(
                r.part.at[to, 1 - ci], r.recc.at[b, to], r.acs.at[s, d], r.acr.at[s, d], mp=xi * 2 + 1 - ci
            ))

        for d in range(1, X):
            pair(d)
        between()
        for d in range(1, X):
            to = lax.rem(xi + d, X)
            arrived(r.recc.at[b, to], r.acr.at[s, d])
            for t in range(NT):
                q = slice(t * 128, (t + 1) * 128)
                r.part[to, ci, q] = (
                    r.part[to, ci, q].astype(F32) + r.recc[b, to, q].astype(F32)
                ).astype(BF)
                sent.append(go(
                    r.part.at[to, ci, q], r.recx.at[b, d - 1, q], r.axs.at[s, d - 1, t], r.axr.at[s, d - 1, t],
                    mp=to * 2 + ci,
                ))
        pair(0)
        return sent

    def sum_arrived(s, b, t):
        if t == 0:
            arrived(r.recc.at[b, xi], r.acr.at[s, 0])
        for d in range(1, X):
            arrived(r.recx.at[b, d - 1, t * 128:(t + 1) * 128], r.axr.at[s, d - 1, t])

    def sum_tile(b, q):
        total = r.part[xi, ci, q].astype(F32) + r.recc[b, xi, q].astype(F32)
        for d in range(1, X):
            total = total + r.recx[b, d - 1, q].astype(F32)
        return total

    flat = p.FD

    def half_of(k):
        size = (F if flat else S) // 2
        return (k - 5) // 2, slice((k - 5) % 2 * size, ((k - 5) % 2 + 1) * size)

    def block_of(k, z, y):
        if k < 5:
            return r.gm.at[k, z, y]
        m, rows = half_of(k)
        return r.gf.at[m, y, rows, rows_of(z, S)] if flat else r.gf.at[m, z, y, rows]

    def from_y(k):
        if k < 5:
            return r.rym.at[k]
        m, rows = half_of(k)
        return r.ryf.at[m, rows] if flat else r.ryf.at[m, :, rows]

    def from_y_block(k, z):
        ref = from_y(k)
        return ref.at[:, rows_of(z, S)] if flat and k >= 5 else ref.at[z]

    def to_y(k):
        if k < 5:
            return r.gm.at[k, :, 1 - yi]
        m, rows = half_of(k)
        return r.gf.at[m, 1 - yi, rows] if flat else r.gf.at[m, :, 1 - yi, rows]

    def from_z(k, d, own=True):
        if not own:
            return (r.othm if k < 5 else r.othf).at[d - 1]
        if k < 5:
            return r.rzm.at[k, d - 1]
        m, rows = half_of(k)
        return r.rzf.at[m, d - 1, rows]

    def handed(k, own=True):
        if not own:
            return (r.othm if k < 5 else r.othf).at[HI - 1]
        if k < 5:
            return r.relm.at[max(k - 3, 0)]
        m, rows = half_of(k)
        return r.relf.at[m, rows]

    def z_sems(k, own):
        if own:
            return r.bzs.at[k], r.bzr.at[k], r.bts.at[k], r.btr.at[k]
        o = Z_FIRST.index(k)
        return r.ozs.at[o], r.ozr.at[o], r.ots.at[o], r.otr.at[o]

    def stepped(k):
        return relays and k not in STRAIGHT

    def far(d, back=False):
        other = lax.rem(zi + (HI - d if back else d), HI)
        return jnp.abs(other - zi) == 3

    def z_send(k, own, ways):
        y = yi if own else 1 - yi
        ssem, rsem, tsem, trsem = z_sems(k, own)
        for d in ways:
            to = lax.rem(zi + d, HI)
            block, dst = block_of(k, to, y), from_z(k, d, own)
            if stepped(k) and d != 2:
                go(block, handed(k, own), tsem, trsem, when=far(d), dp=jnp.where(zi == 0, 1, 2) * LO + yi)
                go(block, dst, ssem.at[d - 1], rsem.at[d - 1], when=jnp.logical_not(far(d)), dp=to * LO + yi)
            else:
                go(block, dst, ssem.at[d - 1], rsem.at[d - 1], dp=to * LO + yi)

    def z_send_handed(k, own):
        block = block_of(k, lax.rem(zi + 2, HI), yi if own else 1 - yi)

        @pl.when(next_to_end)
        def _():
            arrived(handed(k, own), z_sems(k, own)[3])
            block[...] = (block[...].astype(F32) + handed(k, own)[...].astype(F32)).astype(BF)

        z_send(k, own, [2])

    def z_total(k, own):
        for d in range(1, HI):
            wait = partial(arrived, from_z(k, d, own), z_sems(k, own)[1].at[d - 1])
            guarded(jnp.logical_not(far(d, back=True)) if stepped(k) and d != 2 else None, wait)
        total = block_of(k, zi, yi if own else 1 - yi)[...].astype(F32)
        for d in range(1, HI):
            total = total + from_z(k, d, own)[...].astype(F32)
        return total

    def clear_far_places():
        if not relays:
            return
        for d in (1, 3):
            @pl.when(far(d, back=True))
            def _(d=d):
                r.rzm[:, d - 1] = jnp.zeros((5, S, C), BF)
                for m in range(3):
                    r.rzf[m, d - 1] = jnp.zeros(r.rzf.shape[2:], BF)
                r.othm[d - 1] = jnp.zeros(r.othm.shape[1:], BF)
                r.othf[d - 1] = jnp.zeros(r.othf.shape[1:], BF)

    def near_ways(k):
        return [3, 1] if stepped(k) else list(range(1, HI))

    def scatter_first(*pieces):
        for k in pieces:
            if k in Z_FIRST:
                for own in (False, True):
                    z_send(k, own, near_ways(k))
            else:
                go(to_y(k), from_y(k), r.bys.at[k], r.byr.at[k], dp=zi * LO + 1 - yi)

    def scatter_second(*pieces):
        for k in pieces:
            if k in Z_FIRST:
                block = block_of(k, zi, 1 - yi)
                block[...] = z_total(k, False).astype(BF)
                go(block, from_y_block(k, zi), r.bys.at[k], r.byr.at[k], dp=zi * LO + 1 - yi)
                continue
            arrived(from_y(k), r.byr.at[k])
            for d in range(1, HI):
                to = lax.rem(zi + d, HI)
                block = block_of(k, to, yi)
                block[...] = (block[...].astype(F32) + from_y_block(k, to)[...].astype(F32)).astype(BF)
            z_send(k, True, near_ways(k))

    def scatter_handed(*pieces):
        for k in pieces:
            if stepped(k):
                if k in Z_FIRST:
                    z_send_handed(k, False)
                z_send_handed(k, True)

    def scatter_total(k):
        if k in Z_FIRST:
            arrived(from_y_block(k, zi), r.byr.at[k])
        return z_total(k, True) + from_y_block(k, zi)[...].astype(F32)

    def squares_of(total):
        squared = total * total
        if squared.shape[-1] % 128:
            corner = (lax.broadcasted_iota(jnp.int32, (8, 128), 0) + lax.broadcasted_iota(jnp.int32, (8, 128), 1)) == 0
            return jnp.where(corner, jnp.sum(squared), 0.0)
        folded = jnp.sum(squared.reshape(-1, 8, squared.shape[-1]), axis=0)
        return sum(folded[:, c:c + 128] for c in range(0, folded.shape[-1], 128))

    def finish_ff(*pieces):
        for k in pieces:
            m, rows = half_of(k)
            total = scatter_total(k)
            if m == 0:
                r.gso[rows] = total
            else:
                r.geo[m - 1, rows] = total
            r.sqs[...] += squares_of(total)

    def put_grad(k, lhs, rhs, turned=False):
        g = r.gm.at[k] if k < 5 else r.gf.at[k - 5]
        per = TT // (LO * S)

        def tile(t):
            if turned:
                out = dot_nn(lhs[rows_of(t, TT), :], rhs[...])
            else:
                out = dot_tn(lhs[:, rows_of(t, TT)], rhs[...])
            g[pl.ds(t * per, per)] = out.astype(BF).reshape(per, LO, S, out.shape[-1])

        each(D // TT, tile)

    def put_ff_grad(m, units, model):
        if not flat:
            return put_grad(5 + m, model, units)
        for f in range(0, F, 384):
            q = slice(f, min(f + 384, F))
            out = dot_tn(units[:, q], model[...]).astype(BF)
            for y in range(LO):
                for z in range(HI):
                    r.gf[m, y, q, z * S:(z + 1) * S] = out[:, (z * LO + y) * S:(z * LO + y + 1) * S]

    def to_units(a, m):
        return dot_nt(a, r.ffw[m]) if flat else dot_nn(a, r.ffw[m])

    def to_model(a, m):
        return dot_nn(a, r.ffw[m]) if flat else dot_nt(a, r.ffw[m])

    gather_ready(0)
    gather_ready(1)
    enter()
    gather_send(0)
    gather_send(1)
    gather_ready(2)
    gather_send(2)
    r.sqs[...] = jnp.zeros_like(r.sqs)
    clear_far_places()

    length = r.live[0]
    load_x.wait()

    def norm_tile(t):
        q = rows_of(t, 128)
        v = r.xv[q, :].astype(F32)
        r.nin[q, :] = (v * lax.rsqrt(jnp.mean(v * v, axis=-1, keepdims=True) + EPSILON)).astype(BF)

    each(T // 128, norm_tile)
    for k in range(3, 11):
        gather_ready(k)
    load_x_own = load(r.x.at[rows_of(j, TB)], r.xown, 8)
    load_og.wait()
    load_cos = load(r.cos, r.cosv, 0)
    load_sin = load(r.sin, r.sinv, 1)

    def live_tile(t):
        q = rows_of(t, 128)
        place = lax.broadcasted_iota(jnp.int32, (128, D), 0) + t * 128
        r.up[q, :] = jnp.where(place < length, r.up[q, :].astype(F32), 0.0).astype(BF)

    each(T // 128, live_tile)

    place = lax.broadcasted_iota(jnp.int32, (1, T), 1)
    segment = r.seg[...].astype(F32)
    r.segk[...] = jnp.broadcast_to(jnp.where(place < length, segment, -2.0), (8, T))
    seg_q = jnp.where(place < length, segment, -1.0)
    for t in range(T // 128):
        q = slice(t * 128, t * 128 + 128)
        r.segq[q, :] = jnp.transpose(jnp.broadcast_to(seg_q[:, q], (128, 128)))

    down = lax.broadcasted_iota(jnp.int32, (B, B), 0)
    over = lax.broadcasted_iota(jnp.int32, (B, B), 1)
    heads = D // HEAD

    def rate_of(h):
        return -(8.0 * (j * H + h).astype(F32) / heads) * (1.0 - LAYER_PLACE)

    for h in range(H):
        rate = rate_of(h)
        for o in range(2):
            distance = down - over + o * B
            fade = jnp.exp(rate * jnp.maximum(distance, 0).astype(F32))
            r.dec[o, h] = jnp.where(distance >= 0, fade, 0.0)

    for t in range(D // 128):
        q = slice(t * 128, t * 128 + 128)
        r.nint[q, :] = jnp.transpose(r.nin[:, q])
    load_cos.wait()
    load_sin.wait()
    load_x_own.wait()

    def turn_into(pre_ref, rot_ref, k):
        def tile(t):
            q = rows_of(t, TT)
            pre = dot_nn(r.nin[q, :], r.mixw[k])
            pre_ref[q, :] = pre
            act = pre * jax.nn.sigmoid(pre)
            c, s = r.cosv[q, :], r.sinv[q, :]
            for h in range(H):
                a = act[:, h * HEAD:(h + 1) * HEAD]
                rot_ref[q, 2 * h * HEAD:(2 * h + 1) * HEAD] = (a * c).astype(BF)
                rot_ref[q, (2 * h + 1) * HEAD:(2 * h + 2) * HEAD] = (a * s).astype(BF)

        each(T // TT, tile)

    def project_into(ref, k):
        def tile(t):
            q = rows_of(t, TT)
            ref[q, :] = dot_nn(r.nin[q, :], r.mixw[k]).astype(ref.dtype)

        each(T // TT, tile)

    gather_forward(0)
    gather_send(3)
    gather_forward(1)
    gather_send(4)
    gather_wait(0)
    turn_into(r.qpre, r.qrot, 0)
    gather_forward(2)
    gather_send(5)
    gather_wait(1)
    turn_into(r.kpre, r.krot, 1)
    gather_forward(3)
    gather_send(6)
    gather_wait(2)
    project_into(r.val, 2)
    gather_forward(4)
    gather_send(7)
    gather_wait(3)
    project_into(r.gpre, 3)

    def wo_block(owner):
        return r.wo.at[:, pl.ds(pl.multiple_of(owner * C, C), C)]


    NB = T // B
    REACH = LONGEST // B

    def keys_of(qb):
        return slice(max(0, qb - REACH) * B, (qb + 1) * B)

    def weights_of(qb, h):
        key = keys_of(qb)
        width = key.stop - key.start
        fades = [r.dec[min(o, 1), h] for o in range(width // B - 1, -1, -1)]
        for o in range(2, width // B):
            fades[width // B - 1 - o] *= jnp.exp(rate_of(h) * ((o - 1) * B))
        seen = jnp.broadcast_to(r.segk[0:1, key], (B, width))
        same = widen(r.segq[qb * B:(qb + 1) * B, :], width) == seen
        return jnp.where(same, jnp.concatenate(fades, axis=1), 0.0)

    def u_block(qb):
        return lambda owner: r.ufull.at[qb * B:(qb + 1) * B, pl.ds(pl.multiple_of(owner * C, C), C)]

    def attend(qb):
        q = slice(qb * B, (qb + 1) * B)
        squares = jnp.zeros((B, 1), F32)
        for h in range(H):
            rot = slice(2 * h * HEAD, 2 * (h + 1) * HEAD)
            chan = slice(h * HEAD, (h + 1) * HEAD)
            key = keys_of(qb)
            scores = dot_nt(r.qrot[q, rot], r.krot[key, rot]) * weights_of(qb, h)
            total = dot_nn(scores.astype(BF), r.val[key, chan])
            r.mixed[q, chan] = total
            squares = squares + jnp.sum(total * total, axis=-1, keepdims=True)
            r.ufull[q, pl.ds(pl.multiple_of(j * C + h * HEAD, HEAD), HEAD)] = (
                total * r.gpre[q, chan]
            ).astype(BF)
        r.ss[j, :, q] = jnp.transpose(jnp.broadcast_to(squares, (B, 128)))[0:8, :]

    def ss_block(owner):
        return r.ss.at[owner]

    for qb in range(NB):
        attend(qb)
        share_send(1 + qb, u_block(qb))
        if qb == NB - 1:
            share_send(1 + NB, ss_block)
        if qb == 0:
            gather_forward(5)
            gather_send(8)
        if qb == 1:
            gather_wait(4)
            share_send(0, wo_block)
        if qb == 3:
            share_forward(0, wo_block)
        if qb == 2:
            gather_forward(6)
            gather_send(9)
        if qb > 0:
            share_forward(qb, u_block(qb - 1))
    share_forward(NB, u_block(NB - 1))
    share_forward(1 + NB, ss_block)
    gather_forward(7)
    gather_send(10)
    gather_forward(8)
    share_wait(0, wo_block)
    for qb in range(NB):
        share_wait(1 + qb, u_block(qb))
    share_wait(1 + NB, ss_block)
    early = [copy for copy, when in pending]

    total_ss = r.ss[0]
    for owner in range(1, mp):
        total_ss = total_ss + r.ss[owner]
    inverse = lax.rsqrt(total_ss * (1.0 / D) + EPSILON)
    for t in range(T // 128):
        q = slice(t * 128, t * 128 + 128)
        r.rcol[q, :] = jnp.transpose(jnp.broadcast_to(inverse[0:1, q], (128, 128)))

    def hidden_tile(t):
        q = rows_of(t, TB)
        out = widen(r.rcol[q, :], D) * dot_nn(r.ufull[q, :], r.wo[...])
        hidden = r.xv[q, :].astype(F32) + out
        scale = lax.rsqrt(jnp.mean(hidden * hidden, axis=-1, keepdims=True) + EPSILON)
        r.nmid[q, :] = (hidden * scale).astype(BF)

        @pl.when(t == j)
        def _():
            r.hown[...] = hidden

    each(T // TB, hidden_tile)
    gather_wait(5)
    gather_wait(6)

    def gate_tile(t):
        q = rows_of(t, TT)
        r.gact[q, 0:F] = to_units(r.nmid[q, :], 1)

    each(T // TT, gate_tile)
    gather_forward(9)
    gather_wait(7)
    gather_wait(8)

    def up_tile(t):
        q = rows_of(t, TT)
        upper = to_units(r.nmid[q, :], 2)
        r.uact[q, :] = upper.astype(BF)
        r.prod[q, :] = (r.gact[q, 0:F] * upper).astype(BF)

    each(T // TT, up_tile)
    put_ff_grad(0, r.prod, r.up)
    gather_forward(10)
    scatter_first(5, 6)
    gather_wait(9)
    gather_wait(10)

    def mid_pair(x):
        q = rows_of(x, 2 * TB)
        g = to_units(r.up[q, :], 0)
        grad_gate, grad_up = (g * r.uact[q, :].astype(F32)).astype(BF), (g * r.gact[q, 0:F]).astype(BF)
        r.ggate[q, :] = grad_gate
        r.gup[q, :] = grad_up
        r.part[x] = (to_model(grad_gate, 1) + to_model(grad_up, 2)).astype(BF).reshape(2, TB, D)

    used = sum_begin(0, 0, mid_pair, partial(scatter_second, 5))
    put_ff_grad(1, r.ggate, r.nmid)
    scatter_first(7, 8)
    scatter_handed(5)
    scatter_second(6)

    def back_tile(t):
        q = slice(t * 128, (t + 1) * 128)
        here = rows_of(j * (TB // 128) + t, 128)
        grad = sum_tile(0, q)
        hidden = r.hown[q, :]
        scale = lax.rsqrt(jnp.mean(hidden * hidden, axis=-1, keepdims=True) + EPSILON)
        normed = hidden * scale
        inner = jnp.mean(grad * normed, axis=-1, keepdims=True)
        out = r.up[here, :].astype(F32) + scale * (grad - normed * inner)
        low = out.astype(BF)
        for owner in range(mp):
            r.hsend[owner * TB + t * 128:owner * TB + (t + 1) * 128, :] = low[:, owner * C:(owner + 1) * C]
        mixer_out = hidden - r.xown[q, :].astype(F32)
        product = jnp.sum(low.astype(F32) * mixer_out, axis=-1, keepdims=True) * (1.0 / D)
        r.inn[j, :, q] = jnp.transpose(jnp.broadcast_to(product, (128, 128)))[0:8, :]

    def token_block(ref):
        return lambda owner: ref.at[rows_of(owner, TB)]

    BO, GM, IG = 2 + NB, 3 + NB, 8 + NB

    def half_block(ref, t):
        return lambda owner: ref.at[rows_of(owner * NT + t, 128)]

    def peers():
        return [(d, lax.rem(j + d, mp), lax.rem(j - d + mp, mp)) for d in range(1, mp)]

    for t in range(NT):
        sum_arrived(0, 0, t)
        back_tile(t)
    low = jnp.concatenate([r.hsend[owner * TB:(owner + 1) * TB, :] for owner in range(mp)], axis=1)
    grad_gated = dot_nt(low, r.wo[...]).astype(BF)
    for owner in range(mp):
        r.gsend[owner * TB:(owner + 1) * TB, :] = grad_gated[:, owner * C:(owner + 1) * C]
    for d, to, source in peers():
        go(token_block(r.gsend)(to), token_block(r.ggated)(j), r.ags.at[0, d], r.agr.at[0, d], mp=to)
    own_rows = rows_of(j, TB)
    r.ggated[own_rows, :] = r.gsend[own_rows, :]
    r.hcols[own_rows, :] = r.hsend[own_rows, :]
    for d, to, source in peers():
        go(r.inn.at[j], r.inn.at[j], r.ahs.at[0, d], r.ahr.at[0, d], mp=to)
    for d, to, source in peers():
        go(token_block(r.hsend)(to), token_block(r.hcols)(j), r.ahs.at[1, d], r.ahr.at[1, d], mp=to)
    put_ff_grad(2, r.gup, r.nmid)
    scatter_first(9, 10)
    scatter_handed(6)
    scatter_second(7)
    for copy in used:
        settle(copy)

    def expand_tile(t):
        r.part[t // 2, lax.rem(t, 2)] = to_model(r.prod[rows_of(t, TB), :], 0).astype(BF)

    each(mp, expand_tile)
    used = [
        go(r.part.at[to, 1 - ci], r.recc.at[1, to], r.acs.at[1, d], r.acr.at[1, d], mp=xi * 2 + 1 - ci)
        for d, to in [(d, lax.rem(xi + d, X)) for d in range(X)]
    ]
    for d, to, source in peers():
        arrived(token_block(r.ggated)(source), r.agr.at[0, d])
        arrived(r.inn.at[source], r.ahr.at[0, d])
    for owner in range(mp):
        for t in range(TB // 128):
            row = r.inn[owner, 0:1, t * 128:(t + 1) * 128]
            q = slice(owner * TB + t * 128, owner * TB + (t + 1) * 128)
            r.icol[q, :] = jnp.transpose(jnp.broadcast_to(row, (128, 128)))

    def gated_tile(t):
        q = rows_of(t, TT)
        grad = r.ggated[q, :].astype(F32)
        inner = widen(r.icol[q, :], C)
        inverse = widen(r.rcol[q, :], C)
        normed = r.mixed[q, :] * inverse
        r.gproj[3][q, :] = (grad * normed).astype(BF)
        r.gmix[q, :] = (inverse * (grad * r.gpre[q, :] - normed * inner)).astype(BF)

    each(T // TT, gated_tile)

    for d in [*range(1, X), 0]:
        to = lax.rem(xi + d, X)
        arrived(r.recc.at[1, to], r.acr.at[1, d])
        for t in range(NT):
            q = slice(t * 128, (t + 1) * 128)
            r.recc[1, to, q] = (r.part[to, ci, q].astype(F32) + r.recc[1, to, q].astype(F32)).astype(BF)
            if d:
                go(r.recc.at[1, to, q], r.recx.at[1, d - 1, q], r.axs.at[1, d - 1, t], r.axr.at[1, d - 1, t], mp=to * 2 + ci)
    scatter_second(8)

    def output_grad_tile(t):
        q = rows_of(t, TT)
        r.rh[q, :] = (widen(r.rcol[q, :], C) * r.hcols[q, :].astype(F32)).astype(BF)

    def swish_back(pre, grad):
        gate = jax.nn.sigmoid(pre)
        return grad * (gate * (1.0 + pre * (1.0 - gate)))

    def attend_back(qb):
        q, key = slice(qb * B, (qb + 1) * B), keys_of(qb)
        for h in range(H):
            rot = slice(2 * h * HEAD, 2 * (h + 1) * HEAD)
            chan = slice(h * HEAD, (h + 1) * HEAD)
            weights = weights_of(qb, h)
            scores = (dot_nt(r.qrot[q, rot], r.krot[key, rot]) * weights).astype(BF)
            back = (dot_nt(r.gmix[q, chan], r.val[key, chan]) * weights).astype(BF)
            dq = dot_nn(back, r.krot[key, rot])
            turned = dq[:, :HEAD] * r.cosv[q, :] + dq[:, HEAD:] * r.sinv[q, :]
            r.gproj[0][q, chan] = swish_back(r.qpre[q, chan], turned).astype(BF)
            dk = dot_tn(back, r.qrot[q, rot])
            dv = dot_tn(scores, r.gmix[q, chan])
            for kb in range(key.start // B, qb + 1):
                at = slice(kb * B - key.start, (kb + 1) * B - key.start)
                rows = slice(kb * B, (kb + 1) * B)
                dkb, dvb = dk[at], dv[at]
                if qb < min(kb + REACH, NB - 1):
                    dkb, dvb = dkb + r.dk[rows, rot], dvb + r.dv[rows, chan]
                if kb < qb:
                    r.dk[rows, rot], r.dv[rows, chan] = dkb, dvb
                else:
                    turned = dkb[:, :HEAD] * r.cosv[q, :] + dkb[:, HEAD:] * r.sinv[q, :]
                    r.gproj[1][q, chan] = swish_back(r.kpre[q, chan], turned).astype(BF)
                    r.gproj[2][q, chan] = dvb.astype(BF)

    def output_tile(t):
        q = rows_of(t, 128)
        total = r.recc[1, xi, q].astype(F32)
        for d in range(1, X):
            total = total + r.recx[1, d - 1, q].astype(F32)
        r.bov[rows_of(j * NT + t, 128), :] = (r.hown[q, :] + total).astype(BF)

    def late_core(x):
        return pltpu.make_async_remote_copy(
            src_ref=r.part.at[x, 1 - ci], dst_ref=r.recc.at[0, x], send_sem=r.acs.at[2, x], recv_sem=r.acr.at[2, x],
            device_id={"mp": xi * 2 + 1 - ci}, device_id_type=MESH,
        )

    def late_chip(x, d, t):
        q = slice(t * 128, (t + 1) * 128)
        return pltpu.make_async_remote_copy(
            src_ref=r.part.at[x, ci, q], dst_ref=r.recx.at[0, d - 1, q], send_sem=r.axs.at[2, d - 1, t],
            recv_sem=r.axr.at[2, d - 1, t], device_id={"mp": x * 2 + ci}, device_id_type=MESH,
        )

    def blocks_in(qb):
        return [divmod(at, 2) for at in range(qb * B // TB, (qb + 1) * B // TB)]

    def late_begin(x, c):
        q = slice((x * 2 + c) * TB, (x * 2 + c + 1) * TB)
        out = dot_nt(r.gproj[0][q, :], r.mixw[0])
        for k in range(1, 4):
            out = out + dot_nt(r.gproj[k][q, :], r.mixw[k])
        r.part[x, c] = out.astype(BF)

        @pl.when(ci != c)
        def _():
            late_core(x).start()

    def late_pass(x, c):
        @pl.when(ci == c)
        def _():
            arrived(r.recc.at[0, x], r.acr.at[2, x])

        @pl.when((ci == c) & (xi != x))
        def _():
            for t in range(NT):
                q = slice(t * 128, (t + 1) * 128)
                r.part[x, c, q] = (r.part[x, c, q].astype(F32) + r.recc[0, x, q].astype(F32)).astype(BF)
                late_chip(x, lax.rem(x - xi + X, X), t).start()

    put_grad(3, r.nint, r.gproj[3], turned=True)
    scatter_first(3)
    for qb in range(NB - 1, -1, -1):
        attend_back(qb)
        if qb == NB - 1:
            for copy in used + early:
                settle(copy)
        for x, c in blocks_in(qb):
            late_begin(x, c)
        if qb < NB - 1:
            for x, c in blocks_in(qb + 1):
                late_pass(x, c)
        if qb == NB - 1:
            for d, to, source in peers():
                arrived(token_block(r.hcols)(source), r.ahr.at[1, d])
            each(T // TT, output_grad_tile)
            put_grad(4, r.ufull, r.rh)
            scatter_first(4)
            scatter_handed(7, 8, 9)
            scatter_second(10)
            finish_ff(5)
        if qb == max(NB - 2, 0):
            scatter_handed(10)
            scatter_second(3, 9)
            for t in range(NT):
                for d in range(1, X):
                    arrived(r.recx.at[1, d - 1, t * 128:(t + 1) * 128], r.axr.at[1, d - 1, t])
            each(TB // 128, output_tile)
            share_send(BO, token_block(r.bov))
            finish_ff(6)
        if qb == max(NB - 3, 0):
            scatter_handed(4, 3)
            share_forward(BO, token_block(r.bov))
            finish_ff(7)
    for x, c in blocks_in(0):
        late_pass(x, c)
    pending.extend((late_core(x), None) for x in range(X))
    pending.extend((late_chip(lax.rem(xi + d, X), d, t), None) for d in range(1, X) for t in range(NT))
    for k in (2, 0):
        put_grad(k, r.nint, r.gproj[k], turned=True)
        scatter_first(k)
    scatter_second(4)
    put_grad(1, r.nint, r.gproj[1], turned=True)
    scatter_first(1)
    finish_ff(8, 9, 10)
    scatter_second(2, 0)

    def input_tile(t):
        q = slice(t * 128, (t + 1) * 128)
        low = jnp.concatenate(
            [r.hsend[owner * TB + t * 128:owner * TB + (t + 1) * 128, :] for owner in range(mp)], axis=1
        ).astype(F32)
        grad = sum_tile(0, q)
        v = r.xown[q, :].astype(F32)
        scale = lax.rsqrt(jnp.mean(v * v, axis=-1, keepdims=True) + EPSILON)
        normed = v * scale
        inner = jnp.mean(grad * normed, axis=-1, keepdims=True)
        r.igv[rows_of(j * NT + t, 128), :] = (low + scale * (grad - normed * inner)).astype(BF)

    for t in range(NT):
        for d in range(1, X):
            arrived(r.recx.at[0, d - 1, t * 128:(t + 1) * 128], r.axr.at[2, d - 1, t])
        input_tile(t)
        share_send(IG + t, half_block(r.igv, t))
    scatter_second(1)
    scatter_handed(2)
    share_wait(BO, token_block(r.bov))
    stores = [load(r.bov, r.bo, 0)]

    def grad_block(k):
        return lambda owner: r.gmv.at[k * S:(k + 1) * S, pl.ds(pl.multiple_of(owner * C, C), C)]

    for k in (4, 3, 2, 0, 1):
        total = scatter_total(k).astype(BF)
        r.gmv[k * S:(k + 1) * S, jcols] = total
        r.sqs[...] += squares_of(total.astype(F32))
        for d, to, source in peers():
            go(grad_block(k)(j), grad_block(k)(j), r.gms.at[k, d], r.gmr.at[k, d], mp=to)

    if p.N > 1:
        at = i * mp + j
        r.sall[at] = r.sqs[...]
        for d in range(1, p.N):
            go(r.sall.at[at], r.sall.at[at], r.qs.at[d], r.qr.at[d], **whole(d))
        for t in range(NT):
            share_forward(IG + t, half_block(r.igv, t))
        for d in range(1, p.N):
            arrived(r.sall.at[lax.rem(at - d + p.N, p.N)], r.qr.at[d])
        r.sqo[...] = jnp.sum(r.sall[...], axis=0)
    else:
        r.s1[j] = r.sqs[...]
        for d, to, source in peers():
            go(r.s1.at[j], r.s1.at[j], r.q1s.at[d], r.q1r.at[d], mp=to)
        for t in range(NT):
            share_forward(IG + t, half_block(r.igv, t))
        for d, to, source in peers():
            arrived(r.s1.at[source], r.q1r.at[d])
        r.s2[i] = jnp.sum(r.s1[...], axis=0)
        for d in range(1, n):
            go(r.s2.at[i], r.s2.at[i], r.q2s.at[d], r.q2r.at[d], dp=lax.rem(i + d, n))
        for d in range(1, n):
            arrived(r.s2.at[lax.rem(i - d + n, n)], r.q2r.at[d])
        r.sqo[...] = jnp.sum(r.s2[...], axis=0)

    for t in range(NT):
        share_wait(IG + t, half_block(r.igv, t))
    stores.append(load(r.igv, r.ig, 1))
    for k in (4, 3, 2, 0, 1):
        for d, to, source in peers():
            arrived(grad_block(k)(source), r.gmr.at[k, d])
        stores.append(load(r.gmv.at[k * S:(k + 1) * S], r.gmo.at[k], 2 + k))
    for copy in stores:
        copy.wait()
    for copy, when in pending:
        guarded(when, copy.wait_send)


def fused(p, *operands):
    scratch = scratch_of(p)
    names = IN_NAMES + OUT_NAMES + tuple(scratch)
    anywhere = pl.BlockSpec(memory_space=pl.ANY)
    vmem = pl.BlockSpec(memory_space=pltpu.VMEM)
    smem = pl.BlockSpec(memory_space=pltpu.SMEM)
    return pl.pallas_call(
        partial(body, p, names),
        out_shape=(
            jax.ShapeDtypeStruct((p.T, p.D), BF),
            jax.ShapeDtypeStruct((p.T, p.D), BF),
            jax.ShapeDtypeStruct((5, p.S, p.D), BF),
            jax.ShapeDtypeStruct((2, p.F, p.S) if p.FD else (2, p.S, p.F), F32),
            jax.ShapeDtypeStruct((p.F, p.S) if p.FD else (p.S, p.F), F32),
            jax.ShapeDtypeStruct((8, 128), F32),
        ),
        in_specs=[anywhere, anywhere, vmem, smem] + [anywhere] * 5,
        out_specs=(anywhere, anywhere, anywhere, vmem, vmem, vmem),
        scratch_shapes=list(scratch.values()),
        compiler_params=pltpu.CompilerParams(
            collective_id=0, has_side_effects=True, vmem_limit_bytes=VMEM_LIMIT
        ),
    )(*operands)


VMEM_LIMIT = 64 * 2**20 - 2**18


def renew(weight, momentum, shadow, grad, clip_factor):
    clipped = grad * clip_factor
    velocity = MOMENTUM * momentum + clipped
    updated = weight - LEARN_RATE * (clipped + MOMENTUM * velocity)
    average = SHADOW_DECAY * shadow + (1.0 - SHADOW_DECAY) * updated
    return (velocity, average, updated)


def update_body(cuts, *refs):
    kinds, pieces = len(cuts), sum(len(c) for c in cuts)
    sq, carried = refs[0], refs[1:3]
    ins = [refs[3 + 4 * w:7 + 4 * w] for w in range(kinds)]
    refs = refs[3 + 4 * kinds:]
    norm_out, carried_out = refs[0], refs[1:3]
    outs = [refs[3 + 3 * w:6 + 3 * w] for w in range(kinds)]
    refs = refs[3 + 3 * kinds:]
    held = [refs[4 * w:4 * w + 4] for w in range(kinds)]
    made = [refs[4 * kinds + 3 * w:4 * kinds + 3 * w + 3] for w in range(kinds)]
    bounce, (in_sem, out_sem, carry_sem) = refs[7 * kinds:7 * kinds + 2], refs[7 * kinds + 2:]
    order = [(w, c) for w in range(kinds) for c in range(len(cuts[w]))]
    loads, copies = {}, []

    def load_piece(at):
        if at < len(order):
            w, c = order[at]
            loads[at] = [
                pltpu.make_async_copy(ins[w][a].at[cuts[w][c]], held[w][a].at[cuts[w][c]], in_sem.at[at, a]) for a in range(4)
            ]
            for copy in loads[at]:
                copy.start()

    def store(src, dst, sem):
        copies.append(pltpu.make_async_copy(src, dst, sem))
        copies[-1].start()

    for at in range(AHEAD):
        load_piece(at)
    carry = [pltpu.make_async_copy(carried[a], bounce[a], carry_sem.at[a]) for a in range(2)]
    carry[0].start()
    norm = jnp.sqrt(jnp.broadcast_to(jnp.sum(sq[...]), (8, 128)))
    norm_out[0, 0] = jnp.max(norm)
    clip_factor = 1.0 / jnp.maximum(jnp.max(norm), 1.0)
    for at, (w, c) in enumerate(order):
        cut = cuts[w][c]
        for copy in loads[at]:
            copy.wait()
        new = renew(*[held[w][a][cut] for a in range(3)], held[w][3][cut].astype(F32), clip_factor)
        for a in range(3):
            made[w][a][cut] = new[a]
            store(made[w][a].at[cut], outs[w][a].at[cut], out_sem.at[at, a])
        load_piece(at + AHEAD)
        if at in (1, 3):
            a = at // 2
            carry[a].wait()
            store(bounce[a], carried_out[a], carry_sem.at[2 + a])
            if a == 0:
                carry[1].start()
    for copy in copies:
        copy.wait()


AHEAD = 3


def update(sq, carried, weights):
    cuts = [[c for c in range(g[0].shape[0])] if g[0].ndim == 3 else [slice(None)] for g in weights]
    pieces = sum(len(c) for c in cuts)
    anywhere = pl.BlockSpec(memory_space=pl.ANY)
    vmem = pl.BlockSpec(memory_space=pltpu.VMEM)
    flat_in = [a for group in weights for a in group]
    flat_out = [a for group in weights for a in group[:3]]
    dma = pltpu.SemaphoreType.DMA
    size = sum(a.size * a.dtype.itemsize for a in flat_in + flat_out + 2 * list(carried))
    return pl.pallas_call(
        partial(update_body, cuts),
        out_shape=[jax.ShapeDtypeStruct((1, 1), F32)] + [jax.ShapeDtypeStruct(a.shape, a.dtype) for a in [*carried, *flat_out]],
        in_specs=[vmem] + [anywhere] * (2 + len(flat_in)),
        out_specs=[pl.BlockSpec(memory_space=pltpu.SMEM)] + [anywhere] * (2 + len(flat_out)),
        scratch_shapes=[pltpu.VMEM(a.shape, a.dtype) for a in flat_in + flat_out + list(carried)]
        + [dma((pieces, 4)), dma((pieces, 3)), dma((4,))],
        cost_estimate=pl.CostEstimate(flops=size, bytes_accessed=size, transcendentals=0),
        compiler_params=pltpu.CompilerParams(vmem_limit_bytes=VMEM_LIMIT),
    )(sq, *carried, *flat_in)


def turn_tables(tokens):
    theta = np.float32(10000.0) ** (-np.arange(HEAD, dtype=np.float32) / np.float32(HEAD))
    angle = np.arange(tokens, dtype=np.float32)[:, None] * theta.astype(np.float32)[None, :]
    angle = angle.astype(np.float64)
    return np.cos(angle).astype(np.float32), np.sin(angle).astype(np.float32)


def per_device(mesh, block_input, segment_ids, live_length, output_grad, mixer_weight, mixer_momentum, mixer_shadow,
               expand_weight, expand_momentum, expand_shadow, shrink_weight, shrink_momentum, shrink_shadow):
    rows, length, width = block_input.shape
    p = plan_of(mesh, length, width, shrink_weight.shape[0])
    turn = (lambda v: jnp.swapaxes(v, -1, -2)) if p.FD else (lambda v: v)
    if p.FD:
        shards = (turn(expand_weight), shrink_weight)
    else:
        shards = (jnp.concatenate([shrink_weight.T[None], expand_weight], axis=0).astype(BF), shrink_weight)
    cos, sin = turn_tables(length)
    out, grad_in, gm, ge, gs, sq = fused(
        p, block_input[0], output_grad[0], segment_ids, live_length, jnp.asarray(cos), jnp.asarray(sin), mixer_weight, *shards
    )
    new = update(sq, (out, grad_in), (
        (mixer_weight, mixer_momentum, mixer_shadow, gm),
        (turn(expand_weight), turn(expand_momentum), turn(expand_shadow), ge),
        (shrink_weight, shrink_momentum, shrink_shadow, gs if p.FD else gs.T),
    ))
    norm, out, grad_in = new[:3]
    return (out[None], grad_in[None], norm[0, 0], *new[3:6], *(turn(v) for v in new[6:9]), *new[9:12])


def solution(mesh):
    row, mixer, expand, shrink = P("dp", None, None), P(None, "dp", None), P(None, "dp", "mp"), P("mp", "dp")
    return jax.shard_map(
        partial(per_device, mesh),
        mesh=mesh,
        in_specs=(row, P("dp", None), P("dp"), row) + (mixer,) * 3 + (expand,) * 3 + (shrink,) * 3,
        out_specs=(row, row, P()) + (mixer,) * 3 + (expand,) * 3 + (shrink,) * 3,
        check_vma=False,
    )
```

```python
from functools import partial
from types import SimpleNamespace

import jax
import jax.numpy as jnp
import numpy as np
from jax import lax
from jax.experimental import pallas as pl
from jax.experimental.pallas import tpu as pltpu
from jax.sharding import PartitionSpec as P

HEAD = 128
EPSILON = 1e-06
LEARN_RATE = 32.0
MOMENTUM = 0.5
SHADOW_DECAY = 0.5
LAYER_PLACE = 12.0 / 24.0
LONGEST = 512
FF_ORDER = (1, 2, 0)
Y_FIRST = (4, 6)
Z_FIRST = (5, 4)
STRAIGHT = (0, 1)
MESH = pl.DeviceIdType.MESH
BF = jnp.bfloat16
F32 = jnp.float32


def dot_nn(a, b):
    return lax.dot_general(a, b, (((1,), (0,)), ((), ())), preferred_element_type=F32)


def dot_nt(a, b):
    return lax.dot_general(a, b, (((1,), (1,)), ((), ())), preferred_element_type=F32)


def dot_tn(a, b):
    return lax.dot_general(a, b, (((0,), (0,)), ((), ())), preferred_element_type=F32)


def rows_of(index, size):
    return pl.ds(pl.multiple_of(index * size, size), size)


def each(count, body):
    def step(t, carry):
        body(t)
        return carry

    lax.fori_loop(0, count, step, 0)


def widen(column, width):
    return jnp.concatenate([column] * (width // 128), axis=1)


def plan_of(mesh, tokens, width, inner):
    n, mp = mesh.shape["dp"], mesh.shape["mp"]
    lo, core = 2, 2
    return SimpleNamespace(
        n=n, mp=mp, LO=lo, HI=n // lo, X=mp // core, T=tokens, D=width, C=width // mp, F=inner,
        S=width // n, H=width // mp // HEAD, TB=tokens // mp, B=min(256, tokens),
        NT=tokens // mp // 128, FD=(width // n) % 128 == 0,
    )


def scratch_of(p):
    T, D, C, F, S, HI, LO, X, TB, B = p.T, p.D, p.C, p.F, p.S, p.HI, p.LO, p.X, p.TB, p.B
    dma = pltpu.SemaphoreType.DMA
    v = pltpu.VMEM
    return dict(
        mixw=v((4, D, C), BF), wo=v((D, D), BF), ffw=v((3, F, D) if p.FD else (3, D, F), BF),
        xown=v((TB, D), BF), nin=v((T, D), BF), nint=v((D, T), BF), up=v((T, D), BF),
        cosv=v((T, HEAD), F32), sinv=v((T, HEAD), F32),
        segq=v((T, 128), F32), segk=v((8, T), F32), dec=v((2, p.H, B, B), F32),
        qpre=v((T, C), F32), kpre=v((T, C), F32), gpre=v((T, C), F32), val=v((T, C), BF),
        qrot=v((T, 2 * C), BF), krot=v((T, 2 * C), BF), mixed=v((T, C), F32),
        ufull=v((T, D), BF), ss=v((p.mp, 8, T), F32), rcol=v((T, 128), F32),
        inn=v((p.mp, 8, TB), F32), hown=v((TB, D), F32),
        gact=v((T, max(F, 2 * C + HEAD)), F32), uact=v((T, F), BF), prod=v((T, F), BF), ggate=v((T, F), BF), gup=v((T, F), BF),
        part=v((X, 2, TB, D), BF), recc=v((2, X, TB, D), BF), recx=v((2, X - 1, TB, D), BF),
        hlow=v((T, D), BF),
        gm=v((5, HI, LO, S, C), BF), rym=v((5, HI, S, C), BF), rzm=v((5, HI - 1, S, C), BF),
        gf=v((3, LO, F, HI * S) if p.FD else (3, HI, LO, S, F), BF),
        ryf=v((3, F, HI * S) if p.FD else (3, HI, S, F), BF),
        rzf=v((3, HI - 1, F, S) if p.FD else (3, HI - 1, S, F), BF),
        relm=v((3, S, C), BF), relf=v((3, F, S) if p.FD else (3, S, F), BF),
        othm=v((HI, S, C), BF), othf=v((HI, F // 2, S) if p.FD else (HI, S // 2, F), BF),
        sqs=v((8, 128), F32), s1=v((p.mp, 8, 128), F32), s2=v((p.n, 8, 128), F32),
        loc=dma((10,)),
        zs=dma((11, HI - 1)), zr=dma((11, HI - 1)), us=dma((len(Y_FIRST), HI - 1)), ur=dma((len(Y_FIRST), HI - 1)),
        zp=dma((11,)), yp=dma((len(Y_FIRST),)), ys=dma((11, HI)), yr=dma((11, HI)),
        xs=dma((20, X - 1)), xr=dma((20, X - 1)), cs=dma((20, X)), cr=dma((20, X)),
        acs=dma((3, X)), acr=dma((3, X)), axs=dma((3, X - 1, p.NT)), axr=dma((3, X - 1, p.NT)),
        bys=dma((11,)), byr=dma((11,)), bzs=dma((11, HI - 1)), bzr=dma((11, HI - 1)),
        bts=dma((11,)), btr=dma((11,)), ozs=dma((2, HI - 1)), ozr=dma((2, HI - 1)), ots=dma((2,)), otr=dma((2,)),
        q1s=dma((p.mp,)), q1r=dma((p.mp,)), q2s=dma((p.n,)), q2r=dma((p.n,)),
    )


IN_NAMES = ("x", "og", "seg", "live", "cos", "sin", "mixsh", "exsh", "shsh")
OUT_NAMES = ("bo", "ig", "gmo", "geo", "gso", "sqo")


def body(p, names, *refs):
    r = SimpleNamespace(**dict(zip(names, refs)))
    n, mp, LO, HI, X, T, D, C, F, S, H, TB, B = (
        p.n, p.mp, p.LO, p.HI, p.X, p.T, p.D, p.C, p.F, p.S, p.H, p.TB, p.B,
    )
    NT, TT = p.NT, min(512, p.T)
    i, j = lax.axis_index("dp"), lax.axis_index("mp")
    zi, yi = i // LO, lax.rem(i, LO)
    xi, ci = j // 2, lax.rem(j, 2)
    jcols = pl.ds(pl.multiple_of(j * C, C), C)
    pending = []
    r.xv, r.nmid = r.hlow, r.nin
    r.bov, r.igv, r.gmv = r.up, r.ufull, r.wo
    r.dk, r.icol, r.dv = r.gact.at[:, 0:2 * C], r.gact.at[:, 2 * C:2 * C + HEAD], r.mixed
    r.gproj = [r.ggate.at[:, 0:C], r.ggate.at[:, C:2 * C], r.gup.at[:, 0:C], r.gup.at[:, C:2 * C]]
    r.gmix, r.rh = r.prod.at[:, 0:C], r.prod.at[:, C:2 * C]

    def go(src, dst, ssem, rsem, when=None, **device):
        copy = pltpu.make_async_remote_copy(
            src_ref=src, dst_ref=dst, send_sem=ssem, recv_sem=rsem,
            device_id=device, device_id_type=MESH,
        )
        guarded(when, copy.start)
        pending.append((copy, when))
        return copy

    def guarded(when, act):
        if when is None:
            act()
        else:
            pl.when(when)(lambda: act())

    def arrived(dst, sem):
        pltpu.make_async_copy(dst, dst, sem).wait()

    def settle(copy):
        for other, when in pending:
            if other is copy:
                guarded(when, copy.wait_send)
        pending[:] = [entry for entry in pending if entry[0] is not copy]

    def load(src, dst, sem):
        copy = pltpu.make_async_copy(src, dst, r.loc.at[sem])
        copy.start()
        return copy

    own_mix = [load(r.mixsh.at[k, :, jcols], r.qpre.at[k * S:(k + 1) * S], k) for k in range(5)]
    if p.FD:
        stage = [r.gact.at[0:F, m * S:(m + 1) * S] for m in range(3)]
        own_ff = [load(r.shsh if m == 0 else r.exsh.at[m - 1], stage[m], 5 + m) for m in range(3)]
    else:
        own_ff = [load(r.exsh.at[m], r.ffw.at[m, rows_of(i, S)], 5 + m) for m in range(3)]
    load_x = load(r.x, r.xv, 8)
    load_og = load(r.og, r.up, 9)

    def enter():
        barrier = pltpu.get_barrier_semaphore()
        for d in range(1, n):
            pl.semaphore_signal(barrier, inc=1, device_id={"dp": lax.rem(i + d, n)}, device_id_type=MESH)
        for d in range(1, mp):
            pl.semaphore_signal(barrier, inc=1, device_id={"mp": lax.rem(j + d, mp)}, device_id_type=MESH)
        pl.semaphore_wait(barrier, n - 1 + mp - 1)

    def slot(k, device):
        rows = rows_of(device, S)
        if k == 4:
            return r.wo.at[rows, jcols]
        if k < 4:
            return r.mixw.at[k, rows]
        m, half = FF_ORDER[(k - 5) // 2], (k - 5) % 2
        if p.FD:
            return r.ffw.at[m, half * F // 2:(half + 1) * F // 2, rows]
        return r.ffw.at[m, pl.ds(pl.multiple_of(device * S + half * S // 2, S // 2), S // 2)]

    def gather_ready(k):
        if k < 5:
            own_mix[k].wait()
            slot(k, i)[...] = r.qpre[k * S:(k + 1) * S, :].astype(BF)
        else:
            m, half = FF_ORDER[(k - 5) // 2], (k - 5) % 2
            if half == 0:
                own_ff[m].wait()
            if p.FD:
                slot(k, i)[...] = stage[m][half * F // 2:(half + 1) * F // 2, :].astype(BF)

    relays = HI == 4
    next_to_end = (zi == 1) | (zi == 2)

    def along_z(block, ssem, rsem):
        for d in range(1, HI):
            to = lax.rem(zi + d, HI)
            near = (jnp.abs(to - zi) < 3) if relays else None
            go(block, block, ssem.at[d - 1], rsem.at[d - 1], when=near, dp=to * LO + yi)

    def hand_on(block, ssem, rsem):
        if relays:
            end = jnp.where(zi == 2, 3, 0)
            go(block, block, ssem, rsem.at[jnp.where(zi == 2, 2, 0)], when=next_to_end, dp=end * LO + yi)

    def from_z_source(k, d, y):
        return slot(k, lax.rem(zi - d + HI, HI) * LO + y)

    WAYS = [2, 1, *range(3, HI)]

    def gather_send(k):
        src = slot(k, i)
        along_z(src, r.zs.at[k], r.zr.at[k])
        go(src, src, r.ys.at[k, 0], r.yr.at[k, 0], dp=zi * LO + 1 - yi)

    def gather_forward(k):
        if k - 1 in Y_FIRST:
            b = Y_FIRST.index(k - 1)
            block = from_z_source(k - 1, 2, 1 - yi)
            arrived(block, r.ur.at[b, 1])
            hand_on(block, r.yp.at[b], r.ur.at[b])
        if k in Y_FIRST:
            b = Y_FIRST.index(k)
            peers = slot(k, zi * LO + 1 - yi)
            arrived(peers, r.yr.at[k, 0])
            along_z(peers, r.us.at[b], r.ur.at[b])
        for d in WAYS:
            block = from_z_source(k, d, yi)
            arrived(block, r.zr.at[k, d - 1])
            if d == 2:
                hand_on(block, r.zp.at[k], r.zr.at[k])
            if k not in Y_FIRST:
                go(block, block, r.ys.at[k, d], r.yr.at[k, d], dp=zi * LO + 1 - yi)

    def gather_wait(k):
        for d in range(HI):
            if k not in Y_FIRST:
                arrived(from_z_source(k, d, 1 - yi), r.yr.at[k, d])
            elif d in (1, 3) or d > 3:
                arrived(from_z_source(k, d, 1 - yi), r.ur.at[Y_FIRST.index(k), d - 1])

    def share_send(s, block, src=None):
        own = block(j)
        src = own if src is None else src
        for d in range(1, X):
            go(src, own, r.xs.at[s, d - 1], r.xr.at[s, d - 1], mp=lax.rem(xi + d, X) * 2 + ci)
        go(src, own, r.cs.at[s, 0], r.cr.at[s, 0], mp=xi * 2 + 1 - ci)

    def share_forward(s, block):
        for d in range(1, X):
            part = block(lax.rem(xi - d + X, X) * 2 + ci)
            arrived(part, r.xr.at[s, d - 1])
            go(part, part, r.cs.at[s, d], r.cr.at[s, d], mp=xi * 2 + 1 - ci)

    def share_wait(s, block):
        for d in range(X):
            arrived(block(lax.rem(xi - d + X, X) * 2 + 1 - ci), r.cr.at[s, d])

    def sum_begin(s, b, compute):
        sent = []
        for d in [*range(1, X), 0]:
            to = lax.rem(xi + d, X)
            compute(to, 1 - ci)
            sent.append(go(
                r.part.at[to, 1 - ci], r.recc.at[b, to], r.acs.at[s, d], r.acr.at[s, d], mp=xi * 2 + 1 - ci
            ))
        for d in range(1, X):
            to = lax.rem(xi + d, X)
            compute(to, ci)
            arrived(r.recc.at[b, to], r.acr.at[s, d])
            for t in range(NT):
                q = slice(t * 128, (t + 1) * 128)
                r.part[to, ci, q] = (
                    r.part[to, ci, q].astype(F32) + r.recc[b, to, q].astype(F32)
                ).astype(BF)
                sent.append(go(
                    r.part.at[to, ci, q], r.recx.at[b, d - 1, q], r.axs.at[s, d - 1, t], r.axr.at[s, d - 1, t],
                    mp=to * 2 + ci,
                ))
        compute(xi, ci)
        return sent

    def sum_arrived(s, b, t):
        if t == 0:
            arrived(r.recc.at[b, xi], r.acr.at[s, 0])
        for d in range(1, X):
            arrived(r.recx.at[b, d - 1, t * 128:(t + 1) * 128], r.axr.at[s, d - 1, t])

    def sum_tile(b, q):
        total = r.part[xi, ci, q].astype(F32) + r.recc[b, xi, q].astype(F32)
        for d in range(1, X):
            total = total + r.recx[b, d - 1, q].astype(F32)
        return total

    flat = p.FD

    def half_of(k):
        size = (F if flat else S) // 2
        return (k - 5) // 2, slice((k - 5) % 2 * size, ((k - 5) % 2 + 1) * size)

    def block_of(k, z, y):
        if k < 5:
            return r.gm.at[k, z, y]
        m, rows = half_of(k)
        return r.gf.at[m, y, rows, rows_of(z, S)] if flat else r.gf.at[m, z, y, rows]

    def from_y(k):
        if k < 5:
            return r.rym.at[k]
        m, rows = half_of(k)
        return r.ryf.at[m, rows] if flat else r.ryf.at[m, :, rows]

    def from_y_block(k, z):
        ref = from_y(k)
        return ref.at[:, rows_of(z, S)] if flat and k >= 5 else ref.at[z]

    def to_y(k):
        if k < 5:
            return r.gm.at[k, :, 1 - yi]
        m, rows = half_of(k)
        return r.gf.at[m, 1 - yi, rows] if flat else r.gf.at[m, :, 1 - yi, rows]

    def from_z(k, d, own=True):
        if not own:
            return (r.othm if k < 5 else r.othf).at[d - 1]
        if k < 5:
            return r.rzm.at[k, d - 1]
        m, rows = half_of(k)
        return r.rzf.at[m, d - 1, rows]

    def handed(k, own=True):
        if not own:
            return (r.othm if k < 5 else r.othf).at[HI - 1]
        if k < 5:
            return r.relm.at[max(k - 2, 0)]
        m, rows = half_of(k)
        return r.relf.at[m, rows]

    def z_sems(k, own):
        if own:
            return r.bzs.at[k], r.bzr.at[k], r.bts.at[k], r.btr.at[k]
        o = Z_FIRST.index(k)
        return r.ozs.at[o], r.ozr.at[o], r.ots.at[o], r.otr.at[o]

    def stepped(k):
        return relays and k not in STRAIGHT

    def far(d, back=False):
        other = lax.rem(zi + (HI - d if back else d), HI)
        return jnp.abs(other - zi) == 3

    def z_send(k, own, ways):
        y = yi if own else 1 - yi
        ssem, rsem, tsem, trsem = z_sems(k, own)
        for d in ways:
            to = lax.rem(zi + d, HI)
            block, dst = block_of(k, to, y), from_z(k, d, own)
            if stepped(k) and d != 2:
                go(block, handed(k, own), tsem, trsem, when=far(d), dp=jnp.where(zi == 0, 1, 2) * LO + yi)
                go(block, dst, ssem.at[d - 1], rsem.at[d - 1], when=jnp.logical_not(far(d)), dp=to * LO + yi)
            else:
                go(block, dst, ssem.at[d - 1], rsem.at[d - 1], dp=to * LO + yi)

    def z_send_handed(k, own):
        block = block_of(k, lax.rem(zi + 2, HI), yi if own else 1 - yi)

        @pl.when(next_to_end)
        def _():
            arrived(handed(k, own), z_sems(k, own)[3])
            block[...] = (block[...].astype(F32) + handed(k, own)[...].astype(F32)).astype(BF)

        z_send(k, own, [2])

    def z_total(k, own):
        for d in range(1, HI):
            wait = partial(arrived, from_z(k, d, own), z_sems(k, own)[1].at[d - 1])
            guarded(jnp.logical_not(far(d, back=True)) if stepped(k) and d != 2 else None, wait)
        total = block_of(k, zi, yi if own else 1 - yi)[...].astype(F32)
        for d in range(1, HI):
            total = total + from_z(k, d, own)[...].astype(F32)
        return total

    def clear_far_places():
        if not relays:
            return
        for d in (1, 3):
            @pl.when(far(d, back=True))
            def _(d=d):
                r.rzm[:, d - 1] = jnp.zeros((5, S, C), BF)
                for m in range(3):
                    r.rzf[m, d - 1] = jnp.zeros(r.rzf.shape[2:], BF)
                r.othm[d - 1] = jnp.zeros(r.othm.shape[1:], BF)
                r.othf[d - 1] = jnp.zeros(r.othf.shape[1:], BF)

    def near_ways(k):
        return [3, 1] if stepped(k) else list(range(1, HI))

    def scatter_first(*pieces):
        for k in pieces:
            if k in Z_FIRST:
                for own in (False, True):
                    z_send(k, own, near_ways(k))
            else:
                go(to_y(k), from_y(k), r.bys.at[k], r.byr.at[k], dp=zi * LO + 1 - yi)

    def scatter_second(*pieces):
        for k in pieces:
            if k in Z_FIRST:
                block = block_of(k, zi, 1 - yi)
                block[...] = z_total(k, False).astype(BF)
                go(block, from_y_block(k, zi), r.bys.at[k], r.byr.at[k], dp=zi * LO + 1 - yi)
                continue
            arrived(from_y(k), r.byr.at[k])
            for d in range(1, HI):
                to = lax.rem(zi + d, HI)
                block = block_of(k, to, yi)
                block[...] = (block[...].astype(F32) + from_y_block(k, to)[...].astype(F32)).astype(BF)
            z_send(k, True, near_ways(k))

    def scatter_handed(*pieces):
        for k in pieces:
            if stepped(k):
                if k in Z_FIRST:
                    z_send_handed(k, False)
                z_send_handed(k, True)

    def scatter_total(k):
        if k in Z_FIRST:
            arrived(from_y_block(k, zi), r.byr.at[k])
        return z_total(k, True) + from_y_block(k, zi)[...].astype(F32)

    def squares_of(total):
        squared = total * total
        if squared.shape[-1] % 128:
            corner = (lax.broadcasted_iota(jnp.int32, (8, 128), 0) + lax.broadcasted_iota(jnp.int32, (8, 128), 1)) == 0
            return jnp.where(corner, jnp.sum(squared), 0.0)
        folded = jnp.sum(squared.reshape(-1, 8, squared.shape[-1]), axis=0)
        return sum(folded[:, c:c + 128] for c in range(0, folded.shape[-1], 128))

    def finish_ff(*pieces):
        for k in pieces:
            m, rows = half_of(k)
            total = scatter_total(k)
            if m == 0:
                r.gso[rows] = total
            else:
                r.geo[m - 1, rows] = total
            r.sqs[...] += squares_of(total)

    def put_grad(k, lhs, rhs, turned=False):
        g = r.gm.at[k] if k < 5 else r.gf.at[k - 5]
        per = TT // (LO * S)

        def tile(t):
            if turned:
                out = dot_nn(lhs[rows_of(t, TT), :], rhs[...])
            else:
                out = dot_tn(lhs[:, rows_of(t, TT)], rhs[...])
            g[pl.ds(t * per, per)] = out.astype(BF).reshape(per, LO, S, out.shape[-1])

        each(D // TT, tile)

    def put_ff_grad(m, units, model):
        if not flat:
            return put_grad(5 + m, model, units)
        for f in range(0, F, 384):
            q = slice(f, min(f + 384, F))
            out = dot_tn(units[:, q], model[...]).astype(BF)
            for y in range(LO):
                for z in range(HI):
                    r.gf[m, y, q, z * S:(z + 1) * S] = out[:, (z * LO + y) * S:(z * LO + y + 1) * S]

    def to_units(a, m):
        return dot_nt(a, r.ffw[m]) if flat else dot_nn(a, r.ffw[m])

    def to_model(a, m):
        return dot_nn(a, r.ffw[m]) if flat else dot_nt(a, r.ffw[m])

    gather_ready(0)
    gather_ready(1)
    enter()
    gather_send(0)
    gather_send(1)
    gather_ready(2)
    gather_send(2)
    r.sqs[...] = jnp.zeros_like(r.sqs)
    clear_far_places()

    length = r.live[0]
    load_x.wait()

    def norm_tile(t):
        q = rows_of(t, 128)
        v = r.xv[q, :].astype(F32)
        r.nin[q, :] = (v * lax.rsqrt(jnp.mean(v * v, axis=-1, keepdims=True) + EPSILON)).astype(BF)

    each(T // 128, norm_tile)
    for k in range(3, 11):
        gather_ready(k)
    load_x_own = load(r.x.at[rows_of(j, TB)], r.xown, 8)
    load_og.wait()
    load_cos = load(r.cos, r.cosv, 0)
    load_sin = load(r.sin, r.sinv, 1)

    def live_tile(t):
        q = rows_of(t, 128)
        place = lax.broadcasted_iota(jnp.int32, (128, D), 0) + t * 128
        r.up[q, :] = jnp.where(place < length, r.up[q, :].astype(F32), 0.0).astype(BF)

    each(T // 128, live_tile)

    place = lax.broadcasted_iota(jnp.int32, (1, T), 1)
    segment = r.seg[...].astype(F32)
    r.segk[...] = jnp.broadcast_to(jnp.where(place < length, segment, -2.0), (8, T))
    seg_q = jnp.where(place < length, segment, -1.0)
    for t in range(T // 128):
        q = slice(t * 128, t * 128 + 128)
        r.segq[q, :] = jnp.transpose(jnp.broadcast_to(seg_q[:, q], (128, 128)))

    down = lax.broadcasted_iota(jnp.int32, (B, B), 0)
    over = lax.broadcasted_iota(jnp.int32, (B, B), 1)
    heads = D // HEAD

    def rate_of(h):
        return -(8.0 * (j * H + h).astype(F32) / heads) * (1.0 - LAYER_PLACE)

    for h in range(H):
        rate = rate_of(h)
        for o in range(2):
            distance = down - over + o * B
            fade = jnp.exp(rate * jnp.maximum(distance, 0).astype(F32))
            r.dec[o, h] = jnp.where(distance >= 0, fade, 0.0)

    for t in range(D // 128):
        q = slice(t * 128, t * 128 + 128)
        r.nint[q, :] = jnp.transpose(r.nin[:, q])
    load_cos.wait()
    load_sin.wait()
    load_x_own.wait()

    def turn_into(pre_ref, rot_ref, k):
        def tile(t):
            q = rows_of(t, TT)
            pre = dot_nn(r.nin[q, :], r.mixw[k])
            pre_ref[q, :] = pre
            act = pre * jax.nn.sigmoid(pre)
            c, s = r.cosv[q, :], r.sinv[q, :]
            for h in range(H):
                a = act[:, h * HEAD:(h + 1) * HEAD]
                rot_ref[q, 2 * h * HEAD:(2 * h + 1) * HEAD] = (a * c).astype(BF)
                rot_ref[q, (2 * h + 1) * HEAD:(2 * h + 2) * HEAD] = (a * s).astype(BF)

        each(T // TT, tile)

    def project_into(ref, k):
        def tile(t):
            q = rows_of(t, TT)
            ref[q, :] = dot_nn(r.nin[q, :], r.mixw[k]).astype(ref.dtype)

        each(T // TT, tile)

    gather_forward(0)
    gather_send(3)
    gather_forward(1)
    gather_send(4)
    gather_wait(0)
    turn_into(r.qpre, r.qrot, 0)
    gather_forward(2)
    gather_send(5)
    gather_wait(1)
    turn_into(r.kpre, r.krot, 1)
    gather_forward(3)
    gather_send(6)
    gather_wait(2)
    project_into(r.val, 2)
    gather_forward(4)
    gather_send(7)
    gather_wait(3)
    project_into(r.gpre, 3)

    def wo_block(owner):
        return r.wo.at[:, pl.ds(pl.multiple_of(owner * C, C), C)]


    NB = T // B
    REACH = LONGEST // B

    def keys_of(qb):
        return slice(max(0, qb - REACH) * B, (qb + 1) * B)

    def weights_of(qb, h):
        key = keys_of(qb)
        width = key.stop - key.start
        fades = [r.dec[min(o, 1), h] for o in range(width // B - 1, -1, -1)]
        for o in range(2, width // B):
            fades[width // B - 1 - o] *= jnp.exp(rate_of(h) * ((o - 1) * B))
        seen = jnp.broadcast_to(r.segk[0:1, key], (B, width))
        same = widen(r.segq[qb * B:(qb + 1) * B, :], width) == seen
        return jnp.where(same, jnp.concatenate(fades, axis=1), 0.0)

    def u_block(qb):
        return lambda owner: r.ufull.at[qb * B:(qb + 1) * B, pl.ds(pl.multiple_of(owner * C, C), C)]

    def attend(qb):
        q = slice(qb * B, (qb + 1) * B)
        squares = jnp.zeros((B, 1), F32)
        for h in range(H):
            rot = slice(2 * h * HEAD, 2 * (h + 1) * HEAD)
            chan = slice(h * HEAD, (h + 1) * HEAD)
            key = keys_of(qb)
            scores = dot_nt(r.qrot[q, rot], r.krot[key, rot]) * weights_of(qb, h)
            total = dot_nn(scores.astype(BF), r.val[key, chan])
            r.mixed[q, chan] = total
            squares = squares + jnp.sum(total * total, axis=-1, keepdims=True)
            r.ufull[q, pl.ds(pl.multiple_of(j * C + h * HEAD, HEAD), HEAD)] = (
                total * r.gpre[q, chan]
            ).astype(BF)
        r.ss[j, :, q] = jnp.transpose(jnp.broadcast_to(squares, (B, 128)))[0:8, :]

    def ss_block(owner):
        return r.ss.at[owner]

    for qb in range(NB):
        attend(qb)
        share_send(1 + qb, u_block(qb))
        if qb == NB - 1:
            share_send(1 + NB, ss_block)
        if qb == 0:
            gather_forward(5)
            gather_send(8)
        if qb == 1:
            gather_wait(4)
            share_send(0, wo_block)
        if qb == 3:
            share_forward(0, wo_block)
        if qb == 2:
            gather_forward(6)
            gather_send(9)
        if qb > 0:
            share_forward(qb, u_block(qb - 1))
    share_forward(NB, u_block(NB - 1))
    share_forward(1 + NB, ss_block)
    gather_forward(7)
    gather_send(10)
    gather_forward(8)
    share_wait(0, wo_block)
    for qb in range(NB):
        share_wait(1 + qb, u_block(qb))
    share_wait(1 + NB, ss_block)
    early = [copy for copy, when in pending]

    total_ss = r.ss[0]
    for owner in range(1, mp):
        total_ss = total_ss + r.ss[owner]
    inverse = lax.rsqrt(total_ss * (1.0 / D) + EPSILON)
    for t in range(T // 128):
        q = slice(t * 128, t * 128 + 128)
        r.rcol[q, :] = jnp.transpose(jnp.broadcast_to(inverse[0:1, q], (128, 128)))

    def hidden_tile(t):
        q = rows_of(t, TB)
        out = widen(r.rcol[q, :], D) * dot_nn(r.ufull[q, :], r.wo[...])
        hidden = r.xv[q, :].astype(F32) + out
        scale = lax.rsqrt(jnp.mean(hidden * hidden, axis=-1, keepdims=True) + EPSILON)
        r.nmid[q, :] = (hidden * scale).astype(BF)

        @pl.when(t == j)
        def _():
            r.hown[...] = hidden

    each(T // TB, hidden_tile)
    gather_wait(5)
    gather_wait(6)

    def gate_tile(t):
        q = rows_of(t, TT)
        r.gact[q, 0:F] = to_units(r.nmid[q, :], 1)

    each(T // TT, gate_tile)
    gather_forward(9)
    gather_wait(7)
    gather_wait(8)

    def up_tile(t):
        q = rows_of(t, TT)
        upper = to_units(r.nmid[q, :], 2)
        r.uact[q, :] = upper.astype(BF)
        r.prod[q, :] = (r.gact[q, 0:F] * upper).astype(BF)

    each(T // TT, up_tile)
    put_ff_grad(0, r.prod, r.up)
    gather_forward(10)
    scatter_first(5, 6)
    gather_wait(9)
    gather_wait(10)

    def mid_block(x, c):
        q = rows_of(x * 2 + c, TB)
        g = to_units(r.up[q, :], 0)
        grad_gate, grad_up = (g * r.uact[q, :].astype(F32)).astype(BF), (g * r.gact[q, 0:F]).astype(BF)
        r.ggate[q, :] = grad_gate
        r.gup[q, :] = grad_up
        r.part[x, c] = (to_model(grad_gate, 1) + to_model(grad_up, 2)).astype(BF)

    used = sum_begin(0, 0, mid_block)
    scatter_handed(5)
    scatter_second(6)
    put_ff_grad(1, r.ggate, r.nmid)
    scatter_first(7, 8)
    scatter_handed(6)

    def back_tile(t):
        q = rows_of(t, 128)
        here = rows_of(j * (TB // 128) + t, 128)
        grad = sum_tile(0, q)
        hidden = r.hown[q, :]
        scale = lax.rsqrt(jnp.mean(hidden * hidden, axis=-1, keepdims=True) + EPSILON)
        normed = hidden * scale
        inner = jnp.mean(grad * normed, axis=-1, keepdims=True)
        out = r.up[here, :].astype(F32) + scale * (grad - normed * inner)
        low = out.astype(BF)
        r.hlow[here, :] = low
        mixer_out = hidden - r.xown[q, :].astype(F32)
        product = jnp.sum(low.astype(F32) * mixer_out, axis=-1, keepdims=True) * (1.0 / D)
        r.inn[j, :, q] = jnp.transpose(jnp.broadcast_to(product, (128, 128)))[0:8, :]

    def token_block(ref):
        return lambda owner: ref.at[rows_of(owner, TB)]

    BO, IN, GM, HL, IG = 2 + NB, 3 + NB, 4 + NB, 9 + NB, 9 + NB + NT

    def inn_block(owner):
        return r.inn.at[owner]

    def half_block(ref, t):
        return lambda owner: ref.at[rows_of(owner * NT + t, 128)]

    for t in range(NT):
        sum_arrived(0, 0, t)
        back_tile(t)
        share_send(HL + t, half_block(r.hlow, t))
    share_send(IN, inn_block)
    put_ff_grad(2, r.gup, r.nmid)
    scatter_first(9, 10)
    scatter_second(5)
    scatter_second(7)
    for t in range(NT):
        share_forward(HL + t, half_block(r.hlow, t))
    share_forward(IN, inn_block)
    for copy in used:
        settle(copy)

    def expand_block(x, c):
        q = rows_of(x * 2 + c, TB)
        r.part[x, c] = to_model(r.prod[q, :], 0).astype(BF)

    scatter_handed(7)
    scatter_second(8)
    used = sum_begin(1, 1, expand_block)
    for t in range(NT):
        share_wait(HL + t, half_block(r.hlow, t))
    share_wait(IN, inn_block)
    for owner in range(mp):
        for t in range(TB // 128):
            row = r.inn[owner, 0:1, t * 128:(t + 1) * 128]
            q = slice(owner * TB + t * 128, owner * TB + (t + 1) * 128)
            r.icol[q, :] = jnp.transpose(jnp.broadcast_to(row, (128, 128)))

    wo_rows = rows_of(j, C)

    def gated_tile(t):
        q = rows_of(t, TT)
        low = r.hlow[q, :]
        grad = dot_nt(low, r.wo[wo_rows, :])
        inner = widen(r.icol[q, :], C)
        inverse = widen(r.rcol[q, :], C)
        normed = r.mixed[q, :] * inverse
        r.gproj[3][q, :] = (grad * normed).astype(BF)
        r.gmix[q, :] = (inverse * (grad * r.gpre[q, :] - normed * inner)).astype(BF)
        r.rh[q, :] = (inverse * r.hlow[q, jcols].astype(F32)).astype(BF)

    each(T // TT, gated_tile)
    put_grad(4, r.ufull, r.rh)
    scatter_first(4)
    scatter_handed(8)

    def swish_back(pre, grad):
        gate = jax.nn.sigmoid(pre)
        return grad * (gate * (1.0 + pre * (1.0 - gate)))

    def attend_back(qb):
        q, key = slice(qb * B, (qb + 1) * B), keys_of(qb)
        for h in range(H):
            rot = slice(2 * h * HEAD, 2 * (h + 1) * HEAD)
            chan = slice(h * HEAD, (h + 1) * HEAD)
            weights = weights_of(qb, h)
            scores = (dot_nt(r.qrot[q, rot], r.krot[key, rot]) * weights).astype(BF)
            back = (dot_nt(r.gmix[q, chan], r.val[key, chan]) * weights).astype(BF)
            dq = dot_nn(back, r.krot[key, rot])
            turned = dq[:, :HEAD] * r.cosv[q, :] + dq[:, HEAD:] * r.sinv[q, :]
            r.gproj[0][q, chan] = swish_back(r.qpre[q, chan], turned).astype(BF)
            dk = dot_tn(back, r.qrot[q, rot])
            dv = dot_tn(scores, r.gmix[q, chan])
            for kb in range(key.start // B, qb + 1):
                at = slice(kb * B - key.start, (kb + 1) * B - key.start)
                rows = slice(kb * B, (kb + 1) * B)
                dkb, dvb = dk[at], dv[at]
                if qb < min(kb + REACH, NB - 1):
                    dkb, dvb = dkb + r.dk[rows, rot], dvb + r.dv[rows, chan]
                if kb < qb:
                    r.dk[rows, rot], r.dv[rows, chan] = dkb, dvb
                else:
                    turned = dkb[:, :HEAD] * r.cosv[q, :] + dkb[:, HEAD:] * r.sinv[q, :]
                    r.gproj[1][q, chan] = swish_back(r.kpre[q, chan], turned).astype(BF)
                    r.gproj[2][q, chan] = dvb.astype(BF)

    def output_tile(t):
        q = rows_of(t, 128)
        r.bov[rows_of(j * NT + t, 128), :] = (r.hown[q, :] + sum_tile(1, q)).astype(BF)

    def late_core(x):
        return pltpu.make_async_remote_copy(
            src_ref=r.part.at[x, 1 - ci], dst_ref=r.recc.at[0, x], send_sem=r.acs.at[2, x], recv_sem=r.acr.at[2, x],
            device_id={"mp": xi * 2 + 1 - ci}, device_id_type=MESH,
        )

    def late_chip(x, d, t):
        q = slice(t * 128, (t + 1) * 128)
        return pltpu.make_async_remote_copy(
            src_ref=r.part.at[x, ci, q], dst_ref=r.recx.at[0, d - 1, q], send_sem=r.axs.at[2, d - 1, t],
            recv_sem=r.axr.at[2, d - 1, t], device_id={"mp": x * 2 + ci}, device_id_type=MESH,
        )

    def blocks_in(qb):
        return [divmod(at, 2) for at in range(qb * B // TB, (qb + 1) * B // TB)]

    def late_begin(x, c):
        q = slice((x * 2 + c) * TB, (x * 2 + c + 1) * TB)
        out = dot_nt(r.gproj[0][q, :], r.mixw[0])
        for k in range(1, 4):
            out = out + dot_nt(r.gproj[k][q, :], r.mixw[k])
        r.part[x, c] = out.astype(BF)

        @pl.when(ci != c)
        def _():
            late_core(x).start()

    def late_pass(x, c):
        @pl.when(ci == c)
        def _():
            arrived(r.recc.at[0, x], r.acr.at[2, x])

        @pl.when((ci == c) & (xi != x))
        def _():
            for t in range(NT):
                q = slice(t * 128, (t + 1) * 128)
                r.part[x, c, q] = (r.part[x, c, q].astype(F32) + r.recc[0, x, q].astype(F32)).astype(BF)
                late_chip(x, lax.rem(x - xi + X, X), t).start()

    put_grad(3, r.nint, r.gproj[3], turned=True)
    scatter_first(3)
    scatter_second(9)
    for qb in range(NB - 1, -1, -1):
        attend_back(qb)
        if qb == NB - 1:
            for t in range(NT):
                sum_arrived(1, 1, t)
            each(TB // 128, output_tile)
            share_send(BO, token_block(r.bov))
            for copy in used + early:
                settle(copy)
        for x, c in blocks_in(qb):
            late_begin(x, c)
        if qb < NB - 1:
            for x, c in blocks_in(qb + 1):
                late_pass(x, c)
        if qb == NB - 1:
            scatter_handed(9)
            scatter_second(10)
            finish_ff(5)
        if qb == max(NB - 2, 0):
            scatter_handed(4, 10)
            scatter_second(3)
            share_forward(BO, token_block(r.bov))
            finish_ff(6)
        if qb == max(NB - 3, 0):
            scatter_second(4)
            scatter_handed(3)
            finish_ff(7)
    for x, c in blocks_in(0):
        late_pass(x, c)
    pending.extend((late_core(x), None) for x in range(X))
    pending.extend((late_chip(lax.rem(xi + d, X), d, t), None) for d in range(1, X) for t in range(NT))
    for k in (2, 0):
        put_grad(k, r.nint, r.gproj[k], turned=True)
        scatter_first(k)
    finish_ff(8)
    scatter_second(2)
    put_grad(1, r.nint, r.gproj[1], turned=True)
    scatter_first(1)
    scatter_handed(2)
    finish_ff(9, 10)

    def input_tile(t):
        q = rows_of(t, 128)
        grad = sum_tile(0, q)
        v = r.xown[q, :].astype(F32)
        scale = lax.rsqrt(jnp.mean(v * v, axis=-1, keepdims=True) + EPSILON)
        normed = v * scale
        inner = jnp.mean(grad * normed, axis=-1, keepdims=True)
        r.igv[rows_of(j * NT + t, 128), :] = (r.hlow[rows_of(j * NT + t, 128), :].astype(F32) + scale * (grad - normed * inner)).astype(BF)

    for t in range(NT):
        for d in range(1, X):
            arrived(r.recx.at[0, d - 1, t * 128:(t + 1) * 128], r.axr.at[2, d - 1, t])
        input_tile(t)
        share_send(IG + t, half_block(r.igv, t))
    scatter_second(0, 1)
    share_wait(BO, token_block(r.bov))
    stores = [load(r.bov, r.bo, 0)]

    def grad_block(k):
        return lambda owner: r.gmv.at[k * S:(k + 1) * S, pl.ds(pl.multiple_of(owner * C, C), C)]

    for k in (4, 3, 2, 0, 1):
        total = scatter_total(k).astype(BF)
        r.gmv[k * S:(k + 1) * S, jcols] = total
        r.sqs[...] += squares_of(total.astype(F32))
        share_send(GM + k, grad_block(k))

    r.s1[j] = r.sqs[...]
    for d in range(1, mp):
        go(r.s1.at[j], r.s1.at[j], r.q1s.at[d], r.q1r.at[d], mp=lax.rem(j + d, mp))
    for t in range(NT):
        share_forward(IG + t, half_block(r.igv, t))
    for d in range(1, mp):
        arrived(r.s1.at[lax.rem(j - d + mp, mp)], r.q1r.at[d])
    total = r.s1[0]
    for owner in range(1, mp):
        total = total + r.s1[owner]
    r.s2[i] = total
    for d in range(1, n):
        go(r.s2.at[i], r.s2.at[i], r.q2s.at[d], r.q2r.at[d], dp=lax.rem(i + d, n))
    for k in (4, 3, 2, 0, 1):
        share_forward(GM + k, grad_block(k))
    for d in range(1, n):
        arrived(r.s2.at[lax.rem(i - d + n, n)], r.q2r.at[d])
    total = r.s2[0]
    for owner in range(1, n):
        total = total + r.s2[owner]
    r.sqo[...] = total

    for t in range(NT):
        share_wait(IG + t, half_block(r.igv, t))
    stores.append(load(r.igv, r.ig, 1))
    for k in (4, 3, 2, 0, 1):
        share_wait(GM + k, grad_block(k))
        stores.append(load(r.gmv.at[k * S:(k + 1) * S], r.gmo.at[k], 2 + k))
    for copy in stores:
        copy.wait()
    for copy, when in pending:
        guarded(when, copy.wait_send)


def fused(p, *operands):
    scratch = scratch_of(p)
    names = IN_NAMES + OUT_NAMES + tuple(scratch)
    anywhere = pl.BlockSpec(memory_space=pl.ANY)
    vmem = pl.BlockSpec(memory_space=pltpu.VMEM)
    smem = pl.BlockSpec(memory_space=pltpu.SMEM)
    return pl.pallas_call(
        partial(body, p, names),
        out_shape=(
            jax.ShapeDtypeStruct((p.T, p.D), BF),
            jax.ShapeDtypeStruct((p.T, p.D), BF),
            jax.ShapeDtypeStruct((5, p.S, p.D), BF),
            jax.ShapeDtypeStruct((2, p.F, p.S) if p.FD else (2, p.S, p.F), F32),
            jax.ShapeDtypeStruct((p.F, p.S) if p.FD else (p.S, p.F), F32),
            jax.ShapeDtypeStruct((8, 128), F32),
        ),
        in_specs=[anywhere, anywhere, vmem, smem] + [anywhere] * 5,
        out_specs=(anywhere, anywhere, anywhere, vmem, vmem, vmem),
        scratch_shapes=list(scratch.values()),
        compiler_params=pltpu.CompilerParams(
            collective_id=0, has_side_effects=True, vmem_limit_bytes=VMEM_LIMIT
        ),
    )(*operands)


VMEM_LIMIT = 64 * 2**20 - 2**18


def renew(weight, momentum, shadow, grad, clip_factor):
    clipped = grad * clip_factor
    velocity = MOMENTUM * momentum + clipped
    updated = weight - LEARN_RATE * (clipped + MOMENTUM * velocity)
    average = SHADOW_DECAY * shadow + (1.0 - SHADOW_DECAY) * updated
    return (velocity, average, updated)


def update_body(cuts, *refs):
    kinds, pieces = len(cuts), sum(len(c) for c in cuts)
    sq, carried = refs[0], refs[1:3]
    ins = [refs[3 + 4 * w:7 + 4 * w] for w in range(kinds)]
    refs = refs[3 + 4 * kinds:]
    norm_out, carried_out = refs[0], refs[1:3]
    outs = [refs[3 + 3 * w:6 + 3 * w] for w in range(kinds)]
    refs = refs[3 + 3 * kinds:]
    held = [refs[4 * w:4 * w + 4] for w in range(kinds)]
    made = [refs[4 * kinds + 3 * w:4 * kinds + 3 * w + 3] for w in range(kinds)]
    bounce, (in_sem, out_sem, carry_sem) = refs[7 * kinds:7 * kinds + 2], refs[7 * kinds + 2:]
    order = [(w, c) for w in range(kinds) for c in range(len(cuts[w]))]
    loads, copies = {}, []

    def load_piece(at):
        if at < len(order):
            w, c = order[at]
            loads[at] = [
                pltpu.make_async_copy(ins[w][a].at[cuts[w][c]], held[w][a].at[cuts[w][c]], in_sem.at[at, a]) for a in range(4)
            ]
            for copy in loads[at]:
                copy.start()

    def store(src, dst, sem):
        copies.append(pltpu.make_async_copy(src, dst, sem))
        copies[-1].start()

    for at in range(AHEAD):
        load_piece(at)
    carry = [pltpu.make_async_copy(carried[a], bounce[a], carry_sem.at[a]) for a in range(2)]
    carry[0].start()
    norm = jnp.sqrt(jnp.broadcast_to(jnp.sum(sq[...]), (8, 128)))
    norm_out[0, 0] = jnp.max(norm)
    clip_factor = 1.0 / jnp.maximum(jnp.max(norm), 1.0)
    for at, (w, c) in enumerate(order):
        cut = cuts[w][c]
        for copy in loads[at]:
            copy.wait()
        new = renew(*[held[w][a][cut] for a in range(3)], held[w][3][cut].astype(F32), clip_factor)
        for a in range(3):
            made[w][a][cut] = new[a]
            store(made[w][a].at[cut], outs[w][a].at[cut], out_sem.at[at, a])
        load_piece(at + AHEAD)
        if at in (1, 3):
            a = at // 2
            carry[a].wait()
            store(bounce[a], carried_out[a], carry_sem.at[2 + a])
            if a == 0:
                carry[1].start()
    for copy in copies:
        copy.wait()


AHEAD = 3


def update(sq, carried, weights):
    cuts = [[c for c in range(g[0].shape[0])] if g[0].ndim == 3 else [slice(None)] for g in weights]
    pieces = sum(len(c) for c in cuts)
    anywhere = pl.BlockSpec(memory_space=pl.ANY)
    vmem = pl.BlockSpec(memory_space=pltpu.VMEM)
    flat_in = [a for group in weights for a in group]
    flat_out = [a for group in weights for a in group[:3]]
    dma = pltpu.SemaphoreType.DMA
    size = sum(a.size * a.dtype.itemsize for a in flat_in + flat_out + 2 * list(carried))
    return pl.pallas_call(
        partial(update_body, cuts),
        out_shape=[jax.ShapeDtypeStruct((1, 1), F32)] + [jax.ShapeDtypeStruct(a.shape, a.dtype) for a in [*carried, *flat_out]],
        in_specs=[vmem] + [anywhere] * (2 + len(flat_in)),
        out_specs=[pl.BlockSpec(memory_space=pltpu.SMEM)] + [anywhere] * (2 + len(flat_out)),
        scratch_shapes=[pltpu.VMEM(a.shape, a.dtype) for a in flat_in + flat_out + list(carried)]
        + [dma((pieces, 4)), dma((pieces, 3)), dma((4,))],
        cost_estimate=pl.CostEstimate(flops=size, bytes_accessed=size, transcendentals=0),
        compiler_params=pltpu.CompilerParams(vmem_limit_bytes=VMEM_LIMIT),
    )(sq, *carried, *flat_in)


def turn_tables(tokens):
    theta = np.float32(10000.0) ** (-np.arange(HEAD, dtype=np.float32) / np.float32(HEAD))
    angle = np.arange(tokens, dtype=np.float32)[:, None] * theta.astype(np.float32)[None, :]
    angle = angle.astype(np.float64)
    return np.cos(angle).astype(np.float32), np.sin(angle).astype(np.float32)


def per_device(mesh, block_input, segment_ids, live_length, output_grad, mixer_weight, mixer_momentum, mixer_shadow,
               expand_weight, expand_momentum, expand_shadow, shrink_weight, shrink_momentum, shrink_shadow):
    rows, length, width = block_input.shape
    p = plan_of(mesh, length, width, shrink_weight.shape[0])
    turn = (lambda v: jnp.swapaxes(v, -1, -2)) if p.FD else (lambda v: v)
    if p.FD:
        shards = (turn(expand_weight), shrink_weight)
    else:
        shards = (jnp.concatenate([shrink_weight.T[None], expand_weight], axis=0).astype(BF), shrink_weight)
    cos, sin = turn_tables(length)
    out, grad_in, gm, ge, gs, sq = fused(
        p, block_input[0], output_grad[0], segment_ids, live_length, jnp.asarray(cos), jnp.asarray(sin), mixer_weight, *shards
    )
    new = update(sq, (out, grad_in), (
        (mixer_weight, mixer_momentum, mixer_shadow, gm),
        (turn(expand_weight), turn(expand_momentum), turn(expand_shadow), ge),
        (shrink_weight, shrink_momentum, shrink_shadow, gs if p.FD else gs.T),
    ))
    norm, out, grad_in = new[:3]
    return (out[None], grad_in[None], norm[0, 0], *new[3:6], *(turn(v) for v in new[6:9]), *new[9:12])


def solution(mesh):
    row, mixer, expand, shrink = P("dp", None, None), P(None, "dp", None), P(None, "dp", "mp"), P("mp", "dp")
    return jax.shard_map(
        partial(per_device, mesh),
        mesh=mesh,
        in_specs=(row, P("dp", None), P("dp"), row) + (mixer,) * 3 + (expand,) * 3 + (shrink,) * 3,
        out_specs=(row, row, P()) + (mixer,) * 3 + (expand,) * 3 + (shrink,) * 3,
        check_vma=False,
    )
```
